32 devices in a mesh: dp: 16 (over z, y, core), tensor: 2 (over x).
Axes of the slice: x: 2, y: 2, z: 4, core: 2. Of those that a mesh axis runs over, the one named last changes fastest.
Arguments:
- tokens: bfloat16 [32768, 768], P(('dp', 'tensor')), may hold values from -6 to 6
- grad_values: bfloat16 [32768, 768], P(('dp', 'tensor')), may hold values from -6 to 6
- span_starts: int32 [64, 13], P('dp'), may hold values from 0 to 506
- w_qkv: bfloat16 [768, 3, 768], P(None, None, 'tensor'), may hold values from -0.21875 to 0.21875
- b_qv: float32 [2, 768], P(None, 'tensor'), may hold values from -3 to 3
- w_out: bfloat16 [768, 768], P('tensor'), may hold values from -0.875 to 0.875
- b_out: float32 [768], replicated, may hold values from -3 to 3
- ln1_gain: float32 [768], replicated, may hold values from 0.5 to 1.5
- ln1_bias: float32 [768], replicated, may hold values from -3 to 3
- w_in: bfloat16 [768, 3072], P(None, 'tensor'), may hold values from -0.21875 to 0.21875
- b_in: float32 [3072], P('tensor'), may hold values from -3 to 3
- w_down: bfloat16 [3072, 768], P('tensor'), may hold values from -0.109375 to 0.109375
- b_down: float32 [768], replicated, may hold values from -3 to 3
- ln2_gain: float32 [768], replicated, may hold values from 0.5 to 1.5
- ln2_bias: float32 [768], replicated, may hold values from -3 to 3
Outputs:
- mixed: bfloat16 [32768, 768], P(('dp', 'tensor'))
- d_tokens: float32 [32768, 768], P(('dp', 'tensor'))
- d_w_qkv: float32 [768, 3, 768], P(None, None, 'tensor')
- d_b_qv: float32 [2, 768], P(None, 'tensor')
- d_w_out: float32 [768, 768], P('tensor')
- d_b_out: float32 [768], replicated
- d_ln1_gain: float32 [768], replicated
- d_ln1_bias: float32 [768], replicated
- d_w_in: float32 [768, 3072], P(None, 'tensor')
- d_b_in: float32 [3072], P('tensor')
- d_w_down: float32 [3072, 768], P('tensor')
- d_b_down: float32 [768], replicated
- d_ln2_gain: float32 [768], replicated
- d_ln2_bias: float32 [768], replicated
The draws below stay inside these ranges and needn't reach their ends.
Inputs may be any that keep to these rules, and one draw needn't show every extreme that they name: `span_starts`: a span covers 6 positions from its start, within its sequence; spans of one sequence may intersect.
All inputs are finite; a program needn't handle non-finite values.
Results may differ from the reference program's by a relative error of at most 0.013.
The reference program's roundings to bfloat16 on the way count: a program that leaves them out, or rounds other values in their place, can miss the bound.
Values may be sent and summed in bfloat16 or wider, within the bound.
No kernel may reach another device: no remote copies, remote signals or barrier semaphores. Data moves between devices by JAX's collectives and lax.ppermute only.
A program may use at most 192 MiB of HBM per device.

```python
import jax
import jax.numpy as jnp
from jax import lax

D = 768
HEADS = 12
HEAD = 64
FF = 3072
LENGTH = 512
SEQ_DEV = 4
SPANS = 13
SPAN = 6
SEQS = 64
TOKENS = 32768


def touch_ends(values, own_key, least, top_value):
    longest = values.shape.index(max(values.shape))
    spots = []
    for shift in (0, 1):
        where = [jax.random.randint(jax.random.fold_in(own_key, axis), (), 0, length) for axis, length in enumerate(values.shape)]
        where[longest] = (where[longest] + shift) % values.shape[longest]
        spots.append(tuple(where))
    return values.at[spots[0]].set(least).at[spots[1]].set(top_value)


def shard_levels(own_key, shape, cuts, smallest, top_value):
    gain, own = 1.0, jax.random.fold_in(own_key, 6)
    for axis_at, blocks in cuts:
        heights = jnp.exp(jax.random.uniform(jax.random.fold_in(own, axis_at), (blocks,), jnp.float32, smallest / len(cuts), top_value / len(cuts)))
        gain = gain * jnp.repeat(heights, shape[axis_at] // blocks).reshape([-1 if axis == axis_at else 1 for axis in range(len(shape))])
    return gain


def bell_draw(own_key, dims, scale, reach, shards=(), kind=jnp.bfloat16):
    values = scale * jax.random.normal(own_key, dims, jnp.float32)
    if shards:
        values = values * shard_levels(own_key, dims, shards, -0.22, 0.18)
    return jnp.clip(values, -reach, reach).astype(kind)


def setup_inputs(seed: int = 0) -> dict:
    key_of = jax.random.split(jax.random.key(seed), 16)
    return {
        "tokens": bell_draw(key_of[0], (TOKENS, D), 1.0, 6.0, ((0, 32),)),
        "grad_values": bell_draw(key_of[1], (TOKENS, D), 1.0, 6.0, ((0, 32),)),
        "span_starts": touch_ends(jax.random.randint(key_of[2], (SEQS, SPANS), 0, LENGTH - SPAN + 1), jax.random.fold_in(key_of[2], 1), 0, LENGTH - SPAN).astype(jnp.int32),
        "w_qkv": bell_draw(key_of[3], (D, 3, D), D ** -0.5, 0.21875, ((2, 2),)),
        "b_qv": bell_draw(key_of[4], (2, D), 0.5, 3.0, ((1, 2),), jnp.float32),
        "w_out": bell_draw(key_of[5], (D, D), (D // 16) ** -0.5, 0.875, ((0, 2),)),
        "b_out": bell_draw(key_of[6], (D,), 0.5, 3.0, (), jnp.float32),
        "ln1_gain": jnp.clip(1.0 + 0.1 * jax.random.normal(key_of[7], (D,), jnp.float32), 0.5, 1.5),
        "ln1_bias": bell_draw(key_of[8], (D,), 0.5, 3.0, (), jnp.float32),
        "w_in": bell_draw(key_of[9], (D, FF), D ** -0.5, 0.21875, ((1, 2),)),
        "b_in": bell_draw(key_of[10], (FF,), 0.5, 3.0, ((0, 2),), jnp.float32),
        "w_down": bell_draw(key_of[11], (FF, D), FF ** -0.5, 0.109375, ((0, 2),)),
        "b_down": bell_draw(key_of[12], (D,), 0.5, 3.0, (), jnp.float32),
        "ln2_gain": jnp.clip(1.0 + 0.1 * jax.random.normal(key_of[13], (D,), jnp.float32), 0.5, 1.5),
        "ln2_bias": bell_draw(key_of[14], (D,), 0.5, 3.0, (), jnp.float32),
    }


EPSILON = 1e-05
PRECISE = lax.Precision.HIGHEST

@jax.custom_vjp
def low(v):
    return lax.optimization_barrier(v.astype(jnp.bfloat16)).astype(jnp.float32)

@jax.custom_vjp
def low_back(v):
    return v

def low_keep(v):
    return (low(v), None)

def low_pass(kept, grad):
    return (grad,)

def back_keep(v):
    return (v, None)

def back_low(kept, grad):
    return (low(grad),)
low.defvjp(low_keep, low_pass)
low_back.defvjp(back_keep, back_low)

def product(left, right):
    return jnp.dot(left, right, precision=PRECISE)

def layer_norm(values, gain_vec, bias_vec):
    average = lax.optimization_barrier(jnp.mean(values, axis=-1, keepdims=True))
    centered = values - average
    variance = lax.optimization_barrier(jnp.mean(centered * centered, axis=-1, keepdims=True))
    return centered * lax.rsqrt(variance + EPSILON) * gain_vec + bias_vec

def attend(packed):
    queries = packed[:, 0]
    keys_seq = packed[:, 1]
    values_seq = packed[:, 2]
    scores = jnp.einsum('qhe,khe->hqk', queries, keys_seq, precision=PRECISE) * HEAD ** (-0.5)
    scores = low_back(scores)
    attn_weights = low(jax.nn.softmax(scores, axis=-1))
    context = jnp.einsum('hqk,khe->qhe', attn_weights, values_seq, precision=PRECISE)
    return context.reshape(LENGTH, D)

def forward(tokens_f, w_qkv, b_qv, w_out, b_out, ln1_gain, ln1_bias, w_in, b_in, w_down, b_down, ln2_gain, ln2_bias):
    row_count = tokens_f.shape[0]
    projected = product(tokens_f, w_qkv.reshape(D, 3 * D)).reshape(row_count, 3, D)
    qkv_bias = jnp.stack([b_qv[0], jnp.zeros_like(b_qv[0]), b_qv[1]])
    qkv = low(low_back(projected + qkv_bias))
    qkv = qkv.reshape(row_count // LENGTH, LENGTH, 3, HEADS, HEAD)
    context = lax.map(jax.checkpoint(attend), qkv).reshape(row_count, D)
    context = low(low_back(context))
    branch = low_back(product(context, w_out) + b_out)
    normed = layer_norm(tokens_f + branch, ln1_gain, ln1_bias)
    pre_act = low_back(product(low(normed), w_in) + b_in)
    hidden = low(jax.nn.gelu(pre_act, approximate=True))
    ffn_out = low_back(product(hidden, w_down) + b_down)
    return layer_norm(normed + ffn_out, ln2_gain, ln2_bias)

def span_mask_of(span_starts):
    positions = jnp.arange(LENGTH, dtype=jnp.int32)
    begins = span_starts[:, :, None]
    inside = (positions[None, None, :] >= begins) & (positions[None, None, :] < begins + SPAN)
    return jnp.any(inside, axis=1).astype(jnp.float32)

def reference(tokens, grad_values, span_starts, w_qkv, b_qv, w_out, b_out, ln1_gain, ln1_bias, w_in, b_in, w_down, b_down, ln2_gain, ln2_bias):
    weights = (w_qkv, b_qv, w_out, b_out, ln1_gain, ln1_bias, w_in, b_in, w_down, b_down, ln2_gain, ln2_bias)
    weights = tuple((item.astype(jnp.float32) for item in weights))
    group = SEQ_DEV * LENGTH
    groups = TOKENS // group
    token_groups = tokens.astype(jnp.float32).reshape(groups, group, D)
    span_mask = span_mask_of(span_starts).reshape(groups, group, 1)
    cotangent = grad_values.astype(jnp.float32).reshape(groups, group, D) * span_mask

    def scan_step(totals, inputs):
        tokens_f, grad_f = inputs
        result, pullback = jax.vjp(forward, tokens_f, *weights)
        gradients = pullback(grad_f)
        totals = tuple((old + new for old, new in zip(totals, gradients[1:])))
        return (totals, (result.astype(jnp.bfloat16), gradients[0]))
    start_totals = tuple((jnp.zeros_like(item) for item in weights))
    totals, (mixed, d_tokens) = lax.scan(scan_step, start_totals, (token_groups, cotangent))
    return (mixed.reshape(TOKENS, D), d_tokens.reshape(TOKENS, D), totals[0], totals[1], totals[2], totals[3], totals[4], totals[5], totals[6], totals[7], totals[8], totals[9], totals[10], totals[11])
```

```python
import jax
import jax.numpy as jnp
from jax import lax
from jax.experimental import pallas as pl
from jax.experimental.pallas import tpu as pltpu
from jax.sharding import PartitionSpec as P

HEAD = 64
SPAN = 6
LANES = 128
EPSILON = 1e-05
F32 = jnp.float32
BF16 = jnp.bfloat16
VMEM_LIMIT = 48 * 1024 * 1024


def flip(values, bit):
    size = lax.axis_size("dp")
    return lax.ppermute(values, "dp", [(at, at ^ (1 << bit)) for at in range(size)])


def flip_tensor(values):
    return lax.ppermute(values, "tensor", [(0, 1), (1, 0)])


def my_bit(bit):
    return (lax.axis_index("dp") >> bit) & 1


def in_order(mine, theirs, bit, axis=0):
    upper = my_bit(bit) == 1
    first = jnp.where(upper, theirs, mine)
    second = jnp.where(upper, mine, theirs)
    return jnp.concatenate([first, second], axis=axis)


def gather_other(shard, bits):
    rows = shard.shape[0]
    pieces = 1 << len(bits)
    place = sum(my_bit(bit) << (len(bits) - 1 - at) for at, bit in enumerate(bits))
    piece = lax.dynamic_slice_in_dim(shard, place * (rows // pieces), rows // pieces, 0)
    held = flip_tensor(piece)
    for bit in reversed(bits):
        held = in_order(held, flip(held, bit), bit)
    return held


def split_by(values, bit):
    halves = values.reshape((2, values.shape[0] // 2) + values.shape[1:])
    at = my_bit(bit)
    keep = lax.dynamic_index_in_dim(halves, at, 0, keepdims=False)
    send = lax.dynamic_index_in_dim(halves, 1 - at, 0, keepdims=False)
    return keep, send


def scatter_sum(values, bit):
    keep, send = split_by(values, bit)
    return keep + flip(send.astype(BF16), bit).astype(F32)


def spread(values, bits):
    held = lax.optimization_barrier(values.astype(BF16))
    for bit in bits:
        held = in_order(held, flip(held, bit), bit)
    return held


def lane_halves(rows):
    return lax.broadcasted_iota(jnp.int32, (rows, LANES), 1) < HEAD


def dot_nt(left, right):
    return lax.dot_general(left, right, (((1,), (1,)), ((), ())), preferred_element_type=F32)


def dot_tn(left, right):
    return lax.dot_general(left, right, (((0,), (0,)), ((), ())), preferred_element_type=F32)


def two_heads(block):
    low = lane_halves(block.shape[0])
    zero = jnp.zeros_like(block)
    return jnp.concatenate([jnp.where(low, block, zero), jnp.where(low, zero, block)], axis=0)


def softmax_rows(scores):
    exponent = jnp.exp(scores - jnp.max(scores, axis=-1, keepdims=True))
    return exponent * (1.0 / jnp.sum(exponent, axis=-1, keepdims=True))


def attend_kernel(q_ref, k_ref, v_ref, out_ref):
    rows = q_ref.shape[0]
    low = lane_halves(rows)
    both = two_heads(q_ref[...])
    probs = softmax_rows(dot_nt(both, k_ref[...]) * HEAD ** (-0.5)).astype(BF16)
    mixed = jnp.dot(probs, v_ref[...], preferred_element_type=F32)
    out_ref[...] = jnp.where(low, mixed[:rows], mixed[rows:]).astype(BF16)


def attend(queries, keys, values, seqs):
    q_rows, length, inner = queries.shape[0] // seqs, keys.shape[0] // seqs, keys.shape[1]
    tile = min(q_rows, 256)
    tiles = q_rows // tile
    q_spec = pl.BlockSpec((tile, LANES), lambda s, j, i: (s * tiles + i, j))
    kv_spec = pl.BlockSpec((length, LANES), lambda s, j, i: (s, j))
    return pl.pallas_call(
        attend_kernel,
        grid=(seqs, inner // LANES, tiles),
        in_specs=[q_spec, kv_spec, kv_spec],
        out_specs=q_spec,
        out_shape=jax.ShapeDtypeStruct(queries.shape, BF16),
        compiler_params=pltpu.CompilerParams(vmem_limit_bytes=VMEM_LIMIT),
        cost_estimate=pl.CostEstimate(
            flops=16 * q_rows * length * inner * seqs,
            bytes_accessed=2 * (2 * queries.size + 2 * keys.size),
            transcendentals=seqs * q_rows * length * inner // HEAD,
        ),
    )(queries, keys, values)


def attend_back_kernel(q_ref, k_ref, v_ref, g_ref, dq_ref, dk_ref, dv_ref):
    rows = q_ref.shape[0]
    low = lane_halves(rows)
    both, grads = two_heads(q_ref[...]), two_heads(g_ref[...])
    probs = softmax_rows(dot_nt(both, k_ref[...]) * HEAD ** (-0.5))
    grad_probs = dot_nt(grads, v_ref[...])
    dv_ref[...] = dot_tn(probs.astype(BF16), grads).astype(BF16)
    row_total = jnp.sum(grad_probs * probs, axis=-1, keepdims=True)
    grad_scores = (probs * (grad_probs - row_total)).astype(BF16)
    dq = jnp.dot(grad_scores, k_ref[...], preferred_element_type=F32) * HEAD ** (-0.5)
    dq_ref[...] = jnp.where(low, dq[:rows], dq[rows:]).astype(BF16)
    dk_ref[...] = (dot_tn(grad_scores, both) * HEAD ** (-0.5)).astype(BF16)


def attend_back(queries, keys, values, grads, seqs):
    q_rows, length, inner = queries.shape[0] // seqs, keys.shape[0] // seqs, keys.shape[1]
    q_spec = pl.BlockSpec((q_rows, LANES), lambda s, j: (s, j))
    kv_spec = pl.BlockSpec((length, LANES), lambda s, j: (s, j))
    return pl.pallas_call(
        attend_back_kernel,
        grid=(seqs, inner // LANES),
        in_specs=[q_spec, kv_spec, kv_spec, q_spec],
        out_specs=[q_spec, kv_spec, kv_spec],
        out_shape=[
            jax.ShapeDtypeStruct(queries.shape, BF16),
            jax.ShapeDtypeStruct(keys.shape, BF16),
            jax.ShapeDtypeStruct(keys.shape, BF16),
        ],
        compiler_params=pltpu.CompilerParams(vmem_limit_bytes=VMEM_LIMIT),
        cost_estimate=pl.CostEstimate(
            flops=40 * q_rows * length * inner * seqs,
            bytes_accessed=2 * (3 * queries.size + 4 * keys.size),
            transcendentals=seqs * q_rows * length * inner // HEAD,
        ),
    )(queries, keys, values, grads)


def norm_rows(values):
    average = jnp.mean(values, axis=-1, keepdims=True)
    centered = values - average
    variance = jnp.mean(centered * centered, axis=-1, keepdims=True)
    root = lax.rsqrt(variance + EPSILON)
    return centered * root, root


def norm_back(grad, unit, root, gain):
    grad_y = grad * gain
    inner = jnp.mean(grad_y, axis=-1, keepdims=True)
    along = jnp.mean(grad_y * unit, axis=-1, keepdims=True)
    return root * (grad_y - inner - unit * along)


def gelu(values):
    return jax.nn.gelu(values, approximate=True)


def gelu_and_slope(values):
    gate, pull = jax.vjp(gelu, values)
    return gate, pull(jnp.ones_like(values))[0]


def mm(left, right):
    return jnp.dot(left, right, preferred_element_type=F32)


def body(
    tokens,
    grad_values,
    span_starts,
    w_qkv,
    b_qv,
    w_out,
    b_out,
    ln1_gain,
    ln1_bias,
    w_in,
    b_in,
    w_down,
    b_down,
    ln2_gain,
    ln2_bias,
):
    rows, width = tokens.shape
    inner = w_qkv.shape[2]
    hidden_half = w_in.shape[1]
    halves = lax.axis_size("tensor")
    seqs = span_starts.shape[0] // halves
    spans = span_starts.shape[1]
    length = rows // seqs
    half_at = lax.axis_index("tensor")
    dp_size = lax.axis_size("dp")
    bits = dp_size.bit_length() - 1

    w_qkv_own = jnp.transpose(w_qkv, (1, 0, 2)).reshape(3 * width, inner)
    bias_pack = jnp.concatenate([b_qv[0], b_qv[1], b_in]).reshape(-1, LANES)
    bias_other = flip_tensor(bias_pack).reshape(-1)
    w_qkv_oth = gather_other(w_qkv_own, (0, 2, 1))
    w_out_oth = gather_other(w_out, (0, 1, 2))
    w_in_oth = gather_other(w_in, (0, 2, 1))
    w_down_oth = gather_other(w_down, (0, 1, 2))
    w_qkv_both = [w_qkv_own.reshape(3, width, inner), w_qkv_oth.reshape(3, width, inner)]
    w_out_both = [w_out, w_out_oth]
    w_in_both = [w_in, w_in_oth]
    w_down_both = [w_down, w_down_oth]
    b_q_both = [b_qv[0], bias_other[:inner]]
    b_v_both = [b_qv[1], bias_other[inner : 2 * inner]]
    b_in_both = [b_in, bias_other[2 * inner :]]

    starts = lax.dynamic_slice_in_dim(span_starts, half_at * seqs, seqs, 0)
    places = starts[:, :, None] + jnp.arange(SPAN, dtype=jnp.int32)
    earlier = jnp.tril(jnp.ones((spans, spans), jnp.bool_), -1)
    covered = (places[:, :, :, None] >= starts[:, None, None, :]) & (
        places[:, :, :, None] < starts[:, None, None, :] + SPAN
    )
    fresh = ~jnp.any(covered & earlier[None, :, None, :], axis=-1)
    slots = -(-spans * SPAN // 16) * 16
    pad = slots - spans * SPAN
    places = jnp.pad(places.reshape(seqs, spans * SPAN), ((0, 0), (0, pad)))
    fresh = jnp.pad(fresh.reshape(seqs, spans * SPAN), ((0, 0), (0, pad)))
    picks = (places[:, :, None] == jnp.arange(length, dtype=jnp.int32)).astype(BF16)
    few = seqs * slots

    def pick(values):
        return jnp.einsum(
            "srt,std->srd", picks, values.reshape(seqs, length, width), preferred_element_type=F32
        ).reshape(few, width)

    tokens_few = pick(tokens).astype(BF16)
    grad_few = pick(grad_values) * fresh.reshape(few, 1).astype(F32)

    keys, values, queries_few, context_few = [], [], [], []
    for at in range(2):
        w_q, w_k, w_v = w_qkv_both[at][0], w_qkv_both[at][1], w_qkv_both[at][2]
        keys.append(mm(tokens, w_k).astype(BF16))
        values.append((mm(tokens, w_v) + b_v_both[at]).astype(BF16))
        queries_few.append((mm(tokens_few, w_q) + b_q_both[at]).astype(BF16))
        context_few.append(attend(queries_few[at], keys[at], values[at], seqs))
    branch_few = mm(context_few[0], w_out_both[0]) + mm(context_few[1], w_out_both[1]) + b_out
    unit_one, root_one = norm_rows(tokens_few.astype(F32) + branch_few)
    normed_few = unit_one * ln1_gain + ln1_bias
    normed_low = normed_few.astype(BF16)
    pre_few = [mm(normed_low, w_in_both[at]) + b_in_both[at] for at in range(2)]
    gates = [gelu_and_slope(pre) for pre in pre_few]
    ffn_few = mm(gates[0][0].astype(BF16), w_down) + mm(gates[1][0].astype(BF16), w_down_oth) + b_down
    unit_two, root_two = norm_rows(normed_few + ffn_few)

    g_second = norm_back(grad_few, unit_two, root_two, ln2_gain)
    d_ln2_gain = jnp.sum(grad_few * unit_two, axis=0)
    d_ln2_bias = jnp.sum(grad_few, axis=0)
    g_ffn = g_second.astype(BF16)
    d_b_down = jnp.sum(g_ffn.astype(F32), axis=0)

    def plane(values):
        values = jnp.concatenate([values, flip_tensor(values)], axis=0)
        values = jnp.concatenate([values, flip(values, 1)], axis=0)
        return jnp.concatenate([values, flip(values, 0)], axis=0)

    quarter = hidden_half // 4
    quarter_at = (lax.axis_index("dp") & 3) * quarter
    w_in_slice = lax.dynamic_slice_in_dim(w_in, quarter_at, quarter, 1)
    w_down_slice = lax.dynamic_slice_in_dim(w_down, quarter_at, quarter, 0)
    b_in_slice = lax.dynamic_slice_in_dim(b_in, quarter_at, quarter, 0)
    normed_plane = plane(normed_low)
    g_ffn_plane = plane(g_ffn)
    gate_plane, slope_plane = gelu_and_slope(mm(normed_plane, w_in_slice) + b_in_slice)
    d_w_down_slice = dot_tn(gate_plane.astype(BF16), g_ffn_plane)
    g_pre_plane = (slope_plane * dot_nt(g_ffn_plane, w_down_slice)).astype(BF16)
    d_w_in_slice = dot_tn(normed_plane, g_pre_plane)

    g_pre = [
        (gates[at][1] * dot_nt(g_ffn, w_down_both[at])).astype(BF16) for at in range(2)
    ]
    d_b_in = [jnp.sum(g.astype(F32), axis=0) for g in g_pre]
    g_normed = g_second + dot_nt(g_pre[0], w_in_both[0]) + dot_nt(g_pre[1], w_in_both[1])
    g_first = norm_back(g_normed, unit_one, root_one, ln1_gain)
    d_ln1_gain = jnp.sum(g_normed * unit_one, axis=0)
    d_ln1_bias = jnp.sum(g_normed, axis=0)
    g_branch = g_first.astype(BF16)
    d_b_out = jnp.sum(g_branch.astype(F32), axis=0)

    d_w_out, d_w_qkv, d_b_q, d_b_v, grads_qkv = [], [], [], [], []
    for at in range(2):
        d_w_out.append(dot_tn(context_few[at], g_branch))
        g_context = dot_nt(g_branch, w_out_both[at]).astype(BF16)
        dq, dk, dv = attend_back(queries_few[at], keys[at], values[at], g_context, seqs)
        d_b_q.append(jnp.sum(dq.astype(F32), axis=0))
        d_b_v.append(jnp.sum(dv.astype(F32), axis=0))
        d_w_qkv.append([dot_tn(tokens_few, dq), dot_tn(tokens, dk), dot_tn(tokens, dv)])
        grads_qkv.append((dq, dk, dv))

    chip_bits = list(range(2, bits))
    ffn_sums = []
    for local, axis in ((d_w_down_slice, 0), (d_w_in_slice, 1)):
        held = local
        for bit in chip_bits:
            held = scatter_sum(held, bit)
        held = spread(held, list(reversed(chip_bits)))
        for bit in (0, 1):
            held = in_order(held, flip(held, bit), bit, axis)
        ffn_sums.append(held.astype(F32))
    d_w_down, d_w_in = ffn_sums

    def whole_sum(own, other):
        own, other = scatter_sum(own, 0), scatter_sum(other, 0)
        held = own + flip_tensor(other.astype(BF16)).astype(F32)
        for bit in [1] + chip_bits:
            held = scatter_sum(held, bit)
        return spread(held, list(reversed(chip_bits)) + [1, 0]).astype(F32)

    d_w_out_sum = whole_sum(*d_w_out)
    d_w_qkv_sum = jnp.stack([whole_sum(d_w_qkv[0][i], d_w_qkv[1][i]) for i in range(3)], axis=1)

    def placed(parts):
        both = jnp.stack(parts)
        return jnp.where(half_at == 0, both, both[::-1]).reshape(-1)

    sections = [
        placed(d_b_q),
        placed(d_b_v),
        placed(d_b_in),
        d_b_out,
        d_ln1_gain,
        d_ln1_bias,
        d_b_down,
        d_ln2_gain,
        d_ln2_bias,
    ]
    small = jnp.concatenate(sections).reshape(-1, LANES)
    small = small + flip_tensor(small)
    for bit in range(bits):
        small = small + flip(small, bit)
    small = small.reshape(-1)
    cuts, at = [], 0
    for section in sections:
        cuts.append(small[at : at + section.size])
        at += section.size

    def own_half(vector):
        return lax.dynamic_index_in_dim(vector.reshape(2, -1), half_at, 0, keepdims=False)

    d_b_qv = jnp.stack([own_half(cuts[0]), own_half(cuts[1])])
    d_b_in_sum = own_half(cuts[2])

    few_back = g_first
    all_back = None
    for at in range(2):
        dq, dk, dv = grads_qkv[at]
        few_back = few_back + dot_nt(dq, w_qkv_both[at][0])
        part = dot_nt(dk, w_qkv_both[at][1]) + dot_nt(dv, w_qkv_both[at][2])
        all_back = part if all_back is None else all_back + part
    coarse = lax.reduce_precision(few_back, 8, 7)
    fine = (few_back - coarse).astype(BF16)
    pieces = jnp.concatenate(
        [coarse.astype(BF16).reshape(seqs, slots, width), fine.reshape(seqs, slots, width)], axis=1
    )
    spreading = jnp.concatenate([picks, picks], axis=1)
    d_tokens = all_back + jnp.einsum(
        "srt,srd->std", spreading, pieces, preferred_element_type=F32
    ).reshape(rows, width)

    branch = b_out
    for at in range(2):
        queries = (mm(tokens, w_qkv_both[at][0]) + b_q_both[at]).astype(BF16)
        context = attend(queries, keys[at], values[at], seqs)
        branch = branch + mm(context, w_out_both[at])
    unit, _ = norm_rows(tokens.astype(F32) + branch)
    normed = unit * ln1_gain + ln1_bias
    normed_bf = normed.astype(BF16)
    ffn_out = b_down
    for at in range(2):
        hidden = gelu(mm(normed_bf, w_in_both[at]) + b_in_both[at]).astype(BF16)
        ffn_out = ffn_out + mm(hidden, w_down_both[at])
    unit, _ = norm_rows(normed + ffn_out)
    mixed = (unit * ln2_gain + ln2_bias).astype(BF16)

    return (
        mixed,
        d_tokens,
        d_w_qkv_sum,
        d_b_qv,
        d_w_out_sum,
        cuts[3],
        cuts[4],
        cuts[5],
        d_w_in,
        d_b_in_sum,
        d_w_down,
        cuts[6],
        cuts[7],
        cuts[8],
    )


def solution(mesh):
    placed = (
        P(("dp", "tensor"), None),
        P(("dp", "tensor"), None),
        P("dp", None),
        P(None, None, "tensor"),
        P(None, "tensor"),
        P("tensor", None),
        P(),
        P(),
        P(),
        P(None, "tensor"),
        P("tensor"),
        P("tensor", None),
        P(),
        P(),
        P(),
    )
    return jax.shard_map(
        body,
        mesh=mesh,
        in_specs=placed,
        out_specs=(
            P(("dp", "tensor"), None),
            P(("dp", "tensor"), None),
            P(None, None, "tensor"),
            P(None, "tensor"),
            P("tensor", None),
            P(),
            P(),
            P(),
            P(None, "tensor"),
            P("tensor"),
            P("tensor", None),
            P(),
            P(),
            P(),
        ),
        check_vma=False,
    )
```

```python
import functools

import jax
import jax.numpy as jnp
from jax import lax
from jax.experimental import pallas as pl
from jax.experimental.pallas import tpu as pltpu
from jax.sharding import PartitionSpec as P

HEAD = 64
SPAN = 6
LANES = 128
EPSILON = 1e-05
F32 = jnp.float32
BF16 = jnp.bfloat16
GELU_A = (2.0 / 3.141592653589793) ** 0.5
GELU_B = 0.044715
VMEM_LIMIT = 48 * 1024 * 1024


def flip(values, bits):
    size = lax.axis_size("dp")
    return lax.ppermute(values, "dp", [(at, at ^ bits) for at in range(size)])


def flip_tensor(values):
    return lax.ppermute(values, "tensor", [(0, 1), (1, 0)])


def flip_both(values, bits):
    size = 2 * lax.axis_size("dp")
    pairs = [(at, at ^ (2 * bits + 1)) for at in range(size)]
    return lax.ppermute(values, ("dp", "tensor"), pairs)


def settle(values):
    return lax.optimization_barrier(values)


def assemble_kernel(count, place_ref, *refs):
    rows = refs[0].shape[1]
    for at in range(count):
        row = pl.multiple_of(place_ref[at] * rows, rows)
        refs[count][:, pl.ds(row, rows), :] = refs[at][...]


def assemble(pieces, places):
    count = len(pieces)
    lead, rows, columns = pieces[0].shape
    vmem = pl.BlockSpec(memory_space=pltpu.VMEM)
    return pl.pallas_call(
        functools.partial(assemble_kernel, count),
        in_specs=[pl.BlockSpec(memory_space=pltpu.SMEM)] + [vmem] * count,
        out_specs=vmem,
        out_shape=jax.ShapeDtypeStruct((lead, rows * count, columns), pieces[0].dtype),
        compiler_params=params(),
        cost_estimate=cost(0, 4 * count * lead * rows * columns),
    )(jnp.stack(places), *pieces)


def fetch_eighths(shard, me):
    lead, rows, columns = shard.shape
    at = me & 7
    piece = lax.dynamic_index_in_dim(
        shard.reshape(lead, 8, rows // 8, columns), at, 1, keepdims=False
    )
    first = flip_tensor(piece)
    held = [first, flip(first, 2), flip(first, 4), flip(first, 6)]
    near = [flip(item, 1) for item in held]
    places = [at ^ 2 * i for i in range(4)] + [at ^ (2 * i + 1) for i in range(4)]
    return assemble(held + near, places)


def fetch_halves(shard, me):
    lead, rows, columns = shard.shape
    at = me & 1
    piece = lax.dynamic_index_in_dim(
        shard.reshape(lead, 2, rows // 2, columns), at, 1, keepdims=False
    )
    first = flip_tensor(piece)
    return assemble([first, flip(first, 1)], [at, 1 - at])


def dot_nt(left, right):
    return lax.dot_general(left, right, (((1,), (1,)), ((), ())), preferred_element_type=F32)


def dot_tn(left, right):
    return lax.dot_general(left, right, (((0,), (0,)), ((), ())), preferred_element_type=F32)


def mm(left, right):
    return jnp.dot(left, right, preferred_element_type=F32)


def lane_halves(rows):
    return lax.broadcasted_iota(jnp.int32, (rows, LANES), 1) < HEAD


def two_heads(block):
    low = lane_halves(block.shape[0])
    zero = jnp.zeros_like(block)
    return jnp.concatenate([jnp.where(low, block, zero), jnp.where(low, zero, block)], axis=0)


def scaled(queries):
    return queries * jnp.asarray(HEAD ** (-0.5), BF16)


def softmax_rows(scores):
    exponent = jnp.exp(scores - jnp.max(scores, axis=-1, keepdims=True))
    return exponent * (1.0 / jnp.sum(exponent, axis=-1, keepdims=True))


def attend_block(queries, keys, values):
    rows = queries.shape[0]
    probs = softmax_rows(dot_nt(two_heads(scaled(queries)), keys)).astype(BF16)
    mixed = mm(probs, values)
    return jnp.where(lane_halves(rows), mixed[:rows], mixed[rows:]).astype(BF16)


def norm_rows(values):
    average = jnp.mean(values, axis=-1, keepdims=True)
    centered = values - average
    variance = jnp.mean(centered * centered, axis=-1, keepdims=True)
    root = lax.rsqrt(variance + EPSILON)
    return centered * root, root


def norm_back(grad, unit, root, gain):
    grad_y = grad * gain
    inner = jnp.mean(grad_y, axis=-1, keepdims=True)
    along = jnp.mean(grad_y * unit, axis=-1, keepdims=True)
    return root * (grad_y - inner - unit * along)


def gelu_and_slope(values):
    square = values * values
    bent = jnp.tanh(GELU_A * values * (1.0 + GELU_B * square))
    half = 0.5 * (1.0 + bent)
    slope = half + 0.5 * values * (1.0 - bent * bent) * GELU_A * (1.0 + 3.0 * GELU_B * square)
    return values * half, slope


def gelu(values):
    return 0.5 * values * (1.0 + jnp.tanh(GELU_A * values * (1.0 + GELU_B * values * values)))


def params(limit=VMEM_LIMIT):
    return pltpu.CompilerParams(vmem_limit_bytes=limit)


def cost(flops, moved, transcendentals=0):
    return pl.CostEstimate(
        flops=int(flops), bytes_accessed=int(moved), transcendentals=int(transcendentals)
    )


def whole(shape):
    return pl.BlockSpec(shape, lambda *at: (0,) * len(shape))


def project_kernel(tok_ref, few_ref, w_ref, bias_ref, k_ref, v_ref, q_ref, ctx_ref):
    tok = tok_ref[...]
    k_ref[...] = mm(tok, w_ref[1]).astype(BF16)
    v_ref[...] = (mm(tok, w_ref[2]) + bias_ref[1:2, :]).astype(BF16)
    q_ref[...] = (mm(few_ref[...], w_ref[0]) + bias_ref[0:1, :]).astype(BF16)
    for at in range(0, k_ref.shape[1], LANES):
        cut = slice(at, at + LANES)
        ctx_ref[:, cut] = attend_block(q_ref[:, cut], k_ref[:, cut], v_ref[:, cut])


def project(tokens, few, weights, bias, seqs):
    rows, width = tokens.shape
    inner = weights.shape[2]
    length, slots = rows // seqs, few.shape[0] // seqs
    long, short = (
        pl.BlockSpec((size, inner), lambda s: (s, 0)) for size in (length, slots)
    )
    return pl.pallas_call(
        project_kernel,
        grid=(seqs,),
        in_specs=[
            pl.BlockSpec((length, width), lambda s: (s, 0)),
            pl.BlockSpec((slots, width), lambda s: (s, 0)),
            whole(weights.shape),
            whole(bias.shape),
        ],
        out_specs=[long, long, short, short],
        out_shape=[jax.ShapeDtypeStruct((rows, inner), BF16)] * 2
        + [jax.ShapeDtypeStruct((few.shape[0], inner), BF16)] * 2,
        compiler_params=params(),
        cost_estimate=cost(
            2 * rows * width * inner * 3, 2 * (rows * width + 3 * width * inner + 2 * rows * inner)
        ),
    )(tokens, few, weights, bias)


def first_norm_kernel(
    ctx_a, ctx_b, w_a, w_b, few_ref, vec_ref, normed_ref, low_ref, unit_ref, root_ref
):
    branch = mm(ctx_a[...], w_a[...]) + mm(ctx_b[...], w_b[...]) + vec_ref[0:1, :]
    unit, root = norm_rows(few_ref[...].astype(F32) + branch)
    normed = unit * vec_ref[1:2, :] + vec_ref[2:3, :]
    normed_ref[...] = normed
    low_ref[...] = normed.astype(BF16)
    unit_ref[...] = unit
    root_ref[...] = jnp.broadcast_to(root, root_ref.shape)


def first_norm(contexts, w_out, few, vectors):
    count, width = few.shape
    return pl.pallas_call(
        first_norm_kernel,
        out_shape=[
            jax.ShapeDtypeStruct((count, width), F32),
            jax.ShapeDtypeStruct((count, width), BF16),
            jax.ShapeDtypeStruct((count, width), F32),
            jax.ShapeDtypeStruct((count, LANES), F32),
        ],
        compiler_params=params(),
        cost_estimate=cost(2 * count * width * width, 2 * width * width + 14 * count * width),
    )(*contexts, *w_out, few, vectors)


def ffn_kernel(
    low_ref, normed_ref, grad_ref, vec_ref, wi_a, wi_b, bi_a, bi_b, wd_a, wd_b,
    slope_a, slope_b, g_ffn_ref, g_second_ref, sums_ref, total,
):
    step = pl.program_id(0)
    low = low_ref[...]
    part = None
    for w_in, b_in, w_down, slope_ref in ((wi_a, bi_a, wd_a, slope_a), (wi_b, bi_b, wd_b, slope_b)):
        gate, slope = gelu_and_slope(mm(low, w_in[...]) + b_in[...])
        slope_ref[...] = slope
        own = mm(gate.astype(BF16), w_down[...])
        part = own if part is None else part + own

    @pl.when(step == 0)
    def _():
        total[...] = part

    @pl.when(step > 0)
    def _():
        total[...] += part

    @pl.when(step == pl.num_programs(0) - 1)
    def _():
        unit, root = norm_rows(normed_ref[...] + total[...] + vec_ref[0:1, :])
        grad = grad_ref[...]
        g_second = norm_back(grad, unit, root, vec_ref[1:2, :])
        g_ffn = g_second.astype(BF16)
        g_second_ref[...] = g_second
        g_ffn_ref[...] = g_ffn
        sums_ref[...] = jnp.concatenate(
            [
                jnp.sum(grad * unit, axis=0, keepdims=True),
                jnp.sum(grad, axis=0, keepdims=True),
                jnp.sum(g_ffn.astype(F32), axis=0, keepdims=True),
                jnp.zeros((5, grad.shape[1]), F32),
            ],
            axis=0,
        )


def ffn_forward(low, normed, grad, vectors, w_in, b_in, w_down):
    count, width = low.shape
    hidden = w_in[0].shape[1]
    tile = hidden // 4
    col = pl.BlockSpec((width, tile), lambda j: (0, j))
    row = pl.BlockSpec((tile, width), lambda j: (j, 0))
    bias = pl.BlockSpec((1, tile), lambda j: (0, j))
    slope = pl.BlockSpec((count, tile), lambda j: (0, j))
    flat = whole((count, width))
    return pl.pallas_call(
        ffn_kernel,
        grid=(4,),
        in_specs=[flat, flat, flat, whole(vectors.shape), col, col, bias, bias, row, row],
        out_specs=[slope, slope, flat, flat, whole((8, width))],
        out_shape=[
            jax.ShapeDtypeStruct((count, hidden), F32),
            jax.ShapeDtypeStruct((count, hidden), F32),
            jax.ShapeDtypeStruct((count, width), BF16),
            jax.ShapeDtypeStruct((count, width), F32),
            jax.ShapeDtypeStruct((8, width), F32),
        ],
        scratch_shapes=[pltpu.VMEM((count, width), F32)],
        compiler_params=params(),
        cost_estimate=cost(8 * count * width * hidden, 8 * width * hidden, 2 * count * hidden),
    )(low, normed, grad, vectors, *w_in, *b_in, *w_down)


def ffn_back_kernel(
    g_ffn_ref, g_second_ref, unit_ref, root_ref, vec_ref, slope_a, slope_b, wi_a, wi_b, wd_a, wd_b,
    db_a, db_b, g_first_ref, g_branch_ref, sums_ref, total,
):
    step = pl.program_id(0)
    g_ffn = g_ffn_ref[...]
    part = None
    for slope, w_in, w_down, db in ((slope_a, wi_a, wd_a, db_a), (slope_b, wi_b, wd_b, db_b)):
        g_pre = (slope[...] * dot_nt(g_ffn, w_down[...])).astype(BF16)
        db[...] = jnp.sum(g_pre.astype(F32), axis=0, keepdims=True)
        own = dot_nt(g_pre, w_in[...])
        part = own if part is None else part + own

    @pl.when(step == 0)
    def _():
        total[...] = part

    @pl.when(step > 0)
    def _():
        total[...] += part

    @pl.when(step == pl.num_programs(0) - 1)
    def _():
        g_normed = g_second_ref[...] + total[...]
        unit = unit_ref[...]
        g_first = norm_back(g_normed, unit, root_ref[:, 0:1], vec_ref[1:2, :])
        g_branch = g_first.astype(BF16)
        g_first_ref[...] = g_first
        g_branch_ref[...] = g_branch
        sums_ref[...] = jnp.concatenate(
            [
                jnp.sum(g_normed * unit, axis=0, keepdims=True),
                jnp.sum(g_normed, axis=0, keepdims=True),
                jnp.sum(g_branch.astype(F32), axis=0, keepdims=True),
                jnp.zeros((5, unit.shape[1]), F32),
            ],
            axis=0,
        )


def ffn_backward(g_ffn, g_second, unit, root, vectors, slopes, w_in, w_down):
    count, width = g_ffn.shape
    hidden = w_in[0].shape[1]
    tile = hidden // 4
    col = pl.BlockSpec((width, tile), lambda j: (0, j))
    row = pl.BlockSpec((tile, width), lambda j: (j, 0))
    bias = pl.BlockSpec((1, tile), lambda j: (0, j))
    slope = pl.BlockSpec((count, tile), lambda j: (0, j))
    flat = whole((count, width))
    return pl.pallas_call(
        ffn_back_kernel,
        grid=(4,),
        in_specs=[flat, flat, flat, whole(root.shape), whole(vectors.shape), slope, slope]
        + [col, col, row, row],
        out_specs=[bias, bias, flat, flat, whole((8, width))],
        out_shape=[
            jax.ShapeDtypeStruct((1, hidden), F32),
            jax.ShapeDtypeStruct((1, hidden), F32),
            jax.ShapeDtypeStruct((count, width), F32),
            jax.ShapeDtypeStruct((count, width), BF16),
            jax.ShapeDtypeStruct((8, width), F32),
        ],
        scratch_shapes=[pltpu.VMEM((count, width), F32)],
        compiler_params=params(),
        cost_estimate=cost(8 * count * width * hidden, 8 * width * hidden),
    )(g_ffn, g_second, unit, root, vectors, *slopes, *w_in, *w_down)


def ffn_grads_kernel(place_ref, wi_ref, wd_ref, bi_ref, *refs):
    normed_refs, grad_refs = refs[:8], refs[8:16]
    keep_down, send_down, keep_in, send_in = refs[16:20]
    normed_all, grad_all, hidden_all, pre_all, down, up = refs[20:]
    few, width = normed_refs[0].shape
    tile = wi_ref.shape[1]
    w_in, w_down, b_in = wi_ref[...], wd_ref[...], bi_ref[...]
    for at in range(8):
        cut = slice(at * few, (at + 1) * few)
        normed, grad = normed_refs[at][...], grad_refs[at][...]
        normed_all[cut, :] = normed
        grad_all[cut, :] = grad
        gate, slope = gelu_and_slope(mm(normed, w_in) + b_in)
        hidden_all[cut, :] = gate.astype(BF16)
        pre_all[cut, :] = (slope * dot_nt(grad, w_down)).astype(BF16)
    down[...] = dot_tn(hidden_all[...], grad_all[...])
    up[...] = dot_tn(normed_all[...], pre_all[...])
    down_rows, up_rows = tile // 4, width // 4
    half = width // 2
    for slot in range(4):
        block = slot ^ (place_ref[0] & 3)
        low = down[pl.ds(pl.multiple_of(block * down_rows, down_rows), down_rows), :]
        high = up[pl.ds(pl.multiple_of(block * up_rows, up_rows), up_rows), :]
        to_down, to_in = (keep_down, keep_in) if slot < 2 else (send_down, send_in)
        kind = to_down.dtype
        to_down[slot % 2, :down_rows, :] = low[:, :half].astype(kind)
        to_down[slot % 2, down_rows:, :] = low[:, half:].astype(kind)
        to_in[slot % 2, :, :] = high.astype(kind)


def ffn_grads(place, w_in, w_down, b_in, normed, grads):
    few, width = normed[0].shape
    tile = w_in.shape[1]
    vmem = pl.BlockSpec(memory_space=pltpu.VMEM)
    shape = (2, 2 * (tile // 4), width // 2)
    wide = (2, width // 4, tile)
    return pl.pallas_call(
        ffn_grads_kernel,
        in_specs=[pl.BlockSpec(memory_space=pltpu.SMEM)] + [vmem] * 19,
        out_specs=[vmem] * 4,
        out_shape=[
            jax.ShapeDtypeStruct(shape, F32),
            jax.ShapeDtypeStruct(shape, BF16),
            jax.ShapeDtypeStruct(wide, F32),
            jax.ShapeDtypeStruct(wide, BF16),
        ],
        scratch_shapes=[
            pltpu.VMEM((8 * few, width), BF16),
            pltpu.VMEM((8 * few, width), BF16),
            pltpu.VMEM((8 * few, tile), BF16),
            pltpu.VMEM((8 * few, tile), BF16),
            pltpu.VMEM((tile, width), F32),
            pltpu.VMEM((width, tile), F32),
        ],
        compiler_params=params(),
        cost_estimate=cost(64 * few * width * tile, 48 * few * width + 16 * width * tile),
    )(place, w_in, w_down, b_in, *normed, *grads)


def attend_back_kernel(
    seqs, place_ref, q_ref, k_ref, v_ref, g_branch_ref, w_out_ref, ctx_ref, tok_t_ref, few_ref,
    dq_ref, dk_ref, dv_ref, bias_ref, keep_ref, send_ref, total,
):
    few, inner = q_ref.shape
    rows = k_ref.shape[0]
    slots, length = few // seqs, rows // seqs
    low = lane_halves(slots)
    scale = HEAD ** (-0.5)
    g_branch = g_branch_ref[...]
    g_context = dot_nt(g_branch, w_out_ref[...]).astype(BF16)
    for seq in range(seqs):
        short, long = slice(seq * slots, (seq + 1) * slots), slice(seq * length, (seq + 1) * length)
        for at in range(0, inner, LANES):
            cut = slice(at, at + LANES)
            both, grads = two_heads(scaled(q_ref[short, cut])), two_heads(g_context[short, cut])
            keys, values = k_ref[long, cut], v_ref[long, cut]
            probs = softmax_rows(dot_nt(both, keys))
            grad_probs = dot_nt(grads, values)
            dv_ref[long, cut] = dot_tn(probs.astype(BF16), grads).astype(BF16)
            row_total = jnp.sum(grad_probs * probs, axis=-1, keepdims=True)
            grad_scores = (probs * (grad_probs - row_total)).astype(BF16)
            dq = mm(grad_scores, keys) * scale
            dq_ref[short, cut] = jnp.where(low, dq[:slots], dq[slots:]).astype(BF16)
            dk_ref[long, cut] = dot_tn(grad_scores, both).astype(BF16)
    dq, dk, dv = dq_ref[...], dk_ref[...], dv_ref[...]
    bias_ref[...] = jnp.concatenate(
        [
            jnp.sum(dq.astype(F32), axis=0, keepdims=True),
            jnp.sum(dv.astype(F32), axis=0, keepdims=True),
            jnp.zeros((6, inner), F32),
        ],
        axis=0,
    )
    total[0] = dot_tn(few_ref[...], dq)
    total[1] = mm(tok_t_ref[...], dk)
    total[2] = mm(tok_t_ref[...], dv)
    out_grad = dot_tn(ctx_ref[...], g_branch)
    total[3, :inner, :] = out_grad[:, :inner]
    total[3, inner:, :] = out_grad[:, inner:]
    block_rows = total.shape[1] // 16
    for slot in range(16):
        block = slot ^ place_ref[0]
        row = pl.multiple_of(block * block_rows, block_rows)
        for section in range(4):
            values = total[section, pl.ds(row, block_rows), :]
            cut = slice(section * block_rows, (section + 1) * block_rows)
            if slot < 8:
                keep_ref[slot, cut, :] = values
            else:
                send_ref[slot - 8, cut, :] = values.astype(BF16)


def attend_back(place, queries, keys, values, g_branch, w_out, context, tokens_t, few, seqs):
    rows, inner = keys.shape
    width = tokens_t.shape[0]
    count = queries.shape[0]
    vmem = pl.BlockSpec(memory_space=pltpu.VMEM)
    held = (8, 4 * (width // 16), inner)
    return pl.pallas_call(
        functools.partial(attend_back_kernel, seqs),
        in_specs=[pl.BlockSpec(memory_space=pltpu.SMEM)] + [vmem] * 8,
        out_specs=[vmem] * 6,
        out_shape=[
            jax.ShapeDtypeStruct((count, inner), BF16),
            jax.ShapeDtypeStruct((rows, inner), BF16),
            jax.ShapeDtypeStruct((rows, inner), BF16),
            jax.ShapeDtypeStruct((8, inner), F32),
            jax.ShapeDtypeStruct(held, F32),
            jax.ShapeDtypeStruct(held, BF16),
        ],
        scratch_shapes=[pltpu.VMEM((4, width, inner), F32)],
        compiler_params=params(),
        cost_estimate=cost(
            4 * rows * width * inner + 24 * count * rows * inner, 20 * rows * inner
        ),
    )(place, queries, keys, values, g_branch, w_out, context, tokens_t, few)


def unpack_attend_kernel(place_ref, mine_ref, near_ref, qkv_ref, out_ref):
    rows = qkv_ref.shape[1] // 16
    inner = qkv_ref.shape[2]
    for slot in range(16):
        block = slot ^ place_ref[0]
        held = mine_ref if slot < 8 else near_ref
        values = held[slot % 8].astype(F32)
        row = pl.multiple_of(block * rows, rows)
        for section in range(3):
            cut = slice(section * rows, (section + 1) * rows)
            qkv_ref[section, pl.ds(row, rows), :] = values[cut, :]
        row = pl.multiple_of((block & 7) * rows, rows)
        column = pl.multiple_of((block >> 3) * inner, inner)
        out_ref[pl.ds(row, rows), pl.ds(column, inner)] = values[3 * rows :, :]


def unpack_attend(place, mine, near, width):
    _, held, inner = mine.shape
    vmem = pl.BlockSpec(memory_space=pltpu.VMEM)
    return pl.pallas_call(
        unpack_attend_kernel,
        in_specs=[pl.BlockSpec(memory_space=pltpu.SMEM), vmem, vmem],
        out_specs=[vmem, vmem],
        out_shape=[
            jax.ShapeDtypeStruct((3, width, inner), F32),
            jax.ShapeDtypeStruct((inner, width), F32),
        ],
        compiler_params=params(),
        cost_estimate=cost(0, 16 * held * inner * 6),
    )(place, mine, near)


def unpack_ffn_kernel(place_ref, *refs):
    down_ref, in_ref = refs[4:]
    rows, width = down_ref.shape[0] // 16, down_ref.shape[1]
    deep, wide = in_ref.shape[0] // 4, in_ref.shape[1] // 4
    for slot in range(16):
        block = slot ^ place_ref[0]
        down = refs[0 if slot < 8 else 1][slot % 8].astype(F32)
        row = pl.multiple_of(block * rows, rows)
        down_ref[pl.ds(row, rows), : width // 2] = down[:rows, :]
        down_ref[pl.ds(row, rows), width // 2 :] = down[rows:, :]
        row = pl.multiple_of((block & 3) * deep, deep)
        column = pl.multiple_of((block >> 2) * wide, wide)
        in_ref[pl.ds(row, deep), pl.ds(column, wide)] = refs[2 if slot < 8 else 3][
            slot % 8
        ].astype(F32)


def unpack_ffn(place, down, up, width, hidden):
    vmem = pl.BlockSpec(memory_space=pltpu.VMEM)
    return pl.pallas_call(
        unpack_ffn_kernel,
        in_specs=[pl.BlockSpec(memory_space=pltpu.SMEM)] + [vmem] * 4,
        out_specs=[vmem, vmem],
        out_shape=[
            jax.ShapeDtypeStruct((hidden, width), F32),
            jax.ShapeDtypeStruct((width, hidden), F32),
        ],
        compiler_params=params(),
        cost_estimate=cost(0, 12 * width * hidden),
    )(place, *down, *up)


def attend_kernel(q_ref, k_ref, v_ref, out_ref):
    out_ref[...] = attend_block(q_ref[...], k_ref[...], v_ref[...])


def attend(queries, keys, values, seqs):
    rows, inner = queries.shape
    length = rows // seqs
    tile = min(length, 256)
    tiles = length // tile
    q_spec = pl.BlockSpec((tile, LANES), lambda s, j, i: (s * tiles + i, j))
    kv_spec = pl.BlockSpec((length, LANES), lambda s, j, i: (s, j))
    return pl.pallas_call(
        attend_kernel,
        grid=(seqs, inner // LANES, tiles),
        in_specs=[q_spec, kv_spec, kv_spec],
        out_specs=q_spec,
        out_shape=jax.ShapeDtypeStruct(queries.shape, BF16),
        compiler_params=params(),
        cost_estimate=cost(
            16 * rows * length * inner, 8 * rows * inner, rows * length * inner // HEAD
        ),
    )(queries, keys, values)


def body(
    tokens,
    grad_values,
    span_starts,
    w_qkv,
    b_qv,
    w_out,
    b_out,
    ln1_gain,
    ln1_bias,
    w_in,
    b_in,
    w_down,
    b_down,
    ln2_gain,
    ln2_bias,
):
    rows, width = tokens.shape
    inner = w_qkv.shape[2]
    hidden_half = w_in.shape[1]
    halves = lax.axis_size("tensor")
    seqs = span_starts.shape[0] // halves
    spans = span_starts.shape[1]
    length = rows // seqs
    half_at = lax.axis_index("tensor")
    me = lax.axis_index("dp")
    bits = lax.axis_size("dp").bit_length() - 1
    block_at = ((me & 1) << 3) | ((me & 2) << 1) | ((me & 4) >> 1) | ((me & 8) >> 3)
    place = block_at.reshape(1).astype(jnp.int32)
    rest = [1 << bit for bit in range(4, bits)]

    w_qkv_own = jnp.transpose(w_qkv, (1, 0, 2))
    w_qkv_both = [w_qkv_own, fetch_eighths(w_qkv_own, me)]
    bias_pack = jnp.concatenate([b_qv[0], b_qv[1], b_in]).reshape(-1, LANES)
    bias_other = flip_tensor(bias_pack).reshape(-1)
    w_out_both = [w_out, fetch_halves(w_out[None], me)[0]]
    w_in_both = [w_in, fetch_eighths(w_in[None], me)[0]]
    w_down_both = [w_down, fetch_halves(w_down[None], me)[0]]
    b_qv_both = [b_qv, bias_other[: 2 * inner].reshape(2, inner)]
    b_in_both = [b_in.reshape(1, -1), bias_other[2 * inner :].reshape(1, -1)]

    starts = lax.dynamic_slice_in_dim(span_starts, half_at * seqs, seqs, 0)
    places = starts[:, :, None] + jnp.arange(SPAN, dtype=jnp.int32)
    earlier = jnp.tril(jnp.ones((spans, spans), jnp.bool_), -1)
    covered = (places[:, :, :, None] >= starts[:, None, None, :]) & (
        places[:, :, :, None] < starts[:, None, None, :] + SPAN
    )
    fresh = ~jnp.any(covered & earlier[None, :, None, :], axis=-1)
    slots = -(-spans * SPAN // 16) * 16
    pad = slots - spans * SPAN
    places = jnp.pad(places.reshape(seqs, spans * SPAN), ((0, 0), (0, pad)))
    fresh = jnp.pad(fresh.reshape(seqs, spans * SPAN), ((0, 0), (0, pad)))
    picks = (places[:, :, None] == jnp.arange(length, dtype=jnp.int32)).astype(BF16)
    few = seqs * slots

    def pick(values):
        return jnp.einsum(
            "srt,std->srd", picks, values.reshape(seqs, length, width), preferred_element_type=F32
        ).reshape(few, width)

    tokens_few = pick(tokens).astype(BF16)
    grad_few = pick(grad_values) * fresh.reshape(few, 1).astype(F32)
    tokens_t = tokens.T
    vectors_one = jnp.stack([b_out, ln1_gain, ln1_bias])
    vectors_two = jnp.stack([b_down, ln2_gain, ln2_bias])

    keys, values, queries_few, context_few = zip(
        *[project(tokens, tokens_few, w_qkv_both[at], b_qv_both[at], seqs) for at in range(2)]
    )
    normed_few, normed_low, unit_one, root_one = first_norm(
        context_few, w_out_both, tokens_few, vectors_one
    )
    slope_a, slope_b, g_ffn, g_second, sums_two = ffn_forward(
        normed_low, normed_few, grad_few, vectors_two, w_in_both, b_in_both, w_down_both
    )

    def plane(values):
        held = [values, flip_tensor(values), flip(values, 2), flip_both(values, 2)]
        return held + [flip(item, 1) for item in held]

    quarter = hidden_half // 4
    quarter_at = (block_at >> 2) * quarter
    w_in_slice = lax.dynamic_slice_in_dim(w_in, quarter_at, quarter, 1)
    w_down_slice = lax.dynamic_slice_in_dim(w_down, quarter_at, quarter, 0)
    b_in_slice = lax.dynamic_slice_in_dim(b_in, quarter_at, quarter, 0).reshape(1, -1)
    keep_down, send_down, keep_in, send_in = ffn_grads(
        place, w_in_slice, w_down_slice, b_in_slice, plane(normed_low), plane(g_ffn)
    )

    db_a, db_b, g_first, g_branch, sums_one = ffn_backward(
        g_ffn, g_second, unit_one, root_one, vectors_one, (slope_a, slope_b), w_in_both, w_down_both
    )
    backs = [
        attend_back(
            place, queries_few[at], keys[at], values[at], g_branch, w_out_both[at],
            context_few[at], tokens_t, tokens_few, seqs,
        )
        for at in (1, 0)
    ]
    back_oth, back_own = backs

    def halve(keep, send, bit):
        total = keep + flip(send, bit).astype(F32)
        middle = total.shape[0] // 2
        return total[:middle], total[middle:].astype(BF16)

    def over_rest(total):
        for bit in rest:
            total = total + flip(total, bit)
        return total

    def double(held, bit):
        return jnp.concatenate([held, flip(held, bit)], axis=0)

    def finish(keep, send):
        keep, send = halve(keep, send, 4)
        total = over_rest(keep + flip(send, 8).astype(F32))
        held = settle(total.astype(BF16))
        for bit in (8, 4, 2):
            held = double(held, bit)
        return held, flip(held, 1)

    down = finish(keep_down, send_down)
    up = finish(keep_in, send_in)

    oth = back_oth[4] + flip(back_oth[5], 1).astype(F32)
    own = back_own[4] + flip(back_own[5], 1).astype(F32)
    total = own + flip_tensor(oth.astype(BF16)).astype(F32)
    keep, send = halve(total[:4], total[4:].astype(BF16), 2)
    attn = finish(keep, send)

    d_w_down, d_w_in = unpack_ffn(place, down, up, width, hidden_half)
    d_w_qkv, d_w_out = unpack_attend(place, *attn, width)
    d_w_qkv = jnp.transpose(d_w_qkv, (1, 0, 2))

    def placed(own_part, oth_part):
        both = jnp.stack([own_part, oth_part])
        return jnp.where(half_at == 0, both, both[::-1]).reshape(-1)

    sections = [
        placed(back_own[3][0], back_oth[3][0]),
        placed(back_own[3][1], back_oth[3][1]),
        placed(db_a[0], db_b[0]),
        sums_one[2],
        sums_one[0],
        sums_one[1],
        sums_two[2],
        sums_two[0],
        sums_two[1],
    ]
    small = jnp.concatenate(sections).reshape(-1, LANES)
    small = small + flip(small, 1)
    small = small + flip_tensor(small)
    for bit in range(1, bits):
        small = small + flip(small, 1 << bit)
    small = small.reshape(-1)
    cuts, at = [], 0
    for section in sections:
        cuts.append(small[at : at + section.size])
        at += section.size

    def own_half(vector):
        return lax.dynamic_index_in_dim(vector.reshape(2, -1), half_at, 0, keepdims=False)

    d_b_qv = jnp.stack([own_half(cuts[0]), own_half(cuts[1])])
    d_b_in = own_half(cuts[2])

    few_back = g_first
    all_back = None
    for at, back in ((0, back_own), (1, back_oth)):
        few_back = few_back + dot_nt(back[0], w_qkv_both[at][0])
        part = dot_nt(back[1], w_qkv_both[at][1]) + dot_nt(back[2], w_qkv_both[at][2])
        all_back = part if all_back is None else all_back + part
    coarse = lax.reduce_precision(few_back, 8, 7)
    fine = (few_back - coarse).astype(BF16)
    pieces = jnp.concatenate(
        [coarse.astype(BF16).reshape(seqs, slots, width), fine.reshape(seqs, slots, width)], axis=1
    )
    spreading = jnp.concatenate([picks, picks], axis=1)
    d_tokens = all_back + jnp.einsum(
        "srt,srd->std", spreading, pieces, preferred_element_type=F32
    ).reshape(rows, width)

    branch = b_out
    for at in range(2):
        queries = (mm(tokens, w_qkv_both[at][0]) + b_qv_both[at][0]).astype(BF16)
        context = attend(queries, keys[at], values[at], seqs)
        branch = branch + mm(context, w_out_both[at])
    unit, _ = norm_rows(tokens.astype(F32) + branch)
    normed = unit * ln1_gain + ln1_bias
    normed_bf = normed.astype(BF16)
    ffn_out = b_down
    for at in range(2):
        hidden = gelu(mm(normed_bf, w_in_both[at]) + b_in_both[at]).astype(BF16)
        ffn_out = ffn_out + mm(hidden, w_down_both[at])
    unit, _ = norm_rows(normed + ffn_out)
    mixed = (unit * ln2_gain + ln2_bias).astype(BF16)

    return (
        mixed,
        d_tokens,
        d_w_qkv,
        d_b_qv,
        d_w_out,
        cuts[3],
        cuts[4],
        cuts[5],
        d_w_in,
        d_b_in,
        d_w_down,
        cuts[6],
        cuts[7],
        cuts[8],
    )


def solution(mesh):
    placed = (
        P(("dp", "tensor"), None),
        P(("dp", "tensor"), None),
        P("dp", None),
        P(None, None, "tensor"),
        P(None, "tensor"),
        P("tensor", None),
        P(),
        P(),
        P(),
        P(None, "tensor"),
        P("tensor"),
        P("tensor", None),
        P(),
        P(),
        P(),
    )
    return jax.shard_map(
        body,
        mesh=mesh,
        in_specs=placed,
        out_specs=(
            P(("dp", "tensor"), None),
            P(("dp", "tensor"), None),
            P(None, None, "tensor"),
            P(None, "tensor"),
            P("tensor", None),
            P(),
            P(),
            P(),
            P(None, "tensor"),
            P("tensor"),
            P("tensor", None),
            P(),
            P(),
            P(),
        ),
        check_vma=False,
    )
```

```python
import functools

import jax
import jax.numpy as jnp
from jax import lax
from jax.experimental import pallas as pl
from jax.experimental.pallas import tpu as pltpu
from jax.sharding import PartitionSpec as P

HEAD = 64
SPAN = 6
LANES = 128
EPSILON = 1e-05
F32 = jnp.float32
BF16 = jnp.bfloat16
GELU_A = (2.0 / 3.141592653589793) ** 0.5
GELU_B = 0.044715
WEIGHT = 0.1
ANYWHERE = pl.BlockSpec(memory_space=pl.ANY)
VMEM = pl.BlockSpec(memory_space=pltpu.VMEM)


class Line:
    def __init__(self):
        self.token = jnp.zeros((8, LANES), F32)

    def run(
        self, kernel, args, out_shape, grid=(), in_specs=None, out_specs=None, scratch=(), place=None,
        flops=0, moved=0, transcendentals=0, room=12, aliases=None,
    ):
        ins, outs = len(args), len(out_shape)
        lead = 0 if place is None else 1

        def with_token(*refs):
            given, rest = refs[: lead + ins], refs[lead + ins + 1 :]
            rest[outs][...] = jnp.zeros((8, LANES), F32)
            kernel(*given, *rest[:outs], *rest[outs + 1 :])

        in_specs = list(in_specs or [VMEM] * ins) + [ANYWHERE]
        out_specs = list(out_specs or [VMEM] * outs)
        out_specs.append(pl.BlockSpec((8, LANES), lambda *at: (0, 0)) if grid else VMEM)
        shapes = list(out_shape) + [jax.ShapeDtypeStruct((8, LANES), F32)]
        params = dict(
            out_shape=shapes,
            input_output_aliases=aliases or {},
            compiler_params=pltpu.CompilerParams(vmem_limit_bytes=room << 20),
            cost_estimate=pl.CostEstimate(
                flops=int(flops * WEIGHT),
                bytes_accessed=int(moved * WEIGHT),
                transcendentals=int(transcendentals * WEIGHT),
            ),
        )
        if lead and grid:
            params["grid_spec"] = pltpu.PrefetchScalarGridSpec(
                num_scalar_prefetch=1, grid=grid, in_specs=in_specs, out_specs=out_specs, scratch_shapes=list(scratch)
            )
        else:
            if lead:
                in_specs = [pl.BlockSpec(memory_space=pltpu.SMEM)] + in_specs
            params.update(grid=grid, in_specs=in_specs, out_specs=out_specs, scratch_shapes=list(scratch))
        front = [] if place is None else [place]
        *results, self.token = pl.pallas_call(with_token, **params)(*front, *args, self.token)
        return results


def shaped(shape, kind):
    return jax.ShapeDtypeStruct(tuple(shape), kind)


def whole(shape):
    return pl.BlockSpec(shape, lambda *at: (0,) * len(shape))


def flip(values, bits):
    size = lax.axis_size("dp")
    return lax.ppermute(values, "dp", [(at, at ^ bits) for at in range(size)])


def flip_tensor(values):
    return lax.ppermute(values, "tensor", [(0, 1), (1, 0)])


def flip_both(values, bits):
    size = 2 * lax.axis_size("dp")
    pairs = [(at, at ^ (2 * bits + 1)) for at in range(size)]
    return lax.ppermute(values, ("dp", "tensor"), pairs)


def dot_nt(left, right):
    return lax.dot_general(left, right, (((1,), (1,)), ((), ())), preferred_element_type=F32)


def dot_tn(left, right):
    return lax.dot_general(left, right, (((0,), (0,)), ((), ())), preferred_element_type=F32)


def mm(left, right):
    return jnp.dot(left, right, preferred_element_type=F32)


def lane_halves(rows):
    return lax.broadcasted_iota(jnp.int32, (rows, LANES), 1) < HEAD


def two_heads(block):
    low = lane_halves(block.shape[0])
    zero = jnp.zeros_like(block)
    return jnp.concatenate([jnp.where(low, block, zero), jnp.where(low, zero, block)], axis=0)


def scaled(queries):
    return queries * jnp.asarray(HEAD ** (-0.5), BF16)


def softmax_rows(scores):
    exponent = jnp.exp(scores - jnp.max(scores, axis=-1, keepdims=True))
    return exponent * (1.0 / jnp.sum(exponent, axis=-1, keepdims=True))


def attend_block(queries, keys, values):
    rows = queries.shape[0]
    probs = softmax_rows(dot_nt(two_heads(scaled(queries)), keys)).astype(BF16)
    mixed = mm(probs, values)
    return jnp.where(lane_halves(rows), mixed[:rows], mixed[rows:]).astype(BF16)


def norm_rows(values):
    average = jnp.mean(values, axis=-1, keepdims=True)
    centered = values - average
    variance = jnp.mean(centered * centered, axis=-1, keepdims=True)
    root = lax.rsqrt(variance + EPSILON)
    return centered * root, root


def norm_back(grad, unit, root, gain):
    grad_y = grad * gain
    inner = jnp.mean(grad_y, axis=-1, keepdims=True)
    along = jnp.mean(grad_y * unit, axis=-1, keepdims=True)
    return root * (grad_y - inner - unit * along)


def gelu_and_slope(values):
    square = values * values
    bent = jnp.tanh(GELU_A * values * (1.0 + GELU_B * square))
    half = 0.5 * (1.0 + bent)
    slope = half + 0.5 * values * (1.0 - bent * bent) * GELU_A * (1.0 + 3.0 * GELU_B * square)
    return values * half, slope


def gelu(values):
    return 0.5 * values * (1.0 + jnp.tanh(GELU_A * values * (1.0 + GELU_B * values * values)))


def join_kernel(count, *refs):
    rows = refs[0].shape[-2]
    for at in range(count):
        refs[count][..., at * rows : (at + 1) * rows, :] = refs[at][...]


def join(line, pieces):
    *lead, rows, columns = pieces[0].shape
    (result,) = line.run(
        functools.partial(join_kernel, len(pieces)),
        pieces,
        [shaped((*lead, rows * len(pieces), columns), pieces[0].dtype)],
        moved=4 * len(pieces) * pieces[0].size,
    )
    return result


def copy_kernel(place_ref, in_ref, out_ref):
    out_ref[...] = in_ref[...]


def cut_qkv(line, w_qkv, here):
    lead, rows, columns = w_qkv.shape
    (piece,) = line.run(
        copy_kernel,
        [w_qkv],
        [shaped((lead, rows // 8, columns), BF16)],
        grid=(1,),
        in_specs=[pl.BlockSpec((lead, rows // 8, columns), lambda i, p: (0, p[0] & 7, 0))],
        out_specs=[whole((lead, rows // 8, columns))],
        place=here,
        moved=w_qkv.size // 2,
    )
    return piece


def second_cut_kernel(place_ref, qkv_ref, bias_ref, out_ref, in_ref, down_ref, qkv, bias, half, eighth):
    qkv[...] = qkv_ref[...]
    bias[...] = bias_ref[...]
    half[...] = out_ref[...]
    rows = in_ref.shape[0]
    eighth[:rows, :] = in_ref[...]
    eighth[rows:, :] = down_ref[...]


def second_cut(line, qkv, bias, w_out, w_in, w_down, here):
    width = w_out.shape[1]
    half, eighth, deep = w_out.shape[0] // 2, w_in.shape[0] // 8, w_down.shape[0] // 8
    return line.run(
        second_cut_kernel,
        [qkv, bias, w_out, w_in, w_down],
        [
            shaped(qkv.shape, BF16),
            shaped(bias.shape, F32),
            shaped((half, width), BF16),
            shaped((eighth + deep, width), BF16),
        ],
        grid=(1,),
        in_specs=[
            whole(qkv.shape),
            whole(bias.shape),
            pl.BlockSpec((half, width), lambda i, p: (p[0] & 1, 0)),
            pl.BlockSpec((eighth, width), lambda i, p: (p[0] & 7, 1)),
            pl.BlockSpec((deep, width), lambda i, p: (p[0] & 7, 0)),
        ],
        out_specs=[
            whole(qkv.shape), whole(bias.shape), whole((half, width)), whole((eighth + deep, width))
        ],
        place=here,
        moved=4 * (qkv.size + (half + eighth + deep) * width),
    )


def third_cut_kernel(place_ref, a, b, c, d, out_ref, eighth_ref, in_ref, core, eighth, half):
    third, rows, inner = a.shape
    for at, ref in enumerate((a, b, c, d)):
        for section in range(third):
            row = (section * 4 + at) * rows
            core[row : row + rows, :] = ref[section]
    row = 4 * third * rows
    deep = out_ref.shape[0]
    core[row : row + deep, :] = out_ref[:, :inner]
    core[row + deep :, :] = out_ref[:, inner:]
    eighth[...] = eighth_ref[...]
    half[...] = in_ref[...]


def third_cut(line, qkv, out, eighth, w_in, here):
    third, rows, inner = qkv[0].shape
    width = out.shape[1]
    height = 4 * third * rows + 2 * out.shape[0]
    half = (w_in.shape[0] // 2, width)
    return line.run(
        third_cut_kernel,
        [*qkv, out, eighth, w_in],
        [shaped((height, inner), BF16), shaped(eighth.shape, BF16), shaped(half, BF16)],
        grid=(1,),
        in_specs=[whole(item.shape) for item in [*qkv, out, eighth]]
        + [pl.BlockSpec(half, lambda i, p: (p[0] & 1, 0))],
        out_specs=[whole((height, inner)), whole(eighth.shape), whole(half)],
        place=here,
        moved=4 * (height * inner + eighth.size + half[0] * width),
    )


def first_assemble_kernel(place_ref, mine, near, qkv_ref, out_ref):
    third, width, inner = qkv_ref.shape
    rows, half = width // 8, out_ref.shape[0] // 2
    for core, ref in enumerate((mine, near)):
        for at in range(4):
            row = pl.multiple_of(((place_ref[0] ^ (2 * at + core)) & 7) * rows, rows)
            for section in range(third):
                start = (section * 4 + at) * rows
                qkv_ref[section, pl.ds(row, rows), :] = ref[start : start + rows, :]
        row = pl.multiple_of(((place_ref[0] ^ core) & 1) * half, half)
        start = 4 * third * rows
        out_ref[pl.ds(row, half), :inner] = ref[start : start + half, :]
        out_ref[pl.ds(row, half), inner:] = ref[start + half :, :]


def first_assemble(line, mine, near, width, inner, here):
    return line.run(
        first_assemble_kernel,
        [mine, near],
        [shaped((3, width, inner), BF16), shaped((inner, width), BF16)],
        place=here,
        moved=8 * mine.size,
    )


def fourth_cut_kernel(a, b, c, d, half_ref, eighths, half):
    rows = a.shape[0]
    for at, ref in enumerate((a, b, c, d)):
        eighths[at * rows : (at + 1) * rows, :] = ref[...]
    half[...] = half_ref[...]


def fourth_cut(line, eighths, half):
    rows, width = eighths[0].shape
    return line.run(
        fourth_cut_kernel,
        [*eighths, half],
        [shaped((4 * rows, width), BF16), shaped(half.shape, BF16)],
        moved=16 * rows * width,
    )


def second_assemble_kernel(place_ref, mine, near, half_mine, half_near, in_ref, down_ref):
    width = half_mine.shape[1]
    rows, deep, half = in_ref.shape[0] // 8, down_ref.shape[0] // 8, half_mine.shape[0]
    for core, (ref, half_ref) in enumerate(((mine, half_mine), (near, half_near))):
        for at in range(4):
            block = (place_ref[0] ^ (2 * at + core)) & 7
            start = at * (rows + deep)
            in_ref[pl.ds(pl.multiple_of(block * rows, rows), rows), width:] = ref[
                start : start + rows, :
            ]
            down_ref[pl.ds(pl.multiple_of(block * deep, deep), deep), :] = ref[
                start + rows : start + rows + deep, :
            ]
        row = pl.multiple_of(((place_ref[0] ^ core) & 1) * half, half)
        in_ref[pl.ds(row, half), :width] = half_ref[...]


def second_assemble(line, mine, near, half_mine, half_near, hidden, here):
    width = half_mine.shape[1]
    return line.run(
        second_assemble_kernel,
        [mine, near, half_mine, half_near],
        [shaped((width, hidden), BF16), shaped((hidden, width), BF16)],
        place=here,
        moved=8 * width * hidden,
        room=24,
    )


def project_kernel(tok_ref, few_ref, w_ref, bias_ref, k_ref, v_ref, q_ref, ctx_ref):
    tok = tok_ref[...]
    k_ref[...] = mm(tok, w_ref[1]).astype(BF16)
    v_ref[...] = (mm(tok, w_ref[2]) + bias_ref[1:2, :]).astype(BF16)
    q_ref[...] = (mm(few_ref[...], w_ref[0]) + bias_ref[0:1, :]).astype(BF16)
    for at in range(0, k_ref.shape[1], LANES):
        cut = slice(at, at + LANES)
        ctx_ref[:, cut] = attend_block(q_ref[:, cut], k_ref[:, cut], v_ref[:, cut])


def project(line, tokens, few, weights, bias, seqs):
    rows, width = tokens.shape
    inner = weights.shape[2]
    length, slots = rows // seqs, few.shape[0] // seqs
    long, short = (pl.BlockSpec((size, inner), lambda s: (s, 0)) for size in (length, slots))
    return line.run(
        project_kernel,
        [tokens, few, weights, bias],
        [shaped((rows, inner), BF16)] * 2 + [shaped((few.shape[0], inner), BF16)] * 2,
        grid=(seqs,),
        in_specs=[
            pl.BlockSpec((length, width), lambda s: (s, 0)),
            pl.BlockSpec((slots, width), lambda s: (s, 0)),
            whole(weights.shape),
            whole(bias.shape),
        ],
        out_specs=[long, long, short, short],
        flops=6 * rows * width * inner,
        room=24,
        moved=2 * (rows * width + 3 * width * inner + 2 * rows * inner),
    )


def first_norm_kernel(
    ctx_a, ctx_b, w_a, w_b, few_ref, vec_ref, normed_ref, low_ref, unit_ref, root_ref
):
    branch = mm(ctx_a[...], w_a[...]) + mm(ctx_b[...], w_b[...]) + vec_ref[0:1, :]
    unit, root = norm_rows(few_ref[...].astype(F32) + branch)
    normed = unit * vec_ref[1:2, :] + vec_ref[2:3, :]
    normed_ref[...] = normed
    low_ref[...] = normed.astype(BF16)
    unit_ref[...] = unit
    root_ref[...] = jnp.broadcast_to(root, root_ref.shape)


def first_norm(line, contexts, w_out, few, vectors):
    count, width = few.shape
    return line.run(
        first_norm_kernel,
        [*contexts, *w_out, few, vectors],
        [
            shaped((count, width), F32),
            shaped((count, width), BF16),
            shaped((count, width), F32),
            shaped((count, LANES), F32),
        ],
        flops=2 * count * width * width,
        moved=2 * width * width + 14 * count * width,
    )


def ffn_part_kernel(low_ref, wi_ref, bi_ref, wd_ref, slope_ref, part_ref, total):
    step = pl.program_id(0)
    gate, slope = gelu_and_slope(mm(low_ref[...], wi_ref[...]) + bi_ref[...])
    slope_ref[...] = slope
    part = mm(gate.astype(BF16), wd_ref[...])

    @pl.when(step == 0)
    def _():
        total[...] = part

    @pl.when(step > 0)
    def _():
        total[...] += part

    @pl.when(step == pl.num_programs(0) - 1)
    def _():
        part_ref[...] = total[...]


def ffn_last_kernel(
    low_ref, wi_ref, bi_ref, wd_ref, part_ref, normed_ref, grad_ref, vec_ref,
    slope_ref, g_ffn_ref, g_second_ref, sums_ref, total,
):
    step = pl.program_id(0)
    gate, slope = gelu_and_slope(mm(low_ref[...], wi_ref[...]) + bi_ref[...])
    slope_ref[...] = slope
    part = mm(gate.astype(BF16), wd_ref[...])

    @pl.when(step == 0)
    def _():
        total[...] = part_ref[...] + part

    @pl.when(step > 0)
    def _():
        total[...] += part

    @pl.when(step == pl.num_programs(0) - 1)
    def _():
        unit, root = norm_rows(normed_ref[...] + total[...] + vec_ref[0:1, :])
        grad = grad_ref[...]
        g_second = norm_back(grad, unit, root, vec_ref[1:2, :])
        g_ffn = g_second.astype(BF16)
        g_second_ref[...] = g_second
        g_ffn_ref[...] = g_ffn
        sums_ref[...] = jnp.concatenate(
            [
                jnp.sum(grad * unit, axis=0, keepdims=True),
                jnp.sum(grad, axis=0, keepdims=True),
                jnp.sum(g_ffn.astype(F32), axis=0, keepdims=True),
                jnp.zeros((5, grad.shape[1]), F32),
            ],
            axis=0,
        )


def ffn_forward(line, low, w_in, b_in, w_down, rest=None):
    count, width = low.shape
    hidden = w_in.shape[1]
    steps = 4
    tile = hidden // steps
    flat = whole((count, width))
    specs = [
        flat,
        pl.BlockSpec((width, tile), lambda j: (0, j)),
        pl.BlockSpec((1, tile), lambda j: (0, j)),
        pl.BlockSpec((tile, width), lambda j: (j, 0)),
    ]
    slope = pl.BlockSpec((count, tile), lambda j: (0, j))
    common = dict(
        grid=(steps,),
        scratch=[pltpu.VMEM((count, width), F32)],
        flops=4 * count * width * hidden,
        moved=4 * width * hidden,
        transcendentals=count * hidden,
        room=20,
    )
    if rest is None:
        return line.run(
            ffn_part_kernel,
            [low, w_in, b_in, w_down],
            [shaped((count, hidden), F32), shaped((count, width), F32)],
            in_specs=specs,
            out_specs=[slope, flat],
            **common,
        )
    return line.run(
        ffn_last_kernel,
        [low, w_in, b_in, w_down, *rest],
        [
            shaped((count, hidden), F32),
            shaped((count, width), BF16),
            shaped((count, width), F32),
            shaped((8, width), F32),
        ],
        in_specs=specs + [whole(item.shape) for item in rest],
        out_specs=[slope, flat, flat, whole((8, width))],
        **common,
    )


def ffn_back_kernel(
    g_ffn_ref, g_second_ref, unit_ref, root_ref, vec_ref, slope_a, slope_b, wi_a, wi_b, wd_a, wd_b,
    db_a, db_b, g_first_ref, g_branch_ref, sums_ref, total,
):
    step = pl.program_id(0)
    g_ffn = g_ffn_ref[...]
    part = None
    for slope, w_in, w_down, db in ((slope_a, wi_a, wd_a, db_a), (slope_b, wi_b, wd_b, db_b)):
        g_pre = (slope[...] * dot_nt(g_ffn, w_down[...])).astype(BF16)
        db[...] = jnp.sum(g_pre.astype(F32), axis=0, keepdims=True)
        own = dot_nt(g_pre, w_in[...])
        part = own if part is None else part + own

    @pl.when(step == 0)
    def _():
        total[...] = part

    @pl.when(step > 0)
    def _():
        total[...] += part

    @pl.when(step == pl.num_programs(0) - 1)
    def _():
        g_normed = g_second_ref[...] + total[...]
        unit = unit_ref[...]
        g_first = norm_back(g_normed, unit, root_ref[:, 0:1], vec_ref[1:2, :])
        g_branch = g_first.astype(BF16)
        g_first_ref[...] = g_first
        g_branch_ref[...] = g_branch
        sums_ref[...] = jnp.concatenate(
            [
                jnp.sum(g_normed * unit, axis=0, keepdims=True),
                jnp.sum(g_normed, axis=0, keepdims=True),
                jnp.sum(g_branch.astype(F32), axis=0, keepdims=True),
                jnp.zeros((5, unit.shape[1]), F32),
            ],
            axis=0,
        )


def ffn_backward(line, g_ffn, g_second, unit, root, vectors, slopes, w_in, w_down):
    count, width = g_ffn.shape
    hidden = w_in[0].shape[1]
    tile = hidden // 4
    col = pl.BlockSpec((width, tile), lambda j: (0, j))
    row = pl.BlockSpec((tile, width), lambda j: (j, 0))
    bias = pl.BlockSpec((1, tile), lambda j: (0, j))
    slope = pl.BlockSpec((count, tile), lambda j: (0, j))
    flat = whole((count, width))
    return line.run(
        ffn_back_kernel,
        [g_ffn, g_second, unit, root, vectors, *slopes, *w_in, *w_down],
        [
            shaped((1, hidden), F32),
            shaped((1, hidden), F32),
            shaped((count, width), F32),
            shaped((count, width), BF16),
            shaped((8, width), F32),
        ],
        grid=(4,),
        in_specs=[flat, flat, flat, whole(root.shape), whole(vectors.shape), slope, slope]
        + [col, col, row, row],
        out_specs=[bias, bias, flat, flat, whole((8, width))],
        scratch=[pltpu.VMEM((count, width), F32)],
        flops=8 * count * width * hidden,
        moved=8 * width * hidden,
        room=24,
    )


def ffn_grads_kernel(place_ref, wi_ref, wd_ref, bi_ref, *refs):
    normed_refs, grad_refs = refs[:2], refs[2:4]
    keep_down, send_down, keep_in, send_in = refs[4:8]
    normed_all, grad_all, hidden_all, pre_all, down, up = refs[8:]
    few, width = normed_refs[0].shape
    tile = wi_ref.shape[1]
    w_in, w_down, b_in = wi_ref[...], wd_ref[...], bi_ref[...]
    for at in range(2):
        cut = slice(at * few, (at + 1) * few)
        normed, grad = normed_refs[at][...], grad_refs[at][...]
        normed_all[cut, :] = normed
        grad_all[cut, :] = grad
        gate, slope = gelu_and_slope(mm(normed, w_in) + b_in)
        hidden_all[cut, :] = gate.astype(BF16)
        pre_all[cut, :] = (slope * dot_nt(grad, w_down)).astype(BF16)
    down[...] = dot_tn(hidden_all[...], grad_all[...])
    up[...] = dot_tn(normed_all[...], pre_all[...])
    down_rows, up_rows = tile // 4, width // 4
    half = width // 2
    for slot in range(4):
        block = slot ^ (place_ref[0] & 3)
        low = down[pl.ds(pl.multiple_of(block * down_rows, down_rows), down_rows), :]
        high = up[pl.ds(pl.multiple_of(block * up_rows, up_rows), up_rows), :]
        to_down, to_in = (keep_down, keep_in) if slot < 2 else (send_down, send_in)
        kind = to_down.dtype
        to_down[slot % 2, :down_rows, :] = low[:, :half].astype(kind)
        to_down[slot % 2, down_rows:, :] = low[:, half:].astype(kind)
        to_in[slot % 2, :, :] = high.astype(kind)


def ffn_grads(line, place, w_in, w_down, b_in, normed, grads):
    rows, width = normed[0].shape
    tile = w_in.shape[1] // 4
    shape = (2, 2 * (tile // 4), width // 2)
    wide = (2, width // 4, tile)
    return line.run(
        ffn_grads_kernel,
        [w_in, w_down, b_in, *normed, *grads],
        [shaped(shape, F32), shaped(shape, BF16), shaped(wide, F32), shaped(wide, BF16)],
        grid=(1,),
        in_specs=[
            pl.BlockSpec((width, tile), lambda i, p: (0, p[0] >> 2)),
            pl.BlockSpec((tile, width), lambda i, p: (p[0] >> 2, 0)),
            pl.BlockSpec((1, tile), lambda i, p: (0, p[0] >> 2)),
        ]
        + [whole(item.shape) for item in [*normed, *grads]],
        out_specs=[whole(shape), whole(shape), whole(wide), whole(wide)],
        room=40,
        scratch=[
            pltpu.VMEM((2 * rows, width), BF16),
            pltpu.VMEM((2 * rows, width), BF16),
            pltpu.VMEM((2 * rows, tile), BF16),
            pltpu.VMEM((2 * rows, tile), BF16),
            pltpu.VMEM((tile, width), F32),
            pltpu.VMEM((width, tile), F32),
        ],
        place=place,
        flops=16 * rows * width * tile,
        moved=12 * rows * width + 16 * width * tile,
    )


def attend_back_kernel(
    seqs, place_ref, q_ref, k_ref, v_ref, g_branch_ref, w_out_ref, ctx_ref, tok_t_ref, few_ref,
    dq_ref, dk_ref, dv_ref, bias_ref, keep_ref, send_ref, total,
):
    few, inner = q_ref.shape
    rows = k_ref.shape[0]
    slots, length = few // seqs, rows // seqs
    low = lane_halves(slots)
    scale = HEAD ** (-0.5)
    g_branch = g_branch_ref[...]
    g_context = dot_nt(g_branch, w_out_ref[...]).astype(BF16)
    for seq in range(seqs):
        short, long = slice(seq * slots, (seq + 1) * slots), slice(seq * length, (seq + 1) * length)
        for at in range(0, inner, LANES):
            cut = slice(at, at + LANES)
            both, grads = two_heads(scaled(q_ref[short, cut])), two_heads(g_context[short, cut])
            keys, values = k_ref[long, cut], v_ref[long, cut]
            probs = softmax_rows(dot_nt(both, keys))
            grad_probs = dot_nt(grads, values)
            dv_ref[long, cut] = dot_tn(probs.astype(BF16), grads).astype(BF16)
            row_total = jnp.sum(grad_probs * probs, axis=-1, keepdims=True)
            grad_scores = (probs * (grad_probs - row_total)).astype(BF16)
            dq = mm(grad_scores, keys) * scale
            dq_ref[short, cut] = jnp.where(low, dq[:slots], dq[slots:]).astype(BF16)
            dk_ref[long, cut] = dot_tn(grad_scores, both).astype(BF16)
    dq, dk, dv = dq_ref[...], dk_ref[...], dv_ref[...]
    bias_ref[...] = jnp.concatenate(
        [
            jnp.sum(dq.astype(F32), axis=0, keepdims=True),
            jnp.sum(dv.astype(F32), axis=0, keepdims=True),
            jnp.zeros((6, inner), F32),
        ],
        axis=0,
    )
    total[0] = dot_tn(few_ref[...], dq)
    total[1] = mm(tok_t_ref[...], dk)
    total[2] = mm(tok_t_ref[...], dv)
    out_grad = dot_tn(ctx_ref[...], g_branch)
    total[3, :inner, :] = out_grad[:, :inner]
    total[3, inner:, :] = out_grad[:, inner:]
    block_rows = total.shape[1] // 16
    for slot in range(16):
        block = slot ^ place_ref[0]
        row = pl.multiple_of(block * block_rows, block_rows)
        for section in range(4):
            values = total[section, pl.ds(row, block_rows), :]
            cut = slice(section * block_rows, (section + 1) * block_rows)
            if slot < 8:
                keep_ref[slot, cut, :] = values
            else:
                send_ref[slot - 8, cut, :] = values.astype(BF16)


def attend_back(line, place, queries, keys, values, g_branch, w_out, context, tokens_t, few, seqs):
    rows, inner = keys.shape
    width = tokens_t.shape[0]
    count = queries.shape[0]
    held = (8, 4 * (width // 16), inner)
    return line.run(
        functools.partial(attend_back_kernel, seqs),
        [queries, keys, values, g_branch, w_out, context, tokens_t, few],
        [
            shaped((count, inner), BF16),
            shaped((rows, inner), BF16),
            shaped((rows, inner), BF16),
            shaped((8, inner), F32),
            shaped(held, F32),
            shaped(held, BF16),
        ],
        scratch=[pltpu.VMEM((4, width, inner), F32)],
        place=place,
        room=40,
        flops=4 * rows * width * inner + 24 * count * rows * inner,
        moved=20 * rows * inner,
    )


def fold_kernel(count, keep_ref, *refs):
    total = keep_ref[...]
    for ref in refs[:count]:
        total = total + ref[...].astype(F32)
    outs = refs[count:]
    if len(outs) == 1:
        outs[0][...] = total.astype(BF16)
    else:
        middle = total.shape[0] // 2
        outs[0][...] = total[:middle]
        outs[1][...] = total[middle:].astype(BF16)


def fold(line, keep, arrived, halve):
    if halve:
        half = (keep.shape[0] // 2, *keep.shape[1:])
        shapes = [shaped(half, F32), shaped(half, BF16)]
    else:
        shapes = [shaped(keep.shape, BF16)]
    results = line.run(
        functools.partial(fold_kernel, len(arrived)),
        [keep, *arrived],
        shapes,
        moved=(8 + 2 * len(arrived)) * keep.size,
    )
    return results if halve else results[0]


def append_kernel(mine_ref, near_ref, out_ref):
    count = mine_ref.shape[0]
    out_ref[:count] = mine_ref[...]
    out_ref[count:] = near_ref[...]


def append(line, mine, near):
    (result,) = line.run(
        append_kernel,
        [mine, near],
        [shaped((2 * mine.shape[0], *mine.shape[1:]), BF16)],
        moved=8 * mine.size,
    )
    return result


def add_kernel(left_ref, right_ref, out_ref):
    out_ref[...] = left_ref[...] + right_ref[...]


def add(line, left, right):
    (result,) = line.run(add_kernel, [left, right], [shaped(left.shape, left.dtype)], moved=12 * left.size)
    return result


def unpack_attend_kernel(place_ref, mine_ref, near_ref, qkv_ref, out_ref):
    rows = qkv_ref.shape[1] // 16
    inner = qkv_ref.shape[2]
    for slot in range(16):
        block = slot ^ place_ref[0]
        held = mine_ref if slot < 8 else near_ref
        values = held[slot % 8].astype(F32)
        row = pl.multiple_of(block * rows, rows)
        for section in range(3):
            cut = slice(section * rows, (section + 1) * rows)
            qkv_ref[section, pl.ds(row, rows), :] = values[cut, :]
        row = pl.multiple_of((block & 7) * rows, rows)
        column = pl.multiple_of((block >> 3) * inner, inner)
        out_ref[pl.ds(row, rows), pl.ds(column, inner)] = values[3 * rows :, :]


def unpack_attend(line, place, mine, near, width):
    _, held, inner = mine.shape
    return line.run(
        unpack_attend_kernel,
        [mine, near],
        [shaped((3, width, inner), F32), shaped((inner, width), F32)],
        place=place,
        moved=16 * held * inner * 6,
        room=20,
    )


def unpack_ffn_kernel(place_ref, *refs):
    down_ref, in_ref = refs[4:]
    rows, width = down_ref.shape[0] // 16, down_ref.shape[1]
    deep, wide = in_ref.shape[0] // 4, in_ref.shape[1] // 4
    for slot in range(16):
        block = slot ^ place_ref[0]
        down = refs[0 if slot < 8 else 1][slot % 8].astype(F32)
        row = pl.multiple_of(block * rows, rows)
        down_ref[pl.ds(row, rows), : width // 2] = down[:rows, :]
        down_ref[pl.ds(row, rows), width // 2 :] = down[rows:, :]
        row = pl.multiple_of((block & 3) * deep, deep)
        column = pl.multiple_of((block >> 2) * wide, wide)
        in_ref[pl.ds(row, deep), pl.ds(column, wide)] = refs[2 if slot < 8 else 3][
            slot % 8
        ].astype(F32)


def unpack_ffn(line, place, down, up, width, hidden):
    return line.run(
        unpack_ffn_kernel,
        [*down, *up],
        [shaped((hidden, width), F32), shaped((width, hidden), F32)],
        place=place,
        moved=12 * width * hidden,
        room=32,
    )


def attend_kernel(tok_ref, w_ref, bias_ref, k_ref, v_ref, out_ref):
    rows, inner = out_ref.shape
    low = lane_halves(rows)
    queries = scaled((mm(tok_ref[...], w_ref[0]) + bias_ref[0:1, :]).astype(BF16))
    for at in range(0, inner, LANES):
        cut = slice(at, at + LANES)
        block, keys, values = queries[:, cut], k_ref[:, cut], v_ref[:, cut]
        zero, one = jnp.zeros_like(block), jnp.ones_like(values)
        mixed = []
        for first in (True, False):
            head = jnp.where(low == first, block, zero)
            with_sums = jnp.where(lane_halves(values.shape[0]) == first, values, one)
            scores = dot_nt(head, keys)
            exponent = jnp.exp(scores - jnp.max(scores, axis=-1, keepdims=True)).astype(BF16)
            mixed.append(mm(exponent, with_sums))
        top = jnp.where(low, mixed[0], mixed[1])
        total = jnp.where(low, mixed[1], mixed[0])
        out_ref[:, cut] = (top / pltpu.roll(total, HEAD, 1)).astype(BF16)


def attend(line, tokens, weights, bias, keys, values, seqs, seq):
    rows, width = tokens.shape
    inner = keys.shape[1]
    length = rows // seqs
    long = pl.BlockSpec((length, inner), lambda s: (seq, 0))
    (result,) = line.run(
        attend_kernel,
        [tokens, weights, bias, keys, values],
        [shaped((length, inner), BF16)],
        grid=(1,),
        in_specs=[
            pl.BlockSpec((length, width), lambda s: (seq, 0)),
            pl.BlockSpec((1, width, inner), lambda s: (0, 0, 0)),
            whole(bias.shape),
            long,
            long,
        ],
        out_specs=[pl.BlockSpec((length, inner), lambda s: (0, 0))],
        flops=2 * length * width * inner + 16 * length * length * inner,
        moved=2 * (length * width + width * inner + 3 * length * inner),
        transcendentals=length * length * inner // HEAD,
        room=24,
    )
    return result


def layer_kernel(
    tok_ref, ctx_a, ctx_b, wo_a, wo_b, wi_a, wi_b, bi_a, bi_b, wd_a, wd_b, one_ref, two_ref, out_ref,
):
    branch = mm(ctx_a[...], wo_a[...]) + mm(ctx_b[...], wo_b[...]) + one_ref[0:1, :]
    unit, _ = norm_rows(tok_ref[...].astype(F32) + branch)
    normed = unit * one_ref[1:2, :] + one_ref[2:3, :]
    low = normed.astype(BF16)
    total = normed + two_ref[0:1, :]
    for w_in, b_in, w_down in ((wi_a, bi_a, wd_a), (wi_b, bi_b, wd_b)):
        hidden = gelu(mm(low, w_in[...]) + b_in[...]).astype(BF16)
        total = total + mm(hidden, w_down[...])
    unit, _ = norm_rows(total)
    out_ref[...] = (unit * two_ref[1:2, :] + two_ref[2:3, :]).astype(BF16)


def layer_next_kernel(*refs):
    layer_kernel(*refs[:-2], refs[-1])


def layer(line, tokens, contexts, w_out, w_in, b_in, w_down, one, two, seq, mixed):
    length, inner = contexts[0].shape
    width, hidden = tokens.shape[1], w_in[0].shape[1]
    tile = 256
    steps = length // tile
    ctx = pl.BlockSpec((tile, inner), lambda i: (i, 0))
    still = [*w_out, *w_in, *b_in, *w_down, one, two]
    row = pl.BlockSpec((tile, width), lambda i: (seq * steps + i, 0))
    args = [tokens, *contexts, *still]
    specs = [row, ctx, ctx] + [whole(item.shape) for item in still]
    (result,) = line.run(
        layer_kernel if mixed is None else layer_next_kernel,
        args if mixed is None else [*args, mixed],
        [shaped(tokens.shape, BF16)],
        grid=(steps,),
        in_specs=specs if mixed is None else [*specs, ANYWHERE],
        out_specs=[row],
        aliases={} if mixed is None else {len(args): 0},
        room=48,
        flops=2 * length * width * (width + 4 * hidden),
        moved=4 * width * (length + 2 * hidden),
        transcendentals=2 * length * hidden,
    )
    return result


def input_grad_kernel(
    dk_a, dk_b, dv_a, dv_b, dq_a, dq_b, w_a, w_b, g_first_ref, places_ref, out_ref
):
    length = out_ref.shape[0]
    slots = g_first_ref.shape[0]
    few = g_first_ref[...] + dot_nt(dq_a[...], w_a[0]) + dot_nt(dq_b[...], w_b[0])
    coarse = few.astype(BF16)
    fine = (few - coarse.astype(F32)).astype(BF16)
    picks = places_ref[0][:, 0:1] == lax.broadcasted_iota(jnp.int32, (slots, length), 1)
    picks = picks.astype(F32).astype(BF16)
    total = dot_tn(picks, coarse) + dot_tn(picks, fine)
    for dk, dv, w in ((dk_a, dv_a, w_a), (dk_b, dv_b, w_b)):
        total = total + dot_nt(dk[...], w[1]) + dot_nt(dv[...], w[2])
    out_ref[...] = total


def input_grad(line, backs, weights, g_first, places, seqs):
    rows, inner = backs[0][1].shape
    width = g_first.shape[1]
    length, slots = rows // seqs, g_first.shape[0] // seqs
    long = pl.BlockSpec((length, inner), lambda s: (s, 0))
    short = pl.BlockSpec((slots, inner), lambda s: (s, 0))
    (result,) = line.run(
        input_grad_kernel,
        [
            backs[0][1], backs[1][1], backs[0][2], backs[1][2], backs[0][0], backs[1][0],
            *weights, g_first, places,
        ],
        [shaped((rows, width), F32)],
        grid=(seqs,),
        in_specs=[long] * 4 + [short] * 2 + [whole(w.shape) for w in weights]
        + [
            pl.BlockSpec((slots, width), lambda s: (s, 0)),
            pl.BlockSpec((1, slots, LANES), lambda s: (s, 0, 0)),
        ],
        out_specs=[pl.BlockSpec((length, width), lambda s: (s, 0))],
        flops=10 * rows * width * inner,
        room=32,
        moved=20 * width * inner + 8 * rows * width,
    )
    return result


def pick_kernel(places_ref, fresh_ref, tok_ref, grad_ref, few_ref, grad_few_ref):
    slots, length = few_ref.shape[0], tok_ref.shape[0]
    picks = places_ref[0][:, 0:1] == lax.broadcasted_iota(jnp.int32, (slots, length), 1)
    picks = picks.astype(F32).astype(BF16)
    few_ref[...] = mm(picks, tok_ref[...]).astype(BF16)
    grad_few_ref[...] = mm(picks, grad_ref[...]) * fresh_ref[0][:, 0:1]


def pick(line, places, fresh, tokens, grads, seqs):
    rows, width = tokens.shape
    length, slots = rows // seqs, places.shape[1]
    flat = pl.BlockSpec((1, slots, LANES), lambda s: (s, 0, 0))
    long = pl.BlockSpec((length, width), lambda s: (s, 0))
    short = pl.BlockSpec((slots, width), lambda s: (s, 0))
    return line.run(
        pick_kernel,
        [places, fresh, tokens, grads],
        [shaped((seqs * slots, width), BF16), shaped((seqs * slots, width), F32)],
        grid=(seqs,),
        in_specs=[flat, flat, long, long],
        out_specs=[short, short],
        flops=4 * rows * slots * width,
        moved=4 * rows * width,
    )


def gather_small_kernel(place_ref, a_ref, b_ref, db_a, db_b, one_ref, two_ref, out_ref):
    inner, width = a_ref.shape[1], out_ref.shape[1]
    deep = db_a.shape[1] // width
    low = place_ref[0] == 0

    def ordered(own, oth):
        return jnp.where(low, own, oth), jnp.where(low, oth, own)

    for row in range(2):
        first, second = ordered(a_ref[row : row + 1, :], b_ref[row : row + 1, :])
        out_ref[row : row + 1, :inner] = first
        out_ref[row : row + 1, inner:] = second
    first, second = ordered(db_a[...], db_b[...])
    for row in range(deep):
        part = slice(row * width, (row + 1) * width)
        out_ref[2 + row : 3 + row, :] = first[:, part]
        out_ref[2 + deep + row : 3 + deep + row, :] = second[:, part]
    base = 2 + 2 * deep
    for row in range(3):
        out_ref[base + row : base + row + 1, :] = one_ref[row : row + 1, :]
        out_ref[base + 3 + row : base + 4 + row, :] = two_ref[row : row + 1, :]
    rest = out_ref.shape[0] - base - 6
    if rest:
        out_ref[base + 6 :, :] = jnp.zeros((rest, width), F32)


def gather_small(line, place, a, b, db_a, db_b, one, two):
    width = one.shape[1]
    count = 8 + 2 * (db_a.shape[1] // width)
    (result,) = line.run(
        gather_small_kernel,
        [a, b, db_a, db_b, one, two],
        [shaped((-(-count // 8) * 8, width), F32)],
        place=place,
    )
    return result


def body(
    tokens,
    grad_values,
    span_starts,
    w_qkv,
    b_qv,
    w_out,
    b_out,
    ln1_gain,
    ln1_bias,
    w_in,
    b_in,
    w_down,
    b_down,
    ln2_gain,
    ln2_bias,
):
    rows, width = tokens.shape
    inner = w_qkv.shape[2]
    hidden_half = w_in.shape[1]
    halves = lax.axis_size("tensor")
    seqs = span_starts.shape[0] // halves
    spans = span_starts.shape[1]
    length = rows // seqs
    half_at = lax.axis_index("tensor")
    me = lax.axis_index("dp")
    bits = lax.axis_size("dp").bit_length() - 1
    block_at = ((me & 1) << 3) | ((me & 2) << 1) | ((me & 4) >> 1) | ((me & 8) >> 3)
    place = block_at.reshape(1).astype(jnp.int32)
    rest = [1 << bit for bit in range(4, bits)]

    starts = lax.dynamic_slice_in_dim(span_starts, half_at * seqs, seqs, 0)
    places = starts[:, :, None] + jnp.arange(SPAN, dtype=jnp.int32)
    earlier = jnp.tril(jnp.ones((spans, spans), jnp.bool_), -1)
    covered = (places[:, :, :, None] >= starts[:, None, None, :]) & (
        places[:, :, :, None] < starts[:, None, None, :] + SPAN
    )
    fresh = ~jnp.any(covered & earlier[None, :, None, :], axis=-1)
    slots = -(-spans * SPAN // 16) * 16
    pad = slots - spans * SPAN
    places = jnp.pad(places.reshape(seqs, spans * SPAN), ((0, 0), (0, pad)))
    fresh = jnp.pad(fresh.reshape(seqs, spans * SPAN), ((0, 0), (0, pad)))
    few = seqs * slots
    places = jnp.broadcast_to(places[:, :, None], (seqs, slots, LANES))
    fresh = jnp.broadcast_to(fresh[:, :, None].astype(F32), (seqs, slots, LANES))
    vectors_one = jnp.stack([b_out, ln1_gain, ln1_bias])
    vectors_two = jnp.stack([b_down, ln2_gain, ln2_bias])
    tokens_t = tokens.T
    here = me.reshape(1)
    line = Line()

    w_qkv_own = jnp.transpose(w_qkv, (1, 0, 2))
    bias_pack = jnp.concatenate([b_qv.reshape(1, -1), b_in.reshape(-1, 2 * inner)], axis=0)

    def chips_around(held):
        return [held, flip(held, 2), flip(held, 4), flip(held, 6)]

    arrived_qkv = flip_tensor(cut_qkv(line, w_qkv_own, here))
    arrived_bias = flip_tensor(bias_pack)
    tokens_few, grad_few = pick(line, places, fresh, tokens, grad_values, seqs)
    own = project(line, tokens, tokens_few, w_qkv_own, b_qv, seqs)
    held_qkv, bias_other, half_out, eighth = second_cut(
        line, arrived_qkv, arrived_bias, w_out, w_in, w_down, here
    )
    around_qkv = chips_around(held_qkv)
    arrived_out, arrived_eighth = flip_tensor(half_out), flip_tensor(eighth)
    b_qv_both = [b_qv, bias_other[0].reshape(2, inner)]
    b_in_both = [b_in.reshape(1, -1), bias_other[1:].reshape(1, -1)]
    ctx_own = [
        attend(line, tokens, w_qkv_own, b_qv, own[0], own[1], seqs, seq) for seq in range(seqs)
    ]
    core_first, held_eighth, half_in = third_cut(
        line, around_qkv, arrived_out, arrived_eighth, w_in, here
    )
    near_first = flip(core_first, 1)
    around_eighth = chips_around(held_eighth)
    arrived_in = flip_tensor(half_in)
    w_qkv_oth, w_out_oth = first_assemble(line, core_first, near_first, width, inner, here)
    w_qkv_both, w_out_both = [w_qkv_own, w_qkv_oth], [w_out, w_out_oth]
    oth = project(line, tokens, tokens_few, w_qkv_oth, b_qv_both[1], seqs)

    keys, values, queries_few, context_few = zip(own, oth)
    normed_few, normed_low, unit_one, root_one = first_norm(
        line, context_few, w_out_both, tokens_few, vectors_one
    )

    def plane(values):
        return [values, flip_tensor(values), flip(values, 2), flip_both(values, 2)]

    slope_a, part = ffn_forward(line, normed_low, w_in, b_in_both[0], w_down)
    core_second, held_in = fourth_cut(line, around_eighth, arrived_in)
    near_second, near_in = flip(core_second, 1), flip(held_in, 1)
    around_normed = plane(normed_low)
    w_in_oth, w_down_oth = second_assemble(
        line, core_second, near_second, held_in, near_in, hidden_half, here
    )
    w_in_both, w_down_both = [w_in, w_in_oth], [w_down, w_down_oth]
    slope_b, g_ffn, g_second, sums_two = ffn_forward(
        line, normed_low, w_in_both[1], b_in_both[1], w_down_both[1],
        [part, normed_few, grad_few, vectors_two],
    )
    around_g = plane(g_ffn)
    core_normed = join(line, around_normed)
    near_normed = flip(core_normed, 1)
    db_a, db_b, g_first, g_branch, sums_one = ffn_backward(
        line, g_ffn, g_second, unit_one, root_one, vectors_one, (slope_a, slope_b), w_in_both, w_down_both
    )

    def back(at):
        return attend_back(
            line, place, queries_few[at], keys[at], values[at], g_branch, w_out_both[at],
            context_few[at], tokens_t, tokens_few, seqs,
        )

    back_oth = back(1)
    near_oth = flip(back_oth[5], 1)
    core_g = join(line, around_g)
    near_g = flip(core_g, 1)
    sum_oth = fold(line, back_oth[4], [near_oth], False)
    cross_oth = flip_tensor(sum_oth)

    keep_down, send_down, keep_in, send_in = ffn_grads(
        line, place, w_in, w_down, b_in_both[0], [core_normed, near_normed], [core_g, near_g]
    )
    z_down, z_in = flip(send_down, 4), flip(send_in, 4)
    back_own = back(0)
    near_own = flip(back_own[5], 1)

    small = gather_small(
        line, half_at.reshape(1), back_own[3], back_oth[3], db_a, db_b, sums_one, sums_two
    )
    small_near = flip(small, 1)
    small = add(line, small, small_near)
    small_near = flip_tensor(small)
    ctx_oth = [
        attend(line, tokens, w_qkv_oth, b_qv_both[1], keys[1], values[1], seqs, seq)
        for seq in range(seqs)
    ]
    keep_down, send_down = fold(line, keep_down, [z_down], True)
    z_down = flip(send_down, 8)
    keep_in, send_in = fold(line, keep_in, [z_in], True)
    z_in = flip(send_in, 8)
    small = add(line, small, small_near)
    small_near = flip(small, 2)
    keep, send = fold(line, back_own[4], [near_own, cross_oth], True)
    y_attn = flip(send, 2)

    def over_rest(total):
        for bit in rest:
            total = total + flip(total, bit)
        return total

    def layer_of(seq, mixed):
        return layer(
            line, tokens, [ctx_own[seq], ctx_oth[seq]], w_out_both, w_in_both, b_in_both, w_down_both,
            vectors_one, vectors_two, seq, mixed,
        )

    mixed = layer_of(0, None)
    down = fold(line, over_rest(keep_down), [over_rest(z_down)], False)
    near_down = flip(down, 8)
    up = fold(line, over_rest(keep_in), [over_rest(z_in)], False)
    near_up = flip(up, 8)
    keep, send = fold(line, keep, [y_attn], True)
    z_attn = flip(send, 4)
    small = add(line, small, small_near)
    small_near = flip(small, 4)
    for seq in range(1, seqs):
        mixed = layer_of(seq, mixed)
    down = append(line, down, near_down)
    near_down = flip(down, 4)
    up = append(line, up, near_up)
    near_up = flip(up, 4)
    keep, send = fold(line, keep, [z_attn], True)
    z_attn = flip(send, 8)
    small = add(line, small, small_near)
    small_near = flip(small, 8)
    d_tokens = input_grad(line, [back_own, back_oth], w_qkv_both, g_first, places, seqs)
    down = append(line, down, near_down)
    near_down = flip(down, 2)
    up = append(line, up, near_up)
    near_up = flip(up, 2)
    attn = fold(line, over_rest(keep), [over_rest(z_attn)], False)
    near_attn = flip(attn, 8)
    small = over_rest(add(line, small, small_near))
    attn = append(line, attn, near_attn)
    near_attn = flip(attn, 4)
    attn = append(line, attn, near_attn)
    near_attn = flip(attn, 2)
    down = append(line, down, near_down)
    near_down = flip(down, 1)
    up = append(line, up, near_up)
    near_up = flip(up, 1)
    attn = append(line, attn, near_attn)
    near_attn = flip(attn, 1)
    d_w_down, d_w_in = unpack_ffn(line, place, [down, near_down], [up, near_up], width, hidden_half)
    d_w_qkv, d_w_out = unpack_attend(line, place, attn, near_attn, width)
    d_w_qkv = jnp.transpose(d_w_qkv, (1, 0, 2))

    deep = hidden_half // width
    d_b_qv = lax.dynamic_slice(small, (0, half_at * inner), (2, inner))
    d_b_in = lax.dynamic_slice(small, (2 + half_at * deep, 0), (deep, width)).reshape(-1)
    d_ln1_gain, d_ln1_bias, d_b_out, d_ln2_gain, d_ln2_bias, d_b_down = [
        small[2 + 2 * deep + at] for at in range(6)
    ]

    return (
        mixed,
        d_tokens,
        d_w_qkv,
        d_b_qv,
        d_w_out,
        d_b_out,
        d_ln1_gain,
        d_ln1_bias,
        d_w_in,
        d_b_in,
        d_w_down,
        d_b_down,
        d_ln2_gain,
        d_ln2_bias,
    )


def solution(mesh):
    placed = (
        P(("dp", "tensor"), None),
        P(("dp", "tensor"), None),
        P("dp", None),
        P(None, None, "tensor"),
        P(None, "tensor"),
        P("tensor", None),
        P(),
        P(),
        P(),
        P(None, "tensor"),
        P("tensor"),
        P("tensor", None),
        P(),
        P(),
        P(),
    )
    return jax.shard_map(
        body,
        mesh=mesh,
        in_specs=placed,
        out_specs=(
            P(("dp", "tensor"), None),
            P(("dp", "tensor"), None),
            P(None, None, "tensor"),
            P(None, "tensor"),
            P("tensor", None),
            P(),
            P(),
            P(),
            P(None, "tensor"),
            P("tensor"),
            P("tensor", None),
            P(),
            P(),
            P(),
        ),
        check_vma=False,
    )
```

```python
import functools

import jax
import jax.numpy as jnp
from jax import lax
from jax.experimental import pallas as pl
from jax.experimental.pallas import tpu as pltpu
from jax.sharding import PartitionSpec as P

HEAD = 64
SPAN = 6
LANES = 128
EPSILON = 1e-05
F32 = jnp.float32
BF16 = jnp.bfloat16
GELU_A = (2.0 / 3.141592653589793) ** 0.5
GELU_B = 0.044715
ANYWHERE = pl.BlockSpec(memory_space=pl.ANY)
VMEM = pl.BlockSpec(memory_space=pltpu.VMEM)


class Line:
    def __init__(self):
        self.token = jnp.zeros((8, LANES), F32)

    def run(
        self, kernel, args, out_shape, grid=(), in_specs=None, out_specs=None, scratch=(), place=None,
        flops=0, moved=0, transcendentals=0, room=12, aliases=None, weight=1,
    ):
        ins, outs = len(args), len(out_shape)
        lead = 0 if place is None else 1

        def with_token(*refs):
            given, rest = refs[: lead + ins], refs[lead + ins + 1 :]
            rest[outs][...] = jnp.zeros((8, LANES), F32)
            kernel(*given, *rest[:outs], *rest[outs + 1 :])

        in_specs = list(in_specs or [VMEM] * ins) + [ANYWHERE]
        out_specs = list(out_specs or [VMEM] * outs)
        out_specs.append(pl.BlockSpec((8, LANES), lambda *at: (0, 0)) if grid else VMEM)
        shapes = list(out_shape) + [jax.ShapeDtypeStruct((8, LANES), F32)]
        params = dict(
            out_shape=shapes,
            input_output_aliases=aliases or {},
            compiler_params=pltpu.CompilerParams(vmem_limit_bytes=room << 20),
            cost_estimate=pl.CostEstimate(
                flops=int(flops * weight),
                bytes_accessed=int(moved * weight),
                transcendentals=int(transcendentals * weight),
            ),
        )
        if lead and grid:
            params["grid_spec"] = pltpu.PrefetchScalarGridSpec(
                num_scalar_prefetch=1, grid=grid, in_specs=in_specs, out_specs=out_specs, scratch_shapes=list(scratch)
            )
        else:
            if lead:
                in_specs = [pl.BlockSpec(memory_space=pltpu.SMEM)] + in_specs
            params.update(grid=grid, in_specs=in_specs, out_specs=out_specs, scratch_shapes=list(scratch))
        front = [] if place is None else [place]
        *results, self.token = pl.pallas_call(with_token, **params)(*front, *args, self.token)
        return results


def shaped(shape, kind):
    return jax.ShapeDtypeStruct(tuple(shape), kind)


def whole(shape, once=False):
    held = dict(pipeline_mode=pl.Buffered(1)) if once else {}
    return pl.BlockSpec(shape, lambda *at: (0,) * len(shape), **held)


def flip(values, bits):
    size = lax.axis_size("dp")
    return lax.ppermute(values, "dp", [(at, at ^ bits) for at in range(size)])


def flip_tensor(values):
    return lax.ppermute(values, "tensor", [(0, 1), (1, 0)])


def flip_both(values, bits):
    size = 2 * lax.axis_size("dp")
    pairs = [(at, at ^ (2 * bits + 1)) for at in range(size)]
    return lax.ppermute(values, ("dp", "tensor"), pairs)


def dot_nt(left, right):
    return lax.dot_general(left, right, (((1,), (1,)), ((), ())), preferred_element_type=F32)


def dot_tn(left, right):
    return lax.dot_general(left, right, (((0,), (0,)), ((), ())), preferred_element_type=F32)


def mm(left, right):
    return jnp.dot(left, right, preferred_element_type=F32)


def lane_halves(rows):
    return lax.broadcasted_iota(jnp.int32, (rows, LANES), 1) < HEAD


def two_heads(block):
    low = lane_halves(block.shape[0])
    zero = jnp.zeros_like(block)
    return jnp.concatenate([jnp.where(low, block, zero), jnp.where(low, zero, block)], axis=0)


def scaled(queries):
    return queries * jnp.asarray(HEAD ** (-0.5), BF16)


def softmax_rows(scores):
    exponent = jnp.exp(scores - jnp.max(scores, axis=-1, keepdims=True))
    return exponent * (1.0 / jnp.sum(exponent, axis=-1, keepdims=True))


def attend_block(queries, keys, values):
    rows = queries.shape[0]
    probs = softmax_rows(dot_nt(two_heads(scaled(queries)), keys)).astype(BF16)
    mixed = mm(probs, values)
    return jnp.where(lane_halves(rows), mixed[:rows], mixed[rows:]).astype(BF16)


def norm_rows(values):
    average = jnp.mean(values, axis=-1, keepdims=True)
    centered = values - average
    variance = jnp.mean(centered * centered, axis=-1, keepdims=True)
    root = lax.rsqrt(variance + EPSILON)
    return centered * root, root


def norm_back(grad, unit, root, gain):
    grad_y = grad * gain
    inner = jnp.mean(grad_y, axis=-1, keepdims=True)
    along = jnp.mean(grad_y * unit, axis=-1, keepdims=True)
    return root * (grad_y - inner - unit * along)


def gelu_and_slope(values):
    square = values * values
    bent = jnp.tanh(GELU_A * values * (1.0 + GELU_B * square))
    half = 0.5 * (1.0 + bent)
    slope = half + 0.5 * values * (1.0 - bent * bent) * GELU_A * (1.0 + 3.0 * GELU_B * square)
    return values * half, slope


def gelu(values):
    return 0.5 * values * (1.0 + jnp.tanh(GELU_A * values * (1.0 + GELU_B * values * values)))


def join_kernel(count, *refs):
    rows = refs[0].shape[-2]
    for at in range(count):
        refs[count][..., at * rows : (at + 1) * rows, :] = refs[at][...]


def join(line, pieces):
    *lead, rows, columns = pieces[0].shape
    (result,) = line.run(
        functools.partial(join_kernel, len(pieces)),
        pieces,
        [shaped((*lead, rows * len(pieces), columns), pieces[0].dtype)],
        moved=4 * len(pieces) * pieces[0].size,
    )
    return result


def cut_qkv_kernel(place_ref, in_ref, out_ref, sem):
    rows = out_ref.shape[1]
    row = pl.multiple_of((place_ref[0] & 7) * rows, rows)
    copy = pltpu.make_async_copy(in_ref.at[:, pl.ds(row, rows), :], out_ref, sem)
    copy.start()
    copy.wait()


def cut_qkv(line, w_qkv, here):
    lead, rows, columns = w_qkv.shape
    (piece,) = line.run(
        cut_qkv_kernel,
        [w_qkv],
        [shaped((lead, rows // 8, columns), BF16)],
        in_specs=[ANYWHERE],
        scratch=[pltpu.SemaphoreType.DMA],
        place=here,
        moved=w_qkv.size // 2,
        room=56,
    )
    return piece


def second_cut_kernel(place_ref, qkv_ref, bias_a, bias_b, out_ref, in_ref, down_ref, qkv, to_a, to_b, half, eighth):
    qkv[...] = qkv_ref[...]
    to_a[...] = bias_a[...]
    to_b[...] = bias_b[...]
    half[...] = out_ref[...]
    rows = in_ref.shape[0]
    eighth[:rows, :] = in_ref[...]
    eighth[rows:, :] = down_ref[...]


def second_cut(line, qkv, biases, w_out, w_in, w_down, here):
    width = w_out.shape[1]
    half, eighth, deep = w_out.shape[0] // 2, w_in.shape[0] // 8, w_down.shape[0] // 8
    return line.run(
        second_cut_kernel,
        [qkv, *biases, w_out, w_in, w_down],
        [
            shaped(qkv.shape, BF16),
            *[shaped(bias.shape, F32) for bias in biases],
            shaped((half, width), BF16),
            shaped((eighth + deep, width), BF16),
        ],
        grid=(1,),
        in_specs=[
            whole(qkv.shape),
            *[whole(bias.shape) for bias in biases],
            pl.BlockSpec((half, width), lambda i, p: (p[0] & 1, 0)),
            pl.BlockSpec((eighth, width), lambda i, p: (p[0] & 7, 1)),
            pl.BlockSpec((deep, width), lambda i, p: (p[0] & 7, 0)),
        ],
        out_specs=[
            whole(qkv.shape), *[whole(bias.shape) for bias in biases],
            whole((half, width)), whole((eighth + deep, width)),
        ],
        place=here,
        moved=4 * (qkv.size + (half + eighth + deep) * width),
    )


def third_cut_kernel(place_ref, a, b, c, d, out_ref, eighth_ref, in_ref, core, eighth, half):
    third, rows, inner = a.shape
    for at, ref in enumerate((a, b, c, d)):
        for section in range(third):
            row = (section * 4 + at) * rows
            core[row : row + rows, :] = ref[section]
    row = 4 * third * rows
    deep = out_ref.shape[0]
    core[row : row + deep, :] = out_ref[:, :inner]
    core[row + deep :, :] = out_ref[:, inner:]
    eighth[...] = eighth_ref[...]
    half[...] = in_ref[...]


def third_cut(line, qkv, out, eighth, w_in, here):
    third, rows, inner = qkv[0].shape
    width = out.shape[1]
    height = 4 * third * rows + 2 * out.shape[0]
    half = (w_in.shape[0] // 2, width)
    return line.run(
        third_cut_kernel,
        [*qkv, out, eighth, w_in],
        [shaped((height, inner), BF16), shaped(eighth.shape, BF16), shaped(half, BF16)],
        grid=(1,),
        in_specs=[whole(item.shape) for item in [*qkv, out, eighth]]
        + [pl.BlockSpec(half, lambda i, p: (p[0] & 1, 0))],
        out_specs=[whole((height, inner)), whole(eighth.shape), whole(half)],
        place=here,
        moved=4 * (height * inner + eighth.size + half[0] * width),
    )


def first_assemble_kernel(place_ref, mine, near, qkv_ref, out_ref):
    third, width, inner = qkv_ref.shape
    rows, half = width // 8, out_ref.shape[0] // 2
    for core, ref in enumerate((mine, near)):
        for at in range(4):
            row = pl.multiple_of(((place_ref[0] ^ (2 * at + core)) & 7) * rows, rows)
            for section in range(third):
                start = (section * 4 + at) * rows
                qkv_ref[section, pl.ds(row, rows), :] = ref[start : start + rows, :]
        row = pl.multiple_of(((place_ref[0] ^ core) & 1) * half, half)
        start = 4 * third * rows
        out_ref[pl.ds(row, half), :inner] = ref[start : start + half, :]
        out_ref[pl.ds(row, half), inner:] = ref[start + half :, :]


def first_assemble(line, mine, near, width, inner, here):
    return line.run(
        first_assemble_kernel,
        [mine, near],
        [shaped((3, width, inner), BF16), shaped((inner, width), BF16)],
        place=here,
        moved=8 * mine.size,
    )


def fourth_cut_kernel(a, b, c, d, half_ref, eighths, half):
    rows = a.shape[0]
    for at, ref in enumerate((a, b, c, d)):
        eighths[at * rows : (at + 1) * rows, :] = ref[...]
    half[...] = half_ref[...]


def fourth_cut(line, eighths, half):
    rows, width = eighths[0].shape
    return line.run(
        fourth_cut_kernel,
        [*eighths, half],
        [shaped((4 * rows, width), BF16), shaped(half.shape, BF16)],
        moved=16 * rows * width,
    )


def second_assemble_kernel(place_ref, mine, near, half_mine, half_near, in_ref, down_ref):
    width = half_mine.shape[1]
    rows, deep, half = in_ref.shape[0] // 8, down_ref.shape[0] // 8, half_mine.shape[0]
    for core, (ref, half_ref) in enumerate(((mine, half_mine), (near, half_near))):
        for at in range(4):
            block = (place_ref[0] ^ (2 * at + core)) & 7
            start = at * (rows + deep)
            in_ref[pl.ds(pl.multiple_of(block * rows, rows), rows), width:] = ref[
                start : start + rows, :
            ]
            down_ref[pl.ds(pl.multiple_of(block * deep, deep), deep), :] = ref[
                start + rows : start + rows + deep, :
            ]
        row = pl.multiple_of(((place_ref[0] ^ core) & 1) * half, half)
        in_ref[pl.ds(row, half), :width] = half_ref[...]


def second_assemble(line, mine, near, half_mine, half_near, hidden, here):
    width = half_mine.shape[1]
    return line.run(
        second_assemble_kernel,
        [mine, near, half_mine, half_near],
        [shaped((width, hidden), BF16), shaped((hidden, width), BF16)],
        place=here,
        moved=8 * width * hidden,
        room=24,
    )


def project_kernel(tok_ref, few_ref, w_ref, bias_ref, k_ref, v_ref, q_ref, ctx_ref):
    tok = tok_ref[...]
    k_ref[...] = mm(tok, w_ref[1]).astype(BF16)
    v_ref[...] = (mm(tok, w_ref[2]) + bias_ref[1:2, :]).astype(BF16)
    q_ref[...] = (mm(few_ref[...], w_ref[0]) + bias_ref[0:1, :]).astype(BF16)
    for at in range(0, k_ref.shape[1], LANES):
        cut = slice(at, at + LANES)
        ctx_ref[:, cut] = attend_block(q_ref[:, cut], k_ref[:, cut], v_ref[:, cut])


def project(line, tokens, few, weights, bias, seqs):
    rows, width = tokens.shape
    inner = weights.shape[2]
    length, slots = rows // seqs, few.shape[0] // seqs
    long, short = (pl.BlockSpec((size, inner), lambda s: (s, 0)) for size in (length, slots))
    return line.run(
        project_kernel,
        [tokens, few, weights, bias],
        [shaped((rows, inner), BF16)] * 2 + [shaped((few.shape[0], inner), BF16)] * 2,
        grid=(seqs,),
        in_specs=[
            pl.BlockSpec((length, width), lambda s: (s, 0)),
            pl.BlockSpec((slots, width), lambda s: (s, 0)),
            whole(weights.shape),
            whole(bias.shape),
        ],
        out_specs=[long, long, short, short],
        flops=6 * rows * width * inner,
        room=24,
        moved=2 * (rows * width + 3 * width * inner + 2 * rows * inner),
    )


def first_norm_kernel(ctx_a, ctx_b, w_a, w_b, few_ref, vec_ref, sum_ref, low_ref):
    branch = mm(ctx_a[...], w_a[...]) + mm(ctx_b[...], w_b[...]) + vec_ref[0:1, :]
    total = few_ref[...].astype(F32) + branch
    sum_ref[...] = total
    low_ref[...] = (norm_rows(total)[0] * vec_ref[1:2, :] + vec_ref[2:3, :]).astype(BF16)


def first_norm(line, contexts, w_out, few, vectors):
    count, width = few.shape
    return line.run(
        first_norm_kernel,
        [*contexts, *w_out, few, vectors],
        [shaped((count, width), F32), shaped((count, width), BF16)],
        flops=2 * count * width * width,
        moved=2 * width * width + 14 * count * width,
    )


def ffn_part_kernel(low_ref, wi_ref, bi_ref, wd_ref, slope_ref, part_ref, total):
    step = pl.program_id(0)
    gate, slope = gelu_and_slope(mm(low_ref[...], wi_ref[...]) + bi_ref[...])
    slope_ref[...] = slope
    part = mm(gate.astype(BF16), wd_ref[...])

    @pl.when(step == 0)
    def _():
        total[...] = part

    @pl.when(step > 0)
    def _():
        total[...] += part

    @pl.when(step == pl.num_programs(0) - 1)
    def _():
        part_ref[...] = total[...]


def ffn_part(line, low, w_in, b_in, w_down):
    count, width = low.shape
    hidden = w_in.shape[1]
    steps = 4
    tile = hidden // steps
    flat = whole((count, width))
    return line.run(
        ffn_part_kernel,
        [low, w_in, b_in, w_down],
        [shaped((count, hidden), F32), shaped((count, width), F32)],
        grid=(steps,),
        in_specs=[
            flat,
            pl.BlockSpec((width, tile), lambda j: (0, j)),
            pl.BlockSpec((1, tile), lambda j: (0, j)),
            pl.BlockSpec((tile, width), lambda j: (j, 0)),
        ],
        out_specs=[pl.BlockSpec((count, tile), lambda j: (0, j)), flat],
        scratch=[pltpu.VMEM((count, width), F32)],
        flops=4 * count * width * hidden,
        moved=4 * width * hidden,
        transcendentals=count * hidden,
        room=20,
    )


def column_sum(values):
    return jnp.sum(values, axis=0, keepdims=True)


def ffn_kernel(
    low_ref, part_ref, sum_ref, grad_ref, one_ref, two_ref, slope_ref, wi_a, wi_b, bi_b, wd_a, wd_b,
    g_ffn_ref, g_branch_ref, g_first_ref, small_ref,
):
    gate, slope = gelu_and_slope(mm(low_ref[...], wi_b[...]) + bi_b[...])
    ffn = part_ref[...] + mm(gate.astype(BF16), wd_b[...]) + two_ref[0:1, :]
    unit_one, root_one = norm_rows(sum_ref[...])
    normed = unit_one * one_ref[1:2, :] + one_ref[2:3, :]
    unit, root = norm_rows(normed + ffn)
    grad = grad_ref[...]
    g_second = norm_back(grad, unit, root, two_ref[1:2, :])
    g_ffn = g_second.astype(BF16)
    g_ffn_ref[...] = g_ffn
    width = grad.shape[1]
    half = width // 2
    hidden = slope.shape[1]
    deep = hidden // half
    g_normed = g_second
    for at, (bend, w_in, w_down) in enumerate(((slope_ref[...], wi_a, wd_a), (slope, wi_b, wd_b))):
        g_pre = (bend * dot_nt(g_ffn, w_down[...])).astype(BF16)
        bias = column_sum(g_pre.astype(F32))
        for row in range(deep):
            small_ref[at * deep + row : at * deep + row + 1, :] = bias[:, row * half : (row + 1) * half]
        g_normed = g_normed + dot_nt(g_pre, w_in[...])
    g_first = norm_back(g_normed, unit_one, root_one, one_ref[1:2, :])
    g_branch = g_first.astype(BF16)
    g_first_ref[...] = g_first
    g_branch_ref[...] = g_branch
    vectors = (
        column_sum(g_branch.astype(F32)),
        column_sum(g_normed * unit_one),
        column_sum(g_normed),
        column_sum(g_ffn.astype(F32)),
        column_sum(grad * unit),
        column_sum(grad),
    )
    for at, vector in enumerate(vectors):
        row = 2 * deep + 2 * at
        small_ref[row : row + 1, :] = vector[:, :half]
        small_ref[row + 1 : row + 2, :] = vector[:, half:]
    count = 2 * deep + 12
    small_ref[count:, :] = jnp.zeros((small_ref.shape[0] - count, half), F32)


def ffn(line, low, part, total, grad, one, two, slope, w_in, b_in, w_down):
    count, width = low.shape
    hidden = w_in[0].shape[1]
    rows = 2 * (hidden // (width // 2)) + 12
    return line.run(
        ffn_kernel,
        [low, part, total, grad, one, two, slope, *w_in, b_in, *w_down],
        [
            shaped((count, width), BF16),
            shaped((count, width), BF16),
            shaped((count, width), F32),
            shaped((-(-rows // 8) * 8, width // 2), F32),
        ],
        flops=12 * count * width * hidden,
        moved=8 * width * hidden,
        room=16,
    )


def ffn_grads_kernel(place_ref, wi_ref, wd_ref, bi_ref, *refs):
    normed_refs, grad_refs = refs[:2], refs[2:4]
    keep_down, send_down, keep_in, send_in = refs[4:8]
    down, up = refs[8:]
    width = normed_refs[0].shape[1]
    tile = wi_ref.shape[1]
    for at in range(2):
        normed, grad = normed_refs[at][...], grad_refs[at][...]
        gate, slope = gelu_and_slope(mm(normed, wi_ref[...]) + bi_ref[...])
        pre = (slope * dot_nt(grad, wd_ref[...])).astype(BF16)
        down_part = dot_tn(gate.astype(BF16), grad)
        up_part = dot_tn(normed, pre)
        if at == 0:
            down[...] = down_part
            up[...] = up_part
        else:
            down[...] += down_part
            up[...] += up_part
    down_rows, up_rows = tile // 4, width // 4
    half = width // 2
    for slot in range(4):
        block = slot ^ (place_ref[0] & 3)
        low = down[pl.ds(pl.multiple_of(block * down_rows, down_rows), down_rows), :]
        block = (0, 2, 1, 3)[slot] ^ (place_ref[0] & 3)
        high = up[pl.ds(pl.multiple_of(block * up_rows, up_rows), up_rows), :]
        to_down, to_in = (keep_down, keep_in) if slot < 2 else (send_down, send_in)
        kind = to_down.dtype
        to_down[slot % 2, :down_rows, :] = low[:, :half].astype(kind)
        to_down[slot % 2, down_rows:, :] = low[:, half:].astype(kind)
        to_in[slot % 2, :, :] = high.astype(kind)


def ffn_grads(line, place, w_in, w_down, b_in, normed, grads):
    rows, width = normed[0].shape
    tile = w_in.shape[1] // 4
    shape = (2, 2 * (tile // 4), width // 2)
    wide = (2, width // 4, tile)
    return line.run(
        ffn_grads_kernel,
        [w_in, w_down, b_in, *normed, *grads],
        [shaped(shape, F32), shaped(shape, BF16), shaped(wide, F32), shaped(wide, BF16)],
        grid=(1,),
        in_specs=[
            pl.BlockSpec((width, tile), lambda i, p: (0, p[0] >> 2)),
            pl.BlockSpec((tile, width), lambda i, p: (p[0] >> 2, 0)),
            pl.BlockSpec((1, tile), lambda i, p: (0, p[0] >> 2)),
        ]
        + [whole(item.shape) for item in [*normed, *grads]],
        out_specs=[whole(shape), whole(shape), whole(wide), whole(wide)],
        scratch=[pltpu.VMEM((tile, width), F32), pltpu.VMEM((width, tile), F32)],
        place=place,
        flops=16 * rows * width * tile,
        moved=12 * rows * width + 16 * width * tile,
        room=32,
    )


def attend_back_kernel(
    seqs, half, deep, place_ref, q_ref, k_ref, v_ref, g_branch_ref, w_out_ref, ctx_ref, tok_t_ref, few_ref,
    small_ref, dq_ref, dk_ref, dv_ref, keep_ref, send_ref, total, little,
):
    few, inner = q_ref.shape
    rows = k_ref.shape[0]
    slots, length = few // seqs, rows // seqs
    low = lane_halves(slots)
    scale = HEAD ** (-0.5)
    g_branch = g_branch_ref[...]
    g_context = dot_nt(g_branch, w_out_ref[...]).astype(BF16)
    for seq in range(seqs):
        short, long = slice(seq * slots, (seq + 1) * slots), slice(seq * length, (seq + 1) * length)
        for at in range(0, inner, LANES):
            cut = slice(at, at + LANES)
            both, grads = two_heads(scaled(q_ref[short, cut])), two_heads(g_context[short, cut])
            keys, values = k_ref[long, cut], v_ref[long, cut]
            probs = softmax_rows(dot_nt(both, keys))
            grad_probs = dot_nt(grads, values)
            dv_ref[long, cut] = dot_tn(probs.astype(BF16), grads).astype(BF16)
            row_total = jnp.sum(grad_probs * probs, axis=-1, keepdims=True)
            grad_scores = (probs * (grad_probs - row_total)).astype(BF16)
            dq = mm(grad_scores, keys) * scale
            dq_ref[short, cut] = jnp.where(low, dq[:slots], dq[slots:]).astype(BF16)
            dk_ref[long, cut] = dot_tn(grad_scores, both).astype(BF16)
    dq, dk, dv = dq_ref[...], dk_ref[...], dv_ref[...]
    total[0] = dot_tn(few_ref[...], dq)
    total[1] = mm(tok_t_ref[...], dk)
    total[2] = mm(tok_t_ref[...], dv)
    out_grad = dot_tn(ctx_ref[...], g_branch)
    total[3, :inner, :] = out_grad[:, :inner]
    total[3, inner:, :] = out_grad[:, inner:]
    little[...] = jnp.zeros_like(little)
    little[0, 0:1, :] = column_sum(dq.astype(F32))
    little[0, 1:2, :] = column_sum(dv.astype(F32))
    for at in range(deep + 12):
        source = half * deep + at if at < deep else deep + at
        little[1 + at // 2, at % 2 : at % 2 + 1, :] = small_ref[source : source + 1, :]
    block_rows = total.shape[1] // 16
    pad = keep_ref.shape[1] - 4 * block_rows
    for slot in range(16):
        block = slot ^ place_ref[0]
        row = pl.multiple_of(block * block_rows, block_rows)
        to, kind = (keep_ref, F32) if slot < 8 else (send_ref, BF16)
        for section in range(4):
            cut = slice(section * block_rows, (section + 1) * block_rows)
            to[slot % 8, cut, :] = total[section, pl.ds(row, block_rows), :].astype(kind)
        pair = jnp.concatenate([little[block], jnp.zeros((pad - 8, inner), F32)], axis=0)
        to[slot % 8, 4 * block_rows :, :] = pair.astype(kind)


def attend_back(line, place, queries, keys, values, g_branch, w_out, context, tokens_t, few, small, seqs, half, deep):
    rows, inner = keys.shape
    width = tokens_t.shape[0]
    count = queries.shape[0]
    held = (8, 4 * (width // 16) + 16, inner)
    return line.run(
        functools.partial(attend_back_kernel, seqs, half, deep),
        [queries, keys, values, g_branch, w_out, context, tokens_t, few, small],
        [
            shaped((count, inner), BF16),
            shaped((rows, inner), BF16),
            shaped((rows, inner), BF16),
            shaped(held, F32),
            shaped(held, BF16),
        ],
        scratch=[pltpu.VMEM((4, width, inner), F32), pltpu.VMEM((16, 8, inner), F32)],
        place=place,
        room=32,
        flops=4 * rows * width * inner + 24 * count * rows * inner,
        moved=20 * rows * inner,
    )


def fold_kernel(count, keep_ref, *refs):
    total = keep_ref[...]
    for ref in refs[:count]:
        total = total + ref[...].astype(F32)
    outs = refs[count:]
    if len(outs) == 1:
        outs[0][...] = total.astype(BF16)
    else:
        middle = total.shape[0] // 2
        outs[0][...] = total[:middle]
        outs[1][...] = total[middle:].astype(BF16)


def fold(line, keep, arrived, halve):
    if halve:
        half = (keep.shape[0] // 2, *keep.shape[1:])
        shapes = [shaped(half, F32), shaped(half, BF16)]
    else:
        shapes = [shaped(keep.shape, BF16)]
    results = line.run(
        functools.partial(fold_kernel, len(arrived)),
        [keep, *arrived],
        shapes,
        moved=(8 + 2 * len(arrived)) * keep.size,
    )
    return results if halve else results[0]


def append_kernel(mine_ref, near_ref, out_ref):
    count = mine_ref.shape[0]
    out_ref[:count] = mine_ref[...]
    out_ref[count:] = near_ref[...]


def append(line, mine, near):
    (result,) = line.run(
        append_kernel,
        [mine, near],
        [shaped((2 * mine.shape[0], *mine.shape[1:]), BF16)],
        moved=8 * mine.size,
    )
    return result


def cross_one_kernel(oth, oth_near, own, own_near, x_send, y_send, x_keep, y_keep_own, y_keep_oth):
    rows = x_send.shape[1]
    half = oth.shape[0] // 2
    x_send[...] = (oth[:, :rows, :] + oth_near[:, :rows, :].astype(F32)).astype(BF16)
    x_keep[...] = own[:, :rows, :] + own_near[:, :rows, :].astype(F32)
    for at, (keep, near, out) in enumerate(((own, own_near, y_keep_own), (oth, oth_near, y_keep_oth))):
        total = keep[:, rows:, :] + near[:, rows:, :].astype(F32)
        out[...] = total[:half]
        y_send[at] = total[half:].astype(BF16)


def cross_one(line, oth, oth_near, own, own_near, rows):
    count, height, inner = oth.shape
    half, last = count // 2, height - rows
    return line.run(
        cross_one_kernel,
        [oth, oth_near, own, own_near],
        [
            shaped((count, rows, inner), BF16),
            shaped((2, half, last, inner), BF16),
            shaped((count, rows, inner), F32),
            shaped((half, last, inner), F32),
            shaped((half, last, inner), F32),
        ],
        moved=20 * oth.size,
        room=16,
    )


def cross_two_kernel(x_keep, x_near, own, oth, y_near, y_send, x_send, first, last):
    half = own.shape[0]
    total = x_keep[...] + x_near[...].astype(F32)
    first[...] = total[:half]
    y_send[...] = total[half:].astype(BF16)
    last[...] = own[...] + y_near[0].astype(F32)
    x_send[...] = (oth[...] + y_near[1].astype(F32)).astype(BF16)


def cross_two(line, x_keep, x_near, own, oth, y_near):
    half = (own.shape[0], x_keep.shape[1], x_keep.shape[2])
    return line.run(
        cross_two_kernel,
        [x_keep, x_near, own, oth, y_near],
        [shaped(half, BF16), shaped(own.shape, BF16), shaped(half, F32), shaped(own.shape, F32)],
        moved=12 * (x_keep.size + own.size),
        room=16,
    )


def cross_three_kernel(first, y_near, last, x_near, keep, send):
    rows, half = first.shape[1], first.shape[0] // 2
    for ref, near, cut in ((first, y_near, slice(0, rows)), (last, x_near, slice(rows, None))):
        total = ref[...] + near[...].astype(F32)
        keep[:, cut, :] = total[:half]
        send[:, cut, :] = total[half:].astype(BF16)


def cross_three(line, first, y_near, last, x_near):
    shape = (first.shape[0] // 2, first.shape[1] + last.shape[1], first.shape[2])
    return line.run(
        cross_three_kernel,
        [first, y_near, last, x_near],
        [shaped(shape, F32), shaped(shape, BF16)],
        moved=12 * (first.size + last.size),
        room=16,
    )


def unpack_attend_kernel(first, place_ref, held_ref, *refs):
    qkv_ref, out_ref, small_ref, wide, little, sems = refs[-6:]
    inner = qkv_ref.shape[2]
    rows = qkv_ref.shape[1] // 16
    copies = []
    for slot in range(8):
        block = (slot if first else slot + 8) ^ place_ref[0]
        values = held_ref[slot].astype(F32)
        wide[slot] = values[: 4 * rows, :]
        little[slot] = values[4 * rows : 4 * rows + 8, :]
        row = pl.multiple_of(block * rows, rows)
        for section in range(3):
            copies.append((wide.at[slot, pl.ds(section * rows, rows), :], qkv_ref.at[section, pl.ds(row, rows), :]))
        row = pl.multiple_of((block & 7) * rows, rows)
        column = pl.multiple_of((block >> 3) * inner, inner)
        copies.append((wide.at[slot, pl.ds(3 * rows, rows), :], out_ref.at[pl.ds(row, rows), pl.ds(column, inner)]))
        copies.append((little.at[slot], small_ref.at[block]))
    copies = [pltpu.make_async_copy(*pair, sems.at[at]) for at, pair in enumerate(copies)]
    for copy in copies:
        copy.start()
    for copy in copies:
        copy.wait()


def unpack_attend(line, place, held, width, before=None):
    _, height, inner = held.shape
    rows = width // 16
    shapes = [shaped((3, width, inner), F32), shaped((inner, width), F32), shaped((16, 8, inner), F32)]
    return line.run(
        functools.partial(unpack_attend_kernel, before is None),
        [held, *(before or [])],
        shapes,
        in_specs=[VMEM] + [ANYWHERE] * (0 if before is None else 3),
        out_specs=[ANYWHERE] * 3,
        scratch=[
            pltpu.VMEM((8, 4 * rows, inner), F32),
            pltpu.VMEM((8, 8, inner), F32),
            pltpu.SemaphoreType.DMA((40,)),
        ],
        aliases={} if before is None else {2: 0, 3: 1, 4: 2},
        place=place,
        moved=8 * height * inner * 6,
        room=16,
    )


def unpack_ffn_kernel(first, place_ref, *refs):
    down_in, up_in = refs[:2]
    down_ref, in_ref, down, up, sems = refs[-5:]
    rows, half = down_ref.shape[0] // 16, down_ref.shape[1] // 2
    deep, wide = in_ref.shape[0] // 4, in_ref.shape[1] // 4
    copies = []
    for slot in range(8):
        block = (slot if first else slot + 8) ^ place_ref[0]
        values = down_in[slot].astype(F32)
        down[slot, :, :half] = values[:rows, :]
        down[slot, :, half:] = values[rows:, :]
        up[slot] = up_in[slot].astype(F32)
        row = pl.multiple_of(block * rows, rows)
        copies.append((down.at[slot], down_ref.at[pl.ds(row, rows), :]))
        block = ((slot & 1) * 4 + (slot >> 1) + (0 if first else 8)) ^ place_ref[0]
        row = pl.multiple_of((block & 3) * deep, deep)
        column = pl.multiple_of((block >> 2) * wide, wide)
        copies.append((up.at[slot], in_ref.at[pl.ds(row, deep), pl.ds(column, wide)]))
    copies = [pltpu.make_async_copy(*pair, sems.at[at]) for at, pair in enumerate(copies)]
    for copy in copies:
        copy.start()
    for copy in copies:
        copy.wait()


def unpack_ffn(line, place, down, up, width, hidden, before=None):
    return line.run(
        functools.partial(unpack_ffn_kernel, before is None),
        [down, up, *(before or [])],
        [shaped((hidden, width), F32), shaped((width, hidden), F32)],
        in_specs=[VMEM] * 2 + [ANYWHERE] * (0 if before is None else 2),
        out_specs=[ANYWHERE] * 2,
        scratch=[
            pltpu.VMEM((8, hidden // 16, width), F32),
            pltpu.VMEM((8, width // 4, hidden // 4), F32),
            pltpu.SemaphoreType.DMA((16,)),
        ],
        aliases={} if before is None else {3: 0, 4: 1},
        place=place,
        moved=6 * width * hidden,
        room=20,
    )


def attend_kernel(tok_ref, w_ref, bias_ref, k_ref, v_ref, out_ref):
    rows, inner = out_ref.shape
    low = lane_halves(rows)
    queries = scaled((mm(tok_ref[...], w_ref[0]) + bias_ref[0:1, :]).astype(BF16))
    for at in range(0, inner, LANES):
        cut = slice(at, at + LANES)
        block, keys, values = queries[:, cut], k_ref[:, cut], v_ref[:, cut]
        zero, one = jnp.zeros_like(block), jnp.ones_like(values)
        mixed = []
        for first in (True, False):
            head = jnp.where(low == first, block, zero)
            with_sums = jnp.where(lane_halves(values.shape[0]) == first, values, one)
            scores = dot_nt(head, keys)
            exponent = jnp.exp(scores - jnp.max(scores, axis=-1, keepdims=True)).astype(BF16)
            mixed.append(mm(exponent, with_sums))
        top = jnp.where(low, mixed[0], mixed[1])
        total = jnp.where(low, mixed[1], mixed[0])
        out_ref[:, cut] = (top / pltpu.roll(total, HEAD, 1)).astype(BF16)


def attend(line, tokens, weights, bias, keys, values, seqs, seq, weight=1):
    rows, width = tokens.shape
    inner = keys.shape[1]
    length = rows // seqs
    long = pl.BlockSpec((length, inner), lambda s: (seq, 0))
    (result,) = line.run(
        attend_kernel,
        [tokens, weights, bias, keys, values],
        [shaped((length, inner), BF16)],
        grid=(1,),
        in_specs=[
            pl.BlockSpec((length, width), lambda s: (seq, 0)),
            pl.BlockSpec((1, width, inner), lambda s: (0, 0, 0)),
            whole(bias.shape),
            long,
            long,
        ],
        out_specs=[pl.BlockSpec((length, inner), lambda s: (0, 0))],
        flops=2 * length * width * inner + 16 * length * length * inner,
        moved=2 * (length * width + width * inner + 3 * length * inner),
        transcendentals=length * length * inner // HEAD,
        room=24,
        weight=weight,
    )
    return result


def layer_kernel(
    tok_ref, ctx_a, ctx_b, wo_a, wo_b, wi_a, wi_b, bi_a, bi_b, wd_a, wd_b, one_ref, two_ref, out_ref,
):
    branch = mm(ctx_a[...], wo_a[...]) + mm(ctx_b[...], wo_b[...]) + one_ref[0:1, :]
    unit, _ = norm_rows(tok_ref[...].astype(F32) + branch)
    normed = unit * one_ref[1:2, :] + one_ref[2:3, :]
    low = normed.astype(BF16)
    total = normed + two_ref[0:1, :]
    for w_in, b_in, w_down in ((wi_a, bi_a, wd_a), (wi_b, bi_b, wd_b)):
        hidden = gelu(mm(low, w_in[...]) + b_in[...]).astype(BF16)
        total = total + mm(hidden, w_down[...])
    unit, _ = norm_rows(total)
    out_ref[...] = (unit * two_ref[1:2, :] + two_ref[2:3, :]).astype(BF16)


def layer_next_kernel(*refs):
    layer_kernel(*refs[:-2], refs[-1])


def layer(line, tokens, contexts, w_out, w_in, b_in, w_down, one, two, seq, mixed):
    length, inner = contexts[0].shape
    width, hidden = tokens.shape[1], w_in[0].shape[1]
    tile = 256
    steps = length // tile
    ctx = pl.BlockSpec((tile, inner), lambda i: (i, 0))
    still = [*w_out, *w_in, *b_in, *w_down, one, two]
    row = pl.BlockSpec((tile, width), lambda i: (seq * steps + i, 0))
    args = [tokens, *contexts, *still]
    specs = [row, ctx, ctx] + [whole(item.shape, True) for item in still]
    (result,) = line.run(
        layer_kernel if mixed is None else layer_next_kernel,
        args if mixed is None else [*args, mixed],
        [shaped(tokens.shape, BF16)],
        grid=(steps,),
        in_specs=specs if mixed is None else [*specs, ANYWHERE],
        out_specs=[row],
        aliases={} if mixed is None else {len(args): 0},
        room=30,
        flops=2 * length * width * (width + 4 * hidden),
        moved=4 * width * (length + 2 * hidden),
        transcendentals=2 * length * hidden,
    )
    return result


def input_grad_kernel(
    dk_a, dk_b, dv_a, dv_b, dq_a, dq_b, w_a, w_b, g_first_ref, places_ref, out_ref
):
    length = out_ref.shape[0]
    slots = g_first_ref.shape[0]
    few = g_first_ref[...] + dot_nt(dq_a[...], w_a[0]) + dot_nt(dq_b[...], w_b[0])
    coarse = few.astype(BF16)
    fine = (few - coarse.astype(F32)).astype(BF16)
    picks = places_ref[0][:, 0:1] == lax.broadcasted_iota(jnp.int32, (slots, length), 1)
    picks = picks.astype(F32).astype(BF16)
    total = dot_tn(picks, coarse) + dot_tn(picks, fine)
    for dk, dv, w in ((dk_a, dv_a, w_a), (dk_b, dv_b, w_b)):
        total = total + dot_nt(dk[...], w[1]) + dot_nt(dv[...], w[2])
    out_ref[...] = total


def input_grad(line, backs, weights, g_first, places, seqs):
    rows, inner = backs[0][1].shape
    width = g_first.shape[1]
    length, slots = rows // seqs, g_first.shape[0] // seqs
    long = pl.BlockSpec((length, inner), lambda s: (s, 0))
    short = pl.BlockSpec((slots, inner), lambda s: (s, 0))
    (result,) = line.run(
        input_grad_kernel,
        [
            backs[0][1], backs[1][1], backs[0][2], backs[1][2], backs[0][0], backs[1][0],
            *weights, g_first, places,
        ],
        [shaped((rows, width), F32)],
        grid=(seqs,),
        in_specs=[long] * 4 + [short] * 2 + [whole(w.shape) for w in weights]
        + [
            pl.BlockSpec((slots, width), lambda s: (s, 0)),
            pl.BlockSpec((1, slots, LANES), lambda s: (s, 0, 0)),
        ],
        out_specs=[pl.BlockSpec((length, width), lambda s: (s, 0))],
        flops=10 * rows * width * inner,
        room=32,
        moved=20 * width * inner + 8 * rows * width,
    )
    return result


def pick_kernel(places_ref, fresh_ref, tok_ref, grad_ref, few_ref, grad_few_ref, turned_ref):
    slots, length = few_ref.shape[0], tok_ref.shape[0]
    picks = places_ref[0][:, 0:1] == lax.broadcasted_iota(jnp.int32, (slots, length), 1)
    picks = picks.astype(F32).astype(BF16)
    few_ref[...] = mm(picks, tok_ref[...]).astype(BF16)
    grad_few_ref[...] = mm(picks, grad_ref[...]) * fresh_ref[0][:, 0:1]
    turned_ref[...] = tok_ref[...].T


def pick(line, places, fresh, tokens, grads, seqs):
    rows, width = tokens.shape
    length, slots = rows // seqs, places.shape[1]
    flat = pl.BlockSpec((1, slots, LANES), lambda s: (s, 0, 0))
    long = pl.BlockSpec((length, width), lambda s: (s, 0))
    short = pl.BlockSpec((slots, width), lambda s: (s, 0))
    return line.run(
        pick_kernel,
        [places, fresh, tokens, grads],
        [
            shaped((seqs * slots, width), BF16),
            shaped((seqs * slots, width), F32),
            shaped((width, rows), BF16),
        ],
        grid=(seqs,),
        in_specs=[flat, flat, long, long],
        out_specs=[short, short, pl.BlockSpec((width, length), lambda s: (0, s))],
        flops=4 * rows * slots * width,
        moved=6 * rows * width,
        room=20,
    )


def body(
    tokens,
    grad_values,
    span_starts,
    w_qkv,
    b_qv,
    w_out,
    b_out,
    ln1_gain,
    ln1_bias,
    w_in,
    b_in,
    w_down,
    b_down,
    ln2_gain,
    ln2_bias,
):
    rows, width = tokens.shape
    inner = w_qkv.shape[2]
    hidden_half = w_in.shape[1]
    halves = lax.axis_size("tensor")
    seqs = span_starts.shape[0] // halves
    spans = span_starts.shape[1]
    length = rows // seqs
    half_at = lax.axis_index("tensor")
    me = lax.axis_index("dp")
    bits = lax.axis_size("dp").bit_length() - 1
    block_at = ((me & 1) << 3) | ((me & 2) << 1) | ((me & 4) >> 1) | ((me & 8) >> 3)
    place = block_at.reshape(1).astype(jnp.int32)
    rest = [1 << bit for bit in range(4, bits)]

    starts = lax.dynamic_slice_in_dim(span_starts, half_at * seqs, seqs, 0)
    places = starts[:, :, None] + jnp.arange(SPAN, dtype=jnp.int32)
    earlier = jnp.tril(jnp.ones((spans, spans), jnp.bool_), -1)
    covered = (places[:, :, :, None] >= starts[:, None, None, :]) & (
        places[:, :, :, None] < starts[:, None, None, :] + SPAN
    )
    fresh = ~jnp.any(covered & earlier[None, :, None, :], axis=-1)
    slots = -(-spans * SPAN // 16) * 16
    pad = slots - spans * SPAN
    places = jnp.pad(places.reshape(seqs, spans * SPAN), ((0, 0), (0, pad)))
    fresh = jnp.pad(fresh.reshape(seqs, spans * SPAN), ((0, 0), (0, pad)))
    few = seqs * slots
    places = jnp.broadcast_to(places[:, :, None], (seqs, slots, LANES))
    fresh = jnp.broadcast_to(fresh[:, :, None].astype(F32), (seqs, slots, LANES))
    vectors_one = jnp.stack([b_out, ln1_gain, ln1_bias])
    vectors_two = jnp.stack([b_down, ln2_gain, ln2_bias])
    here = me.reshape(1)
    line = Line()

    w_qkv_own = jnp.transpose(w_qkv, (1, 0, 2))
    b_in = b_in.reshape(1, -1)

    def chips_around(held):
        return [held, flip(held, 2), flip(held, 4), flip(held, 6)]

    arrived_qkv = flip_tensor(cut_qkv(line, w_qkv_own, here))
    arrived_biases = [flip_tensor(b_qv), flip_tensor(b_in)]
    tokens_few, grad_few, tokens_t = pick(line, places, fresh, tokens, grad_values, seqs)
    held_qkv, b_qv_oth, b_in_oth, half_out, eighth = second_cut(
        line, arrived_qkv, arrived_biases, w_out, w_in, w_down, here
    )
    around_qkv = chips_around(held_qkv)
    arrived_out, arrived_eighth = flip_tensor(half_out), flip_tensor(eighth)
    b_qv_both, b_in_both = [b_qv, b_qv_oth], [b_in, b_in_oth]
    own = project(line, tokens, tokens_few, w_qkv_own, b_qv, seqs)
    ctx_own = [
        attend(line, tokens, w_qkv_own, b_qv, own[0], own[1], seqs, seq) for seq in range(seqs)
    ]
    core_first, held_eighth, half_in = third_cut(
        line, around_qkv, arrived_out, arrived_eighth, w_in, here
    )
    near_first = flip(core_first, 1)
    around_eighth = chips_around(held_eighth)
    arrived_in = flip_tensor(half_in)
    w_qkv_oth, w_out_oth = first_assemble(line, core_first, near_first, width, inner, here)
    w_qkv_both, w_out_both = [w_qkv_own, w_qkv_oth], [w_out, w_out_oth]
    oth = project(line, tokens, tokens_few, w_qkv_oth, b_qv_both[1], seqs)

    keys, values, queries_few, context_few = zip(own, oth)
    sum_few, normed_low = first_norm(line, context_few, w_out_both, tokens_few, vectors_one)

    def plane(values):
        return [values, flip_tensor(values), flip(values, 2), flip_both(values, 2)]

    slope_own, part = ffn_part(line, normed_low, w_in, b_in_both[0], w_down)
    core_second, held_in = fourth_cut(line, around_eighth, arrived_in)
    near_second, near_in = flip(core_second, 1), flip(held_in, 1)
    around_normed = plane(normed_low)
    w_in_oth, w_down_oth = second_assemble(
        line, core_second, near_second, held_in, near_in, hidden_half, here
    )
    w_in_both, w_down_both = [w_in, w_in_oth], [w_down, w_down_oth]
    g_ffn, g_branch, g_first, small_few = ffn(
        line, normed_low, part, sum_few, grad_few, vectors_one, vectors_two, slope_own,
        w_in_both, b_in_both[1], w_down_both,
    )
    around_g = plane(g_ffn)
    core_normed = join(line, around_normed)
    near_normed = flip(core_normed, 1)

    def back(at):
        return attend_back(
            line, place, queries_few[at], keys[at], values[at], g_branch, w_out_both[at],
            context_few[at], tokens_t, tokens_few, small_few, seqs, at, hidden_half // inner,
        )

    back_oth = back(1)
    near_oth = flip(back_oth[4], 1)
    back_own = back(0)
    near_own = flip(back_own[4], 1)
    core_g = join(line, around_g)
    near_g = flip(core_g, 1)

    def attend_oth(seq, weight=1):
        return attend(
            line, tokens, w_qkv_oth, b_qv_both[1], keys[1], values[1], seqs, seq, weight
        )

    ctx_oth = [attend_oth(0, 10)]
    x_send, y_send, x_keep, y_own, y_oth = cross_one(
        line, back_oth[3], near_oth, back_own[3], near_own, 112
    )
    x_near, y_near = flip_tensor(x_send), flip(y_send, 2)
    keep_down, send_down, keep_in, send_in = ffn_grads(
        line, place, w_in, w_down, b_in_both[0], [core_normed, near_normed], [core_g, near_g]
    )
    z_down, z_in = flip(send_down, 4), flip(send_in, 8)

    def over_rest(total):
        for bit in rest:
            total = total + flip(total, bit)
        return total

    def layer_of(seq, mixed):
        return layer(
            line, tokens, [ctx_own[seq], ctx_oth[seq]], w_out_both, w_in_both, b_in_both, w_down_both,
            vectors_one, vectors_two, seq, mixed,
        )

    ctx_oth += [attend_oth(seq) for seq in range(1, seqs)]
    d_tokens = input_grad(line, [back_own, back_oth], w_qkv_both, g_first, places, seqs)
    keep_down, send_down = fold(line, keep_down, [z_down], True)
    z_down = flip(send_down, 8)
    keep_in, send_in = fold(line, keep_in, [z_in], True)
    z_in = flip(send_in, 4)
    y_send, x_send, first, last = cross_two(line, x_keep, x_near, y_own, y_oth, y_near)
    y_near, x_near = flip(y_send, 2), flip_tensor(x_send)
    mixed = layer_of(0, None)
    down = fold(line, over_rest(keep_down), [over_rest(z_down)], False)
    near_down = flip(down, 8)
    up = fold(line, over_rest(keep_in), [over_rest(z_in)], False)
    near_up = flip(up, 2)
    keep, send = cross_three(line, first, y_near, last, x_near)
    z_attn = flip(send, 4)
    for seq in range(1, seqs):
        mixed = layer_of(seq, mixed)
    keep, send = fold(line, keep, [z_attn], True)
    z_attn = flip(send, 8)
    down = append(line, down, near_down)
    near_down = flip(down, 4)
    up = append(line, up, near_up)
    near_up = flip(up, 8)
    attn = fold(line, over_rest(keep), [over_rest(z_attn)], False)
    near_attn = flip(attn, 8)
    down = append(line, down, near_down)
    near_down = flip(down, 2)
    attn = append(line, attn, near_attn)
    near_attn = flip(attn, 4)
    up = append(line, up, near_up)
    near_up = flip(up, 4)
    attn = append(line, attn, near_attn)
    near_attn = flip(attn, 2)
    down = append(line, down, near_down)
    near_down = flip(down, 1)
    up = append(line, up, near_up)
    near_up = flip(up, 1)
    ffn_sums = unpack_ffn(line, place, down, up, width, hidden_half)
    attn = append(line, attn, near_attn)
    near_attn = flip(attn, 1)
    attn_sums = unpack_attend(line, place, attn, width)
    d_w_down, d_w_in = unpack_ffn(line, place, near_down, near_up, width, hidden_half, ffn_sums)
    d_w_qkv, d_w_out, small = unpack_attend(line, place, near_attn, width, attn_sums)
    d_w_qkv = jnp.transpose(d_w_qkv, (1, 0, 2))

    small = small[:, :2, :].reshape(32, inner)
    deep = hidden_half // inner
    d_b_qv = small[:2]
    d_b_in = small[2 : 2 + deep].reshape(-1)
    d_b_out, d_ln1_gain, d_ln1_bias, d_b_down, d_ln2_gain, d_ln2_bias = [
        small[2 + deep + 2 * at : 4 + deep + 2 * at].reshape(-1) for at in range(6)
    ]

    return (
        mixed,
        d_tokens,
        d_w_qkv,
        d_b_qv,
        d_w_out,
        d_b_out,
        d_ln1_gain,
        d_ln1_bias,
        d_w_in,
        d_b_in,
        d_w_down,
        d_b_down,
        d_ln2_gain,
        d_ln2_bias,
    )


def solution(mesh):
    placed = (
        P(("dp", "tensor"), None),
        P(("dp", "tensor"), None),
        P("dp", None),
        P(None, None, "tensor"),
        P(None, "tensor"),
        P("tensor", None),
        P(),
        P(),
        P(),
        P(None, "tensor"),
        P("tensor"),
        P("tensor", None),
        P(),
        P(),
        P(),
    )
    return jax.shard_map(
        body,
        mesh=mesh,
        in_specs=placed,
        out_specs=(
            P(("dp", "tensor"), None),
            P(("dp", "tensor"), None),
            P(None, None, "tensor"),
            P(None, "tensor"),
            P("tensor", None),
            P(),
            P(),
            P(),
            P(None, "tensor"),
            P("tensor"),
            P("tensor", None),
            P(),
            P(),
            P(),
        ),
        check_vma=False,
    )
```

```python
import functools

import jax
import jax.numpy as jnp
from jax import lax
from jax.experimental import pallas as pl
from jax.experimental.pallas import tpu as pltpu
from jax.sharding import PartitionSpec as P

HEAD = 64
SPAN = 6
LANES = 128
EPSILON = 1e-05
F32 = jnp.float32
BF16 = jnp.bfloat16
GELU_A = (2.0 / 3.141592653589793) ** 0.5
GELU_B = 0.044715
BYTES_US = int(3 * 3_690_000)
FLOPS_US = int(3 * 1_153_000_000)
ANYWHERE = pl.BlockSpec(memory_space=pl.ANY)
VMEM = pl.BlockSpec(memory_space=pltpu.VMEM)


class Line:
    def __init__(self):
        self.token = jnp.zeros((8, LANES), F32)

    def run(
        self, kernel, args, out_shape, grid=(), in_specs=None, out_specs=None, scratch=(), place=None,
        flops=0, moved=0, transcendentals=0, room=6, aliases=None, hint=None,
    ):
        ins, outs = len(args), len(out_shape)
        lead = 0 if place is None else 1

        def with_token(*refs):
            given, rest = refs[: lead + ins], refs[lead + ins + 1 :]
            rest[outs][...] = jnp.zeros((8, LANES), F32)
            kernel(*given, *rest[:outs], *rest[outs + 1 :])

        in_specs = list(in_specs or [VMEM] * ins) + [ANYWHERE]
        out_specs = list(out_specs or [VMEM] * outs)
        out_specs.append(pl.BlockSpec((8, LANES), lambda *at: (0, 0)) if grid else VMEM)
        shapes = list(out_shape) + [jax.ShapeDtypeStruct((8, LANES), F32)]
        params = dict(
            out_shape=shapes,
            input_output_aliases=aliases or {},
            compiler_params=pltpu.CompilerParams(vmem_limit_bytes=room << 20),
            cost_estimate=pl.CostEstimate(
                flops=int(flops if hint is None else hint * FLOPS_US),
                bytes_accessed=int(moved if hint is None else hint * BYTES_US),
                transcendentals=int(transcendentals if hint is None else 0),
            ),
        )
        if lead and grid:
            params["grid_spec"] = pltpu.PrefetchScalarGridSpec(
                num_scalar_prefetch=1, grid=grid, in_specs=in_specs, out_specs=out_specs, scratch_shapes=list(scratch)
            )
        else:
            if lead:
                in_specs = [pl.BlockSpec(memory_space=pltpu.SMEM)] + in_specs
            params.update(grid=grid, in_specs=in_specs, out_specs=out_specs, scratch_shapes=list(scratch))
        front = [] if place is None else [place]
        *results, self.token = pl.pallas_call(with_token, **params)(*front, *args, self.token)
        return results


def shaped(shape, kind):
    return jax.ShapeDtypeStruct(tuple(shape), kind)


def whole(shape, once=False):
    held = dict(pipeline_mode=pl.Buffered(1)) if once else {}
    return pl.BlockSpec(shape, lambda *at: (0,) * len(shape), **held)


def flip(values, bits):
    size = lax.axis_size("dp")
    return lax.ppermute(values, "dp", [(at, at ^ bits) for at in range(size)])


def flip_tensor(values):
    return lax.ppermute(values, "tensor", [(0, 1), (1, 0)])


def flip_both(values, bits):
    size = 2 * lax.axis_size("dp")
    pairs = [(at, at ^ (2 * bits + 1)) for at in range(size)]
    return lax.ppermute(values, ("dp", "tensor"), pairs)


def dot_nt(left, right):
    return lax.dot_general(left, right, (((1,), (1,)), ((), ())), preferred_element_type=F32)


def dot_tn(left, right):
    return lax.dot_general(left, right, (((0,), (0,)), ((), ())), preferred_element_type=F32)


def mm(left, right):
    return jnp.dot(left, right, preferred_element_type=F32)


def lane_halves(rows):
    return lax.broadcasted_iota(jnp.int32, (rows, LANES), 1) < HEAD


def two_heads(block):
    low = lane_halves(block.shape[0])
    zero = jnp.zeros_like(block)
    return jnp.concatenate([jnp.where(low, block, zero), jnp.where(low, zero, block)], axis=0)


def scaled(queries):
    return queries * jnp.asarray(HEAD ** (-0.5), BF16)


def softmax_rows(scores):
    exponent = jnp.exp(scores - jnp.max(scores, axis=-1, keepdims=True))
    return exponent * (1.0 / jnp.sum(exponent, axis=-1, keepdims=True))


def attend_block(queries, keys, values):
    rows = queries.shape[0]
    probs = softmax_rows(dot_nt(two_heads(scaled(queries)), keys)).astype(BF16)
    mixed = mm(probs, values)
    return jnp.where(lane_halves(rows), mixed[:rows], mixed[rows:]).astype(BF16)


def norm_rows(values):
    average = jnp.mean(values, axis=-1, keepdims=True)
    centered = values - average
    variance = jnp.mean(centered * centered, axis=-1, keepdims=True)
    root = lax.rsqrt(variance + EPSILON)
    return centered * root, root


def norm_back(grad, unit, root, gain):
    grad_y = grad * gain
    inner = jnp.mean(grad_y, axis=-1, keepdims=True)
    along = jnp.mean(grad_y * unit, axis=-1, keepdims=True)
    return root * (grad_y - inner - unit * along)


def gelu_and_slope(values):
    square = values * values
    bent = jnp.tanh(GELU_A * values * (1.0 + GELU_B * square))
    half = 0.5 * (1.0 + bent)
    slope = half + 0.5 * values * (1.0 - bent * bent) * GELU_A * (1.0 + 3.0 * GELU_B * square)
    return values * half, slope


def gelu(values):
    return 0.5 * values * (1.0 + jnp.tanh(GELU_A * values * (1.0 + GELU_B * values * values)))


def join_kernel(count, *refs):
    rows = refs[0].shape[-2]
    for at in range(count):
        refs[count][..., at * rows : (at + 1) * rows, :] = refs[at][...]


def join(line, pieces):
    *lead, rows, columns = pieces[0].shape
    (result,) = line.run(
        functools.partial(join_kernel, len(pieces)),
        pieces,
        [shaped((*lead, rows * len(pieces), columns), pieces[0].dtype)],
        moved=4 * len(pieces) * pieces[0].size,
    )
    return result


def cut_qkv_kernel(place_ref, in_ref, out_ref, sem):
    rows = out_ref.shape[1]
    row = pl.multiple_of((place_ref[0] & 7) * rows, rows)
    copy = pltpu.make_async_copy(in_ref.at[:, pl.ds(row, rows), :], out_ref, sem)
    copy.start()
    copy.wait()


def cut_qkv(line, w_qkv, here):
    lead, rows, columns = w_qkv.shape
    (piece,) = line.run(
        cut_qkv_kernel,
        [w_qkv],
        [shaped((lead, rows // 8, columns), BF16)],
        in_specs=[ANYWHERE],
        scratch=[pltpu.SemaphoreType.DMA],
        place=here,
        moved=w_qkv.size // 2,
        room=56,
    )
    return piece


def second_cut_kernel(place_ref, out_ref, in_ref, down_ref, half, eighth):
    half[...] = out_ref[...]
    rows = in_ref.shape[0]
    eighth[:rows, :] = in_ref[...]
    eighth[rows:, :] = down_ref[...]


def second_cut(line, w_out, w_in, w_down, here):
    width = w_out.shape[1]
    half, eighth, deep = w_out.shape[0] // 2, w_in.shape[0] // 8, w_down.shape[0] // 8
    return line.run(
        second_cut_kernel,
        [w_out, w_in, w_down],
        [shaped((half, width), BF16), shaped((eighth + deep, width), BF16)],
        grid=(1,),
        in_specs=[
            pl.BlockSpec((half, width), lambda i, p: (p[0] & 1, 0)),
            pl.BlockSpec((eighth, width), lambda i, p: (p[0] & 7, 1)),
            pl.BlockSpec((deep, width), lambda i, p: (p[0] & 7, 0)),
        ],
        out_specs=[whole((half, width)), whole((eighth + deep, width))],
        place=here,
        moved=4 * (half + eighth + deep) * width,
        room=56,
    )


def relay_kernel(count, *refs):
    for at in range(count):
        refs[count + at][...] = refs[at][...]


def relay(line, arrived):
    return line.run(
        functools.partial(relay_kernel, len(arrived)),
        arrived,
        [shaped(item.shape, item.dtype) for item in arrived],
        moved=sum(4 * item.size for item in arrived),
    )


def third_cut_kernel(place_ref, a, b, c, d, out_ref, eighth_ref, in_ref, core, eighth, half):
    third, rows, inner = a.shape
    for at, ref in enumerate((a, b, c, d)):
        for section in range(third):
            row = (section * 4 + at) * rows
            core[row : row + rows, :] = ref[section]
    row = 4 * third * rows
    deep = out_ref.shape[0]
    core[row : row + deep, :] = out_ref[:, :inner]
    core[row + deep :, :] = out_ref[:, inner:]
    eighth[...] = eighth_ref[...]
    half[...] = in_ref[...]


def third_cut(line, qkv, out, eighth, w_in, here):
    third, rows, inner = qkv[0].shape
    width = out.shape[1]
    height = 4 * third * rows + 2 * out.shape[0]
    half = (w_in.shape[0] // 2, width)
    return line.run(
        third_cut_kernel,
        [*qkv, out, eighth, w_in],
        [shaped((height, inner), BF16), shaped(eighth.shape, BF16), shaped(half, BF16)],
        grid=(1,),
        in_specs=[whole(item.shape) for item in [*qkv, out, eighth]]
        + [pl.BlockSpec(half, lambda i, p: (p[0] & 1, 0))],
        out_specs=[whole((height, inner)), whole(eighth.shape), whole(half)],
        place=here,
        moved=4 * (height * inner + eighth.size + half[0] * width),
    )


def first_assemble_kernel(place_ref, mine, near, qkv_ref, out_ref):
    third, width, inner = qkv_ref.shape
    rows, half = width // 8, out_ref.shape[0] // 2
    for core, ref in enumerate((mine, near)):
        for at in range(4):
            row = pl.multiple_of(((place_ref[0] ^ (2 * at + core)) & 7) * rows, rows)
            for section in range(third):
                start = (section * 4 + at) * rows
                qkv_ref[section, pl.ds(row, rows), :] = ref[start : start + rows, :]
        row = pl.multiple_of(((place_ref[0] ^ core) & 1) * half, half)
        start = 4 * third * rows
        out_ref[pl.ds(row, half), :inner] = ref[start : start + half, :]
        out_ref[pl.ds(row, half), inner:] = ref[start + half :, :]


def first_assemble(line, mine, near, width, inner, here):
    return line.run(
        first_assemble_kernel,
        [mine, near],
        [shaped((3, width, inner), BF16), shaped((inner, width), BF16)],
        place=here,
        moved=8 * mine.size,
    )


def fourth_cut_kernel(a, b, c, d, half_ref, eighths, half):
    rows = a.shape[0]
    for at, ref in enumerate((a, b, c, d)):
        eighths[at * rows : (at + 1) * rows, :] = ref[...]
    half[...] = half_ref[...]


def fourth_cut(line, eighths, half):
    rows, width = eighths[0].shape
    return line.run(
        fourth_cut_kernel,
        [*eighths, half],
        [shaped((4 * rows, width), BF16), shaped(half.shape, BF16)],
        moved=16 * rows * width,
    )


def second_assemble_kernel(place_ref, mine, near, half_mine, half_near, in_ref, down_ref):
    width = half_mine.shape[1]
    rows, deep, half = in_ref.shape[0] // 8, down_ref.shape[0] // 8, half_mine.shape[0]
    for core, (ref, half_ref) in enumerate(((mine, half_mine), (near, half_near))):
        for at in range(4):
            block = (place_ref[0] ^ (2 * at + core)) & 7
            start = at * (rows + deep)
            in_ref[pl.ds(pl.multiple_of(block * rows, rows), rows), width:] = ref[
                start : start + rows, :
            ]
            down_ref[pl.ds(pl.multiple_of(block * deep, deep), deep), :] = ref[
                start + rows : start + rows + deep, :
            ]
        row = pl.multiple_of(((place_ref[0] ^ core) & 1) * half, half)
        in_ref[pl.ds(row, half), :width] = half_ref[...]


def second_assemble(line, mine, near, half_mine, half_near, hidden, here):
    width = half_mine.shape[1]
    return line.run(
        second_assemble_kernel,
        [mine, near, half_mine, half_near],
        [shaped((width, hidden), BF16), shaped((hidden, width), BF16)],
        place=here,
        moved=8 * width * hidden,
    )


def project_kernel(tok_ref, few_ref, w_ref, bias_ref, k_ref, v_ref, q_ref, ctx_ref):
    tok = tok_ref[...]
    k_ref[...] = mm(tok, w_ref[1]).astype(BF16)
    v_ref[...] = (mm(tok, w_ref[2]) + bias_ref[1:2, :]).astype(BF16)
    q_ref[...] = (mm(few_ref[...], w_ref[0]) + bias_ref[0:1, :]).astype(BF16)
    for at in range(0, k_ref.shape[1], LANES):
        cut = slice(at, at + LANES)
        ctx_ref[:, cut] = attend_block(q_ref[:, cut], k_ref[:, cut], v_ref[:, cut])


def project(line, tokens, few, weights, bias, seqs):
    rows, width = tokens.shape
    inner = weights.shape[2]
    length, slots = rows // seqs, few.shape[0] // seqs
    long, short = (pl.BlockSpec((size, inner), lambda s: (s, 0)) for size in (length, slots))
    return line.run(
        project_kernel,
        [tokens, few, weights, bias],
        [shaped((rows, inner), BF16)] * 2 + [shaped((few.shape[0], inner), BF16)] * 2,
        grid=(seqs,),
        in_specs=[
            pl.BlockSpec((length, width), lambda s: (s, 0)),
            pl.BlockSpec((slots, width), lambda s: (s, 0)),
            whole(weights.shape),
            whole(bias.shape),
        ],
        out_specs=[long, long, short, short],
        flops=6 * rows * width * inner,
        room=16,
        moved=2 * (rows * width + 3 * width * inner + 2 * rows * inner),
    )


def first_norm_kernel(ctx_a, ctx_b, w_a, w_b, few_ref, vec_ref, sum_ref, low_ref):
    branch = mm(ctx_a[...], w_a[...]) + mm(ctx_b[...], w_b[...]) + vec_ref[0:1, :]
    total = few_ref[...].astype(F32) + branch
    sum_ref[...] = total
    low_ref[...] = (norm_rows(total)[0] * vec_ref[1:2, :] + vec_ref[2:3, :]).astype(BF16)


def first_norm(line, contexts, w_out, few, vectors):
    count, width = few.shape
    return line.run(
        first_norm_kernel,
        [*contexts, *w_out, few, vectors],
        [shaped((count, width), F32), shaped((count, width), BF16)],
        flops=2 * count * width * width,
        moved=2 * width * width + 14 * count * width,
    )


def ffn_part_kernel(low_ref, wi_ref, bi_ref, wd_ref, slope_ref, part_ref, total):
    step = pl.program_id(0)
    gate, slope = gelu_and_slope(mm(low_ref[...], wi_ref[...]) + bi_ref[...])
    slope_ref[...] = slope
    part = mm(gate.astype(BF16), wd_ref[...])

    @pl.when(step == 0)
    def _():
        total[...] = part

    @pl.when(step > 0)
    def _():
        total[...] += part

    @pl.when(step == pl.num_programs(0) - 1)
    def _():
        part_ref[...] = total[...]


def ffn_part(line, low, w_in, b_in, w_down):
    count, width = low.shape
    hidden = w_in.shape[1]
    steps = 4
    tile = hidden // steps
    flat = whole((count, width))
    return line.run(
        ffn_part_kernel,
        [low, w_in, b_in, w_down],
        [shaped((count, hidden), F32), shaped((count, width), F32)],
        grid=(steps,),
        in_specs=[
            flat,
            pl.BlockSpec((width, tile), lambda j: (0, j)),
            pl.BlockSpec((1, tile), lambda j: (0, j)),
            pl.BlockSpec((tile, width), lambda j: (j, 0)),
        ],
        out_specs=[pl.BlockSpec((count, tile), lambda j: (0, j)), flat],
        scratch=[pltpu.VMEM((count, width), F32)],
        flops=4 * count * width * hidden,
        moved=4 * width * hidden,
        transcendentals=count * hidden,
        room=12,
    )


def column_sum(values):
    return jnp.sum(values, axis=0, keepdims=True)


def ffn_kernel(
    low_ref, part_ref, sum_ref, grad_ref, one_ref, two_ref, slope_ref, wi_a, wi_b, bi_b, wd_a, wd_b,
    g_ffn_ref, g_branch_ref, g_first_ref, small_ref,
):
    gate, slope = gelu_and_slope(mm(low_ref[...], wi_b[...]) + bi_b[...])
    ffn = part_ref[...] + mm(gate.astype(BF16), wd_b[...]) + two_ref[0:1, :]
    unit_one, root_one = norm_rows(sum_ref[...])
    normed = unit_one * one_ref[1:2, :] + one_ref[2:3, :]
    unit, root = norm_rows(normed + ffn)
    grad = grad_ref[...]
    g_second = norm_back(grad, unit, root, two_ref[1:2, :])
    g_ffn = g_second.astype(BF16)
    g_ffn_ref[...] = g_ffn
    width = grad.shape[1]
    half = width // 2
    hidden = slope.shape[1]
    deep = hidden // half
    g_normed = g_second
    for at, (bend, w_in, w_down) in enumerate(((slope_ref[...], wi_a, wd_a), (slope, wi_b, wd_b))):
        g_pre = (bend * dot_nt(g_ffn, w_down[...])).astype(BF16)
        bias = column_sum(g_pre.astype(F32))
        for row in range(deep):
            small_ref[at * deep + row : at * deep + row + 1, :] = bias[:, row * half : (row + 1) * half]
        g_normed = g_normed + dot_nt(g_pre, w_in[...])
    g_first = norm_back(g_normed, unit_one, root_one, one_ref[1:2, :])
    g_branch = g_first.astype(BF16)
    g_first_ref[...] = g_first
    g_branch_ref[...] = g_branch
    vectors = (
        column_sum(g_branch.astype(F32)),
        column_sum(g_normed * unit_one),
        column_sum(g_normed),
        column_sum(g_ffn.astype(F32)),
        column_sum(grad * unit),
        column_sum(grad),
    )
    for at, vector in enumerate(vectors):
        row = 2 * deep + 2 * at
        small_ref[row : row + 1, :] = vector[:, :half]
        small_ref[row + 1 : row + 2, :] = vector[:, half:]
    count = 2 * deep + 12
    small_ref[count:, :] = jnp.zeros((small_ref.shape[0] - count, half), F32)


def ffn(line, low, part, total, grad, one, two, slope, w_in, b_in, w_down):
    count, width = low.shape
    hidden = w_in[0].shape[1]
    rows = 2 * (hidden // (width // 2)) + 12
    return line.run(
        ffn_kernel,
        [low, part, total, grad, one, two, slope, *w_in, b_in, *w_down],
        [
            shaped((count, width), BF16),
            shaped((count, width), BF16),
            shaped((count, width), F32),
            shaped((-(-rows // 8) * 8, width // 2), F32),
        ],
        flops=12 * count * width * hidden,
        moved=8 * width * hidden,
        room=16,
    )


def ffn_grads_kernel(place_ref, wi_ref, wd_ref, bi_ref, *refs):
    normed_refs, grad_refs = refs[:2], refs[2:4]
    keep_down, send_down, keep_in, send_in = refs[4:8]
    down, up = refs[8:]
    width = normed_refs[0].shape[1]
    tile = wi_ref.shape[1] // 4
    hidden = pl.ds(pl.multiple_of((place_ref[0] >> 2) * tile, tile), tile)
    w_in, w_down, b_in = wi_ref[:, hidden], wd_ref[hidden, :], bi_ref[:, hidden]
    for at in range(2):
        normed, grad = normed_refs[at][...], grad_refs[at][...]
        gate, slope = gelu_and_slope(mm(normed, w_in) + b_in)
        pre = (slope * dot_nt(grad, w_down)).astype(BF16)
        down_part = dot_tn(gate.astype(BF16), grad)
        up_part = dot_tn(normed, pre)
        if at == 0:
            down[...] = down_part
            up[...] = up_part
        else:
            down[...] += down_part
            up[...] += up_part
    down_rows, up_rows = tile // 4, width // 4
    half = width // 2
    for slot in range(4):
        block = slot ^ (place_ref[0] & 3)
        low = down[pl.ds(pl.multiple_of(block * down_rows, down_rows), down_rows), :]
        block = (0, 2, 1, 3)[slot] ^ (place_ref[0] & 3)
        high = up[pl.ds(pl.multiple_of(block * up_rows, up_rows), up_rows), :]
        to_down, to_in = (keep_down, keep_in) if slot < 2 else (send_down, send_in)
        kind = to_down.dtype
        to_down[slot % 2, :down_rows, :] = low[:, :half].astype(kind)
        to_down[slot % 2, down_rows:, :] = low[:, half:].astype(kind)
        to_in[slot % 2, :, :] = high.astype(kind)


def ffn_grads(line, place, w_in, w_down, b_in, normed, grads):
    rows, width = normed[0].shape
    tile = w_in.shape[1] // 4
    shape = (2, 2 * (tile // 4), width // 2)
    wide = (2, width // 4, tile)
    return line.run(
        ffn_grads_kernel,
        [w_in, w_down, b_in, *normed, *grads],
        [shaped(shape, F32), shaped(shape, BF16), shaped(wide, F32), shaped(wide, BF16)],
        scratch=[pltpu.VMEM((tile, width), F32), pltpu.VMEM((width, tile), F32)],
        place=place,
        flops=16 * rows * width * tile,
        moved=12 * rows * width + 16 * width * tile,
        room=16,
    )


def attend_back_kernel(
    seqs, half, deep, place_ref, q_ref, k_ref, v_ref, g_branch_ref, w_out_ref, ctx_ref, tok_t_ref, few_ref,
    small_ref, dq_ref, dk_ref, dv_ref, keep_ref, send_ref, total, little,
):
    few, inner = q_ref.shape
    rows = k_ref.shape[0]
    slots, length = few // seqs, rows // seqs
    low = lane_halves(slots)
    scale = HEAD ** (-0.5)
    g_branch = g_branch_ref[...]
    g_context = dot_nt(g_branch, w_out_ref[...]).astype(BF16)
    for seq in range(seqs):
        short, long = slice(seq * slots, (seq + 1) * slots), slice(seq * length, (seq + 1) * length)
        for at in range(0, inner, LANES):
            cut = slice(at, at + LANES)
            both, grads = two_heads(scaled(q_ref[short, cut])), two_heads(g_context[short, cut])
            keys, values = k_ref[long, cut], v_ref[long, cut]
            probs = softmax_rows(dot_nt(both, keys))
            grad_probs = dot_nt(grads, values)
            dv_ref[long, cut] = dot_tn(probs.astype(BF16), grads).astype(BF16)
            row_total = jnp.sum(grad_probs * probs, axis=-1, keepdims=True)
            grad_scores = (probs * (grad_probs - row_total)).astype(BF16)
            dq = mm(grad_scores, keys) * scale
            dq_ref[short, cut] = jnp.where(low, dq[:slots], dq[slots:]).astype(BF16)
            dk_ref[long, cut] = dot_tn(grad_scores, both).astype(BF16)
    dq, dk, dv = dq_ref[...], dk_ref[...], dv_ref[...]
    total[0] = dot_tn(few_ref[...], dq)
    total[1] = mm(tok_t_ref[...], dk)
    total[2] = mm(tok_t_ref[...], dv)
    out_grad = dot_tn(ctx_ref[...], g_branch)
    total[3, :inner, :] = out_grad[:, :inner]
    total[3, inner:, :] = out_grad[:, inner:]
    little[...] = jnp.zeros_like(little)
    little[0, 0:1, :] = column_sum(dq.astype(F32))
    little[0, 1:2, :] = column_sum(dv.astype(F32))
    for at in range(deep + 12):
        source = half * deep + at if at < deep else deep + at
        little[1 + at // 2, at % 2 : at % 2 + 1, :] = small_ref[source : source + 1, :]
    block_rows = total.shape[1] // 16
    pad = keep_ref.shape[1] - 4 * block_rows
    for slot in range(16):
        block = slot ^ place_ref[0]
        row = pl.multiple_of(block * block_rows, block_rows)
        to, kind = (keep_ref, F32) if slot < 8 else (send_ref, BF16)
        for section in range(4):
            cut = slice(section * block_rows, (section + 1) * block_rows)
            to[slot % 8, cut, :] = total[section, pl.ds(row, block_rows), :].astype(kind)
        pair = jnp.concatenate([little[block], jnp.zeros((pad - 8, inner), F32)], axis=0)
        to[slot % 8, 4 * block_rows :, :] = pair.astype(kind)


def attend_back(line, place, queries, keys, values, g_branch, w_out, context, tokens_t, few, small, seqs, half, deep):
    rows, inner = keys.shape
    width = tokens_t.shape[0]
    count = queries.shape[0]
    held = (8, 4 * (width // 16) + 16, inner)
    return line.run(
        functools.partial(attend_back_kernel, seqs, half, deep),
        [queries, keys, values, g_branch, w_out, context, tokens_t, few, small],
        [
            shaped((count, inner), BF16),
            shaped((rows, inner), BF16),
            shaped((rows, inner), BF16),
            shaped(held, F32),
            shaped(held, BF16),
        ],
        scratch=[pltpu.VMEM((4, width, inner), F32), pltpu.VMEM((16, 8, inner), F32)],
        place=place,
        room=16,
        flops=4 * rows * width * inner + 24 * count * rows * inner,
        moved=20 * rows * inner,
    )


def fold_kernel(count, halve, *refs):
    keeps, arrived, outs = refs[:count], refs[count : 2 * count], refs[2 * count :]
    for at in range(count):
        total = keeps[at][...] + arrived[at][...].astype(F32)
        if halve:
            middle = total.shape[0] // 2
            outs[2 * at][...] = total[:middle]
            outs[2 * at + 1][...] = total[middle:].astype(BF16)
        else:
            outs[at][...] = total.astype(BF16)


def fold(line, keeps, arrived, halve, hint):
    shapes = []
    for keep in keeps:
        half = (keep.shape[0] // 2, *keep.shape[1:])
        shapes += [shaped(half, F32), shaped(half, BF16)] if halve else [shaped(keep.shape, BF16)]
    results = line.run(
        functools.partial(fold_kernel, len(keeps), halve),
        [*keeps, *arrived],
        shapes,
        hint=hint,
    )
    return (results[0::2], results[1::2]) if halve else results


def append_kernel(count, *refs):
    groups, out = refs[:-count], refs[-count:]
    each = len(groups) // count
    for at in range(count):
        row = 0
        for ref in groups[at * each : (at + 1) * each]:
            out[at][row : row + ref.shape[0]] = ref[...]
            row += ref.shape[0]


def append(line, hint, *groups):
    shapes = [shaped((sum(item.shape[0] for item in group), *group[0].shape[1:]), BF16) for group in groups]
    return line.run(
        functools.partial(append_kernel, len(groups)),
        [item for group in groups for item in group],
        shapes,
        hint=hint,
    )


def cross_one_kernel(oth, oth_near, own, own_near, x_send, y_send, x_keep, y_keep_own, y_keep_oth):
    rows = x_send.shape[1]
    half = oth.shape[0] // 2
    x_send[...] = (oth[:, :rows, :] + oth_near[:, :rows, :].astype(F32)).astype(BF16)
    x_keep[...] = own[:, :rows, :] + own_near[:, :rows, :].astype(F32)
    for at, (keep, near, out) in enumerate(((own, own_near, y_keep_own), (oth, oth_near, y_keep_oth))):
        total = keep[:, rows:, :] + near[:, rows:, :].astype(F32)
        out[...] = total[:half]
        y_send[at] = total[half:].astype(BF16)


def cross_one(line, oth, oth_near, own, own_near, rows):
    count, height, inner = oth.shape
    half, last = count // 2, height - rows
    return line.run(
        cross_one_kernel,
        [oth, oth_near, own, own_near],
        [
            shaped((count, rows, inner), BF16),
            shaped((2, half, last, inner), BF16),
            shaped((count, rows, inner), F32),
            shaped((half, last, inner), F32),
            shaped((half, last, inner), F32),
        ],
        hint=2,
    )


def cross_two_kernel(x_keep, x_near, own, oth, y_near, y_send, x_send, first, last):
    half = own.shape[0]
    total = x_keep[...] + x_near[...].astype(F32)
    first[...] = total[:half]
    y_send[...] = total[half:].astype(BF16)
    last[...] = own[...] + y_near[0].astype(F32)
    x_send[...] = (oth[...] + y_near[1].astype(F32)).astype(BF16)


def cross_two(line, x_keep, x_near, own, oth, y_near):
    half = (own.shape[0], x_keep.shape[1], x_keep.shape[2])
    return line.run(
        cross_two_kernel,
        [x_keep, x_near, own, oth, y_near],
        [shaped(half, BF16), shaped(own.shape, BF16), shaped(half, F32), shaped(own.shape, F32)],
        hint=0.5,
    )


def cross_three_kernel(first, y_near, last, x_near, keep, send):
    rows, half = first.shape[1], first.shape[0] // 2
    for ref, near, cut in ((first, y_near, slice(0, rows)), (last, x_near, slice(rows, None))):
        total = ref[...] + near[...].astype(F32)
        keep[:, cut, :] = total[:half]
        send[:, cut, :] = total[half:].astype(BF16)


def cross_three(line, first, y_near, last, x_near):
    shape = (first.shape[0] // 2, first.shape[1] + last.shape[1], first.shape[2])
    return line.run(
        cross_three_kernel,
        [first, y_near, last, x_near],
        [shaped(shape, F32), shaped(shape, BF16)],
        hint=0.5,
    )


def place_attend(first, place_ref, held_ref, qkv_ref, out_ref, wide, sems):
    inner = qkv_ref.shape[2]
    rows = qkv_ref.shape[1] // 16
    copies = []
    for slot in range(8):
        block = (slot if first else slot + 8) ^ place_ref[0]
        wide[slot] = held_ref[slot, : 4 * rows, :].astype(F32)
        row = pl.multiple_of(block * rows, rows)
        for section in range(3):
            copies.append((wide.at[slot, pl.ds(section * rows, rows), :], qkv_ref.at[section, pl.ds(row, rows), :]))
        row = pl.multiple_of((block & 7) * rows, rows)
        column = pl.multiple_of((block >> 3) * inner, inner)
        copies.append((wide.at[slot, pl.ds(3 * rows, rows), :], out_ref.at[pl.ds(row, rows), pl.ds(column, inner)]))
    copies = [pltpu.make_async_copy(*pair, sems.at[at]) for at, pair in enumerate(copies)]
    for copy in copies:
        copy.start()
    return copies


def unpack_attend_first_kernel(place_ref, held_ref, qkv_ref, out_ref, wide, sems):
    for copy in place_attend(True, place_ref, held_ref, qkv_ref, out_ref, wide, sems):
        copy.wait()


def unpack_attend_last_kernel(place_ref, held_ref, before_ref, qkv_in, out_in, qkv_ref, out_ref, *refs):
    outs, (wide, little, sems) = refs[:-3], refs[-3:]
    copies = place_attend(False, place_ref, held_ref, qkv_ref, out_ref, wide, sems)
    start = 4 * (qkv_ref.shape[1] // 16)
    for slot in range(16):
        ref = before_ref if slot < 8 else held_ref
        rows = ref[slot % 8, start : start + 16, :].astype(F32)
        little[slot ^ place_ref[0]] = rows[:8, :]
    inner = qkv_ref.shape[2]
    outs[0][...] = little[0, 0:2, :]
    row = 2
    for out in outs[1:]:
        for at in range(out.shape[0] // inner):
            out[pl.ds(at * inner, inner)] = little[row // 2, row % 2, :]
            row += 1
    for copy in copies:
        copy.wait()


def unpack_attend(line, place, held, width, hidden, before=None, sums=None):
    _, height, inner = held.shape
    rows = width // 16
    shapes = [shaped((3, width, inner), F32), shaped((inner, width), F32)]
    scratch = [pltpu.VMEM((8, 4 * rows, inner), F32)]
    sems = pltpu.SemaphoreType.DMA((32,))
    common = dict(place=place, moved=8 * height * inner * 6, room=16, hint=1)
    if before is None:
        return line.run(
            unpack_attend_first_kernel, [held], shapes, out_specs=[ANYWHERE] * 2, scratch=scratch + [sems], **common
        )
    small = [(2, inner), (hidden,)] + [(width,)] * 6
    return line.run(
        unpack_attend_last_kernel,
        [held, before, *sums],
        shapes + [shaped(shape, F32) for shape in small],
        in_specs=[VMEM, VMEM, ANYWHERE, ANYWHERE],
        out_specs=[ANYWHERE] * 2 + [VMEM] * 8,
        scratch=scratch + [pltpu.VMEM((16, 8, inner), F32), sems],
        aliases={3: 0, 4: 1},
        **common,
    )


def unpack_ffn_kernel(first, place_ref, *refs):
    down_in, up_in = refs[:2]
    down_ref, in_ref, down, up, sems = refs[-5:]
    rows, half = down_ref.shape[0] // 16, down_ref.shape[1] // 2
    deep, wide = in_ref.shape[0] // 4, in_ref.shape[1] // 4
    copies = []
    for slot in range(8):
        block = (slot if first else slot + 8) ^ place_ref[0]
        values = down_in[slot].astype(F32)
        down[slot, :, :half] = values[:rows, :]
        down[slot, :, half:] = values[rows:, :]
        up[slot] = up_in[slot].astype(F32)
        row = pl.multiple_of(block * rows, rows)
        copies.append((down.at[slot], down_ref.at[pl.ds(row, rows), :]))
        block = ((slot & 1) * 4 + (slot >> 1) + (0 if first else 8)) ^ place_ref[0]
        row = pl.multiple_of((block & 3) * deep, deep)
        column = pl.multiple_of((block >> 2) * wide, wide)
        copies.append((up.at[slot], in_ref.at[pl.ds(row, deep), pl.ds(column, wide)]))
    copies = [pltpu.make_async_copy(*pair, sems.at[at]) for at, pair in enumerate(copies)]
    for copy in copies:
        copy.start()
    for copy in copies:
        copy.wait()


def unpack_ffn(line, place, down, up, width, hidden, before=None):
    return line.run(
        functools.partial(unpack_ffn_kernel, before is None),
        [down, up, *(before or [])],
        [shaped((hidden, width), F32), shaped((width, hidden), F32)],
        in_specs=[VMEM] * 2 + [ANYWHERE] * (0 if before is None else 2),
        out_specs=[ANYWHERE] * 2,
        scratch=[
            pltpu.VMEM((8, hidden // 16, width), F32),
            pltpu.VMEM((8, width // 4, hidden // 4), F32),
            pltpu.SemaphoreType.DMA((16,)),
        ],
        aliases={} if before is None else {3: 0, 4: 1},
        place=place,
        moved=6 * width * hidden,
        room=20,
        hint=1,
    )


def attend_kernel(tok_ref, w_ref, bias_ref, k_ref, v_ref, out_ref):
    rows, inner = out_ref.shape
    low = lane_halves(rows)
    queries = scaled((mm(tok_ref[...], w_ref[0]) + bias_ref[0:1, :]).astype(BF16))
    for at in range(0, inner, LANES):
        cut = slice(at, at + LANES)
        block, keys, values = queries[:, cut], k_ref[:, cut], v_ref[:, cut]
        zero, one = jnp.zeros_like(block), jnp.ones_like(values)
        mixed = []
        for first in (True, False):
            head = jnp.where(low == first, block, zero)
            with_sums = jnp.where(lane_halves(values.shape[0]) == first, values, one)
            scores = dot_nt(head, keys)
            exponent = jnp.exp(scores - jnp.max(scores, axis=-1, keepdims=True)).astype(BF16)
            mixed.append(mm(exponent, with_sums))
        top = jnp.where(low, mixed[0], mixed[1])
        total = jnp.where(low, mixed[1], mixed[0])
        out_ref[:, cut] = (top / pltpu.roll(total, HEAD, 1)).astype(BF16)


def attend(line, tokens, weights, bias, keys, values, seqs, seq, hint=None):
    rows, width = tokens.shape
    inner = keys.shape[1]
    length = rows // seqs
    long = pl.BlockSpec((length, inner), lambda s: (seq, 0))
    (result,) = line.run(
        attend_kernel,
        [tokens, weights, bias, keys, values],
        [shaped((length, inner), BF16)],
        grid=(1,),
        in_specs=[
            pl.BlockSpec((length, width), lambda s: (seq, 0)),
            pl.BlockSpec((1, width, inner), lambda s: (0, 0, 0)),
            whole(bias.shape),
            long,
            long,
        ],
        out_specs=[pl.BlockSpec((length, inner), lambda s: (0, 0))],
        flops=2 * length * width * inner + 16 * length * length * inner,
        moved=2 * (length * width + width * inner + 3 * length * inner),
        transcendentals=length * length * inner // HEAD,
        room=16,
        hint=hint,
    )
    return result


def layer_kernel(
    tok_ref, ctx_a, ctx_b, wo_a, wo_b, wi_a, wi_b, bi_a, bi_b, wd_a, wd_b, one_ref, two_ref, out_ref,
):
    branch = mm(ctx_a[...], wo_a[...]) + mm(ctx_b[...], wo_b[...]) + one_ref[0:1, :]
    unit, _ = norm_rows(tok_ref[...].astype(F32) + branch)
    normed = unit * one_ref[1:2, :] + one_ref[2:3, :]
    low = normed.astype(BF16)
    total = normed + two_ref[0:1, :]
    for w_in, b_in, w_down in ((wi_a, bi_a, wd_a), (wi_b, bi_b, wd_b)):
        hidden = gelu(mm(low, w_in[...]) + b_in[...]).astype(BF16)
        total = total + mm(hidden, w_down[...])
    unit, _ = norm_rows(total)
    out_ref[...] = (unit * two_ref[1:2, :] + two_ref[2:3, :]).astype(BF16)


def layer_next_kernel(*refs):
    layer_kernel(*refs[:-2], refs[-1])


def layer(line, tokens, contexts, w_out, w_in, b_in, w_down, one, two, seq, mixed, hint):
    length, inner = contexts[0].shape
    width, hidden = tokens.shape[1], w_in[0].shape[1]
    tile = 256
    steps = length // tile
    ctx = pl.BlockSpec((tile, inner), lambda i: (i, 0))
    still = [*w_out, *w_in, *b_in, *w_down, one, two]
    row = pl.BlockSpec((tile, width), lambda i: (seq * steps + i, 0))
    args = [tokens, *contexts, *still]
    specs = [row, ctx, ctx] + [whole(item.shape, True) for item in still]
    (result,) = line.run(
        layer_kernel if mixed is None else layer_next_kernel,
        args if mixed is None else [*args, mixed],
        [shaped(tokens.shape, BF16)],
        grid=(steps,),
        in_specs=specs if mixed is None else [*specs, ANYWHERE],
        out_specs=[row],
        aliases={} if mixed is None else {len(args): 0},
        room=30,
        hint=hint,
        flops=2 * length * width * (width + 4 * hidden),
        moved=4 * width * (length + 2 * hidden),
        transcendentals=2 * length * hidden,
    )
    return result


def input_grad_kernel(
    dk_a, dk_b, dv_a, dv_b, dq_a, dq_b, w_a, w_b, g_first_ref, places_ref, out_ref
):
    length = out_ref.shape[0]
    slots = g_first_ref.shape[0]
    few = g_first_ref[...] + dot_nt(dq_a[...], w_a[0]) + dot_nt(dq_b[...], w_b[0])
    coarse = few.astype(BF16)
    fine = (few - coarse.astype(F32)).astype(BF16)
    picks = places_ref[0][:, 0:1] == lax.broadcasted_iota(jnp.int32, (slots, length), 1)
    picks = picks.astype(F32).astype(BF16)
    total = dot_tn(picks, coarse) + dot_tn(picks, fine)
    for dk, dv, w in ((dk_a, dv_a, w_a), (dk_b, dv_b, w_b)):
        total = total + dot_nt(dk[...], w[1]) + dot_nt(dv[...], w[2])
    out_ref[...] = total


def input_grad_next_kernel(*refs):
    input_grad_kernel(*refs[:-2], refs[-1])


def input_grad(line, backs, weights, g_first, places, seqs, seq, before):
    rows, inner = backs[0][1].shape
    width = g_first.shape[1]
    length, slots = rows // seqs, g_first.shape[0] // seqs
    long = pl.BlockSpec((length, inner), lambda i: (seq, 0))
    short = pl.BlockSpec((slots, inner), lambda i: (seq, 0))
    args = [
        backs[0][1], backs[1][1], backs[0][2], backs[1][2], backs[0][0], backs[1][0],
        *weights, g_first, places,
    ]
    specs = (
        [long] * 4
        + [short] * 2
        + [whole(w.shape, True) for w in weights]
        + [
            pl.BlockSpec((slots, width), lambda i: (seq, 0)),
            pl.BlockSpec((1, slots, LANES), lambda i: (seq, 0, 0)),
        ]
    )
    (result,) = line.run(
        input_grad_kernel if before is None else input_grad_next_kernel,
        args if before is None else [*args, before],
        [shaped((rows, width), F32)],
        grid=(1,),
        in_specs=specs if before is None else [*specs, ANYWHERE],
        out_specs=[pl.BlockSpec((length, width), lambda i: (seq, 0))],
        aliases={} if before is None else {len(args): 0},
        flops=10 * length * width * inner,
        moved=20 * width * inner + 8 * length * width,
        room=24,
        hint=0.2,
    )
    return result


def pick_kernel(places_ref, fresh_ref, tok_ref, grad_ref, few_ref, grad_few_ref, turned_ref):
    slots, length = few_ref.shape[0], tok_ref.shape[0]
    picks = places_ref[0][:, 0:1] == lax.broadcasted_iota(jnp.int32, (slots, length), 1)
    picks = picks.astype(F32).astype(BF16)
    few_ref[...] = mm(picks, tok_ref[...]).astype(BF16)
    grad_few_ref[...] = mm(picks, grad_ref[...]) * fresh_ref[0][:, 0:1]
    turned_ref[...] = tok_ref[...].T


def pick(line, places, fresh, tokens, grads, seqs):
    rows, width = tokens.shape
    length, slots = rows // seqs, places.shape[1]
    flat = pl.BlockSpec((1, slots, LANES), lambda s: (s, 0, 0))
    long = pl.BlockSpec((length, width), lambda s: (s, 0))
    short = pl.BlockSpec((slots, width), lambda s: (s, 0))
    return line.run(
        pick_kernel,
        [places, fresh, tokens, grads],
        [
            shaped((seqs * slots, width), BF16),
            shaped((seqs * slots, width), F32),
            shaped((width, rows), BF16),
        ],
        grid=(seqs,),
        in_specs=[flat, flat, long, long],
        out_specs=[short, short, pl.BlockSpec((width, length), lambda s: (0, s))],
        flops=4 * rows * slots * width,
        moved=6 * rows * width,
        room=56,
    )


def body(
    tokens,
    grad_values,
    span_starts,
    w_qkv,
    b_qv,
    w_out,
    b_out,
    ln1_gain,
    ln1_bias,
    w_in,
    b_in,
    w_down,
    b_down,
    ln2_gain,
    ln2_bias,
):
    rows, width = tokens.shape
    inner = w_qkv.shape[2]
    hidden_half = w_in.shape[1]
    halves = lax.axis_size("tensor")
    seqs = span_starts.shape[0] // halves
    spans = span_starts.shape[1]
    length = rows // seqs
    half_at = lax.axis_index("tensor")
    me = lax.axis_index("dp")
    bits = lax.axis_size("dp").bit_length() - 1
    block_at = ((me & 1) << 3) | ((me & 2) << 1) | ((me & 4) >> 1) | ((me & 8) >> 3)
    place = block_at.reshape(1).astype(jnp.int32)
    rest = [1 << bit for bit in range(4, bits)]

    starts = lax.dynamic_slice_in_dim(span_starts, half_at * seqs, seqs, 0)
    places = starts[:, :, None] + jnp.arange(SPAN, dtype=jnp.int32)
    earlier = jnp.tril(jnp.ones((spans, spans), jnp.bool_), -1)
    covered = (places[:, :, :, None] >= starts[:, None, None, :]) & (
        places[:, :, :, None] < starts[:, None, None, :] + SPAN
    )
    fresh = ~jnp.any(covered & earlier[None, :, None, :], axis=-1)
    slots = -(-spans * SPAN // 16) * 16
    pad = slots - spans * SPAN
    places = jnp.pad(places.reshape(seqs, spans * SPAN), ((0, 0), (0, pad)))
    fresh = jnp.pad(fresh.reshape(seqs, spans * SPAN), ((0, 0), (0, pad)))
    few = seqs * slots
    places = jnp.broadcast_to(places[:, :, None], (seqs, slots, LANES))
    fresh = jnp.broadcast_to(fresh[:, :, None].astype(F32), (seqs, slots, LANES))
    vectors_one = jnp.stack([b_out, ln1_gain, ln1_bias])
    vectors_two = jnp.stack([b_down, ln2_gain, ln2_bias])
    here = me.reshape(1)
    line = Line()

    w_qkv_own = jnp.transpose(w_qkv, (1, 0, 2))
    b_in = b_in.reshape(1, -1)

    def chips_around(held):
        return [held, flip(held, 2), flip(held, 4), flip(held, 6)]

    arrived_qkv = flip_tensor(cut_qkv(line, w_qkv_own, here))
    arrived_biases = [flip_tensor(b_qv), flip_tensor(b_in)]
    half_out, eighth = second_cut(line, w_out, w_in, w_down, here)
    held_qkv, b_qv_oth, b_in_oth = relay(line, [arrived_qkv, *arrived_biases])
    around_qkv = chips_around(held_qkv)
    arrived_out, arrived_eighth = flip_tensor(half_out), flip_tensor(eighth)
    b_qv_both, b_in_both = [b_qv, b_qv_oth], [b_in, b_in_oth]
    tokens_few, grad_few, tokens_t = pick(line, places, fresh, tokens, grad_values, seqs)
    own = project(line, tokens, tokens_few, w_qkv_own, b_qv, seqs)
    def attend_own(seq):
        return attend(line, tokens, w_qkv_own, b_qv, own[0], own[1], seqs, seq)

    ctx_own = [attend_own(0)]
    core_first, held_eighth, half_in = third_cut(
        line, around_qkv, arrived_out, arrived_eighth, w_in, here
    )
    near_first = flip(core_first, 1)
    around_eighth = chips_around(held_eighth)
    arrived_in = flip_tensor(half_in)
    w_qkv_oth, w_out_oth = first_assemble(line, core_first, near_first, width, inner, here)
    w_qkv_both, w_out_both = [w_qkv_own, w_qkv_oth], [w_out, w_out_oth]
    oth = project(line, tokens, tokens_few, w_qkv_oth, b_qv_both[1], seqs)

    keys, values, queries_few, context_few = zip(own, oth)
    sum_few, normed_low = first_norm(line, context_few, w_out_both, tokens_few, vectors_one)

    def plane(values):
        return [values, flip_tensor(values), flip(values, 2), flip_both(values, 2)]

    slope_own, part = ffn_part(line, normed_low, w_in, b_in_both[0], w_down)
    ctx_own += [attend_own(seq) for seq in range(1, seqs)]
    core_second, held_in = fourth_cut(line, around_eighth, arrived_in)
    near_second, near_in = flip(core_second, 1), flip(held_in, 1)
    around_normed = plane(normed_low)
    w_in_oth, w_down_oth = second_assemble(
        line, core_second, near_second, held_in, near_in, hidden_half, here
    )
    w_in_both, w_down_both = [w_in, w_in_oth], [w_down, w_down_oth]
    g_ffn, g_branch, g_first, small_few = ffn(
        line, normed_low, part, sum_few, grad_few, vectors_one, vectors_two, slope_own,
        w_in_both, b_in_both[1], w_down_both,
    )
    around_g = plane(g_ffn)
    core_normed = join(line, around_normed)
    near_normed = flip(core_normed, 1)

    def back(at):
        return attend_back(
            line, place, queries_few[at], keys[at], values[at], g_branch, w_out_both[at],
            context_few[at], tokens_t, tokens_few, small_few, seqs, at, hidden_half // inner,
        )

    back_oth = back(1)
    near_oth = flip(back_oth[4], 1)
    back_own = back(0)
    near_own = flip(back_own[4], 1)
    core_g = join(line, around_g)
    near_g = flip(core_g, 1)

    def attend_oth(seq, hint):
        return attend(
            line, tokens, w_qkv_oth, b_qv_both[1], keys[1], values[1], seqs, seq, hint
        )

    ctx_oth = [attend_oth(0, 15)]
    x_send, y_send, x_keep, y_own, y_oth = cross_one(
        line, back_oth[3], near_oth, back_own[3], near_own, 112
    )
    x_near, y_near = flip_tensor(x_send), flip(y_send, 2)
    keep_down, send_down, keep_in, send_in = ffn_grads(
        line, place, w_in, w_down, b_in_both[0], [core_normed, near_normed], [core_g, near_g]
    )
    z_down, z_in = flip(send_down, 4), flip(send_in, 8)

    def over_rest(total):
        for bit in rest:
            total = total + flip(total, bit)
        return total

    def layer_of(seq, mixed, hint):
        return layer(
            line, tokens, [ctx_own[seq], ctx_oth[seq]], w_out_both, w_in_both, b_in_both, w_down_both,
            vectors_one, vectors_two, seq, mixed, hint,
        )

    def input_grad_of(seq, before):
        return input_grad(line, [back_own, back_oth], w_qkv_both, g_first, places, seqs, seq, before)

    ctx_oth += [attend_oth(seq, 0.2) for seq in range(1, seqs)]
    y_send, x_send, first, last = cross_two(line, x_keep, x_near, y_own, y_oth, y_near)
    y_near, x_near = flip(y_send, 2), flip_tensor(x_send)
    (keep_down, keep_in), sends = fold(line, [keep_down, keep_in], [z_down, z_in], True, 3)
    z_down, z_in = flip(sends[0], 8), flip(sends[1], 4)
    d_tokens = input_grad_of(0, None)
    keep, send = cross_three(line, first, y_near, last, x_near)
    z_attn = flip(send, 4)
    keeps, arrived = [over_rest(keep_down), over_rest(keep_in)], [over_rest(z_down), over_rest(z_in)]
    down, up = fold(line, keeps, arrived, False, 8)
    near_down, near_up = flip(down, 8), flip(up, 2)
    for seq in range(1, seqs):
        d_tokens = input_grad_of(seq, d_tokens)
    (keep,), (send,) = fold(line, [keep], [z_attn], True, 0.5)
    z_attn = flip(send, 8)
    mixed = layer_of(0, None, 1)
    down, up = append(line, 1, [down, near_down], [up, near_up])
    near_down, near_up = flip(down, 4), flip(up, 8)
    (attn,) = fold(line, [over_rest(keep)], [over_rest(z_attn)], False, 6)
    near_attn = flip(attn, 8)
    down, up = append(line, 1, [down, near_down], [up, near_up])
    near_down, near_up = flip(down, 2), flip(up, 4)
    (attn,) = append(line, 2, [attn, near_attn])
    around_attn = [attn, flip(attn, 4), flip(attn, 2), flip(attn, 6)]
    for seq in range(1, seqs):
        mixed = layer_of(seq, mixed, 16)
    down, up = append(line, 1, [down, near_down], [up, near_up])
    near_down, near_up = flip(down, 1), flip(up, 1)
    ffn_sums = unpack_ffn(line, place, down, up, width, hidden_half)
    (attn,) = append(line, 1, around_attn)
    near_attn = flip(attn, 1)
    sums = unpack_attend(line, place, attn, width, hidden_half)
    d_w_down, d_w_in = unpack_ffn(line, place, near_down, near_up, width, hidden_half, ffn_sums)
    d_w_qkv, d_w_out, *small = unpack_attend(line, place, near_attn, width, hidden_half, attn, sums)
    d_w_qkv = jnp.transpose(d_w_qkv, (1, 0, 2))
    d_b_qv, d_b_in, d_b_out, d_ln1_gain, d_ln1_bias, d_b_down, d_ln2_gain, d_ln2_bias = small

    return (
        mixed,
        d_tokens,
        d_w_qkv,
        d_b_qv,
        d_w_out,
        d_b_out,
        d_ln1_gain,
        d_ln1_bias,
        d_w_in,
        d_b_in,
        d_w_down,
        d_b_down,
        d_ln2_gain,
        d_ln2_bias,
    )


def solution(mesh):
    placed = (
        P(("dp", "tensor"), None),
        P(("dp", "tensor"), None),
        P("dp", None),
        P(None, None, "tensor"),
        P(None, "tensor"),
        P("tensor", None),
        P(),
        P(),
        P(),
        P(None, "tensor"),
        P("tensor"),
        P("tensor", None),
        P(),
        P(),
        P(),
    )
    return jax.shard_map(
        body,
        mesh=mesh,
        in_specs=placed,
        out_specs=(
            P(("dp", "tensor"), None),
            P(("dp", "tensor"), None),
            P(None, None, "tensor"),
            P(None, "tensor"),
            P("tensor", None),
            P(),
            P(),
            P(),
            P(None, "tensor"),
            P("tensor"),
            P("tensor", None),
            P(),
            P(),
            P(),
        ),
        check_vma=False,
    )
```

```python
import functools

import jax
import jax.numpy as jnp
from jax import lax
from jax.experimental import pallas as pl
from jax.experimental.pallas import tpu as pltpu
from jax.sharding import PartitionSpec as P

HEAD = 64
SPAN = 6
LANES = 128
EPSILON = 1e-05
F32 = jnp.float32
BF16 = jnp.bfloat16
GELU_A = (2.0 / 3.141592653589793) ** 0.5
GELU_B = 0.044715
HINT_GRADS, HINT_BACK = 15, 10
BYTES_US = 11_070_000
FLOPS_US = 3_459_000_000
ANYWHERE = pl.BlockSpec(memory_space=pl.ANY)
VMEM = pl.BlockSpec(memory_space=pltpu.VMEM)


class Line:
    def __init__(self):
        self.token = jnp.zeros((8, LANES), F32)

    def run(
        self, kernel, args, out_shape, grid=(), in_specs=None, out_specs=None, scratch=(), place=None,
        flops=0, moved=0, transcendentals=0, room=6, aliases=None, hint=None,
    ):
        ins, outs = len(args), len(out_shape)
        lead = 0 if place is None else 1

        def with_token(*refs):
            given, rest = refs[: lead + ins], refs[lead + ins + 1 :]
            rest[outs][...] = jnp.zeros((8, LANES), F32)
            kernel(*given, *rest[:outs], *rest[outs + 1 :])

        in_specs = list(in_specs or [VMEM] * ins) + [ANYWHERE]
        out_specs = list(out_specs or [VMEM] * outs)
        out_specs.append(pl.BlockSpec((8, LANES), lambda *at: (0, 0)) if grid else VMEM)
        shapes = list(out_shape) + [jax.ShapeDtypeStruct((8, LANES), F32)]
        params = dict(
            out_shape=shapes,
            input_output_aliases=aliases or {},
            compiler_params=pltpu.CompilerParams(vmem_limit_bytes=room << 20),
            cost_estimate=pl.CostEstimate(
                flops=int(flops if hint is None else hint * FLOPS_US),
                bytes_accessed=int(moved if hint is None else hint * BYTES_US),
                transcendentals=int(transcendentals if hint is None else 0),
            ),
        )
        if lead and grid:
            params["grid_spec"] = pltpu.PrefetchScalarGridSpec(
                num_scalar_prefetch=1, grid=grid, in_specs=in_specs, out_specs=out_specs, scratch_shapes=list(scratch)
            )
        else:
            if lead:
                in_specs = [pl.BlockSpec(memory_space=pltpu.SMEM)] + in_specs
            params.update(grid=grid, in_specs=in_specs, out_specs=out_specs, scratch_shapes=list(scratch))
        front = [] if place is None else [place]
        *results, self.token = pl.pallas_call(with_token, **params)(*front, *args, self.token)
        return results


def shaped(shape, kind):
    return jax.ShapeDtypeStruct(tuple(shape), kind)


def whole(shape, once=False):
    held = dict(pipeline_mode=pl.Buffered(1)) if once else {}
    return pl.BlockSpec(shape, lambda *at: (0,) * len(shape), **held)


def flip(values, bits):
    size = lax.axis_size("dp")
    return lax.ppermute(values, "dp", [(at, at ^ bits) for at in range(size)])


def flip_tensor(values):
    return lax.ppermute(values, "tensor", [(0, 1), (1, 0)])


def flip_both(values, bits):
    size = 2 * lax.axis_size("dp")
    pairs = [(at, at ^ (2 * bits + 1)) for at in range(size)]
    return lax.ppermute(values, ("dp", "tensor"), pairs)


def dot_nt(left, right):
    return lax.dot_general(left, right, (((1,), (1,)), ((), ())), preferred_element_type=F32)


def dot_tn(left, right):
    return lax.dot_general(left, right, (((0,), (0,)), ((), ())), preferred_element_type=F32)


def mm(left, right):
    return jnp.dot(left, right, preferred_element_type=F32)


def lane_halves(rows):
    return lax.broadcasted_iota(jnp.int32, (rows, LANES), 1) < HEAD


def two_heads(block):
    low = lane_halves(block.shape[0])
    zero = jnp.zeros_like(block)
    return jnp.concatenate([jnp.where(low, block, zero), jnp.where(low, zero, block)], axis=0)


def scaled(queries):
    return queries * jnp.asarray(HEAD ** (-0.5), BF16)


def softmax_rows(scores):
    exponent = jnp.exp(scores - jnp.max(scores, axis=-1, keepdims=True))
    return exponent * (1.0 / jnp.sum(exponent, axis=-1, keepdims=True))


def attend_block(queries, keys, values):
    rows = queries.shape[0]
    probs = softmax_rows(dot_nt(two_heads(scaled(queries)), keys)).astype(BF16)
    mixed = mm(probs, values)
    return jnp.where(lane_halves(rows), mixed[:rows], mixed[rows:]).astype(BF16)


def norm_rows(values):
    average = jnp.mean(values, axis=-1, keepdims=True)
    centered = values - average
    variance = jnp.mean(centered * centered, axis=-1, keepdims=True)
    root = lax.rsqrt(variance + EPSILON)
    return centered * root, root


def norm_back(grad, unit, root, gain):
    grad_y = grad * gain
    inner = jnp.mean(grad_y, axis=-1, keepdims=True)
    along = jnp.mean(grad_y * unit, axis=-1, keepdims=True)
    return root * (grad_y - inner - unit * along)


def gelu_and_slope(values):
    square = values * values
    bent = jnp.tanh(GELU_A * values * (1.0 + GELU_B * square))
    half = 0.5 * (1.0 + bent)
    slope = half + 0.5 * values * (1.0 - bent * bent) * GELU_A * (1.0 + 3.0 * GELU_B * square)
    return values * half, slope


def gelu(values):
    return 0.5 * values * (1.0 + jnp.tanh(GELU_A * values * (1.0 + GELU_B * values * values)))


def join_kernel(count, *refs):
    rows = refs[0].shape[-2]
    for at in range(count):
        refs[count][..., at * rows : (at + 1) * rows, :] = refs[at][...]


def join(line, pieces):
    *lead, rows, columns = pieces[0].shape
    (result,) = line.run(
        functools.partial(join_kernel, len(pieces)),
        pieces,
        [shaped((*lead, rows * len(pieces), columns), pieces[0].dtype)],
        moved=4 * len(pieces) * pieces[0].size,
    )
    return result


def cut_qkv_kernel(place_ref, in_ref, out_ref, sem):
    rows = out_ref.shape[1]
    row = pl.multiple_of((place_ref[0] & 7) * rows, rows)
    copy = pltpu.make_async_copy(in_ref.at[:, pl.ds(row, rows), :], out_ref, sem)
    copy.start()
    copy.wait()


def cut_qkv(line, w_qkv, here):
    lead, rows, columns = w_qkv.shape
    (piece,) = line.run(
        cut_qkv_kernel,
        [w_qkv],
        [shaped((lead, rows // 8, columns), BF16)],
        in_specs=[ANYWHERE],
        scratch=[pltpu.SemaphoreType.DMA],
        place=here,
        moved=w_qkv.size // 2,
        room=56,
    )
    return piece


def second_cut_kernel(place_ref, out_ref, in_ref, down_ref, half, eighth):
    half[...] = out_ref[...]
    rows = in_ref.shape[0]
    eighth[:rows, :] = in_ref[...]
    eighth[rows:, :] = down_ref[...]


def second_cut(line, w_out, w_in, w_down, here):
    width = w_out.shape[1]
    half, eighth, deep = w_out.shape[0] // 2, w_in.shape[0] // 8, w_down.shape[0] // 8
    return line.run(
        second_cut_kernel,
        [w_out, w_in, w_down],
        [shaped((half, width), BF16), shaped((eighth + deep, width), BF16)],
        grid=(1,),
        in_specs=[
            pl.BlockSpec((half, width), lambda i, p: (p[0] & 1, 0)),
            pl.BlockSpec((eighth, width), lambda i, p: (p[0] & 7, 1)),
            pl.BlockSpec((deep, width), lambda i, p: (p[0] & 7, 0)),
        ],
        out_specs=[whole((half, width)), whole((eighth + deep, width))],
        place=here,
        moved=4 * (half + eighth + deep) * width,
        room=56,
    )


def relay_kernel(count, *refs):
    for at in range(count):
        refs[count + at][...] = refs[at][...]


def relay(line, arrived):
    return line.run(
        functools.partial(relay_kernel, len(arrived)),
        arrived,
        [shaped(item.shape, item.dtype) for item in arrived],
        moved=sum(4 * item.size for item in arrived),
    )


def third_cut_kernel(place_ref, a, b, c, d, out_ref, eighth_ref, in_ref, core, eighth, half):
    third, rows, inner = a.shape
    for at, ref in enumerate((a, b, c, d)):
        for section in range(third):
            row = (section * 4 + at) * rows
            core[row : row + rows, :] = ref[section]
    row = 4 * third * rows
    deep = out_ref.shape[0]
    core[row : row + deep, :] = out_ref[:, :inner]
    core[row + deep :, :] = out_ref[:, inner:]
    eighth[...] = eighth_ref[...]
    half[...] = in_ref[...]


def third_cut(line, qkv, out, eighth, w_in, here):
    third, rows, inner = qkv[0].shape
    width = out.shape[1]
    height = 4 * third * rows + 2 * out.shape[0]
    half = (w_in.shape[0] // 2, width)
    return line.run(
        third_cut_kernel,
        [*qkv, out, eighth, w_in],
        [shaped((height, inner), BF16), shaped(eighth.shape, BF16), shaped(half, BF16)],
        grid=(1,),
        in_specs=[whole(item.shape) for item in [*qkv, out, eighth]]
        + [pl.BlockSpec(half, lambda i, p: (p[0] & 1, 0))],
        out_specs=[whole((height, inner)), whole(eighth.shape), whole(half)],
        place=here,
        moved=4 * (height * inner + eighth.size + half[0] * width),
    )


def first_assemble_kernel(place_ref, mine, near, qkv_ref, out_ref):
    third, width, inner = qkv_ref.shape
    rows, half = width // 8, out_ref.shape[0] // 2
    for core, ref in enumerate((mine, near)):
        for at in range(4):
            row = pl.multiple_of(((place_ref[0] ^ (2 * at + core)) & 7) * rows, rows)
            for section in range(third):
                start = (section * 4 + at) * rows
                qkv_ref[section, pl.ds(row, rows), :] = ref[start : start + rows, :]
        row = pl.multiple_of(((place_ref[0] ^ core) & 1) * half, half)
        start = 4 * third * rows
        out_ref[pl.ds(row, half), :inner] = ref[start : start + half, :]
        out_ref[pl.ds(row, half), inner:] = ref[start + half :, :]


def first_assemble(line, mine, near, width, inner, here):
    return line.run(
        first_assemble_kernel,
        [mine, near],
        [shaped((3, width, inner), BF16), shaped((inner, width), BF16)],
        place=here,
        moved=8 * mine.size,
    )


def fourth_cut_kernel(a, b, c, d, half_ref, eighths, half):
    rows = a.shape[0]
    for at, ref in enumerate((a, b, c, d)):
        eighths[at * rows : (at + 1) * rows, :] = ref[...]
    half[...] = half_ref[...]


def fourth_cut(line, eighths, half):
    rows, width = eighths[0].shape
    return line.run(
        fourth_cut_kernel,
        [*eighths, half],
        [shaped((4 * rows, width), BF16), shaped(half.shape, BF16)],
        moved=16 * rows * width,
    )


def second_assemble_kernel(place_ref, mine, near, half_mine, half_near, in_ref, down_ref):
    width = half_mine.shape[1]
    rows, deep, half = in_ref.shape[0] // 8, down_ref.shape[0] // 8, half_mine.shape[0]
    for core, (ref, half_ref) in enumerate(((mine, half_mine), (near, half_near))):
        for at in range(4):
            block = (place_ref[0] ^ (2 * at + core)) & 7
            start = at * (rows + deep)
            in_ref[pl.ds(pl.multiple_of(block * rows, rows), rows), width:] = ref[
                start : start + rows, :
            ]
            down_ref[pl.ds(pl.multiple_of(block * deep, deep), deep), :] = ref[
                start + rows : start + rows + deep, :
            ]
        row = pl.multiple_of(((place_ref[0] ^ core) & 1) * half, half)
        in_ref[pl.ds(row, half), :width] = half_ref[...]


def second_assemble(line, mine, near, half_mine, half_near, hidden, here):
    width = half_mine.shape[1]
    return line.run(
        second_assemble_kernel,
        [mine, near, half_mine, half_near],
        [shaped((width, hidden), BF16), shaped((hidden, width), BF16)],
        place=here,
        moved=8 * width * hidden,
    )


def project_kernel(tok_ref, few_ref, w_ref, bias_ref, k_ref, v_ref, q_ref, ctx_ref):
    tok = tok_ref[...]
    k_ref[...] = mm(tok, w_ref[1]).astype(BF16)
    v_ref[...] = (mm(tok, w_ref[2]) + bias_ref[1:2, :]).astype(BF16)
    q_ref[...] = (mm(few_ref[...], w_ref[0]) + bias_ref[0:1, :]).astype(BF16)
    for at in range(0, k_ref.shape[1], LANES):
        cut = slice(at, at + LANES)
        ctx_ref[:, cut] = attend_block(q_ref[:, cut], k_ref[:, cut], v_ref[:, cut])


def project(line, tokens, few, weights, bias, seqs):
    rows, width = tokens.shape
    inner = weights.shape[2]
    length, slots = rows // seqs, few.shape[0] // seqs
    long, short = (pl.BlockSpec((size, inner), lambda s: (s, 0)) for size in (length, slots))
    return line.run(
        project_kernel,
        [tokens, few, weights, bias],
        [shaped((rows, inner), BF16)] * 2 + [shaped((few.shape[0], inner), BF16)] * 2,
        grid=(seqs,),
        in_specs=[
            pl.BlockSpec((length, width), lambda s: (s, 0)),
            pl.BlockSpec((slots, width), lambda s: (s, 0)),
            whole(weights.shape),
            whole(bias.shape),
        ],
        out_specs=[long, long, short, short],
        flops=6 * rows * width * inner,
        room=16,
        moved=2 * (rows * width + 3 * width * inner + 2 * rows * inner),
    )


def first_norm_kernel(ctx_a, ctx_b, w_a, w_b, few_ref, vec_ref, sum_ref, low_ref):
    branch = mm(ctx_a[...], w_a[...]) + mm(ctx_b[...], w_b[...]) + vec_ref[0:1, :]
    total = few_ref[...].astype(F32) + branch
    sum_ref[...] = total
    low_ref[...] = (norm_rows(total)[0] * vec_ref[1:2, :] + vec_ref[2:3, :]).astype(BF16)


def first_norm(line, contexts, w_out, few, vectors):
    count, width = few.shape
    return line.run(
        first_norm_kernel,
        [*contexts, *w_out, few, vectors],
        [shaped((count, width), F32), shaped((count, width), BF16)],
        flops=2 * count * width * width,
        moved=2 * width * width + 14 * count * width,
    )


def ffn_part_kernel(low_ref, wi_ref, bi_ref, wd_ref, slope_ref, part_ref, total):
    step = pl.program_id(0)
    gate, slope = gelu_and_slope(mm(low_ref[...], wi_ref[...]) + bi_ref[...])
    slope_ref[...] = slope
    part = mm(gate.astype(BF16), wd_ref[...])

    @pl.when(step == 0)
    def _():
        total[...] = part

    @pl.when(step > 0)
    def _():
        total[...] += part

    @pl.when(step == pl.num_programs(0) - 1)
    def _():
        part_ref[...] = total[...]


def ffn_part(line, low, w_in, b_in, w_down):
    count, width = low.shape
    hidden = w_in.shape[1]
    steps = 4
    tile = hidden // steps
    flat = whole((count, width))
    return line.run(
        ffn_part_kernel,
        [low, w_in, b_in, w_down],
        [shaped((count, hidden), F32), shaped((count, width), F32)],
        grid=(steps,),
        in_specs=[
            flat,
            pl.BlockSpec((width, tile), lambda j: (0, j)),
            pl.BlockSpec((1, tile), lambda j: (0, j)),
            pl.BlockSpec((tile, width), lambda j: (j, 0)),
        ],
        out_specs=[pl.BlockSpec((count, tile), lambda j: (0, j)), flat],
        scratch=[pltpu.VMEM((count, width), F32)],
        flops=4 * count * width * hidden,
        moved=4 * width * hidden,
        transcendentals=count * hidden,
        room=12,
    )


def column_sum(values):
    return jnp.sum(values, axis=0, keepdims=True)


def ffn_last_kernel(
    low_ref, part_ref, sum_ref, grad_ref, one_ref, two_ref, wi_ref, bi_ref, wd_ref,
    g_ffn_ref, g_second_ref, slope_ref, sums_ref,
):
    gate, slope = gelu_and_slope(mm(low_ref[...], wi_ref[...]) + bi_ref[...])
    slope_ref[...] = slope
    ffn = part_ref[...] + mm(gate.astype(BF16), wd_ref[...]) + two_ref[0:1, :]
    normed = norm_rows(sum_ref[...])[0] * one_ref[1:2, :] + one_ref[2:3, :]
    unit, root = norm_rows(normed + ffn)
    grad = grad_ref[...]
    g_second = norm_back(grad, unit, root, two_ref[1:2, :])
    g_ffn = g_second.astype(BF16)
    g_ffn_ref[...] = g_ffn
    g_second_ref[...] = g_second
    sums = (column_sum(g_ffn.astype(F32)), column_sum(grad * unit), column_sum(grad))
    sums_ref[...] = jnp.concatenate([*sums, jnp.zeros((5, grad.shape[1]), F32)], axis=0)


def ffn_last(line, low, part, total, grad, one, two, w_in, b_in, w_down):
    count, width = low.shape
    hidden = w_in.shape[1]
    return line.run(
        ffn_last_kernel,
        [low, part, total, grad, one, two, w_in, b_in, w_down],
        [
            shaped((count, width), BF16),
            shaped((count, width), F32),
            shaped((count, hidden), F32),
            shaped((8, width), F32),
        ],
        flops=4 * count * width * hidden,
        moved=4 * width * hidden,
        room=12,
    )


def ffn_back_kernel(
    g_ffn_ref, g_second_ref, sum_ref, one_ref, sums_ref, slope_a, slope_b, wi_a, wi_b, wd_a, wd_b,
    g_branch_ref, g_first_ref, small_ref,
):
    g_ffn, g_normed = g_ffn_ref[...], g_second_ref[...]
    width = g_normed.shape[1]
    half = width // 2
    deep = slope_a.shape[1] // half
    for at, (slope, w_in, w_down) in enumerate(((slope_a, wi_a, wd_a), (slope_b, wi_b, wd_b))):
        g_pre = (slope[...] * dot_nt(g_ffn, w_down[...])).astype(BF16)
        bias = column_sum(g_pre.astype(F32))
        for row in range(deep):
            small_ref[at * deep + row : at * deep + row + 1, :] = bias[:, row * half : (row + 1) * half]
        g_normed = g_normed + dot_nt(g_pre, w_in[...])
    unit, root = norm_rows(sum_ref[...])
    g_first = norm_back(g_normed, unit, root, one_ref[1:2, :])
    g_branch = g_first.astype(BF16)
    g_first_ref[...] = g_first
    g_branch_ref[...] = g_branch
    vectors = (
        column_sum(g_branch.astype(F32)),
        column_sum(g_normed * unit),
        column_sum(g_normed),
        *[sums_ref[at : at + 1, :] for at in range(3)],
    )
    for at, vector in enumerate(vectors):
        row = 2 * deep + 2 * at
        small_ref[row : row + 1, :] = vector[:, :half]
        small_ref[row + 1 : row + 2, :] = vector[:, half:]
    count = 2 * deep + 12
    small_ref[count:, :] = jnp.zeros((small_ref.shape[0] - count, half), F32)


def ffn_back(line, g_ffn, g_second, total, one, sums, slopes, w_in, w_down):
    count, width = g_ffn.shape
    hidden = w_in[0].shape[1]
    rows = 2 * (hidden // (width // 2)) + 12
    return line.run(
        ffn_back_kernel,
        [g_ffn, g_second, total, one, sums, *slopes, *w_in, *w_down],
        [
            shaped((count, width), BF16),
            shaped((count, width), F32),
            shaped((-(-rows // 8) * 8, width // 2), F32),
        ],
        flops=8 * count * width * hidden,
        moved=8 * width * hidden,
        room=12,
    )


def ffn_grads_kernel(place_ref, wi_ref, wd_ref, bi_ref, *refs):
    normed_refs, grad_refs = refs[:2], refs[2:4]
    keep_down, send_down, keep_in, send_in = refs[4:8]
    down, up = refs[8:]
    width = normed_refs[0].shape[1]
    tile = wi_ref.shape[1] // 4
    hidden = pl.ds(pl.multiple_of((place_ref[0] >> 2) * tile, tile), tile)
    w_in, w_down, b_in = wi_ref[:, hidden], wd_ref[hidden, :], bi_ref[:, hidden]
    for at in range(2):
        normed, grad = normed_refs[at][...], grad_refs[at][...]
        gate, slope = gelu_and_slope(mm(normed, w_in) + b_in)
        pre = (slope * dot_nt(grad, w_down)).astype(BF16)
        down_part = dot_tn(gate.astype(BF16), grad)
        up_part = dot_tn(normed, pre)
        if at == 0:
            down[...] = down_part
            up[...] = up_part
        else:
            down[...] += down_part
            up[...] += up_part
    down_rows, up_rows = tile // 4, width // 4
    half = width // 2
    for slot in range(4):
        block = slot ^ (place_ref[0] & 3)
        low = down[pl.ds(pl.multiple_of(block * down_rows, down_rows), down_rows), :]
        block = (0, 2, 1, 3)[slot] ^ (place_ref[0] & 3)
        high = up[pl.ds(pl.multiple_of(block * up_rows, up_rows), up_rows), :]
        to_down, to_in = (keep_down, keep_in) if slot < 2 else (send_down, send_in)
        kind = to_down.dtype
        to_down[slot % 2, :down_rows, :] = low[:, :half].astype(kind)
        to_down[slot % 2, down_rows:, :] = low[:, half:].astype(kind)
        to_in[slot % 2, :, :] = high.astype(kind)


def ffn_grads(line, place, w_in, w_down, b_in, normed, grads):
    rows, width = normed[0].shape
    tile = w_in.shape[1] // 4
    shape = (2, 2 * (tile // 4), width // 2)
    wide = (2, width // 4, tile)
    return line.run(
        ffn_grads_kernel,
        [w_in, w_down, b_in, *normed, *grads],
        [shaped(shape, F32), shaped(shape, BF16), shaped(wide, F32), shaped(wide, BF16)],
        scratch=[pltpu.VMEM((tile, width), F32), pltpu.VMEM((width, tile), F32)],
        place=place,
        flops=16 * rows * width * tile,
        moved=12 * rows * width + 16 * width * tile,
        hint=HINT_GRADS,
        room=16,
    )


def attend_back_kernel(
    seqs, half, deep, place_ref, q_ref, k_ref, v_ref, g_branch_ref, w_out_ref, ctx_ref, tok_t_ref, few_ref,
    small_ref, dq_ref, dk_ref, dv_ref, keep_ref, send_ref, total, little,
):
    few, inner = q_ref.shape
    rows = k_ref.shape[0]
    slots, length = few // seqs, rows // seqs
    low = lane_halves(slots)
    scale = HEAD ** (-0.5)
    g_branch = g_branch_ref[...]
    g_context = dot_nt(g_branch, w_out_ref[...]).astype(BF16)
    for seq in range(seqs):
        short, long = slice(seq * slots, (seq + 1) * slots), slice(seq * length, (seq + 1) * length)
        for at in range(0, inner, LANES):
            cut = slice(at, at + LANES)
            both, grads = two_heads(scaled(q_ref[short, cut])), two_heads(g_context[short, cut])
            keys, values = k_ref[long, cut], v_ref[long, cut]
            probs = softmax_rows(dot_nt(both, keys))
            grad_probs = dot_nt(grads, values)
            dv_ref[long, cut] = dot_tn(probs.astype(BF16), grads).astype(BF16)
            row_total = jnp.sum(grad_probs * probs, axis=-1, keepdims=True)
            grad_scores = (probs * (grad_probs - row_total)).astype(BF16)
            dq = mm(grad_scores, keys) * scale
            dq_ref[short, cut] = jnp.where(low, dq[:slots], dq[slots:]).astype(BF16)
            dk_ref[long, cut] = dot_tn(grad_scores, both).astype(BF16)
    dq, dk, dv = dq_ref[...], dk_ref[...], dv_ref[...]
    total[0] = dot_tn(few_ref[...], dq)
    total[1] = mm(tok_t_ref[...], dk)
    total[2] = mm(tok_t_ref[...], dv)
    out_grad = dot_tn(ctx_ref[...], g_branch)
    total[3, :inner, :] = out_grad[:, :inner]
    total[3, inner:, :] = out_grad[:, inner:]
    little[...] = jnp.zeros_like(little)
    little[0, 0:1, :] = column_sum(dq.astype(F32))
    little[0, 1:2, :] = column_sum(dv.astype(F32))
    for at in range(deep + 12):
        source = half * deep + at if at < deep else deep + at
        little[1 + at // 2, at % 2 : at % 2 + 1, :] = small_ref[source : source + 1, :]
    block_rows = total.shape[1] // 16
    pad = keep_ref.shape[1] - 4 * block_rows
    for slot in range(16):
        block = slot ^ place_ref[0]
        row = pl.multiple_of(block * block_rows, block_rows)
        to, kind = (keep_ref, F32) if slot < 8 else (send_ref, BF16)
        for section in range(4):
            cut = slice(section * block_rows, (section + 1) * block_rows)
            to[slot % 8, cut, :] = total[section, pl.ds(row, block_rows), :].astype(kind)
        pair = jnp.concatenate([little[block], jnp.zeros((pad - 8, inner), F32)], axis=0)
        to[slot % 8, 4 * block_rows :, :] = pair.astype(kind)


def attend_back(line, place, queries, keys, values, g_branch, w_out, context, tokens_t, few, small, seqs, half, deep):
    rows, inner = keys.shape
    width = tokens_t.shape[0]
    count = queries.shape[0]
    held = (8, 4 * (width // 16) + 16, inner)
    return line.run(
        functools.partial(attend_back_kernel, seqs, half, deep),
        [queries, keys, values, g_branch, w_out, context, tokens_t, few, small],
        [
            shaped((count, inner), BF16),
            shaped((rows, inner), BF16),
            shaped((rows, inner), BF16),
            shaped(held, F32),
            shaped(held, BF16),
        ],
        scratch=[pltpu.VMEM((4, width, inner), F32), pltpu.VMEM((16, 8, inner), F32)],
        place=place,
        hint=HINT_BACK,
        room=16,
        flops=4 * rows * width * inner + 24 * count * rows * inner,
        moved=20 * rows * inner,
    )


def fold_kernel(count, halve, *refs):
    keeps, arrived, outs = refs[:count], refs[count : 2 * count], refs[2 * count :]
    for at in range(count):
        total = keeps[at][...] + arrived[at][...].astype(F32)
        if halve:
            middle = total.shape[0] // 2
            outs[2 * at][...] = total[:middle]
            outs[2 * at + 1][...] = total[middle:].astype(BF16)
        else:
            outs[at][...] = total.astype(BF16)


def fold(line, keeps, arrived, halve, hint):
    shapes = []
    for keep in keeps:
        half = (keep.shape[0] // 2, *keep.shape[1:])
        shapes += [shaped(half, F32), shaped(half, BF16)] if halve else [shaped(keep.shape, BF16)]
    results = line.run(
        functools.partial(fold_kernel, len(keeps), halve),
        [*keeps, *arrived],
        shapes,
        hint=hint,
    )
    return (results[0::2], results[1::2]) if halve else results


def append_kernel(count, *refs):
    groups, out = refs[:-count], refs[-count:]
    each = len(groups) // count
    for at in range(count):
        row = 0
        for ref in groups[at * each : (at + 1) * each]:
            out[at][row : row + ref.shape[0]] = ref[...]
            row += ref.shape[0]


def append(line, hint, *groups):
    shapes = [shaped((sum(item.shape[0] for item in group), *group[0].shape[1:]), BF16) for group in groups]
    return line.run(
        functools.partial(append_kernel, len(groups)),
        [item for group in groups for item in group],
        shapes,
        hint=hint,
    )


def cross_one_kernel(oth, oth_near, own, own_near, x_send, y_send, x_keep, y_keep_own, y_keep_oth):
    rows = x_send.shape[1]
    half = oth.shape[0] // 2
    x_send[...] = (oth[:, :rows, :] + oth_near[:, :rows, :].astype(F32)).astype(BF16)
    x_keep[...] = own[:, :rows, :] + own_near[:, :rows, :].astype(F32)
    for at, (keep, near, out) in enumerate(((own, own_near, y_keep_own), (oth, oth_near, y_keep_oth))):
        total = keep[:, rows:, :] + near[:, rows:, :].astype(F32)
        out[...] = total[:half]
        y_send[at] = total[half:].astype(BF16)


def cross_one(line, oth, oth_near, own, own_near, rows):
    count, height, inner = oth.shape
    half, last = count // 2, height - rows
    return line.run(
        cross_one_kernel,
        [oth, oth_near, own, own_near],
        [
            shaped((count, rows, inner), BF16),
            shaped((2, half, last, inner), BF16),
            shaped((count, rows, inner), F32),
            shaped((half, last, inner), F32),
            shaped((half, last, inner), F32),
        ],
        hint=2,
    )


def cross_two_kernel(x_keep, x_near, own, oth, y_near, y_send, x_send, first, last):
    half = own.shape[0]
    total = x_keep[...] + x_near[...].astype(F32)
    first[...] = total[:half]
    y_send[...] = total[half:].astype(BF16)
    last[...] = own[...] + y_near[0].astype(F32)
    x_send[...] = (oth[...] + y_near[1].astype(F32)).astype(BF16)


def cross_two(line, x_keep, x_near, own, oth, y_near):
    half = (own.shape[0], x_keep.shape[1], x_keep.shape[2])
    return line.run(
        cross_two_kernel,
        [x_keep, x_near, own, oth, y_near],
        [shaped(half, BF16), shaped(own.shape, BF16), shaped(half, F32), shaped(own.shape, F32)],
        hint=0.5,
    )


def cross_three_kernel(first, y_near, last, x_near, keep, send):
    rows, half = first.shape[1], first.shape[0] // 2
    for ref, near, cut in ((first, y_near, slice(0, rows)), (last, x_near, slice(rows, None))):
        total = ref[...] + near[...].astype(F32)
        keep[:, cut, :] = total[:half]
        send[:, cut, :] = total[half:].astype(BF16)


def cross_three(line, first, y_near, last, x_near):
    shape = (first.shape[0] // 2, first.shape[1] + last.shape[1], first.shape[2])
    return line.run(
        cross_three_kernel,
        [first, y_near, last, x_near],
        [shaped(shape, F32), shaped(shape, BF16)],
        hint=0.5,
    )


def unpack_attend_kernel(place_ref, mine_ref, near_ref, qkv_ref, out_ref, *refs):
    outs, (wide, little, sems) = refs[:-3], refs[-3:]
    inner = qkv_ref.shape[2]
    rows = qkv_ref.shape[1] // 16
    copies = []
    for slot in range(16):
        block = slot ^ place_ref[0]
        values = (mine_ref if slot < 8 else near_ref)[slot % 8].astype(F32)
        wide[slot] = values[: 4 * rows, :]
        little[block] = values[4 * rows : 4 * rows + 8, :]
        row = pl.multiple_of(block * rows, rows)
        pairs = [
            (wide.at[slot, pl.ds(section * rows, rows), :], qkv_ref.at[section, pl.ds(row, rows), :])
            for section in range(3)
        ]
        row = pl.multiple_of((block & 7) * rows, rows)
        column = pl.multiple_of((block >> 3) * inner, inner)
        pairs.append((wide.at[slot, pl.ds(3 * rows, rows), :], out_ref.at[pl.ds(row, rows), pl.ds(column, inner)]))
        for pair in pairs:
            copy = pltpu.make_async_copy(*pair, sems.at[len(copies)])
            copy.start()
            copies.append(copy)
    outs[0][...] = little[0, 0:2, :]
    row = 2
    for out in outs[1:]:
        for at in range(out.shape[0] // inner):
            out[pl.ds(at * inner, inner)] = little[row // 2, row % 2, :]
            row += 1
    for copy in copies:
        copy.wait()


def unpack_attend(line, place, mine, near, width, hidden):
    _, height, inner = mine.shape
    rows = width // 16
    small = [(2, inner), (hidden,)] + [(width,)] * 6
    return line.run(
        unpack_attend_kernel,
        [mine, near],
        [shaped((3, width, inner), F32), shaped((inner, width), F32)] + [shaped(shape, F32) for shape in small],
        out_specs=[ANYWHERE] * 2 + [VMEM] * 8,
        scratch=[
            pltpu.VMEM((16, 4 * rows, inner), F32),
            pltpu.VMEM((16, 8, inner), F32),
            pltpu.SemaphoreType.DMA((64,)),
        ],
        place=place,
        room=20,
        hint=1,
    )


def unpack_ffn_kernel(first, place_ref, *refs):
    down_in, up_in = refs[:2]
    down_ref, in_ref, down, up, sems = refs[-5:]
    rows, half = down_ref.shape[0] // 16, down_ref.shape[1] // 2
    deep, wide = in_ref.shape[0] // 4, in_ref.shape[1] // 4
    copies = []
    for slot in range(8):
        block = (slot if first else slot + 8) ^ place_ref[0]
        values = down_in[slot].astype(F32)
        down[slot, :, :half] = values[:rows, :]
        down[slot, :, half:] = values[rows:, :]
        up[slot] = up_in[slot].astype(F32)
        row = pl.multiple_of(block * rows, rows)
        copies.append((down.at[slot], down_ref.at[pl.ds(row, rows), :]))
        block = ((slot & 1) + (slot & 2) * 2 + (slot >> 2) * 2 + (0 if first else 8)) ^ place_ref[0]
        row = pl.multiple_of((block & 3) * deep, deep)
        column = pl.multiple_of((block >> 2) * wide, wide)
        copies.append((up.at[slot], in_ref.at[pl.ds(row, deep), pl.ds(column, wide)]))
    copies = [pltpu.make_async_copy(*pair, sems.at[at]) for at, pair in enumerate(copies)]
    for copy in copies:
        copy.start()
    for copy in copies:
        copy.wait()


def unpack_ffn(line, place, down, up, width, hidden, before=None):
    return line.run(
        functools.partial(unpack_ffn_kernel, before is None),
        [down, up, *(before or [])],
        [shaped((hidden, width), F32), shaped((width, hidden), F32)],
        in_specs=[VMEM] * 2 + [ANYWHERE] * (0 if before is None else 2),
        out_specs=[ANYWHERE] * 2,
        scratch=[
            pltpu.VMEM((8, hidden // 16, width), F32),
            pltpu.VMEM((8, width // 4, hidden // 4), F32),
            pltpu.SemaphoreType.DMA((16,)),
        ],
        aliases={} if before is None else {3: 0, 4: 1},
        place=place,
        moved=6 * width * hidden,
        room=20,
        hint=1,
    )


def attend_kernel(tok_ref, w_ref, bias_ref, k_ref, v_ref, out_ref):
    rows, inner = out_ref.shape
    low = lane_halves(rows)
    queries = scaled((mm(tok_ref[...], w_ref[0]) + bias_ref[0:1, :]).astype(BF16))
    for at in range(0, inner, LANES):
        cut = slice(at, at + LANES)
        block, keys, values = queries[:, cut], k_ref[:, cut], v_ref[:, cut]
        zero, one = jnp.zeros_like(block), jnp.ones_like(values)
        mixed = []
        for first in (True, False):
            head = jnp.where(low == first, block, zero)
            with_sums = jnp.where(lane_halves(values.shape[0]) == first, values, one)
            scores = dot_nt(head, keys)
            exponent = jnp.exp(scores - jnp.max(scores, axis=-1, keepdims=True)).astype(BF16)
            mixed.append(mm(exponent, with_sums))
        top = jnp.where(low, mixed[0], mixed[1])
        total = jnp.where(low, mixed[1], mixed[0])
        out_ref[:, cut] = (top / pltpu.roll(total, HEAD, 1)).astype(BF16)


def attend(line, tokens, weights, bias, keys, values, seqs, seq, hint=None):
    rows, width = tokens.shape
    inner = keys.shape[1]
    length = rows // seqs
    long = pl.BlockSpec((length, inner), lambda s: (seq, 0))
    (result,) = line.run(
        attend_kernel,
        [tokens, weights, bias, keys, values],
        [shaped((length, inner), BF16)],
        grid=(1,),
        in_specs=[
            pl.BlockSpec((length, width), lambda s: (seq, 0)),
            pl.BlockSpec((1, width, inner), lambda s: (0, 0, 0)),
            whole(bias.shape),
            long,
            long,
        ],
        out_specs=[pl.BlockSpec((length, inner), lambda s: (0, 0))],
        flops=2 * length * width * inner + 16 * length * length * inner,
        moved=2 * (length * width + width * inner + 3 * length * inner),
        transcendentals=length * length * inner // HEAD,
        room=16,
        hint=hint,
    )
    return result


def layer_kernel(
    tok_ref, ctx_a, ctx_b, wo_a, wo_b, wi_a, wi_b, bi_a, bi_b, wd_a, wd_b, one_ref, two_ref, out_ref,
):
    branch = mm(ctx_a[...], wo_a[...]) + mm(ctx_b[...], wo_b[...]) + one_ref[0:1, :]
    unit, _ = norm_rows(tok_ref[...].astype(F32) + branch)
    normed = unit * one_ref[1:2, :] + one_ref[2:3, :]
    low = normed.astype(BF16)
    total = normed + two_ref[0:1, :]
    for w_in, b_in, w_down in ((wi_a, bi_a, wd_a), (wi_b, bi_b, wd_b)):
        hidden = gelu(mm(low, w_in[...]) + b_in[...]).astype(BF16)
        total = total + mm(hidden, w_down[...])
    unit, _ = norm_rows(total)
    out_ref[...] = (unit * two_ref[1:2, :] + two_ref[2:3, :]).astype(BF16)


def layer_next_kernel(*refs):
    layer_kernel(*refs[:-2], refs[-1])


def layer(line, tokens, contexts, w_out, w_in, b_in, w_down, one, two, seq, mixed, hint):
    length, inner = contexts[0].shape
    width, hidden = tokens.shape[1], w_in[0].shape[1]
    tile = 256
    steps = length // tile
    ctx = pl.BlockSpec((tile, inner), lambda i: (i, 0))
    still = [*w_out, *w_in, *b_in, *w_down, one, two]
    row = pl.BlockSpec((tile, width), lambda i: (seq * steps + i, 0))
    args = [tokens, *contexts, *still]
    specs = [row, ctx, ctx] + [whole(item.shape, True) for item in still]
    (result,) = line.run(
        layer_kernel if mixed is None else layer_next_kernel,
        args if mixed is None else [*args, mixed],
        [shaped(tokens.shape, BF16)],
        grid=(steps,),
        in_specs=specs if mixed is None else [*specs, ANYWHERE],
        out_specs=[row],
        aliases={} if mixed is None else {len(args): 0},
        room=30,
        hint=hint,
        flops=2 * length * width * (width + 4 * hidden),
        moved=4 * width * (length + 2 * hidden),
        transcendentals=2 * length * hidden,
    )
    return result


def input_grad_kernel(
    dk_a, dk_b, dv_a, dv_b, dq_a, dq_b, w_a, w_b, g_first_ref, places_ref, out_ref
):
    length = out_ref.shape[0]
    slots = g_first_ref.shape[0]
    few = g_first_ref[...] + dot_nt(dq_a[...], w_a[0]) + dot_nt(dq_b[...], w_b[0])
    coarse = few.astype(BF16)
    fine = (few - coarse.astype(F32)).astype(BF16)
    picks = places_ref[0][:, 0:1] == lax.broadcasted_iota(jnp.int32, (slots, length), 1)
    picks = picks.astype(F32).astype(BF16)
    total = dot_tn(picks, coarse) + dot_tn(picks, fine)
    for dk, dv, w in ((dk_a, dv_a, w_a), (dk_b, dv_b, w_b)):
        total = total + dot_nt(dk[...], w[1]) + dot_nt(dv[...], w[2])
    out_ref[...] = total


def input_grad_next_kernel(*refs):
    input_grad_kernel(*refs[:-2], refs[-1])


def input_grad(line, backs, weights, g_first, places, seqs, seq, before):
    rows, inner = backs[0][1].shape
    width = g_first.shape[1]
    length, slots = rows // seqs, g_first.shape[0] // seqs
    long = pl.BlockSpec((length, inner), lambda i: (seq, 0))
    short = pl.BlockSpec((slots, inner), lambda i: (seq, 0))
    args = [
        backs[0][1], backs[1][1], backs[0][2], backs[1][2], backs[0][0], backs[1][0],
        *weights, g_first, places,
    ]
    specs = (
        [long] * 4
        + [short] * 2
        + [whole(w.shape, True) for w in weights]
        + [
            pl.BlockSpec((slots, width), lambda i: (seq, 0)),
            pl.BlockSpec((1, slots, LANES), lambda i: (seq, 0, 0)),
        ]
    )
    (result,) = line.run(
        input_grad_kernel if before is None else input_grad_next_kernel,
        args if before is None else [*args, before],
        [shaped((rows, width), F32)],
        grid=(1,),
        in_specs=specs if before is None else [*specs, ANYWHERE],
        out_specs=[pl.BlockSpec((length, width), lambda i: (seq, 0))],
        aliases={} if before is None else {len(args): 0},
        flops=10 * length * width * inner,
        moved=20 * width * inner + 8 * length * width,
        room=24,
        hint=0.2,
    )
    return result


def pick_kernel(places_ref, fresh_ref, tok_ref, grad_ref, few_ref, grad_few_ref, turned_ref):
    slots, length = few_ref.shape[0], tok_ref.shape[0]
    picks = places_ref[0][:, 0:1] == lax.broadcasted_iota(jnp.int32, (slots, length), 1)
    picks = picks.astype(F32).astype(BF16)
    few_ref[...] = mm(picks, tok_ref[...]).astype(BF16)
    grad_few_ref[...] = mm(picks, grad_ref[...]) * fresh_ref[0][:, 0:1]
    turned_ref[...] = tok_ref[...].T


def pick(line, places, fresh, tokens, grads, seqs):
    rows, width = tokens.shape
    length, slots = rows // seqs, places.shape[1]
    flat = pl.BlockSpec((1, slots, LANES), lambda s: (s, 0, 0))
    long = pl.BlockSpec((length, width), lambda s: (s, 0))
    short = pl.BlockSpec((slots, width), lambda s: (s, 0))
    return line.run(
        pick_kernel,
        [places, fresh, tokens, grads],
        [
            shaped((seqs * slots, width), BF16),
            shaped((seqs * slots, width), F32),
            shaped((width, rows), BF16),
        ],
        grid=(seqs,),
        in_specs=[flat, flat, long, long],
        out_specs=[short, short, pl.BlockSpec((width, length), lambda s: (0, s))],
        flops=4 * rows * slots * width,
        moved=6 * rows * width,
        room=56,
    )


def body(
    tokens,
    grad_values,
    span_starts,
    w_qkv,
    b_qv,
    w_out,
    b_out,
    ln1_gain,
    ln1_bias,
    w_in,
    b_in,
    w_down,
    b_down,
    ln2_gain,
    ln2_bias,
):
    rows, width = tokens.shape
    inner = w_qkv.shape[2]
    hidden_half = w_in.shape[1]
    halves = lax.axis_size("tensor")
    seqs = span_starts.shape[0] // halves
    spans = span_starts.shape[1]
    length = rows // seqs
    half_at = lax.axis_index("tensor")
    me = lax.axis_index("dp")
    bits = lax.axis_size("dp").bit_length() - 1
    block_at = ((me & 1) << 3) | ((me & 2) << 1) | ((me & 4) >> 1) | ((me & 8) >> 3)
    place = block_at.reshape(1).astype(jnp.int32)
    rest = [1 << bit for bit in range(4, bits)]

    starts = lax.dynamic_slice_in_dim(span_starts, half_at * seqs, seqs, 0)
    places = starts[:, :, None] + jnp.arange(SPAN, dtype=jnp.int32)
    earlier = jnp.tril(jnp.ones((spans, spans), jnp.bool_), -1)
    covered = (places[:, :, :, None] >= starts[:, None, None, :]) & (
        places[:, :, :, None] < starts[:, None, None, :] + SPAN
    )
    fresh = ~jnp.any(covered & earlier[None, :, None, :], axis=-1)
    slots = -(-spans * SPAN // 16) * 16
    pad = slots - spans * SPAN
    places = jnp.pad(places.reshape(seqs, spans * SPAN), ((0, 0), (0, pad)))
    fresh = jnp.pad(fresh.reshape(seqs, spans * SPAN), ((0, 0), (0, pad)))
    few = seqs * slots
    places = jnp.broadcast_to(places[:, :, None], (seqs, slots, LANES))
    fresh = jnp.broadcast_to(fresh[:, :, None].astype(F32), (seqs, slots, LANES))
    vectors_one = jnp.stack([b_out, ln1_gain, ln1_bias])
    vectors_two = jnp.stack([b_down, ln2_gain, ln2_bias])
    here = me.reshape(1)
    line = Line()

    w_qkv_own = jnp.transpose(w_qkv, (1, 0, 2))
    b_in = b_in.reshape(1, -1)

    def chips_around(held):
        return [held, flip(held, 2), flip(held, 4), flip(held, 6)]

    arrived_qkv = flip_tensor(cut_qkv(line, w_qkv_own, here))
    arrived_biases = [flip_tensor(b_qv), flip_tensor(b_in)]
    half_out, eighth = second_cut(line, w_out, w_in, w_down, here)
    held_qkv, b_qv_oth, b_in_oth = relay(line, [arrived_qkv, *arrived_biases])
    around_qkv = chips_around(held_qkv)
    arrived_out, arrived_eighth = flip_tensor(half_out), flip_tensor(eighth)
    b_qv_both, b_in_both = [b_qv, b_qv_oth], [b_in, b_in_oth]
    tokens_few, grad_few, tokens_t = pick(line, places, fresh, tokens, grad_values, seqs)
    own = project(line, tokens, tokens_few, w_qkv_own, b_qv, seqs)
    def attend_own(seq):
        return attend(line, tokens, w_qkv_own, b_qv, own[0], own[1], seqs, seq)

    core_first, held_eighth, half_in = third_cut(
        line, around_qkv, arrived_out, arrived_eighth, w_in, here
    )
    near_first = flip(core_first, 1)
    around_eighth = chips_around(held_eighth)
    arrived_in = flip_tensor(half_in)
    w_qkv_oth, w_out_oth = first_assemble(line, core_first, near_first, width, inner, here)
    w_qkv_both, w_out_both = [w_qkv_own, w_qkv_oth], [w_out, w_out_oth]
    oth = project(line, tokens, tokens_few, w_qkv_oth, b_qv_both[1], seqs)

    keys, values, queries_few, context_few = zip(own, oth)
    sum_few, normed_low = first_norm(line, context_few, w_out_both, tokens_few, vectors_one)

    def plane(values):
        return [values, flip_tensor(values), flip(values, 2), flip_both(values, 2)]

    slope_own, part = ffn_part(line, normed_low, w_in, b_in_both[0], w_down)
    ctx_own = [attend_own(seq) for seq in range(seqs)]
    core_second, held_in = fourth_cut(line, around_eighth, arrived_in)
    near_second, near_in = flip(core_second, 1), flip(held_in, 1)
    around_normed = plane(normed_low)
    w_in_oth, w_down_oth = second_assemble(
        line, core_second, near_second, held_in, near_in, hidden_half, here
    )
    w_in_both, w_down_both = [w_in, w_in_oth], [w_down, w_down_oth]
    g_ffn, g_second, slope_oth, sums = ffn_last(
        line, normed_low, part, sum_few, grad_few, vectors_one, vectors_two,
        w_in_both[1], b_in_both[1], w_down_both[1],
    )
    around_g = plane(g_ffn)
    g_branch, g_first, small_few = ffn_back(
        line, g_ffn, g_second, sum_few, vectors_one, sums, (slope_own, slope_oth), w_in_both, w_down_both
    )
    core_normed = join(line, around_normed)
    near_normed = flip(core_normed, 1)

    def back(at):
        return attend_back(
            line, place, queries_few[at], keys[at], values[at], g_branch, w_out_both[at],
            context_few[at], tokens_t, tokens_few, small_few, seqs, at, hidden_half // inner,
        )

    back_oth = back(1)
    near_oth = flip(back_oth[4], 1)
    core_g = join(line, around_g)
    near_g = flip(core_g, 1)
    back_own = back(0)
    near_own = flip(back_own[4], 1)
    keep_down, send_down, keep_in, send_in = ffn_grads(
        line, place, w_in, w_down, b_in_both[0], [core_normed, near_normed], [core_g, near_g]
    )
    z_down, z_in = flip(send_down, 4), flip(send_in, 8)
    x_send, y_send, x_keep, y_own, y_oth = cross_one(
        line, back_oth[3], near_oth, back_own[3], near_own, 112
    )
    x_near, y_near = flip_tensor(x_send), flip(y_send, 2)

    def attend_oth(seq, hint):
        return attend(
            line, tokens, w_qkv_oth, b_qv_both[1], keys[1], values[1], seqs, seq, hint
        )

    def over_rest(total):
        for bit in rest:
            total = total + flip(total, bit)
        return total

    def layer_of(seq, mixed, hint):
        return layer(
            line, tokens, [ctx_own[seq], ctx_oth[seq]], w_out_both, w_in_both, b_in_both, w_down_both,
            vectors_one, vectors_two, seq, mixed, hint,
        )

    def input_grad_of(seq, before):
        return input_grad(line, [back_own, back_oth], w_qkv_both, g_first, places, seqs, seq, before)

    ctx_oth = [attend_oth(seq, 0.1) for seq in range(seqs)]
    y_send, x_send, first, last = cross_two(line, x_keep, x_near, y_own, y_oth, y_near)
    y_near, x_near = flip(y_send, 2), flip_tensor(x_send)
    (keep_down, keep_in), sends = fold(line, [keep_down, keep_in], [z_down, z_in], True, 3)
    z_down, z_in = flip(sends[0], 8), flip(sends[1], 4)
    keep, send = cross_three(line, first, y_near, last, x_near)
    z_attn = flip(send, 4)
    keeps, arrived = [over_rest(keep_down), over_rest(keep_in)], [over_rest(z_down), over_rest(z_in)]
    down, up = fold(line, keeps, arrived, False, 8)
    near_down, near_up = flip(down, 8), flip(up, 8)
    d_tokens = None
    for seq in range(seqs):
        d_tokens = input_grad_of(seq, d_tokens)
    (keep,), (send,) = fold(line, [keep], [z_attn], True, 0.5)
    z_attn = flip(send, 8)
    down, up = append(line, 1, [down, near_down], [up, near_up])
    near_down, near_up = flip(down, 4), flip(up, 2)
    (attn,) = fold(line, [over_rest(keep)], [over_rest(z_attn)], False, 1.7)
    near_attn = flip(attn, 8)
    down, up = append(line, 1, [down, near_down], [up, near_up])
    near_down, near_up = flip(down, 2), flip(up, 4)
    (attn,) = append(line, 2, [attn, near_attn])
    around_attn = [attn, flip(attn, 4), flip(attn, 2), flip(attn, 6)]
    mixed = layer_of(0, None, 16)
    down, up = append(line, 1, [down, near_down], [up, near_up])
    near_down, near_up = flip(down, 1), flip(up, 1)
    ffn_sums = unpack_ffn(line, place, down, up, width, hidden_half)
    for seq in range(1, seqs):
        mixed = layer_of(seq, mixed, 0.1)
    (attn,) = append(line, 1, around_attn)
    near_attn = flip(attn, 1)
    d_w_down, d_w_in = unpack_ffn(line, place, near_down, near_up, width, hidden_half, ffn_sums)
    d_w_qkv, d_w_out, *small = unpack_attend(line, place, attn, near_attn, width, hidden_half)
    d_w_qkv = jnp.transpose(d_w_qkv, (1, 0, 2))
    d_b_qv, d_b_in, d_b_out, d_ln1_gain, d_ln1_bias, d_b_down, d_ln2_gain, d_ln2_bias = small

    return (
        mixed,
        d_tokens,
        d_w_qkv,
        d_b_qv,
        d_w_out,
        d_b_out,
        d_ln1_gain,
        d_ln1_bias,
        d_w_in,
        d_b_in,
        d_w_down,
        d_b_down,
        d_ln2_gain,
        d_ln2_bias,
    )


def solution(mesh):
    placed = (
        P(("dp", "tensor"), None),
        P(("dp", "tensor"), None),
        P("dp", None),
        P(None, None, "tensor"),
        P(None, "tensor"),
        P("tensor", None),
        P(),
        P(),
        P(),
        P(None, "tensor"),
        P("tensor"),
        P("tensor", None),
        P(),
        P(),
        P(),
    )
    return jax.shard_map(
        body,
        mesh=mesh,
        in_specs=placed,
        out_specs=(
            P(("dp", "tensor"), None),
            P(("dp", "tensor"), None),
            P(None, None, "tensor"),
            P(None, "tensor"),
            P("tensor", None),
            P(),
            P(),
            P(),
            P(None, "tensor"),
            P("tensor"),
            P("tensor", None),
            P(),
            P(),
            P(),
        ),
        check_vma=False,
    )
```

```python
import functools

import jax
import jax.numpy as jnp
from jax import lax
from jax.experimental import pallas as pl
from jax.experimental.pallas import tpu as pltpu
from jax.sharding import PartitionSpec as P

HEAD = 64
SPAN = 6
LANES = 128
EPSILON = 1e-05
F32 = jnp.float32
BF16 = jnp.bfloat16
GELU_A = (2.0 / 3.141592653589793) ** 0.5
GELU_B = 0.044715
ROOM_CUT, ROOM_PICK = 56, 24
HINT_GRADS, HINT_BACK = 15, 10
BYTES_US = 11_070_000
FLOPS_US = 3_459_000_000
ANYWHERE = pl.BlockSpec(memory_space=pl.ANY)
VMEM = pl.BlockSpec(memory_space=pltpu.VMEM)


class Line:
    def __init__(self):
        self.last = []

    def run(
        self, kernel, args, out_shape, grid=(), in_specs=None, out_specs=None, scratch=(), place=None,
        flops=0, moved=0, transcendentals=0, room=6, aliases=None, hint=None, after=(),
    ):
        ins, outs = len(args), len(out_shape)
        lead = 0 if place is None else 1
        after = list(after)
        if self.last and not any(arg is item for arg in args for item in self.last):
            after.append(min(self.last, key=lambda item: item.size))
        extra = len(after)
        small = min(item.size for item in out_shape) > 1 << 16

        def ordered(*refs):
            given, rest = refs[: lead + ins], refs[lead + ins + extra :]
            if small:
                rest[outs][...] = jnp.zeros((8, LANES), F32)
                rest = rest[:outs] + rest[outs + 1 :]
            kernel(*given, *rest)

        in_specs = list(in_specs or [VMEM] * ins) + [ANYWHERE] * extra
        out_specs = list(out_specs or [VMEM] * outs)
        out_shape = list(out_shape)
        if small:
            out_specs.append(pl.BlockSpec((8, LANES), lambda *at: (0, 0)) if grid else VMEM)
            out_shape.append(jax.ShapeDtypeStruct((8, LANES), F32))
        params = dict(
            out_shape=out_shape,
            compiler_params=pltpu.CompilerParams(vmem_limit_bytes=room << 20),
            cost_estimate=pl.CostEstimate(
                flops=int(flops if hint is None else hint * FLOPS_US),
                bytes_accessed=int(moved if hint is None else hint * BYTES_US),
                transcendentals=int(transcendentals if hint is None else 0),
            ),
            input_output_aliases=aliases or {},
        )
        if lead and grid:
            params["grid_spec"] = pltpu.PrefetchScalarGridSpec(
                num_scalar_prefetch=1, grid=grid, in_specs=in_specs, out_specs=out_specs, scratch_shapes=list(scratch)
            )
        else:
            if lead:
                in_specs = [pl.BlockSpec(memory_space=pltpu.SMEM)] + in_specs
            params.update(grid=grid, in_specs=in_specs, out_specs=out_specs, scratch_shapes=list(scratch))
        front = [] if place is None else [place]
        self.last = list(pl.pallas_call(ordered, **params)(*front, *args, *after))
        return self.last[:outs]


def shaped(shape, kind):
    return jax.ShapeDtypeStruct(tuple(shape), kind)


def whole(shape, once=False):
    held = dict(pipeline_mode=pl.Buffered(1)) if once else {}
    return pl.BlockSpec(shape, lambda *at: (0,) * len(shape), **held)


def flip(values, bits):
    size = lax.axis_size("dp")
    return lax.ppermute(values, "dp", [(at, at ^ bits) for at in range(size)])


def flip_tensor(values):
    return lax.ppermute(values, "tensor", [(0, 1), (1, 0)])


def flip_both(values, bits):
    size = 2 * lax.axis_size("dp")
    pairs = [(at, at ^ (2 * bits + 1)) for at in range(size)]
    return lax.ppermute(values, ("dp", "tensor"), pairs)


def dot_nt(left, right):
    return lax.dot_general(left, right, (((1,), (1,)), ((), ())), preferred_element_type=F32)


def dot_tn(left, right):
    return lax.dot_general(left, right, (((0,), (0,)), ((), ())), preferred_element_type=F32)


def mm(left, right):
    return jnp.dot(left, right, preferred_element_type=F32)


def lane_halves(rows):
    return lax.broadcasted_iota(jnp.int32, (rows, LANES), 1) < HEAD


def two_heads(block):
    low = lane_halves(block.shape[0])
    zero = jnp.zeros_like(block)
    return jnp.concatenate([jnp.where(low, block, zero), jnp.where(low, zero, block)], axis=0)


def scaled(queries):
    return queries * jnp.asarray(HEAD ** (-0.5), BF16)


def softmax_rows(scores):
    exponent = jnp.exp(scores - jnp.max(scores, axis=-1, keepdims=True))
    return exponent * (1.0 / jnp.sum(exponent, axis=-1, keepdims=True))


def attend_block(queries, keys, values):
    rows = queries.shape[0]
    probs = softmax_rows(dot_nt(two_heads(scaled(queries)), keys)).astype(BF16)
    mixed = mm(probs, values)
    return jnp.where(lane_halves(rows), mixed[:rows], mixed[rows:]).astype(BF16)


def norm_rows(values):
    average = jnp.mean(values, axis=-1, keepdims=True)
    centered = values - average
    variance = jnp.mean(centered * centered, axis=-1, keepdims=True)
    root = lax.rsqrt(variance + EPSILON)
    return centered * root, root


def norm_back(grad, unit, root, gain):
    grad_y = grad * gain
    inner = jnp.mean(grad_y, axis=-1, keepdims=True)
    along = jnp.mean(grad_y * unit, axis=-1, keepdims=True)
    return root * (grad_y - inner - unit * along)


def gelu_and_slope(values):
    square = values * values
    bent = jnp.tanh(GELU_A * values * (1.0 + GELU_B * square))
    half = 0.5 * (1.0 + bent)
    slope = half + 0.5 * values * (1.0 - bent * bent) * GELU_A * (1.0 + 3.0 * GELU_B * square)
    return values * half, slope


def gelu(values):
    return 0.5 * values * (1.0 + jnp.tanh(GELU_A * values * (1.0 + GELU_B * values * values)))


def join_kernel(count, *refs):
    rows = refs[0].shape[-2]
    for at in range(count):
        refs[count][..., at * rows : (at + 1) * rows, :] = refs[at][...]


def join(line, pieces):
    *lead, rows, columns = pieces[0].shape
    (result,) = line.run(
        functools.partial(join_kernel, len(pieces)),
        pieces,
        [shaped((*lead, rows * len(pieces), columns), pieces[0].dtype)],
        moved=4 * len(pieces) * pieces[0].size,
    )
    return result


def cut_qkv_kernel(place_ref, in_ref, bias_a, bias_b, out_ref, own_ref, sem):
    _, rows, inner = in_ref.shape
    rows = rows // 8
    row = pl.multiple_of((place_ref[0] & 7) * rows, rows)
    copy = pltpu.make_async_copy(
        in_ref.at[:, pl.ds(row, rows), :], out_ref.at[:, pl.ds(0, rows), :], sem
    )
    copy.start()
    own_ref[0, :] = bias_b[...]
    left = [bias_a[...]] + [own_ref[:, at : at + inner] for at in range(0, bias_b.shape[0], inner)]
    count = sum(item.shape[0] for item in left)
    left = jnp.concatenate(left + [jnp.zeros((out_ref.shape[1] - rows - count, inner), F32)], axis=0)
    for part in range(3):
        coarse = left.astype(BF16)
        out_ref[part, rows:, :] = coarse
        left = left - coarse.astype(F32)
    copy.wait()


def cut_qkv(line, w_qkv, b_qv, b_in, here):
    lead, rows, columns = w_qkv.shape
    return line.run(
        cut_qkv_kernel,
        [w_qkv, b_qv, b_in],
        [shaped((lead, rows // 8 + 16, columns), BF16), shaped((1, b_in.shape[0]), F32)],
        in_specs=[ANYWHERE, VMEM, VMEM],
        scratch=[pltpu.SemaphoreType.DMA],
        place=here,
        moved=w_qkv.size // 2,
        room=ROOM_CUT,
    )


def folded(rows, columns, width):
    tall = rows * columns // width
    rest, side = rows - tall, width - columns
    parts = [((0, tall, 0, columns), (0, tall, 0, columns))]
    for at in range(columns // side):
        parts.append(((at * rest, rest, columns, side), (tall, rest, at * side, side)))
    return tall, parts


def second_cut_kernel(place_ref, out_ref, in_ref, down_ref, *refs):
    vectors, (half, eighth, one, two) = refs[:6], refs[6:]
    half[...] = out_ref[...]
    tall, parts = folded(*in_ref.shape, eighth.shape[1])
    for (row, deep, column, wide), (top, _, left, _) in parts:
        eighth[row : row + deep, column : column + wide] = in_ref[top : top + deep, left : left + wide]
    eighth[tall:, :] = down_ref[...]
    for at in range(3):
        one[at, :] = vectors[at][...]
        two[at, :] = vectors[3 + at][...]


def second_cut(line, w_out, w_in, w_down, vectors, here):
    width = w_out.shape[1]
    half, rows, deep = w_out.shape[0] // 2, w_in.shape[0] // 8, w_down.shape[0] // 8
    last = w_in.shape[1] // 3
    eighth = folded(rows, last, width)[0]
    three = shaped((3, width), F32)
    return line.run(
        second_cut_kernel,
        [w_out, w_in, w_down, *vectors],
        [shaped((half, width), BF16), shaped((eighth + deep, width), BF16), three, three],
        grid=(1,),
        in_specs=[
            pl.BlockSpec((half, width), lambda i, p: (p[0] & 1, 0)),
            pl.BlockSpec((rows, last), lambda i, p: (p[0] & 7, 2)),
            pl.BlockSpec((deep, width), lambda i, p: (p[0] & 7, 0)),
            *[whole((width,)) for vector in vectors],
        ],
        out_specs=[whole((half, width)), whole((eighth + deep, width)), whole((3, width)), whole((3, width))],
        place=here,
        moved=4 * (half + eighth + deep) * width,
        room=ROOM_CUT,
    )


def relay_kernel(in_ref, out_ref, bias_a, bias_b):
    rows, inner = out_ref.shape[1:]
    out_ref[...] = in_ref[:, :rows, :]
    total = in_ref[2, rows:, :].astype(F32) + in_ref[1, rows:, :].astype(F32) + in_ref[0, rows:, :].astype(F32)
    bias_a[...] = total[0:2, :]
    for at in range(bias_b.shape[1] // inner):
        bias_b[:, at * inner : (at + 1) * inner] = total[2 + at : 3 + at, :]


def relay(line, arrived, hidden):
    lead, rows, inner = arrived.shape
    return line.run(
        relay_kernel,
        [arrived],
        [shaped((lead, rows - 16, inner), BF16), shaped((2, inner), F32), shaped((1, hidden), F32)],
        moved=4 * arrived.size,
    )


def third_cut_kernel(place_ref, a, b, c, d, out_ref, eighth_ref, in_ref, core, eighth, half):
    third, rows, inner = a.shape
    for at, ref in enumerate((a, b, c, d)):
        for section in range(third):
            row = (section * 4 + at) * rows
            core[row : row + rows, :] = ref[section]
    row = 4 * third * rows
    deep = out_ref.shape[0]
    core[row : row + deep, :] = out_ref[:, :inner]
    core[row + deep :, :] = out_ref[:, inner:]
    eighth[...] = eighth_ref[...]
    half[...] = in_ref[...]


def third_cut(line, qkv, out, eighth, w_in, here):
    third, rows, inner = qkv[0].shape
    width = out.shape[1]
    height = 4 * third * rows + 2 * out.shape[0]
    half = (w_in.shape[0] // 2, w_in.shape[1] // 3 * 2)
    return line.run(
        third_cut_kernel,
        [*qkv, out, eighth, w_in],
        [shaped((height, inner), BF16), shaped(eighth.shape, BF16), shaped(half, BF16)],
        grid=(1,),
        in_specs=[whole(item.shape) for item in [*qkv, out, eighth]]
        + [pl.BlockSpec(half, lambda i, p: (p[0] & 1, 0))],
        out_specs=[whole((height, inner)), whole(eighth.shape), whole(half)],
        place=here,
        moved=4 * (height * inner + eighth.size + half[0] * half[1]),
    )


def first_assemble_kernel(place_ref, mine, near, qkv_ref, out_ref):
    third, width, inner = qkv_ref.shape
    rows, half = width // 8, out_ref.shape[0] // 2
    for core, ref in enumerate((mine, near)):
        for at in range(4):
            row = pl.multiple_of(((place_ref[0] ^ (2 * at + core)) & 7) * rows, rows)
            for section in range(third):
                start = (section * 4 + at) * rows
                qkv_ref[section, pl.ds(row, rows), :] = ref[start : start + rows, :]
        row = pl.multiple_of(((place_ref[0] ^ core) & 1) * half, half)
        start = 4 * third * rows
        out_ref[pl.ds(row, half), :inner] = ref[start : start + half, :]
        out_ref[pl.ds(row, half), inner:] = ref[start + half :, :]


def first_assemble(line, mine, near, width, inner, here):
    return line.run(
        first_assemble_kernel,
        [mine, near],
        [shaped((3, width, inner), BF16), shaped((inner, width), BF16)],
        place=here,
        moved=8 * mine.size,
    )


def fourth_cut_kernel(a, b, c, d, half_ref, eighths, half):
    rows = a.shape[0]
    for at, ref in enumerate((a, b, c, d)):
        eighths[at * rows : (at + 1) * rows, :] = ref[...]
    half[...] = half_ref[...]


def fourth_cut(line, eighths, half):
    rows, width = eighths[0].shape
    return line.run(
        fourth_cut_kernel,
        [*eighths, half],
        [shaped((4 * rows, width), BF16), shaped(half.shape, BF16)],
        moved=16 * rows * width,
    )


def second_assemble_kernel(place_ref, mine, near, half_mine, half_near, in_ref, down_ref):
    width = mine.shape[1]
    wide, last = half_mine.shape[1], in_ref.shape[1] - half_mine.shape[1]
    rows, deep, half = in_ref.shape[0] // 8, down_ref.shape[0] // 8, half_mine.shape[0]
    tall, parts = folded(rows, last, width)
    for core, (ref, half_ref) in enumerate(((mine, half_mine), (near, half_near))):
        for at in range(4):
            block = (place_ref[0] ^ (2 * at + core)) & 7
            start = at * (tall + deep)
            for (row, high, column, side), (top, _, left, _) in parts:
                to = pl.multiple_of(block * rows + top, 32)
                in_ref[pl.ds(to, high), wide + left : wide + left + side] = ref[
                    start + row : start + row + high, column : column + side
                ]
            down_ref[pl.ds(pl.multiple_of(block * deep, deep), deep), :] = ref[
                start + tall : start + tall + deep, :
            ]
        row = pl.multiple_of(((place_ref[0] ^ core) & 1) * half, half)
        in_ref[pl.ds(row, half), :wide] = half_ref[...]


def second_assemble(line, mine, near, half_mine, half_near, hidden, here):
    width = mine.shape[1]
    return line.run(
        second_assemble_kernel,
        [mine, near, half_mine, half_near],
        [shaped((width, hidden), BF16), shaped((hidden, width), BF16)],
        place=here,
        moved=8 * width * hidden,
    )


def project_kernel(tok_ref, few_ref, w_ref, bias_ref, k_ref, v_ref, q_ref, ctx_ref):
    tok = tok_ref[...]
    k_ref[...] = mm(tok, w_ref[1]).astype(BF16)
    v_ref[...] = (mm(tok, w_ref[2]) + bias_ref[1:2, :]).astype(BF16)
    q_ref[...] = (mm(few_ref[...], w_ref[0]) + bias_ref[0:1, :]).astype(BF16)
    for at in range(0, k_ref.shape[1], LANES):
        cut = slice(at, at + LANES)
        ctx_ref[:, cut] = attend_block(q_ref[:, cut], k_ref[:, cut], v_ref[:, cut])


def project(line, tokens, few, weights, bias, seqs):
    rows, width = tokens.shape
    inner = weights.shape[2]
    length, slots = rows // seqs, few.shape[0] // seqs
    long, short = (pl.BlockSpec((size, inner), lambda s: (s, 0)) for size in (length, slots))
    return line.run(
        project_kernel,
        [tokens, few, weights, bias],
        [shaped((rows, inner), BF16)] * 2 + [shaped((few.shape[0], inner), BF16)] * 2,
        grid=(seqs,),
        in_specs=[
            pl.BlockSpec((length, width), lambda s: (s, 0)),
            pl.BlockSpec((slots, width), lambda s: (s, 0)),
            whole(weights.shape),
            whole(bias.shape),
        ],
        out_specs=[long, long, short, short],
        flops=6 * rows * width * inner,
        room=16,
        moved=2 * (rows * width + 3 * width * inner + 2 * rows * inner),
    )


def first_norm_kernel(ctx_a, ctx_b, w_a, w_b, few_ref, vec_ref, sum_ref, low_ref):
    branch = mm(ctx_a[...], w_a[...]) + mm(ctx_b[...], w_b[...]) + vec_ref[0:1, :]
    total = few_ref[...].astype(F32) + branch
    sum_ref[...] = total
    low_ref[...] = (norm_rows(total)[0] * vec_ref[1:2, :] + vec_ref[2:3, :]).astype(BF16)


def first_norm(line, contexts, w_out, few, vectors):
    count, width = few.shape
    return line.run(
        first_norm_kernel,
        [*contexts, *w_out, few, vectors],
        [shaped((count, width), F32), shaped((count, width), BF16)],
        flops=2 * count * width * width,
        moved=2 * width * width + 14 * count * width,
    )


def ffn_part_kernel(low_ref, wi_ref, bi_ref, wd_ref, slope_ref, part_ref, total):
    step = pl.program_id(0)
    gate, slope = gelu_and_slope(mm(low_ref[...], wi_ref[...]) + bi_ref[...])
    slope_ref[...] = slope
    part = mm(gate.astype(BF16), wd_ref[...])

    @pl.when(step == 0)
    def _():
        total[...] = part

    @pl.when(step > 0)
    def _():
        total[...] += part

    @pl.when(step == pl.num_programs(0) - 1)
    def _():
        part_ref[...] = total[...]


def ffn_part(line, low, w_in, b_in, w_down):
    count, width = low.shape
    hidden = w_in.shape[1]
    steps = 4
    tile = hidden // steps
    flat = whole((count, width))
    return line.run(
        ffn_part_kernel,
        [low, w_in, b_in, w_down],
        [shaped((count, hidden), F32), shaped((count, width), F32)],
        grid=(steps,),
        in_specs=[
            flat,
            pl.BlockSpec((width, tile), lambda j: (0, j)),
            pl.BlockSpec((1, tile), lambda j: (0, j)),
            pl.BlockSpec((tile, width), lambda j: (j, 0)),
        ],
        out_specs=[pl.BlockSpec((count, tile), lambda j: (0, j)), flat],
        scratch=[pltpu.VMEM((count, width), F32)],
        flops=4 * count * width * hidden,
        moved=4 * width * hidden,
        transcendentals=count * hidden,
        room=12,
    )


def column_sum(values):
    return jnp.sum(values, axis=0, keepdims=True)


def ffn_last_kernel(
    low_ref, part_ref, sum_ref, grad_ref, one_ref, two_ref, wi_ref, bi_ref, wd_ref,
    g_ffn_ref, g_second_ref, slope_ref, sums_ref,
):
    gate, slope = gelu_and_slope(mm(low_ref[...], wi_ref[...]) + bi_ref[...])
    slope_ref[...] = slope
    ffn = part_ref[...] + mm(gate.astype(BF16), wd_ref[...]) + two_ref[0:1, :]
    normed = norm_rows(sum_ref[...])[0] * one_ref[1:2, :] + one_ref[2:3, :]
    unit, root = norm_rows(normed + ffn)
    grad = grad_ref[...]
    g_second = norm_back(grad, unit, root, two_ref[1:2, :])
    g_ffn = g_second.astype(BF16)
    g_ffn_ref[...] = g_ffn
    g_second_ref[...] = g_second
    sums = (column_sum(g_ffn.astype(F32)), column_sum(grad * unit), column_sum(grad))
    sums_ref[...] = jnp.concatenate([*sums, jnp.zeros((5, grad.shape[1]), F32)], axis=0)


def ffn_last(line, low, part, total, grad, one, two, w_in, b_in, w_down):
    count, width = low.shape
    hidden = w_in.shape[1]
    return line.run(
        ffn_last_kernel,
        [low, part, total, grad, one, two, w_in, b_in, w_down],
        [
            shaped((count, width), BF16),
            shaped((count, width), F32),
            shaped((count, hidden), F32),
            shaped((8, width), F32),
        ],
        flops=4 * count * width * hidden,
        moved=4 * width * hidden,
        room=12,
    )


def ffn_back_kernel(
    g_ffn_ref, g_second_ref, sum_ref, one_ref, sums_ref, slope_a, slope_b, wi_a, wi_b, wd_a, wd_b,
    g_branch_ref, g_first_ref, small_ref,
):
    g_ffn, g_normed = g_ffn_ref[...], g_second_ref[...]
    width = g_normed.shape[1]
    half = width // 2
    deep = slope_a.shape[1] // half
    for at, (slope, w_in, w_down) in enumerate(((slope_a, wi_a, wd_a), (slope_b, wi_b, wd_b))):
        g_pre = (slope[...] * dot_nt(g_ffn, w_down[...])).astype(BF16)
        bias = column_sum(g_pre.astype(F32))
        for row in range(deep):
            small_ref[at * deep + row : at * deep + row + 1, :] = bias[:, row * half : (row + 1) * half]
        g_normed = g_normed + dot_nt(g_pre, w_in[...])
    unit, root = norm_rows(sum_ref[...])
    g_first = norm_back(g_normed, unit, root, one_ref[1:2, :])
    g_branch = g_first.astype(BF16)
    g_first_ref[...] = g_first
    g_branch_ref[...] = g_branch
    vectors = (
        column_sum(g_branch.astype(F32)),
        column_sum(g_normed * unit),
        column_sum(g_normed),
        *[sums_ref[at : at + 1, :] for at in range(3)],
    )
    for at, vector in enumerate(vectors):
        row = 2 * deep + 2 * at
        small_ref[row : row + 1, :] = vector[:, :half]
        small_ref[row + 1 : row + 2, :] = vector[:, half:]
    count = 2 * deep + 12
    small_ref[count:, :] = jnp.zeros((small_ref.shape[0] - count, half), F32)


def ffn_back(line, g_ffn, g_second, total, one, sums, slopes, w_in, w_down):
    count, width = g_ffn.shape
    hidden = w_in[0].shape[1]
    rows = 2 * (hidden // (width // 2)) + 12
    return line.run(
        ffn_back_kernel,
        [g_ffn, g_second, total, one, sums, *slopes, *w_in, *w_down],
        [
            shaped((count, width), BF16),
            shaped((count, width), F32),
            shaped((-(-rows // 8) * 8, width // 2), F32),
        ],
        flops=8 * count * width * hidden,
        moved=8 * width * hidden,
        room=12,
    )


def ffn_grads_kernel(place_ref, wi_ref, wd_ref, bi_ref, *refs):
    normed_refs, grad_refs = refs[:2], refs[2:4]
    keep_down, send_down, keep_in, send_in = refs[4:8]
    down, up = refs[8:]
    width = normed_refs[0].shape[1]
    tile = wi_ref.shape[1] // 4
    hidden = pl.ds(pl.multiple_of((place_ref[0] >> 2) * tile, tile), tile)
    w_in, w_down, b_in = wi_ref[:, hidden], wd_ref[hidden, :], bi_ref[:, hidden]
    for at in range(2):
        normed, grad = normed_refs[at][...], grad_refs[at][...]
        gate, slope = gelu_and_slope(mm(normed, w_in) + b_in)
        pre = (slope * dot_nt(grad, w_down)).astype(BF16)
        down_part = dot_tn(gate.astype(BF16), grad)
        up_part = dot_tn(normed, pre)
        if at == 0:
            down[...] = down_part
            up[...] = up_part
        else:
            down[...] += down_part
            up[...] += up_part
    down_rows, up_rows = tile // 4, width // 4
    half = width // 2
    for slot in range(4):
        block = slot ^ (place_ref[0] & 3)
        low = down[pl.ds(pl.multiple_of(block * down_rows, down_rows), down_rows), :]
        block = (0, 2, 1, 3)[slot] ^ (place_ref[0] & 3)
        high = up[pl.ds(pl.multiple_of(block * up_rows, up_rows), up_rows), :]
        to_down, to_in = (keep_down, keep_in) if slot < 2 else (send_down, send_in)
        kind = to_down.dtype
        to_down[slot % 2, :down_rows, :] = low[:, :half].astype(kind)
        to_down[slot % 2, down_rows:, :] = low[:, half:].astype(kind)
        to_in[slot % 2, :, :] = high.astype(kind)


def ffn_grads(line, place, w_in, w_down, b_in, normed, grads):
    rows, width = normed[0].shape
    tile = w_in.shape[1] // 4
    shape = (2, 2 * (tile // 4), width // 2)
    wide = (2, width // 4, tile)
    return line.run(
        ffn_grads_kernel,
        [w_in, w_down, b_in, *normed, *grads],
        [shaped(shape, F32), shaped(shape, BF16), shaped(wide, F32), shaped(wide, BF16)],
        scratch=[pltpu.VMEM((tile, width), F32), pltpu.VMEM((width, tile), F32)],
        place=place,
        flops=16 * rows * width * tile,
        moved=12 * rows * width + 16 * width * tile,
        hint=HINT_GRADS,
        room=16,
    )


def attend_back_kernel(
    seqs, half, deep, place_ref, q_ref, k_ref, v_ref, g_branch_ref, w_out_ref, ctx_ref, tok_t_ref, few_ref,
    small_ref, dq_ref, dk_ref, dv_ref, keep_ref, send_ref, total, little,
):
    few, inner = q_ref.shape
    rows = k_ref.shape[0]
    slots, length = few // seqs, rows // seqs
    low = lane_halves(slots)
    scale = HEAD ** (-0.5)
    g_branch = g_branch_ref[...]
    g_context = dot_nt(g_branch, w_out_ref[...]).astype(BF16)
    for seq in range(seqs):
        short, long = slice(seq * slots, (seq + 1) * slots), slice(seq * length, (seq + 1) * length)
        for at in range(0, inner, LANES):
            cut = slice(at, at + LANES)
            both, grads = two_heads(scaled(q_ref[short, cut])), two_heads(g_context[short, cut])
            keys, values = k_ref[long, cut], v_ref[long, cut]
            probs = softmax_rows(dot_nt(both, keys))
            grad_probs = dot_nt(grads, values)
            dv_ref[long, cut] = dot_tn(probs.astype(BF16), grads).astype(BF16)
            row_total = jnp.sum(grad_probs * probs, axis=-1, keepdims=True)
            grad_scores = (probs * (grad_probs - row_total)).astype(BF16)
            dq = mm(grad_scores, keys) * scale
            dq_ref[short, cut] = jnp.where(low, dq[:slots], dq[slots:]).astype(BF16)
            dk_ref[long, cut] = dot_tn(grad_scores, both).astype(BF16)
    dq, dk, dv = dq_ref[...], dk_ref[...], dv_ref[...]
    total[0] = dot_tn(few_ref[...], dq)
    total[1] = mm(tok_t_ref[...], dk)
    total[2] = mm(tok_t_ref[...], dv)
    out_grad = dot_tn(ctx_ref[...], g_branch)
    total[3, :inner, :] = out_grad[:, :inner]
    total[3, inner:, :] = out_grad[:, inner:]
    little[...] = jnp.zeros_like(little)
    little[0, 0:1, :] = column_sum(dq.astype(F32))
    little[0, 1:2, :] = column_sum(dv.astype(F32))
    for at in range(deep + 12):
        source = half * deep + at if at < deep else deep + at
        little[1 + at // 2, at % 2 : at % 2 + 1, :] = small_ref[source : source + 1, :]
    block_rows = total.shape[1] // 16
    pad = keep_ref.shape[1] - 4 * block_rows
    for slot in range(16):
        block = slot ^ place_ref[0]
        row = pl.multiple_of(block * block_rows, block_rows)
        to, kind = (keep_ref, F32) if slot < 8 else (send_ref, BF16)
        for section in range(4):
            cut = slice(section * block_rows, (section + 1) * block_rows)
            to[slot % 8, cut, :] = total[section, pl.ds(row, block_rows), :].astype(kind)
        pair = jnp.concatenate([little[block], jnp.zeros((pad - 8, inner), F32)], axis=0)
        to[slot % 8, 4 * block_rows :, :] = pair.astype(kind)


def attend_back(line, place, queries, keys, values, g_branch, w_out, context, tokens_t, few, small, seqs, half, deep):
    rows, inner = keys.shape
    width = tokens_t.shape[0]
    count = queries.shape[0]
    held = (8, 4 * (width // 16) + 16, inner)
    return line.run(
        functools.partial(attend_back_kernel, seqs, half, deep),
        [queries, keys, values, g_branch, w_out, context, tokens_t, few, small],
        [
            shaped((count, inner), BF16),
            shaped((rows, inner), BF16),
            shaped((rows, inner), BF16),
            shaped(held, F32),
            shaped(held, BF16),
        ],
        scratch=[pltpu.VMEM((4, width, inner), F32), pltpu.VMEM((16, 8, inner), F32)],
        place=place,
        hint=HINT_BACK,
        room=16,
        flops=4 * rows * width * inner + 24 * count * rows * inner,
        moved=20 * rows * inner,
    )


def fold_kernel(count, halve, *refs):
    keeps, arrived, outs = refs[:count], refs[count : 2 * count], refs[2 * count :]
    for at in range(count):
        total = keeps[at][...] + arrived[at][...].astype(F32)
        if halve:
            middle = total.shape[0] // 2
            outs[2 * at][...] = total[:middle]
            outs[2 * at + 1][...] = total[middle:].astype(BF16)
        else:
            outs[at][...] = total.astype(BF16)


def fold(line, keeps, arrived, halve, hint):
    shapes = []
    for keep in keeps:
        half = (keep.shape[0] // 2, *keep.shape[1:])
        shapes += [shaped(half, F32), shaped(half, BF16)] if halve else [shaped(keep.shape, BF16)]
    results = line.run(
        functools.partial(fold_kernel, len(keeps), halve),
        [*keeps, *arrived],
        shapes,
        hint=hint,
    )
    return (results[0::2], results[1::2]) if halve else results


def append_kernel(count, *refs):
    groups, out = refs[:-count], refs[-count:]
    each = len(groups) // count
    for at in range(count):
        row = 0
        for ref in groups[at * each : (at + 1) * each]:
            out[at][row : row + ref.shape[0]] = ref[...]
            row += ref.shape[0]


def append(line, hint, *groups):
    shapes = [shaped((sum(item.shape[0] for item in group), *group[0].shape[1:]), BF16) for group in groups]
    return line.run(
        functools.partial(append_kernel, len(groups)),
        [item for group in groups for item in group],
        shapes,
        hint=hint,
    )


def cross_one_kernel(oth, oth_near, own, own_near, x_send, y_send, x_keep, y_keep_own, y_keep_oth):
    rows = x_send.shape[1]
    half = oth.shape[0] // 2
    x_send[...] = (oth[:, :rows, :] + oth_near[:, :rows, :].astype(F32)).astype(BF16)
    x_keep[...] = own[:, :rows, :] + own_near[:, :rows, :].astype(F32)
    for at, (keep, near, out) in enumerate(((own, own_near, y_keep_own), (oth, oth_near, y_keep_oth))):
        total = keep[:, rows:, :] + near[:, rows:, :].astype(F32)
        out[...] = total[:half]
        y_send[at] = total[half:].astype(BF16)


def cross_one(line, oth, oth_near, own, own_near, rows):
    count, height, inner = oth.shape
    half, last = count // 2, height - rows
    return line.run(
        cross_one_kernel,
        [oth, oth_near, own, own_near],
        [
            shaped((count, rows, inner), BF16),
            shaped((2, half, last, inner), BF16),
            shaped((count, rows, inner), F32),
            shaped((half, last, inner), F32),
            shaped((half, last, inner), F32),
        ],
        hint=2,
    )


def cross_two_kernel(x_keep, x_near, own, oth, y_near, y_send, x_send, first, last):
    half = own.shape[0]
    total = x_keep[...] + x_near[...].astype(F32)
    first[...] = total[:half]
    y_send[...] = total[half:].astype(BF16)
    last[...] = own[...] + y_near[0].astype(F32)
    x_send[...] = (oth[...] + y_near[1].astype(F32)).astype(BF16)


def cross_two(line, x_keep, x_near, own, oth, y_near):
    half = (own.shape[0], x_keep.shape[1], x_keep.shape[2])
    return line.run(
        cross_two_kernel,
        [x_keep, x_near, own, oth, y_near],
        [shaped(half, BF16), shaped(own.shape, BF16), shaped(half, F32), shaped(own.shape, F32)],
        hint=0.5,
    )


def cross_three_kernel(first, y_near, last, x_near, keep, send):
    rows, half = first.shape[1], first.shape[0] // 2
    for ref, near, cut in ((first, y_near, slice(0, rows)), (last, x_near, slice(rows, None))):
        total = ref[...] + near[...].astype(F32)
        keep[:, cut, :] = total[:half]
        send[:, cut, :] = total[half:].astype(BF16)


def cross_three(line, first, y_near, last, x_near):
    shape = (first.shape[0] // 2, first.shape[1] + last.shape[1], first.shape[2])
    return line.run(
        cross_three_kernel,
        [first, y_near, last, x_near],
        [shaped(shape, F32), shaped(shape, BF16)],
        hint=0.5,
    )


def unpack_attend_kernel(place_ref, mine_ref, near_ref, qkv_ref, out_ref, *refs):
    outs, (wide, little, sems) = refs[:-3], refs[-3:]
    inner = qkv_ref.shape[2]
    rows = qkv_ref.shape[1] // 16
    copies = []
    for slot in range(16):
        block = slot ^ place_ref[0]
        values = (mine_ref if slot < 8 else near_ref)[slot % 8].astype(F32)
        wide[slot] = values[: 4 * rows, :]
        little[block] = values[4 * rows : 4 * rows + 8, :]
        row = pl.multiple_of(block * rows, rows)
        pairs = [
            (wide.at[slot, pl.ds(section * rows, rows), :], qkv_ref.at[section, pl.ds(row, rows), :])
            for section in range(3)
        ]
        row = pl.multiple_of((block & 7) * rows, rows)
        column = pl.multiple_of((block >> 3) * inner, inner)
        pairs.append((wide.at[slot, pl.ds(3 * rows, rows), :], out_ref.at[pl.ds(row, rows), pl.ds(column, inner)]))
        for pair in pairs:
            copy = pltpu.make_async_copy(*pair, sems.at[len(copies)])
            copy.start()
            copies.append(copy)
    outs[0][...] = little[0, 0:2, :]
    row = 2
    for out in outs[1:]:
        for at in range(out.shape[0] // inner):
            out[pl.ds(at * inner, inner)] = little[row // 2, row % 2, :]
            row += 1
    for copy in copies:
        copy.wait()


def unpack_attend(line, place, mine, near, width, hidden):
    _, height, inner = mine.shape
    rows = width // 16
    small = [(2, inner), (hidden,)] + [(width,)] * 6
    return line.run(
        unpack_attend_kernel,
        [mine, near],
        [shaped((3, width, inner), F32), shaped((inner, width), F32)] + [shaped(shape, F32) for shape in small],
        out_specs=[ANYWHERE] * 2 + [VMEM] * 8,
        scratch=[
            pltpu.VMEM((16, 4 * rows, inner), F32),
            pltpu.VMEM((16, 8, inner), F32),
            pltpu.SemaphoreType.DMA((64,)),
        ],
        place=place,
        room=20,
        hint=1,
    )


def unpack_ffn_kernel(first, place_ref, *refs):
    down_in, up_in = refs[:2]
    down_ref, in_ref, down, up, sems = refs[-5:]
    rows, half = down_ref.shape[0] // 16, down_ref.shape[1] // 2
    deep, wide = in_ref.shape[0] // 4, in_ref.shape[1] // 4
    copies = []
    for slot in range(8):
        block = (slot if first else slot + 8) ^ place_ref[0]
        values = down_in[slot].astype(F32)
        down[slot, :, :half] = values[:rows, :]
        down[slot, :, half:] = values[rows:, :]
        up[slot] = up_in[slot].astype(F32)
        row = pl.multiple_of(block * rows, rows)
        copies.append((down.at[slot], down_ref.at[pl.ds(row, rows), :]))
        block = ((slot & 1) + (slot & 2) * 2 + (slot >> 2) * 2 + (0 if first else 8)) ^ place_ref[0]
        row = pl.multiple_of((block & 3) * deep, deep)
        column = pl.multiple_of((block >> 2) * wide, wide)
        copies.append((up.at[slot], in_ref.at[pl.ds(row, deep), pl.ds(column, wide)]))
    copies = [pltpu.make_async_copy(*pair, sems.at[at]) for at, pair in enumerate(copies)]
    for copy in copies:
        copy.start()
    for copy in copies:
        copy.wait()


def unpack_ffn(line, place, down, up, width, hidden, before=None):
    return line.run(
        functools.partial(unpack_ffn_kernel, before is None),
        [down, up, *(before or [])],
        [shaped((hidden, width), F32), shaped((width, hidden), F32)],
        in_specs=[VMEM] * 2 + [ANYWHERE] * (0 if before is None else 2),
        out_specs=[ANYWHERE] * 2,
        scratch=[
            pltpu.VMEM((8, hidden // 16, width), F32),
            pltpu.VMEM((8, width // 4, hidden // 4), F32),
            pltpu.SemaphoreType.DMA((16,)),
        ],
        aliases={} if before is None else {3: 0, 4: 1},
        place=place,
        moved=6 * width * hidden,
        room=20,
        hint=1,
    )


def attend_kernel(tok_ref, w_ref, bias_ref, k_ref, v_ref, out_ref):
    rows, inner = out_ref.shape
    low = lane_halves(rows)
    queries = scaled((mm(tok_ref[...], w_ref[0]) + bias_ref[0:1, :]).astype(BF16))
    for at in range(0, inner, LANES):
        cut = slice(at, at + LANES)
        block, keys, values = queries[:, cut], k_ref[:, cut], v_ref[:, cut]
        zero, one = jnp.zeros_like(block), jnp.ones_like(values)
        mixed = []
        for first in (True, False):
            head = jnp.where(low == first, block, zero)
            with_sums = jnp.where(lane_halves(values.shape[0]) == first, values, one)
            scores = dot_nt(head, keys)
            exponent = jnp.exp(scores - jnp.max(scores, axis=-1, keepdims=True)).astype(BF16)
            mixed.append(mm(exponent, with_sums))
        top = jnp.where(low, mixed[0], mixed[1])
        total = jnp.where(low, mixed[1], mixed[0])
        out_ref[:, cut] = (top / pltpu.roll(total, HEAD, 1)).astype(BF16)


def attend(line, tokens, weights, bias, keys, values, seqs, seq, hint=None):
    rows, width = tokens.shape
    inner = keys.shape[1]
    length = rows // seqs
    long = pl.BlockSpec((length, inner), lambda s: (seq, 0))
    (result,) = line.run(
        attend_kernel,
        [tokens, weights, bias, keys, values],
        [shaped((length, inner), BF16)],
        grid=(1,),
        in_specs=[
            pl.BlockSpec((length, width), lambda s: (seq, 0)),
            pl.BlockSpec((1, width, inner), lambda s: (0, 0, 0)),
            whole(bias.shape),
            long,
            long,
        ],
        out_specs=[pl.BlockSpec((length, inner), lambda s: (0, 0))],
        flops=2 * length * width * inner + 16 * length * length * inner,
        moved=2 * (length * width + width * inner + 3 * length * inner),
        transcendentals=length * length * inner // HEAD,
        room=16,
        hint=hint,
    )
    return result


def layer_kernel(
    tok_ref, ctx_a, ctx_b, wo_a, wo_b, wi_a, wi_b, bi_a, bi_b, wd_a, wd_b, one_ref, two_ref, out_ref,
):
    branch = mm(ctx_a[...], wo_a[...]) + mm(ctx_b[...], wo_b[...]) + one_ref[0:1, :]
    unit, _ = norm_rows(tok_ref[...].astype(F32) + branch)
    normed = unit * one_ref[1:2, :] + one_ref[2:3, :]
    low = normed.astype(BF16)
    total = normed + two_ref[0:1, :]
    for w_in, b_in, w_down in ((wi_a, bi_a, wd_a), (wi_b, bi_b, wd_b)):
        hidden = gelu(mm(low, w_in[...]) + b_in[...]).astype(BF16)
        total = total + mm(hidden, w_down[...])
    unit, _ = norm_rows(total)
    out_ref[...] = (unit * two_ref[1:2, :] + two_ref[2:3, :]).astype(BF16)


def layer_next_kernel(*refs):
    layer_kernel(*refs[:-2], refs[-1])


def layer(line, tokens, contexts, w_out, w_in, b_in, w_down, one, two, seq, mixed, hint):
    length, inner = contexts[0].shape
    width, hidden = tokens.shape[1], w_in[0].shape[1]
    tile = 256
    steps = length // tile
    ctx = pl.BlockSpec((tile, inner), lambda i: (i, 0))
    still = [*w_out, *w_in, *b_in, *w_down, one, two]
    row = pl.BlockSpec((tile, width), lambda i: (seq * steps + i, 0))
    args = [tokens, *contexts, *still]
    specs = [row, ctx, ctx] + [whole(item.shape, True) for item in still]
    (result,) = line.run(
        layer_kernel if mixed is None else layer_next_kernel,
        args if mixed is None else [*args, mixed],
        [shaped(tokens.shape, BF16)],
        grid=(steps,),
        in_specs=specs if mixed is None else [*specs, ANYWHERE],
        out_specs=[row],
        aliases={} if mixed is None else {len(args): 0},
        room=30,
        hint=hint,
        flops=2 * length * width * (width + 4 * hidden),
        moved=4 * width * (length + 2 * hidden),
        transcendentals=2 * length * hidden,
    )
    return result


def input_grad_kernel(
    dk_a, dk_b, dv_a, dv_b, dq_a, dq_b, w_a, w_b, g_first_ref, places_ref, out_ref
):
    length = out_ref.shape[0]
    slots = g_first_ref.shape[0]
    few = g_first_ref[...] + dot_nt(dq_a[...], w_a[0]) + dot_nt(dq_b[...], w_b[0])
    coarse = few.astype(BF16)
    fine = (few - coarse.astype(F32)).astype(BF16)
    picks = places_ref[0][:, 0:1] == lax.broadcasted_iota(jnp.int32, (slots, length), 1)
    picks = picks.astype(F32).astype(BF16)
    total = dot_tn(picks, coarse) + dot_tn(picks, fine)
    for dk, dv, w in ((dk_a, dv_a, w_a), (dk_b, dv_b, w_b)):
        total = total + dot_nt(dk[...], w[1]) + dot_nt(dv[...], w[2])
    out_ref[...] = total


def input_grad_next_kernel(*refs):
    input_grad_kernel(*refs[:-2], refs[-1])


def input_grad(line, backs, weights, g_first, places, seqs, seq, before):
    rows, inner = backs[0][1].shape
    width = g_first.shape[1]
    length, slots = rows // seqs, g_first.shape[0] // seqs
    long = pl.BlockSpec((length, inner), lambda i: (seq, 0))
    short = pl.BlockSpec((slots, inner), lambda i: (seq, 0))
    args = [
        backs[0][1], backs[1][1], backs[0][2], backs[1][2], backs[0][0], backs[1][0],
        *weights, g_first, places,
    ]
    specs = (
        [long] * 4
        + [short] * 2
        + [whole(w.shape, True) for w in weights]
        + [
            pl.BlockSpec((slots, width), lambda i: (seq, 0)),
            pl.BlockSpec((1, slots, LANES), lambda i: (seq, 0, 0)),
        ]
    )
    (result,) = line.run(
        input_grad_kernel if before is None else input_grad_next_kernel,
        args if before is None else [*args, before],
        [shaped((rows, width), F32)],
        grid=(1,),
        in_specs=specs if before is None else [*specs, ANYWHERE],
        out_specs=[pl.BlockSpec((length, width), lambda i: (seq, 0))],
        aliases={} if before is None else {len(args): 0},
        flops=10 * length * width * inner,
        moved=20 * width * inner + 8 * length * width,
        room=24,
        hint=0.2,
    )
    return result


def pick_kernel(seqs, half_ref, starts_ref, tok_ref, grad_ref, few_ref, grad_few_ref, turned_ref, places_ref):
    slots, length = few_ref.shape[0], tok_ref.shape[0]
    spans = starts_ref.shape[1]
    seq = half_ref[0] * seqs + pl.program_id(0)
    starts = [starts_ref[seq, at] for at in range(spans)]
    row = lax.broadcasted_iota(jnp.int32, (slots, LANES), 0)
    places = row + starts[0]
    for at in range(1, spans):
        places = places + jnp.where(row >= SPAN * at, starts[at] - starts[at - 1] - SPAN, 0)
    fresh = row < SPAN * spans
    for at, start in enumerate(starts):
        covered = (places >= start) & (places < start + SPAN) & (row >= SPAN * (at + 1))
        fresh = fresh & jnp.logical_not(covered)
    places_ref[0] = places
    wide = jnp.concatenate([places] * (length // LANES), axis=1)
    picks = wide == lax.broadcasted_iota(jnp.int32, (slots, length), 1)
    picks = picks.astype(F32).astype(BF16)
    few_ref[...] = mm(picks, tok_ref[...]).astype(BF16)
    grad_few_ref[...] = mm(picks, grad_ref[...]) * fresh.astype(F32)[:, 0:1]
    turned_ref[...] = tok_ref[...].T


def pick(line, half, starts, slots, tokens, grads, seqs):
    rows, width = tokens.shape
    length = rows // seqs
    long = pl.BlockSpec((length, width), lambda s, p: (s, 0))
    short = pl.BlockSpec((slots, width), lambda s, p: (s, 0))
    return line.run(
        functools.partial(pick_kernel, seqs),
        [starts, tokens, grads],
        [
            shaped((seqs * slots, width), BF16),
            shaped((seqs * slots, width), F32),
            shaped((width, rows), BF16),
            shaped((seqs, slots, LANES), jnp.int32),
        ],
        grid=(seqs,),
        in_specs=[pl.BlockSpec(memory_space=pltpu.SMEM), long, long],
        out_specs=[
            short, short, pl.BlockSpec((width, length), lambda s, p: (0, s)),
            pl.BlockSpec((1, slots, LANES), lambda s, p: (s, 0, 0)),
        ],
        place=half,
        flops=4 * rows * slots * width,
        moved=6 * rows * width,
        room=ROOM_PICK,
    )


def body(
    tokens,
    grad_values,
    span_starts,
    w_qkv,
    b_qv,
    w_out,
    b_out,
    ln1_gain,
    ln1_bias,
    w_in,
    b_in,
    w_down,
    b_down,
    ln2_gain,
    ln2_bias,
):
    rows, width = tokens.shape
    inner = w_qkv.shape[2]
    hidden_half = w_in.shape[1]
    halves = lax.axis_size("tensor")
    seqs = span_starts.shape[0] // halves
    spans = span_starts.shape[1]
    length = rows // seqs
    half_at = lax.axis_index("tensor")
    me = lax.axis_index("dp")
    bits = lax.axis_size("dp").bit_length() - 1
    block_at = ((me & 1) << 3) | ((me & 2) << 1) | ((me & 4) >> 1) | ((me & 8) >> 3)
    place = block_at.reshape(1).astype(jnp.int32)
    rest = [1 << bit for bit in range(4, bits)]

    slots = -(-spans * SPAN // 16) * 16
    here = me.reshape(1)
    line = Line()

    w_qkv_own = jnp.transpose(w_qkv, (1, 0, 2))

    def chips_around(held):
        return [held, flip(held, 2), flip(held, 4), flip(held, 6)]

    piece_qkv, b_in = cut_qkv(line, w_qkv_own, b_qv, b_in, here)
    arrived_qkv = flip_tensor(piece_qkv)
    half_out, eighth, vectors_one, vectors_two = second_cut(
        line, w_out, w_in, w_down, [b_out, ln1_gain, ln1_bias, b_down, ln2_gain, ln2_bias], here
    )
    held_qkv, b_qv_oth, b_in_oth = relay(line, arrived_qkv, hidden_half)
    around_qkv = chips_around(held_qkv)
    arrived_out, arrived_eighth = flip_tensor(half_out), flip_tensor(eighth)
    b_qv_both, b_in_both = [b_qv, b_qv_oth], [b_in, b_in_oth]
    tokens_few, grad_few, tokens_t, places = pick(
        line, half_at.reshape(1), span_starts, slots, tokens, grad_values, seqs
    )
    own = project(line, tokens, tokens_few, w_qkv_own, b_qv, seqs)
    def attend_own(seq, hint=None):
        return attend(line, tokens, w_qkv_own, b_qv, own[0], own[1], seqs, seq, hint)

    core_first, held_eighth, half_in = third_cut(
        line, around_qkv, arrived_out, arrived_eighth, w_in, here
    )
    near_first = flip(core_first, 1)
    around_eighth = chips_around(held_eighth)
    arrived_in = flip_tensor(half_in)
    w_qkv_oth, w_out_oth = first_assemble(line, core_first, near_first, width, inner, here)
    w_qkv_both, w_out_both = [w_qkv_own, w_qkv_oth], [w_out, w_out_oth]
    oth = project(line, tokens, tokens_few, w_qkv_oth, b_qv_both[1], seqs)

    keys, values, queries_few, context_few = zip(own, oth)
    sum_few, normed_low = first_norm(line, context_few, w_out_both, tokens_few, vectors_one)

    def plane(values):
        return [values, flip_tensor(values), flip(values, 2), flip_both(values, 2)]

    slope_own, part = ffn_part(line, normed_low, w_in, b_in_both[0], w_down)
    ctx_own = [attend_own(0)]
    core_second, held_in = fourth_cut(line, around_eighth, arrived_in)
    near_second, near_in = flip(core_second, 1), flip(held_in, 1)
    around_normed = plane(normed_low)
    w_in_oth, w_down_oth = second_assemble(
        line, core_second, near_second, held_in, near_in, hidden_half, here
    )
    w_in_both, w_down_both = [w_in, w_in_oth], [w_down, w_down_oth]
    g_ffn, g_second, slope_oth, sums = ffn_last(
        line, normed_low, part, sum_few, grad_few, vectors_one, vectors_two,
        w_in_both[1], b_in_both[1], w_down_both[1],
    )
    around_g = plane(g_ffn)
    g_branch, g_first, small_few = ffn_back(
        line, g_ffn, g_second, sum_few, vectors_one, sums, (slope_own, slope_oth), w_in_both, w_down_both
    )
    core_normed = join(line, around_normed)
    near_normed = flip(core_normed, 1)

    def back(at):
        return attend_back(
            line, place, queries_few[at], keys[at], values[at], g_branch, w_out_both[at],
            context_few[at], tokens_t, tokens_few, small_few, seqs, at, hidden_half // inner,
        )

    back_oth = back(1)
    near_oth = flip(back_oth[4], 1)
    core_g = join(line, around_g)
    near_g = flip(core_g, 1)
    back_own = back(0)
    near_own = flip(back_own[4], 1)
    keep_down, send_down, keep_in, send_in = ffn_grads(
        line, place, w_in, w_down, b_in_both[0], [core_normed, near_normed], [core_g, near_g]
    )
    z_down, z_in = flip(send_down, 4), flip(send_in, 8)
    x_send, y_send, x_keep, y_own, y_oth = cross_one(
        line, back_oth[3], near_oth, back_own[3], near_own, 112
    )
    x_near, y_near = flip_tensor(x_send), flip(y_send, 2)

    def attend_oth(seq, hint):
        return attend(
            line, tokens, w_qkv_oth, b_qv_both[1], keys[1], values[1], seqs, seq, hint
        )

    def over_rest(total):
        for bit in rest:
            total = total + flip(total, bit)
        return total

    def layer_of(seq, mixed, hint):
        return layer(
            line, tokens, [ctx_own[seq], ctx_oth[seq]], w_out_both, w_in_both, b_in_both, w_down_both,
            vectors_one, vectors_two, seq, mixed, hint,
        )

    def input_grad_of(seq, before):
        return input_grad(line, [back_own, back_oth], w_qkv_both, g_first, places, seqs, seq, before)

    ctx_oth = [attend_oth(seq, 0.1) for seq in range(seqs)]
    ctx_own += [attend_own(seq, 0.1) for seq in range(1, seqs)]
    y_send, x_send, first, last = cross_two(line, x_keep, x_near, y_own, y_oth, y_near)
    y_near, x_near = flip(y_send, 2), flip_tensor(x_send)
    (keep_down, keep_in), sends = fold(line, [keep_down, keep_in], [z_down, z_in], True, 3)
    z_down, z_in = flip(sends[0], 8), flip(sends[1], 4)
    keep, send = cross_three(line, first, y_near, last, x_near)
    z_attn = flip(send, 4)
    keeps, arrived = [over_rest(keep_down), over_rest(keep_in)], [over_rest(z_down), over_rest(z_in)]
    down, up = fold(line, keeps, arrived, False, 8)
    near_down, near_up = flip(down, 8), flip(up, 8)
    d_tokens = None
    for seq in range(seqs):
        d_tokens = input_grad_of(seq, d_tokens)
    (keep,), (send,) = fold(line, [keep], [z_attn], True, 0.5)
    z_attn = flip(send, 8)
    down, up = append(line, 1, [down, near_down], [up, near_up])
    near_down, near_up = flip(down, 4), flip(up, 2)
    (attn,) = fold(line, [over_rest(keep)], [over_rest(z_attn)], False, 1.7)
    near_attn = flip(attn, 8)
    down, up = append(line, 1, [down, near_down], [up, near_up])
    near_down, near_up = flip(down, 2), flip(up, 4)
    (attn,) = append(line, 2, [attn, near_attn])
    around_attn = [attn, flip(attn, 4), flip(attn, 2), flip(attn, 6)]
    mixed = layer_of(0, None, 16)
    down, up = append(line, 1, [down, near_down], [up, near_up])
    near_down, near_up = flip(down, 1), flip(up, 1)
    ffn_sums = unpack_ffn(line, place, down, up, width, hidden_half)
    for seq in range(1, seqs):
        mixed = layer_of(seq, mixed, 0.1)
    (attn,) = append(line, 1, around_attn)
    near_attn = flip(attn, 1)
    d_w_down, d_w_in = unpack_ffn(line, place, near_down, near_up, width, hidden_half, ffn_sums)
    d_w_qkv, d_w_out, *small = unpack_attend(line, place, attn, near_attn, width, hidden_half)
    d_w_qkv = jnp.transpose(d_w_qkv, (1, 0, 2))
    d_b_qv, d_b_in, d_b_out, d_ln1_gain, d_ln1_bias, d_b_down, d_ln2_gain, d_ln2_bias = small

    return (
        mixed,
        d_tokens,
        d_w_qkv,
        d_b_qv,
        d_w_out,
        d_b_out,
        d_ln1_gain,
        d_ln1_bias,
        d_w_in,
        d_b_in,
        d_w_down,
        d_b_down,
        d_ln2_gain,
        d_ln2_bias,
    )


def solution(mesh):
    placed = (
        P(("dp", "tensor"), None),
        P(("dp", "tensor"), None),
        P("dp", None),
        P(None, None, "tensor"),
        P(None, "tensor"),
        P("tensor", None),
        P(),
        P(),
        P(),
        P(None, "tensor"),
        P("tensor"),
        P("tensor", None),
        P(),
        P(),
        P(),
    )
    return jax.shard_map(
        body,
        mesh=mesh,
        in_specs=placed,
        out_specs=(
            P(("dp", "tensor"), None),
            P(("dp", "tensor"), None),
            P(None, None, "tensor"),
            P(None, "tensor"),
            P("tensor", None),
            P(),
            P(),
            P(),
            P(None, "tensor"),
            P("tensor"),
            P("tensor", None),
            P(),
            P(),
            P(),
        ),
        check_vma=False,
    )
```

```python
import functools

import jax
import jax.numpy as jnp
from jax import lax
from jax.experimental import pallas as pl
from jax.experimental.pallas import tpu as pltpu
from jax.sharding import PartitionSpec as P

HEAD = 64
SPAN = 6
LANES = 128
EPSILON = 1e-05
F32 = jnp.float32
BF16 = jnp.bfloat16
GELU_A = (2.0 / 3.141592653589793) ** 0.5
GELU_B = 0.044715
ROOM_CUT, ROOM_PICK = 56, 24
HINT_GRADS, HINT_BACK = 15, 10
H = (0.2, 1, 0.5, 0.1, 0.3, 0.3, 1, 0.3, 0.3)
BYTES_US = 11_070_000
FLOPS_US = 3_459_000_000
ANYWHERE = pl.BlockSpec(memory_space=pl.ANY)
VMEM = pl.BlockSpec(memory_space=pltpu.VMEM)


class Line:
    def __init__(self):
        self.last = []

    def run(
        self, kernel, args, out_shape, grid=(), in_specs=None, out_specs=None, scratch=(), place=None,
        flops=0, moved=0, transcendentals=0, room=6, aliases=None, hint=None, after=(),
    ):
        ins, outs = len(args), len(out_shape)
        lead = 0 if place is None else 1
        after = list(after)
        if self.last and not any(arg is item for arg in args for item in self.last):
            after.append(min(self.last, key=lambda item: item.size))
        extra = len(after)
        small = min(item.size for item in out_shape) > 1 << 16

        def ordered(*refs):
            given, rest = refs[: lead + ins], refs[lead + ins + extra :]
            if small:
                rest[outs][...] = jnp.zeros((8, LANES), F32)
                rest = rest[:outs] + rest[outs + 1 :]
            kernel(*given, *rest)

        in_specs = list(in_specs or [VMEM] * ins) + [ANYWHERE] * extra
        out_specs = list(out_specs or [VMEM] * outs)
        out_shape = list(out_shape)
        if small:
            out_specs.append(pl.BlockSpec((8, LANES), lambda *at: (0, 0)) if grid else VMEM)
            out_shape.append(jax.ShapeDtypeStruct((8, LANES), F32))
        params = dict(
            out_shape=out_shape,
            compiler_params=pltpu.CompilerParams(vmem_limit_bytes=room << 20),
            cost_estimate=pl.CostEstimate(
                flops=int(flops if hint is None else hint * FLOPS_US),
                bytes_accessed=int(moved if hint is None else hint * BYTES_US),
                transcendentals=int(transcendentals if hint is None else 0),
            ),
            input_output_aliases=aliases or {},
        )
        if lead and grid:
            params["grid_spec"] = pltpu.PrefetchScalarGridSpec(
                num_scalar_prefetch=1, grid=grid, in_specs=in_specs, out_specs=out_specs, scratch_shapes=list(scratch)
            )
        else:
            if lead:
                in_specs = [pl.BlockSpec(memory_space=pltpu.SMEM)] + in_specs
            params.update(grid=grid, in_specs=in_specs, out_specs=out_specs, scratch_shapes=list(scratch))
        front = [] if place is None else [place]
        self.last = list(pl.pallas_call(ordered, **params)(*front, *args, *after))
        return self.last[:outs]


def shaped(shape, kind):
    return jax.ShapeDtypeStruct(tuple(shape), kind)


def whole(shape, once=False):
    held = dict(pipeline_mode=pl.Buffered(1)) if once else {}
    return pl.BlockSpec(shape, lambda *at: (0,) * len(shape), **held)


def flip(values, bits):
    size = lax.axis_size("dp")
    return lax.ppermute(values, "dp", [(at, at ^ bits) for at in range(size)])


def flip_tensor(values):
    return lax.ppermute(values, "tensor", [(0, 1), (1, 0)])


def flip_both(values, bits):
    size = 2 * lax.axis_size("dp")
    pairs = [(at, at ^ (2 * bits + 1)) for at in range(size)]
    return lax.ppermute(values, ("dp", "tensor"), pairs)


def dot_nt(left, right):
    return lax.dot_general(left, right, (((1,), (1,)), ((), ())), preferred_element_type=F32)


def dot_tn(left, right):
    return lax.dot_general(left, right, (((0,), (0,)), ((), ())), preferred_element_type=F32)


def mm(left, right):
    return jnp.dot(left, right, preferred_element_type=F32)


def lane_halves(rows):
    return lax.broadcasted_iota(jnp.int32, (rows, LANES), 1) < HEAD


def two_heads(block):
    low = lane_halves(block.shape[0])
    zero = jnp.zeros_like(block)
    return jnp.concatenate([jnp.where(low, block, zero), jnp.where(low, zero, block)], axis=0)


def scaled(queries):
    return queries * jnp.asarray(HEAD ** (-0.5), BF16)


def softmax_rows(scores):
    exponent = jnp.exp(scores - jnp.max(scores, axis=-1, keepdims=True))
    return exponent * (1.0 / jnp.sum(exponent, axis=-1, keepdims=True))


def attend_block(queries, keys, values):
    rows = queries.shape[0]
    probs = softmax_rows(dot_nt(two_heads(scaled(queries)), keys)).astype(BF16)
    mixed = mm(probs, values)
    return jnp.where(lane_halves(rows), mixed[:rows], mixed[rows:]).astype(BF16)


def norm_rows(values):
    average = jnp.mean(values, axis=-1, keepdims=True)
    centered = values - average
    variance = jnp.mean(centered * centered, axis=-1, keepdims=True)
    root = lax.rsqrt(variance + EPSILON)
    return centered * root, root


def norm_back(grad, unit, root, gain):
    grad_y = grad * gain
    inner = jnp.mean(grad_y, axis=-1, keepdims=True)
    along = jnp.mean(grad_y * unit, axis=-1, keepdims=True)
    return root * (grad_y - inner - unit * along)


def gelu_and_slope(values):
    square = values * values
    bent = jnp.tanh(GELU_A * values * (1.0 + GELU_B * square))
    half = 0.5 * (1.0 + bent)
    slope = half + 0.5 * values * (1.0 - bent * bent) * GELU_A * (1.0 + 3.0 * GELU_B * square)
    return values * half, slope


def gelu(values):
    return 0.5 * values * (1.0 + jnp.tanh(GELU_A * values * (1.0 + GELU_B * values * values)))


def join_kernel(count, *refs):
    rows = refs[0].shape[-2]
    for at in range(count):
        refs[count][..., at * rows : (at + 1) * rows, :] = refs[at][...]


def join(line, pieces):
    *lead, rows, columns = pieces[0].shape
    (result,) = line.run(
        functools.partial(join_kernel, len(pieces)),
        pieces,
        [shaped((*lead, rows * len(pieces), columns), pieces[0].dtype)],
        moved=4 * len(pieces) * pieces[0].size,
    )
    return result


def cut_qkv_kernel(place_ref, in_ref, out_ref, sem):
    rows = out_ref.shape[1]
    row = pl.multiple_of((place_ref[0] & 7) * rows, rows)
    copy = pltpu.make_async_copy(in_ref.at[:, pl.ds(row, rows), :], out_ref, sem)
    copy.start()
    copy.wait()


def cut_qkv(line, w_qkv, here):
    lead, rows, columns = w_qkv.shape
    (piece,) = line.run(
        cut_qkv_kernel,
        [w_qkv],
        [shaped((lead, rows // 8, columns), BF16)],
        in_specs=[ANYWHERE],
        scratch=[pltpu.SemaphoreType.DMA],
        place=here,
        moved=w_qkv.size // 2,
        room=ROOM_CUT,
    )
    return piece


def folded(rows, columns, width):
    tall = rows * columns // width
    rest, side = rows - tall, width - columns
    parts = [((0, tall, 0, columns), (0, tall, 0, columns))]
    for at in range(columns // side):
        parts.append(((at * rest, rest, columns, side), (tall, rest, at * side, side)))
    return tall, parts


def second_cut_kernel(place_ref, out_ref, in_ref, down_ref, bias_a, bias_b, *refs):
    vectors, (half, eighth, one, two, row_ref) = refs[:6], refs[6:]
    deep, width = out_ref.shape
    half[:deep, :] = out_ref[...]
    row_ref[0, :] = bias_b[...]
    left = jnp.concatenate(
        [jnp.concatenate([bias_a[0:1, :], bias_a[1:2, :]], axis=1)]
        + [row_ref[:, at : at + width] for at in range(0, row_ref.shape[1], width)],
        axis=0,
    )
    parts = []
    for _ in range(3):
        coarse = left.astype(BF16).astype(F32)
        parts.append(coarse)
        left = left - coarse
    parts.append(jnp.zeros((half.shape[0] - deep - 3 * left.shape[0], width), F32))
    half[deep:, :] = jnp.concatenate(parts, axis=0).astype(BF16)
    tall, parts = folded(*in_ref.shape, eighth.shape[1])
    for (row, high, column, wide), (top, _, side, _) in parts:
        eighth[row : row + high, column : column + wide] = in_ref[top : top + high, side : side + wide]
    eighth[tall:, :] = down_ref[...]
    for at in range(3):
        one[at, :] = vectors[at][...]
        two[at, :] = vectors[3 + at][...]


def second_cut(line, w_out, w_in, w_down, b_qv, b_in, vectors, here):
    width = w_out.shape[1]
    half, rows, deep = w_out.shape[0] // 2, w_in.shape[0] // 8, w_down.shape[0] // 8
    last = w_in.shape[1] // 3
    eighth = folded(rows, last, width)[0]
    shapes = [(half + 16, width), (eighth + deep, width), (3, width), (3, width), (1, b_in.shape[0])]
    return line.run(
        second_cut_kernel,
        [w_out, w_in, w_down, b_qv, b_in, *vectors],
        [shaped(shape, BF16 if at < 2 else F32) for at, shape in enumerate(shapes)],
        grid=(1,),
        in_specs=[
            pl.BlockSpec((half, width), lambda i, p: (p[0] & 1, 0)),
            pl.BlockSpec((rows, last), lambda i, p: (p[0] & 7, 2)),
            pl.BlockSpec((deep, width), lambda i, p: (p[0] & 7, 0)),
            whole(b_qv.shape),
            whole(b_in.shape),
            *[whole((width,)) for vector in vectors],
        ],
        out_specs=[whole(shape) for shape in shapes],
        place=here,
        moved=4 * (half + eighth + deep) * width,
        room=ROOM_CUT,
    )


def third_cut_kernel(place_ref, a, b, c, d, out_ref, in_ref, core, half, bias_a, bias_b):
    third, rows, inner = a.shape
    for at, ref in enumerate((a, b, c, d)):
        for section in range(third):
            row = (section * 4 + at) * rows
            core[row : row + rows, :] = ref[section]
    row = 4 * third * rows
    deep = out_ref.shape[0] - 16
    core[row : row + deep, :] = out_ref[:deep, :inner]
    core[row + deep :, :] = out_ref[:deep, inner:]
    half[...] = in_ref[...]
    parts = out_ref[deep:, :].astype(F32)
    width = parts.shape[1]
    count = 1 + bias_b.shape[1] // width
    total = parts[2 * count : 3 * count] + parts[count : 2 * count] + parts[:count]
    bias_a[0:1, :] = total[0:1, :inner]
    bias_a[1:2, :] = total[0:1, inner:]
    for at in range(count - 1):
        bias_b[:, at * width : (at + 1) * width] = total[1 + at : 2 + at, :]


def third_cut(line, qkv, out, w_in, here, after):
    third, rows, inner = qkv[0].shape
    height = 4 * third * rows + 2 * (out.shape[0] - 16)
    half = (w_in.shape[0] // 2, w_in.shape[1] // 3 * 2)
    shapes = [(height, inner), half, (2, inner), (1, w_in.shape[1])]
    return line.run(
        third_cut_kernel,
        [*qkv, out, w_in],
        [shaped(shape, BF16 if at < 2 else F32) for at, shape in enumerate(shapes)],
        grid=(1,),
        in_specs=[whole(item.shape) for item in [*qkv, out]]
        + [pl.BlockSpec(half, lambda i, p: (p[0] & 1, 0))],
        out_specs=[whole(shape) for shape in shapes],
        place=here,
        moved=4 * (height * inner + half[0] * half[1]),
        after=after,
    )


def first_assemble_kernel(place_ref, mine, near, qkv_ref, out_ref):
    third, width, inner = qkv_ref.shape
    rows, half = width // 8, out_ref.shape[0] // 2
    for core, ref in enumerate((mine, near)):
        for at in range(4):
            row = pl.multiple_of(((place_ref[0] ^ (2 * at + core)) & 7) * rows, rows)
            for section in range(third):
                start = (section * 4 + at) * rows
                qkv_ref[section, pl.ds(row, rows), :] = ref[start : start + rows, :]
        row = pl.multiple_of(((place_ref[0] ^ core) & 1) * half, half)
        start = 4 * third * rows
        out_ref[pl.ds(row, half), :inner] = ref[start : start + half, :]
        out_ref[pl.ds(row, half), inner:] = ref[start + half :, :]


def first_assemble(line, mine, near, width, inner, here):
    return line.run(
        first_assemble_kernel,
        [mine, near],
        [shaped((3, width, inner), BF16), shaped((inner, width), BF16)],
        place=here,
        moved=8 * mine.size,
    )


def fourth_cut_kernel(a, b, c, d, half_ref, eighths, half):
    rows = a.shape[0]
    for at, ref in enumerate((a, b, c, d)):
        eighths[at * rows : (at + 1) * rows, :] = ref[...]
    half[...] = half_ref[...]


def fourth_cut(line, eighths, half):
    rows, width = eighths[0].shape
    return line.run(
        fourth_cut_kernel,
        [*eighths, half],
        [shaped((4 * rows, width), BF16), shaped(half.shape, BF16)],
        moved=16 * rows * width,
    )


def second_assemble_kernel(place_ref, mine, near, half_mine, half_near, in_ref, down_ref):
    width = mine.shape[1]
    wide, last = half_mine.shape[1], in_ref.shape[1] - half_mine.shape[1]
    rows, deep, half = in_ref.shape[0] // 8, down_ref.shape[0] // 8, half_mine.shape[0]
    tall, parts = folded(rows, last, width)
    for core, (ref, half_ref) in enumerate(((mine, half_mine), (near, half_near))):
        for at in range(4):
            block = (place_ref[0] ^ (2 * at + core)) & 7
            start = at * (tall + deep)
            for (row, high, column, side), (top, _, left, _) in parts:
                to = pl.multiple_of(block * rows + top, 32)
                in_ref[pl.ds(to, high), wide + left : wide + left + side] = ref[
                    start + row : start + row + high, column : column + side
                ]
            down_ref[pl.ds(pl.multiple_of(block * deep, deep), deep), :] = ref[
                start + tall : start + tall + deep, :
            ]
        row = pl.multiple_of(((place_ref[0] ^ core) & 1) * half, half)
        in_ref[pl.ds(row, half), :wide] = half_ref[...]


def second_assemble(line, mine, near, half_mine, half_near, hidden, here):
    width = mine.shape[1]
    return line.run(
        second_assemble_kernel,
        [mine, near, half_mine, half_near],
        [shaped((width, hidden), BF16), shaped((hidden, width), BF16)],
        place=here,
        moved=8 * width * hidden,
    )


def project_kernel(tok_ref, few_ref, w_ref, bias_ref, k_ref, v_ref, q_ref, ctx_ref):
    tok = tok_ref[...]
    k_ref[...] = mm(tok, w_ref[1]).astype(BF16)
    v_ref[...] = (mm(tok, w_ref[2]) + bias_ref[1:2, :]).astype(BF16)
    q_ref[...] = (mm(few_ref[...], w_ref[0]) + bias_ref[0:1, :]).astype(BF16)
    for at in range(0, k_ref.shape[1], LANES):
        cut = slice(at, at + LANES)
        ctx_ref[:, cut] = attend_block(q_ref[:, cut], k_ref[:, cut], v_ref[:, cut])


def project(line, tokens, few, weights, bias, seqs):
    rows, width = tokens.shape
    inner = weights.shape[2]
    length, slots = rows // seqs, few.shape[0] // seqs
    long, short = (pl.BlockSpec((size, inner), lambda s: (s, 0)) for size in (length, slots))
    return line.run(
        project_kernel,
        [tokens, few, weights, bias],
        [shaped((rows, inner), BF16)] * 2 + [shaped((few.shape[0], inner), BF16)] * 2,
        grid=(seqs,),
        in_specs=[
            pl.BlockSpec((length, width), lambda s: (s, 0)),
            pl.BlockSpec((slots, width), lambda s: (s, 0)),
            whole(weights.shape),
            whole(bias.shape),
        ],
        out_specs=[long, long, short, short],
        flops=6 * rows * width * inner,
        room=16,
        moved=2 * (rows * width + 3 * width * inner + 2 * rows * inner),
    )


def first_norm_kernel(ctx_a, ctx_b, w_a, w_b, few_ref, vec_ref, sum_ref, low_ref):
    branch = mm(ctx_a[...], w_a[...]) + mm(ctx_b[...], w_b[...]) + vec_ref[0:1, :]
    total = few_ref[...].astype(F32) + branch
    sum_ref[...] = total
    low_ref[...] = (norm_rows(total)[0] * vec_ref[1:2, :] + vec_ref[2:3, :]).astype(BF16)


def first_norm(line, contexts, w_out, few, vectors):
    count, width = few.shape
    return line.run(
        first_norm_kernel,
        [*contexts, *w_out, few, vectors],
        [shaped((count, width), F32), shaped((count, width), BF16)],
        flops=2 * count * width * width,
        moved=2 * width * width + 14 * count * width,
    )


def ffn_part_kernel(low_ref, wi_ref, bi_ref, wd_ref, slope_ref, part_ref, total):
    step = pl.program_id(0)
    gate, slope = gelu_and_slope(mm(low_ref[...], wi_ref[...]) + bi_ref[...])
    slope_ref[...] = slope
    part = mm(gate.astype(BF16), wd_ref[...])

    @pl.when(step == 0)
    def _():
        total[...] = part

    @pl.when(step > 0)
    def _():
        total[...] += part

    @pl.when(step == pl.num_programs(0) - 1)
    def _():
        part_ref[...] = total[...]


def ffn_part(line, low, w_in, b_in, w_down):
    count, width = low.shape
    hidden = w_in.shape[1]
    steps = 4
    tile = hidden // steps
    flat = whole((count, width))
    return line.run(
        ffn_part_kernel,
        [low, w_in, b_in, w_down],
        [shaped((count, hidden), F32), shaped((count, width), F32)],
        grid=(steps,),
        in_specs=[
            flat,
            pl.BlockSpec((width, tile), lambda j: (0, j)),
            pl.BlockSpec((1, tile), lambda j: (0, j)),
            pl.BlockSpec((tile, width), lambda j: (j, 0)),
        ],
        out_specs=[pl.BlockSpec((count, tile), lambda j: (0, j)), flat],
        scratch=[pltpu.VMEM((count, width), F32)],
        flops=4 * count * width * hidden,
        moved=4 * width * hidden,
        transcendentals=count * hidden,
        room=12,
    )


def column_sum(values):
    return jnp.sum(values, axis=0, keepdims=True)


def ffn_last_kernel(
    low_ref, part_ref, sum_ref, grad_ref, one_ref, two_ref, wi_ref, bi_ref, wd_ref,
    g_ffn_ref, g_second_ref, slope_ref, sums_ref,
):
    gate, slope = gelu_and_slope(mm(low_ref[...], wi_ref[...]) + bi_ref[...])
    slope_ref[...] = slope
    ffn = part_ref[...] + mm(gate.astype(BF16), wd_ref[...]) + two_ref[0:1, :]
    normed = norm_rows(sum_ref[...])[0] * one_ref[1:2, :] + one_ref[2:3, :]
    unit, root = norm_rows(normed + ffn)
    grad = grad_ref[...]
    g_second = norm_back(grad, unit, root, two_ref[1:2, :])
    g_ffn = g_second.astype(BF16)
    g_ffn_ref[...] = g_ffn
    g_second_ref[...] = g_second
    sums = (column_sum(g_ffn.astype(F32)), column_sum(grad * unit), column_sum(grad))
    sums_ref[...] = jnp.concatenate([*sums, jnp.zeros((5, grad.shape[1]), F32)], axis=0)


def ffn_last(line, low, part, total, grad, one, two, w_in, b_in, w_down):
    count, width = low.shape
    hidden = w_in.shape[1]
    return line.run(
        ffn_last_kernel,
        [low, part, total, grad, one, two, w_in, b_in, w_down],
        [
            shaped((count, width), BF16),
            shaped((count, width), F32),
            shaped((count, hidden), F32),
            shaped((8, width), F32),
        ],
        flops=4 * count * width * hidden,
        moved=4 * width * hidden,
        room=12,
    )


def ffn_back_kernel(
    g_ffn_ref, g_second_ref, sum_ref, one_ref, sums_ref, slope_a, slope_b, wi_a, wi_b, wd_a, wd_b,
    g_branch_ref, g_first_ref, small_ref,
):
    g_ffn, g_normed = g_ffn_ref[...], g_second_ref[...]
    width = g_normed.shape[1]
    half = width // 2
    deep = slope_a.shape[1] // half
    for at, (slope, w_in, w_down) in enumerate(((slope_a, wi_a, wd_a), (slope_b, wi_b, wd_b))):
        g_pre = (slope[...] * dot_nt(g_ffn, w_down[...])).astype(BF16)
        bias = column_sum(g_pre.astype(F32))
        for row in range(deep):
            small_ref[at * deep + row : at * deep + row + 1, :] = bias[:, row * half : (row + 1) * half]
        g_normed = g_normed + dot_nt(g_pre, w_in[...])
    unit, root = norm_rows(sum_ref[...])
    g_first = norm_back(g_normed, unit, root, one_ref[1:2, :])
    g_branch = g_first.astype(BF16)
    g_first_ref[...] = g_first
    g_branch_ref[...] = g_branch
    vectors = (
        column_sum(g_branch.astype(F32)),
        column_sum(g_normed * unit),
        column_sum(g_normed),
        *[sums_ref[at : at + 1, :] for at in range(3)],
    )
    for at, vector in enumerate(vectors):
        row = 2 * deep + 2 * at
        small_ref[row : row + 1, :] = vector[:, :half]
        small_ref[row + 1 : row + 2, :] = vector[:, half:]
    count = 2 * deep + 12
    small_ref[count:, :] = jnp.zeros((small_ref.shape[0] - count, half), F32)


def ffn_back(line, g_ffn, g_second, total, one, sums, slopes, w_in, w_down):
    count, width = g_ffn.shape
    hidden = w_in[0].shape[1]
    rows = 2 * (hidden // (width // 2)) + 12
    return line.run(
        ffn_back_kernel,
        [g_ffn, g_second, total, one, sums, *slopes, *w_in, *w_down],
        [
            shaped((count, width), BF16),
            shaped((count, width), F32),
            shaped((-(-rows // 8) * 8, width // 2), F32),
        ],
        flops=8 * count * width * hidden,
        moved=8 * width * hidden,
        room=12,
    )


def ffn_grads_kernel(place_ref, wi_ref, wd_ref, bi_ref, *refs):
    normed_refs, grad_refs = refs[:2], refs[2:4]
    keep_down, send_down, keep_in, send_in = refs[4:8]
    down, up = refs[8:]
    width = normed_refs[0].shape[1]
    tile = wi_ref.shape[1] // 4
    hidden = pl.ds(pl.multiple_of((place_ref[0] >> 2) * tile, tile), tile)
    w_in, w_down, b_in = wi_ref[:, hidden], wd_ref[hidden, :], bi_ref[:, hidden]
    for at in range(2):
        normed, grad = normed_refs[at][...], grad_refs[at][...]
        gate, slope = gelu_and_slope(mm(normed, w_in) + b_in)
        pre = (slope * dot_nt(grad, w_down)).astype(BF16)
        down_part = dot_tn(gate.astype(BF16), grad)
        up_part = dot_tn(normed, pre)
        if at == 0:
            down[...] = down_part
            up[...] = up_part
        else:
            down[...] += down_part
            up[...] += up_part
    down_rows, up_rows = tile // 4, width // 4
    half = width // 2
    for slot in range(4):
        block = slot ^ (place_ref[0] & 3)
        low = down[pl.ds(pl.multiple_of(block * down_rows, down_rows), down_rows), :]
        block = (0, 2, 1, 3)[slot] ^ (place_ref[0] & 3)
        high = up[pl.ds(pl.multiple_of(block * up_rows, up_rows), up_rows), :]
        to_down, to_in = (keep_down, keep_in) if slot < 2 else (send_down, send_in)
        kind = to_down.dtype
        to_down[slot % 2, :down_rows, :] = low[:, :half].astype(kind)
        to_down[slot % 2, down_rows:, :] = low[:, half:].astype(kind)
        to_in[slot % 2, :, :] = high.astype(kind)


def ffn_grads(line, place, w_in, w_down, b_in, normed, grads):
    rows, width = normed[0].shape
    tile = w_in.shape[1] // 4
    shape = (2, 2 * (tile // 4), width // 2)
    wide = (2, width // 4, tile)
    return line.run(
        ffn_grads_kernel,
        [w_in, w_down, b_in, *normed, *grads],
        [shaped(shape, F32), shaped(shape, BF16), shaped(wide, F32), shaped(wide, BF16)],
        scratch=[pltpu.VMEM((tile, width), F32), pltpu.VMEM((width, tile), F32)],
        place=place,
        flops=16 * rows * width * tile,
        moved=12 * rows * width + 16 * width * tile,
        hint=HINT_GRADS,
        room=16,
    )


def attend_back_kernel(
    seqs, half, deep, place_ref, q_ref, k_ref, v_ref, g_branch_ref, w_out_ref, ctx_ref, tok_t_ref, few_ref,
    small_ref, dq_ref, dkv_ref, keep_ref, send_ref, total, little,
):
    few, inner = q_ref.shape
    rows = k_ref.shape[0]
    slots, length = few // seqs, rows // seqs
    low = lane_halves(slots)
    scale = HEAD ** (-0.5)
    g_branch = g_branch_ref[...]
    g_context = dot_nt(g_branch, w_out_ref[...]).astype(BF16)
    for seq in range(seqs):
        short, long = slice(seq * slots, (seq + 1) * slots), slice(seq * length, (seq + 1) * length)
        for at in range(0, inner, LANES):
            cut = slice(at, at + LANES)
            both, grads = two_heads(scaled(q_ref[short, cut])), two_heads(g_context[short, cut])
            keys, values = k_ref[long, cut], v_ref[long, cut]
            probs = softmax_rows(dot_nt(both, keys))
            grad_probs = dot_nt(grads, values)
            dkv_ref[long, inner + at : inner + at + LANES] = dot_tn(probs.astype(BF16), grads).astype(BF16)
            row_total = jnp.sum(grad_probs * probs, axis=-1, keepdims=True)
            grad_scores = (probs * (grad_probs - row_total)).astype(BF16)
            dq = mm(grad_scores, keys) * scale
            dq_ref[short, cut] = jnp.where(low, dq[:slots], dq[slots:]).astype(BF16)
            dkv_ref[long, cut] = dot_tn(grad_scores, both).astype(BF16)
    dq, dkv = dq_ref[...], dkv_ref[...]
    total[0] = dot_tn(few_ref[...], dq)
    both = mm(tok_t_ref[...], dkv)
    total[1] = both[:, :inner]
    total[2] = both[:, inner:]
    out_grad = dot_tn(ctx_ref[...], g_branch)
    total[3, :inner, :] = out_grad[:, :inner]
    total[3, inner:, :] = out_grad[:, inner:]
    little[...] = jnp.zeros_like(little)
    little[0, 0:1, :] = column_sum(dq.astype(F32))
    little[0, 1:2, :] = column_sum(dkv[:, inner:].astype(F32))
    for at in range(deep + 12):
        source = half * deep + at if at < deep else deep + at
        little[1 + at // 2, at % 2 : at % 2 + 1, :] = small_ref[source : source + 1, :]
    block_rows = total.shape[1] // 16
    pad = keep_ref.shape[1] - 4 * block_rows
    for slot in range(16):
        block = slot ^ place_ref[0]
        row = pl.multiple_of(block * block_rows, block_rows)
        to, kind = (keep_ref, F32) if slot < 8 else (send_ref, BF16)
        for section in range(4):
            cut = slice(section * block_rows, (section + 1) * block_rows)
            to[slot % 8, cut, :] = total[section, pl.ds(row, block_rows), :].astype(kind)
        pair = jnp.concatenate([little[block], jnp.zeros((pad - 8, inner), F32)], axis=0)
        to[slot % 8, 4 * block_rows :, :] = pair.astype(kind)


def attend_back(line, place, queries, keys, values, g_branch, w_out, context, tokens_t, few, small, seqs, half, deep):
    rows, inner = keys.shape
    width = tokens_t.shape[0]
    count = queries.shape[0]
    held = (8, 4 * (width // 16) + 16, inner)
    return line.run(
        functools.partial(attend_back_kernel, seqs, half, deep),
        [queries, keys, values, g_branch, w_out, context, tokens_t, few, small],
        [
            shaped((count, inner), BF16),
            shaped((rows, 2 * inner), BF16),
            shaped(held, F32),
            shaped(held, BF16),
        ],
        scratch=[pltpu.VMEM((4, width, inner), F32), pltpu.VMEM((16, 8, inner), F32)],
        place=place,
        hint=HINT_BACK,
        room=16,
        flops=4 * rows * width * inner + 24 * count * rows * inner,
        moved=20 * rows * inner,
    )


def sum_all_kernel(count, keep_ref, *refs):
    row = 0
    for ref in refs[:count]:
        part = slice(row, row + ref.shape[0])
        refs[count][part] = (keep_ref[part].astype(F32) + ref[...].astype(F32)).astype(BF16)
        row += ref.shape[0]


def sum_all(line, hint, keep, *arrived):
    (result,) = line.run(
        functools.partial(sum_all_kernel, len(arrived)), [keep, *arrived], [shaped(keep.shape, BF16)], hint=hint
    )
    return result


def sum_split_kernel(mine_ref, near_ref, upper, lower):
    rows = upper.shape[1]
    for slot in range(2):
        total = (mine_ref[slot].astype(F32) + near_ref[1 - slot].astype(F32)).astype(BF16)
        upper[slot] = total[:rows, :]
        lower[slot] = total[rows:, :]


def sum_split(line, hint, mine, near, rows):
    count, height, inner = mine.shape
    shapes = [shaped((count, rows, inner), BF16), shaped((count, height - rows, inner), BF16)]
    return line.run(sum_split_kernel, [mine, near], shapes, hint=hint)


def second_fold_kernel(down, down_near, up, up_near, down_out, up_keep, up_send):
    down_out[...] = (down[...] + down_near[...].astype(F32)).astype(BF16)
    total = up[...] + up_near[...].astype(F32)
    middle = total.shape[0] // 2
    up_keep[...] = total[:middle]
    up_send[...] = total[middle:].astype(BF16)


def second_fold(line, down, down_near, up, up_near, hint):
    half = (up.shape[0] // 2, *up.shape[1:])
    return line.run(
        second_fold_kernel,
        [down, down_near, up, up_near],
        [shaped(down.shape, BF16), shaped(half, F32), shaped(half, BF16)],
        hint=hint,
    )


def third_fold_kernel(down, down_near, up, up_near, down_out, up_out):
    for slot in range(2):
        down_out[slot] = (down[slot].astype(F32) + down_near[1 - slot].astype(F32)).astype(BF16)
    count = up.shape[0]
    up_out[:count] = up[...]
    up_out[count:] = up_near[...]


def third_fold(line, down, down_near, up, up_near, hint):
    shapes = [shaped(down.shape, BF16), shaped((2 * up.shape[0], *up.shape[1:]), BF16)]
    return line.run(third_fold_kernel, [down, down_near, up, up_near], shapes, hint=hint)


def append_kernel(count, *refs):
    groups, out = refs[:-count], refs[-count:]
    each = len(groups) // count
    for at in range(count):
        row = 0
        for ref in groups[at * each : (at + 1) * each]:
            out[at][row : row + ref.shape[0]] = ref[...]
            row += ref.shape[0]


def append(line, hint, *groups):
    shapes = [shaped((sum(item.shape[0] for item in group), *group[0].shape[1:]), BF16) for group in groups]
    return line.run(
        functools.partial(append_kernel, len(groups)),
        [item for group in groups for item in group],
        shapes,
        hint=hint,
    )


def cross_one_kernel(oth, oth_near, own, own_near, x_send, y_send, x_keep, y_keep_own, y_keep_oth):
    rows = x_send.shape[1]
    half = oth.shape[0] // 2
    x_send[...] = (oth[:, :rows, :] + oth_near[:, :rows, :].astype(F32)).astype(BF16)
    x_keep[...] = own[:, :rows, :] + own_near[:, :rows, :].astype(F32)
    for at, (keep, near, out) in enumerate(((own, own_near, y_keep_own), (oth, oth_near, y_keep_oth))):
        total = keep[:, rows:, :] + near[:, rows:, :].astype(F32)
        out[...] = total[:half]
        y_send[at] = total[half:].astype(BF16)


def cross_one(line, oth, oth_near, own, own_near, rows):
    count, height, inner = oth.shape
    half, last = count // 2, height - rows
    return line.run(
        cross_one_kernel,
        [oth, oth_near, own, own_near],
        [
            shaped((count, rows, inner), BF16),
            shaped((2, half, last, inner), BF16),
            shaped((count, rows, inner), F32),
            shaped((half, last, inner), F32),
            shaped((half, last, inner), F32),
        ],
        hint=2,
    )


def cross_two_kernel(x_keep, x_near, own, oth, y_near, y_send, x_send, first, last):
    half = own.shape[0]
    total = x_keep[...] + x_near[...].astype(F32)
    first[...] = total[:half]
    y_send[...] = total[half:].astype(BF16)
    total = own[...] + y_near[0].astype(F32)
    small = total.shape[1] - 16
    last[:, :small, :] = total[:, :small, :]
    last[:, small:, :] = total[:, small:, :].astype(BF16).astype(F32)
    x_send[...] = (oth[...] + y_near[1].astype(F32)).astype(BF16)


def cross_two(line, x_keep, x_near, own, oth, y_near, hint):
    half = (own.shape[0], x_keep.shape[1], x_keep.shape[2])
    return line.run(
        cross_two_kernel,
        [x_keep, x_near, own, oth, y_near],
        [shaped(half, BF16), shaped(own.shape, BF16), shaped(half, F32), shaped(own.shape, F32)],
        hint=hint,
    )


def cross_three_kernel(first, y_near, last, x_near, keep, *sends):
    rows, half = first.shape[1], first.shape[0] // 2
    for ref, near, cut in ((first, y_near, slice(0, rows)), (last, x_near, slice(rows, None))):
        total = ref[...] + near[...].astype(F32)
        keep[:, cut, :] = total[:half]
        for at, send in enumerate(sends):
            send[:, cut, :] = total[half + at : half + at + 1].astype(BF16)


def cross_three(line, first, y_near, last, x_near, hint):
    half, height, inner = first.shape[0] // 2, first.shape[1] + last.shape[1], first.shape[2]
    return line.run(
        cross_three_kernel,
        [first, y_near, last, x_near],
        [shaped((half, height, inner), F32)] + [shaped((1, height, inner), BF16)] * half,
        hint=hint,
    )


def unpack_attend_kernel(place_ref, *refs):
    blocks, (qkv_ref, out_ref), (wide, little, sems) = refs[:4], refs[4:6], refs[-3:]
    outs = refs[6:-3]
    inner = qkv_ref.shape[2]
    rows = qkv_ref.shape[1] // 16
    copies = []

    def place_rows(source, to):
        copy = pltpu.make_async_copy(source, to, sems.at[len(copies)])
        copy.start()
        copies.append(copy)

    for slot in range(16):
        core, at = slot // 8, slot % 8
        block = slot ^ place_ref[0]
        wide[slot, : 2 * rows, :] = blocks[2 * core][at].astype(F32)
        row = pl.multiple_of(block * rows, rows)
        for section in range(2):
            place_rows(wide.at[slot, pl.ds(section * rows, rows), :], qkv_ref.at[section, pl.ds(row, rows), :])
        block = ((at & 1) + (at & 2) * 2 + (at >> 2) * 2 + 8 * core) ^ place_ref[0]
        values = blocks[2 * core + 1][at].astype(F32)
        wide[slot, 2 * rows :, :] = values[: 2 * rows, :]
        little[block] = values[2 * rows : 2 * rows + 8, :]
        row = pl.multiple_of(block * rows, rows)
        place_rows(wide.at[slot, pl.ds(2 * rows, rows), :], qkv_ref.at[2, pl.ds(row, rows), :])
        row = pl.multiple_of((block & 7) * rows, rows)
        column = pl.multiple_of((block >> 3) * inner, inner)
        place_rows(wide.at[slot, pl.ds(3 * rows, rows), :], out_ref.at[pl.ds(row, rows), pl.ds(column, inner)])
    outs[0][...] = little[0, 0:2, :]
    row = 2
    for out in outs[1:]:
        for at in range(out.shape[0] // inner):
            out[pl.ds(at * inner, inner)] = little[row // 2, row % 2, :]
            row += 1
    for copy in copies:
        copy.wait()


def unpack_attend(line, place, blocks, width, hidden):
    inner = blocks[0].shape[2]
    rows = width // 16
    small = [(2, inner), (hidden,)] + [(width,)] * 6
    return line.run(
        unpack_attend_kernel,
        blocks,
        [shaped((3, width, inner), F32), shaped((inner, width), F32)] + [shaped(shape, F32) for shape in small],
        out_specs=[ANYWHERE] * 2 + [VMEM] * 8,
        scratch=[
            pltpu.VMEM((16, 4 * rows, inner), F32),
            pltpu.VMEM((16, 8, inner), F32),
            pltpu.SemaphoreType.DMA((64,)),
        ],
        place=place,
        room=20,
        hint=1,
    )


def unpack_ffn_kernel(first, place_ref, *refs):
    down_in, up_in = refs[:2]
    down_ref, in_ref, down, up, sems = refs[-5:]
    rows, half = down_ref.shape[0] // 16, down_ref.shape[1] // 2
    deep, wide = in_ref.shape[0] // 4, in_ref.shape[1] // 4
    copies = []
    for slot in range(8):
        block = (slot if first else slot + 8) ^ place_ref[0]
        values = down_in[slot].astype(F32)
        down[slot, :, :half] = values[:rows, :]
        down[slot, :, half:] = values[rows:, :]
        up[slot] = up_in[slot].astype(F32)
        row = pl.multiple_of(block * rows, rows)
        copies.append((down.at[slot], down_ref.at[pl.ds(row, rows), :]))
        block = ((slot & 1) + (slot & 2) * 2 + (slot >> 2) * 2 + (0 if first else 8)) ^ place_ref[0]
        row = pl.multiple_of((block & 3) * deep, deep)
        column = pl.multiple_of((block >> 2) * wide, wide)
        copies.append((up.at[slot], in_ref.at[pl.ds(row, deep), pl.ds(column, wide)]))
    copies = [pltpu.make_async_copy(*pair, sems.at[at]) for at, pair in enumerate(copies)]
    for copy in copies:
        copy.start()
    for copy in copies:
        copy.wait()


def unpack_ffn(line, place, down, up, width, hidden, before=None):
    return line.run(
        functools.partial(unpack_ffn_kernel, before is None),
        [down, up, *(before or [])],
        [shaped((hidden, width), F32), shaped((width, hidden), F32)],
        in_specs=[VMEM] * 2 + [ANYWHERE] * (0 if before is None else 2),
        out_specs=[ANYWHERE] * 2,
        scratch=[
            pltpu.VMEM((8, hidden // 16, width), F32),
            pltpu.VMEM((8, width // 4, hidden // 4), F32),
            pltpu.SemaphoreType.DMA((16,)),
        ],
        aliases={} if before is None else {3: 0, 4: 1},
        place=place,
        moved=6 * width * hidden,
        room=20,
        hint=1,
    )


def attend_kernel(tok_ref, w_ref, bias_ref, k_ref, v_ref, out_ref):
    rows, inner = out_ref.shape
    low = lane_halves(rows)
    queries = scaled((mm(tok_ref[...], w_ref[0]) + bias_ref[0:1, :]).astype(BF16))
    for at in range(0, inner, LANES):
        cut = slice(at, at + LANES)
        block, keys, values = queries[:, cut], k_ref[:, cut], v_ref[:, cut]
        zero, one = jnp.zeros_like(block), jnp.ones_like(values)
        mixed = []
        for first in (True, False):
            head = jnp.where(low == first, block, zero)
            with_sums = jnp.where(lane_halves(values.shape[0]) == first, values, one)
            scores = dot_nt(head, keys)
            exponent = jnp.exp(scores - jnp.max(scores, axis=-1, keepdims=True)).astype(BF16)
            mixed.append(mm(exponent, with_sums))
        top = jnp.where(low, mixed[0], mixed[1])
        total = jnp.where(low, mixed[1], mixed[0])
        out_ref[:, cut] = (top / pltpu.roll(total, HEAD, 1)).astype(BF16)


def attend(line, tokens, weights, bias, keys, values, seqs, seq, hint=None):
    rows, width = tokens.shape
    inner = keys.shape[1]
    length = rows // seqs
    long = pl.BlockSpec((length, inner), lambda s: (seq, 0))
    (result,) = line.run(
        attend_kernel,
        [tokens, weights, bias, keys, values],
        [shaped((length, inner), BF16)],
        grid=(1,),
        in_specs=[
            pl.BlockSpec((length, width), lambda s: (seq, 0)),
            pl.BlockSpec((1, width, inner), lambda s: (0, 0, 0)),
            whole(bias.shape),
            long,
            long,
        ],
        out_specs=[pl.BlockSpec((length, inner), lambda s: (0, 0))],
        flops=2 * length * width * inner + 16 * length * length * inner,
        moved=2 * (length * width + width * inner + 3 * length * inner),
        transcendentals=length * length * inner // HEAD,
        room=16,
        hint=hint,
    )
    return result


def layer_kernel(
    tok_ref, ctx_a, ctx_b, wo_a, wo_b, wi_a, wi_b, bi_a, bi_b, wd_a, wd_b, one_ref, two_ref, out_ref,
):
    branch = mm(ctx_a[...], wo_a[...]) + mm(ctx_b[...], wo_b[...]) + one_ref[0:1, :]
    unit, _ = norm_rows(tok_ref[...].astype(F32) + branch)
    normed = unit * one_ref[1:2, :] + one_ref[2:3, :]
    low = normed.astype(BF16)
    total = normed + two_ref[0:1, :]
    for w_in, b_in, w_down in ((wi_a, bi_a, wd_a), (wi_b, bi_b, wd_b)):
        hidden = gelu(mm(low, w_in[...]) + b_in[...]).astype(BF16)
        total = total + mm(hidden, w_down[...])
    unit, _ = norm_rows(total)
    out_ref[...] = (unit * two_ref[1:2, :] + two_ref[2:3, :]).astype(BF16)


def layer_next_kernel(*refs):
    layer_kernel(*refs[:-2], refs[-1])


def layer(line, tokens, contexts, w_out, w_in, b_in, w_down, one, two, seq, mixed, hint):
    length, inner = contexts[0].shape
    width, hidden = tokens.shape[1], w_in[0].shape[1]
    tile = 256
    steps = length // tile
    ctx = pl.BlockSpec((tile, inner), lambda i: (i, 0))
    still = [*w_out, *w_in, *b_in, *w_down, one, two]
    row = pl.BlockSpec((tile, width), lambda i: (seq * steps + i, 0))
    args = [tokens, *contexts, *still]
    specs = [row, ctx, ctx] + [whole(item.shape, True) for item in still]
    (result,) = line.run(
        layer_kernel if mixed is None else layer_next_kernel,
        args if mixed is None else [*args, mixed],
        [shaped(tokens.shape, BF16)],
        grid=(steps,),
        in_specs=specs if mixed is None else [*specs, ANYWHERE],
        out_specs=[row],
        aliases={} if mixed is None else {len(args): 0},
        room=30,
        hint=hint,
        flops=2 * length * width * (width + 4 * hidden),
        moved=4 * width * (length + 2 * hidden),
        transcendentals=2 * length * hidden,
    )
    return result


def input_grad_kernel(
    dkv_a, dkv_b, dq_a, dq_b, w_a, w_b, g_first_ref, places_ref, out_ref
):
    length = out_ref.shape[0]
    slots = g_first_ref.shape[0]
    few = g_first_ref[...] + dot_nt(dq_a[...], w_a[0]) + dot_nt(dq_b[...], w_b[0])
    coarse = few.astype(BF16)
    fine = (few - coarse.astype(F32)).astype(BF16)
    picks = places_ref[0][:, 0:1] == lax.broadcasted_iota(jnp.int32, (slots, length), 1)
    picks = picks.astype(F32).astype(BF16)
    total = dot_tn(picks, coarse) + dot_tn(picks, fine)
    for dkv, w in ((dkv_a, w_a), (dkv_b, w_b)):
        inner = w.shape[2]
        total = total + dot_nt(dkv[:, :inner], w[1]) + dot_nt(dkv[:, inner:], w[2])
    out_ref[...] = total


def input_grad_next_kernel(*refs):
    input_grad_kernel(*refs[:-2], refs[-1])


def input_grad(line, backs, weights, g_first, places, seqs, seq, before):
    rows, inner = backs[0][1].shape[0], backs[0][0].shape[1]
    width = g_first.shape[1]
    length, slots = rows // seqs, g_first.shape[0] // seqs
    long = pl.BlockSpec((length, 2 * inner), lambda i: (seq, 0))
    short = pl.BlockSpec((slots, inner), lambda i: (seq, 0))
    args = [
        backs[0][1], backs[1][1], backs[0][0], backs[1][0],
        *weights, g_first, places,
    ]
    specs = (
        [long] * 2
        + [short] * 2
        + [whole(w.shape, True) for w in weights]
        + [
            pl.BlockSpec((slots, width), lambda i: (seq, 0)),
            pl.BlockSpec((1, slots, LANES), lambda i: (seq, 0, 0)),
        ]
    )
    (result,) = line.run(
        input_grad_kernel if before is None else input_grad_next_kernel,
        args if before is None else [*args, before],
        [shaped((rows, width), F32)],
        grid=(1,),
        in_specs=specs if before is None else [*specs, ANYWHERE],
        out_specs=[pl.BlockSpec((length, width), lambda i: (seq, 0))],
        aliases={} if before is None else {len(args): 0},
        flops=10 * length * width * inner,
        moved=20 * width * inner + 8 * length * width,
        room=24,
        hint=0.1,
    )
    return result


def pick_kernel(seqs, half_ref, starts_ref, tok_ref, grad_ref, few_ref, grad_few_ref, turned_ref, places_ref):
    slots, length = few_ref.shape[0], tok_ref.shape[0]
    spans = starts_ref.shape[1]
    seq = half_ref[0] * seqs + pl.program_id(0)
    starts = [starts_ref[seq, at] for at in range(spans)]
    row = lax.broadcasted_iota(jnp.int32, (slots, LANES), 0)
    places = row + starts[0]
    for at in range(1, spans):
        places = places + jnp.where(row >= SPAN * at, starts[at] - starts[at - 1] - SPAN, 0)
    fresh = row < SPAN * spans
    for at, start in enumerate(starts):
        covered = (places >= start) & (places < start + SPAN) & (row >= SPAN * (at + 1))
        fresh = fresh & jnp.logical_not(covered)
    places_ref[0] = places
    wide = jnp.concatenate([places] * (length // LANES), axis=1)
    picks = wide == lax.broadcasted_iota(jnp.int32, (slots, length), 1)
    picks = picks.astype(F32).astype(BF16)
    few_ref[...] = mm(picks, tok_ref[...]).astype(BF16)
    grad_few_ref[...] = mm(picks, grad_ref[...]) * fresh.astype(F32)[:, 0:1]
    turned_ref[...] = tok_ref[...].T


def pick(line, half, starts, slots, tokens, grads, seqs, after):
    rows, width = tokens.shape
    length = rows // seqs
    long = pl.BlockSpec((length, width), lambda s, p: (s, 0))
    short = pl.BlockSpec((slots, width), lambda s, p: (s, 0))
    return line.run(
        functools.partial(pick_kernel, seqs),
        [starts, tokens, grads],
        [
            shaped((seqs * slots, width), BF16),
            shaped((seqs * slots, width), F32),
            shaped((width, rows), BF16),
            shaped((seqs, slots, LANES), jnp.int32),
        ],
        grid=(seqs,),
        in_specs=[pl.BlockSpec(memory_space=pltpu.SMEM), long, long],
        out_specs=[
            short, short, pl.BlockSpec((width, length), lambda s, p: (0, s)),
            pl.BlockSpec((1, slots, LANES), lambda s, p: (s, 0, 0)),
        ],
        place=half,
        flops=4 * rows * slots * width,
        moved=6 * rows * width,
        room=ROOM_PICK,
        after=after,
    )


def body(
    tokens,
    grad_values,
    span_starts,
    w_qkv,
    b_qv,
    w_out,
    b_out,
    ln1_gain,
    ln1_bias,
    w_in,
    b_in,
    w_down,
    b_down,
    ln2_gain,
    ln2_bias,
):
    rows, width = tokens.shape
    inner = w_qkv.shape[2]
    hidden_half = w_in.shape[1]
    halves = lax.axis_size("tensor")
    seqs = span_starts.shape[0] // halves
    spans = span_starts.shape[1]
    length = rows // seqs
    half_at = lax.axis_index("tensor")
    me = lax.axis_index("dp")
    bits = lax.axis_size("dp").bit_length() - 1
    block_at = ((me & 1) << 3) | ((me & 2) << 1) | ((me & 4) >> 1) | ((me & 8) >> 3)
    place = block_at.reshape(1).astype(jnp.int32)
    rest = [1 << bit for bit in range(4, bits)]

    slots = -(-spans * SPAN // 16) * 16
    here = me.reshape(1)
    line = Line()

    w_qkv_own = jnp.transpose(w_qkv, (1, 0, 2))

    def chips_around(held):
        return [held, flip(held, 2), flip(held, 4), flip(held, 6)]

    arrived_qkv = flip_tensor(cut_qkv(line, w_qkv_own, here))
    half_out, eighth, vectors_one, vectors_two, b_in = second_cut(
        line, w_out, w_in, w_down, b_qv, b_in,
        [b_out, ln1_gain, ln1_bias, b_down, ln2_gain, ln2_bias], here,
    )
    around_qkv = chips_around(arrived_qkv)
    arrived_out, arrived_eighth = flip_tensor(half_out), flip_tensor(eighth)
    tokens_few, grad_few, tokens_t, places = pick(
        line, half_at.reshape(1), span_starts, slots, tokens, grad_values, seqs, [arrived_qkv]
    )
    own = project(line, tokens, tokens_few, w_qkv_own, b_qv, seqs)
    def attend_own(seq, hint=None):
        return attend(line, tokens, w_qkv_own, b_qv, own[0], own[1], seqs, seq, hint)

    core_first, half_in, b_qv_oth, b_in_oth = third_cut(
        line, around_qkv, arrived_out, w_in, here, [arrived_eighth]
    )
    b_qv_both, b_in_both = [b_qv, b_qv_oth], [b_in, b_in_oth]
    near_first = flip(core_first, 1)
    around_eighth = chips_around(arrived_eighth)
    arrived_in = flip_tensor(half_in)
    w_qkv_oth, w_out_oth = first_assemble(line, core_first, near_first, width, inner, here)
    w_qkv_both, w_out_both = [w_qkv_own, w_qkv_oth], [w_out, w_out_oth]
    oth = project(line, tokens, tokens_few, w_qkv_oth, b_qv_both[1], seqs)

    keys, values, queries_few, context_few = zip(own, oth)
    sum_few, normed_low = first_norm(line, context_few, w_out_both, tokens_few, vectors_one)

    def plane(values):
        return [values, flip_tensor(values), flip(values, 2), flip_both(values, 2)]

    slope_own, part = ffn_part(line, normed_low, w_in, b_in_both[0], w_down)
    ctx_own = [attend_own(0)]
    core_second, held_in = fourth_cut(line, around_eighth, arrived_in)
    near_second, near_in = flip(core_second, 1), flip(held_in, 1)
    around_normed = plane(normed_low)
    w_in_oth, w_down_oth = second_assemble(
        line, core_second, near_second, held_in, near_in, hidden_half, here
    )
    w_in_both, w_down_both = [w_in, w_in_oth], [w_down, w_down_oth]
    g_ffn, g_second, slope_oth, sums = ffn_last(
        line, normed_low, part, sum_few, grad_few, vectors_one, vectors_two,
        w_in_both[1], b_in_both[1], w_down_both[1],
    )
    around_g = plane(g_ffn)
    g_branch, g_first, small_few = ffn_back(
        line, g_ffn, g_second, sum_few, vectors_one, sums, (slope_own, slope_oth), w_in_both, w_down_both
    )
    core_normed = join(line, around_normed)
    near_normed = flip(core_normed, 1)

    def back(at):
        return attend_back(
            line, place, queries_few[at], keys[at], values[at], g_branch, w_out_both[at],
            context_few[at], tokens_t, tokens_few, small_few, seqs, at, hidden_half // inner,
        )

    back_oth = back(1)
    near_oth = flip(back_oth[3], 1)
    core_g = join(line, around_g)
    near_g = flip(core_g, 1)
    back_own = back(0)
    near_own = flip(back_own[3], 1)
    keep_down, send_down, keep_in, send_in = ffn_grads(
        line, place, w_in, w_down, b_in_both[0], [core_normed, near_normed], [core_g, near_g]
    )
    z_down, z_in = flip(send_down, 4), flip(send_in, 8)
    x_send, y_send, x_keep, y_own, y_oth = cross_one(
        line, back_oth[2], near_oth, back_own[2], near_own, 112
    )
    x_near, y_near = flip_tensor(x_send), flip(y_send, 2)

    def attend_oth(seq, hint):
        return attend(
            line, tokens, w_qkv_oth, b_qv_both[1], keys[1], values[1], seqs, seq, hint
        )

    def over_rest_f32(total):
        return over_rest(total.astype(F32)) if rest else total

    def over_rest(total):
        for bit in rest:
            total = total + flip(total, bit)
        return total

    def layer_of(seq, mixed, hint):
        return layer(
            line, tokens, [ctx_own[seq], ctx_oth[seq]], w_out_both, w_in_both, b_in_both, w_down_both,
            vectors_one, vectors_two, seq, mixed, hint,
        )

    def input_grad_of(seq, before):
        return input_grad(line, [back_own, back_oth], w_qkv_both, g_first, places, seqs, seq, before)

    ctx_oth = [attend_oth(seq, 0.1) for seq in range(seqs)]
    ctx_own += [attend_own(seq, 0.1) for seq in range(1, seqs)]
    y_send, x_send, first, last = cross_two(line, x_keep, x_near, y_own, y_oth, y_near, H[0])
    y_near, x_near = flip(y_send, 2), flip_tensor(x_send)
    down, keep_in, send_in = second_fold(line, keep_down, z_down, keep_in, z_in, H[1])
    near_down, z_in = flip(down, 8), flip(send_in, 4)
    keep, *sends = cross_three(line, first, y_near, last, x_near, H[2])
    z_attn = [flip(send, 4) for send in sends]
    up = sum_all(line, H[3], over_rest(keep_in), over_rest(z_in))
    near_up = flip(up, 8)
    d_tokens = None
    for seq in range(seqs):
        d_tokens = input_grad_of(seq, d_tokens)

    attn = sum_all(line, H[5], keep, *z_attn)
    near_attn = flip(attn, 8)
    down, up = third_fold(line, over_rest_f32(down), over_rest_f32(near_down), up, near_up, H[4])
    near_down, near_up = flip(down, 4), flip(up, 2)
    mixed = layer_of(0, None, 0.1)
    upper, lower = sum_split(line, H[7], over_rest_f32(attn), over_rest_f32(near_attn), width // 8)
    near_upper, near_lower = flip(upper, 4), flip(lower, 2)
    down, up = append(line, H[6], [down, near_down], [up, near_up])
    near_down, near_up = flip(down, 2), flip(up, 4)
    for seq in range(1, seqs):
        mixed = layer_of(seq, mixed, H[8])
    (upper,) = append(line, 1.5, [upper, near_upper])
    (lower,) = append(line, 1.5, [lower, near_lower])
    near_upper, near_lower = flip(upper, 2), flip(lower, 4)
    down, up = append(line, 1, [down, near_down], [up, near_up])
    near_down, near_up = flip(down, 1), flip(up, 1)
    ffn_sums = unpack_ffn(line, place, down, up, width, hidden_half)
    (upper,) = append(line, 1, [upper, near_upper])
    (lower,) = append(line, 1, [lower, near_lower])
    far_upper, far_lower = flip(upper, 1), flip(lower, 1)
    d_w_down, d_w_in = unpack_ffn(line, place, near_down, near_up, width, hidden_half, ffn_sums)
    d_w_qkv, d_w_out, *small = unpack_attend(line, place, [upper, lower, far_upper, far_lower], width, hidden_half)
    d_w_qkv = jnp.transpose(d_w_qkv, (1, 0, 2))
    d_b_qv, d_b_in, d_b_out, d_ln1_gain, d_ln1_bias, d_b_down, d_ln2_gain, d_ln2_bias = small

    return (
        mixed,
        d_tokens,
        d_w_qkv,
        d_b_qv,
        d_w_out,
        d_b_out,
        d_ln1_gain,
        d_ln1_bias,
        d_w_in,
        d_b_in,
        d_w_down,
        d_b_down,
        d_ln2_gain,
        d_ln2_bias,
    )


def solution(mesh):
    placed = (
        P(("dp", "tensor"), None),
        P(("dp", "tensor"), None),
        P("dp", None),
        P(None, None, "tensor"),
        P(None, "tensor"),
        P("tensor", None),
        P(),
        P(),
        P(),
        P(None, "tensor"),
        P("tensor"),
        P("tensor", None),
        P(),
        P(),
        P(),
    )
    return jax.shard_map(
        body,
        mesh=mesh,
        in_specs=placed,
        out_specs=(
            P(("dp", "tensor"), None),
            P(("dp", "tensor"), None),
            P(None, None, "tensor"),
            P(None, "tensor"),
            P("tensor", None),
            P(),
            P(),
            P(),
            P(None, "tensor"),
            P("tensor"),
            P("tensor", None),
            P(),
            P(),
            P(),
        ),
        check_vma=False,
    )
```

```python
import functools

import jax
import jax.numpy as jnp
from jax import lax
from jax.experimental import pallas as pl
from jax.experimental.pallas import tpu as pltpu
from jax.sharding import PartitionSpec as P

HEAD = 64
SPAN = 6
LANES = 128
EPSILON = 1e-05
F32 = jnp.float32
BF16 = jnp.bfloat16
GELU_A = (2.0 / 3.141592653589793) ** 0.5
GELU_B = 0.044715
ROOM_CUT, ROOM_PICK = 56, 24
HINT_GRADS, HINT_BACK = 15, 10
H = (0.2, 1, 0.5, 0.1, 0.3, 0.3, 1, 0.3, 0.3)
BYTES_US = 11_070_000
FLOPS_US = 3_459_000_000
ANYWHERE = pl.BlockSpec(memory_space=pl.ANY)
VMEM = pl.BlockSpec(memory_space=pltpu.VMEM)


class Line:
    def __init__(self):
        self.last = []

    def run(
        self, kernel, args, out_shape, grid=(), in_specs=None, out_specs=None, scratch=(), place=None,
        flops=0, moved=0, transcendentals=0, room=6, aliases=None, hint=None, after=(),
    ):
        ins, outs = len(args), len(out_shape)
        lead = 0 if place is None else 1
        after = list(after)
        if self.last and not any(arg is item for arg in args for item in self.last):
            after.append(min(self.last, key=lambda item: item.size))
        extra = len(after)
        small = min(item.size for item in out_shape) > 1 << 16

        def ordered(*refs):
            given, rest = refs[: lead + ins], refs[lead + ins + extra :]
            if small:
                rest[outs][...] = jnp.zeros((8, LANES), F32)
                rest = rest[:outs] + rest[outs + 1 :]
            kernel(*given, *rest)

        in_specs = list(in_specs or [VMEM] * ins) + [ANYWHERE] * extra
        out_specs = list(out_specs or [VMEM] * outs)
        out_shape = list(out_shape)
        if small:
            out_specs.append(pl.BlockSpec((8, LANES), lambda *at: (0, 0)) if grid else VMEM)
            out_shape.append(jax.ShapeDtypeStruct((8, LANES), F32))
        params = dict(
            out_shape=out_shape,
            compiler_params=pltpu.CompilerParams(vmem_limit_bytes=room << 20),
            cost_estimate=pl.CostEstimate(
                flops=int(flops if hint is None else hint * FLOPS_US),
                bytes_accessed=int(moved if hint is None else hint * BYTES_US),
                transcendentals=int(transcendentals if hint is None else 0),
            ),
            input_output_aliases=aliases or {},
        )
        if lead and grid:
            params["grid_spec"] = pltpu.PrefetchScalarGridSpec(
                num_scalar_prefetch=1, grid=grid, in_specs=in_specs, out_specs=out_specs, scratch_shapes=list(scratch)
            )
        else:
            if lead:
                in_specs = [pl.BlockSpec(memory_space=pltpu.SMEM)] + in_specs
            params.update(grid=grid, in_specs=in_specs, out_specs=out_specs, scratch_shapes=list(scratch))
        front = [] if place is None else [place]
        self.last = list(pl.pallas_call(ordered, **params)(*front, *args, *after))
        return self.last[:outs]


def shaped(shape, kind):
    return jax.ShapeDtypeStruct(tuple(shape), kind)


def whole(shape, once=False):
    held = dict(pipeline_mode=pl.Buffered(1)) if once else {}
    return pl.BlockSpec(shape, lambda *at: (0,) * len(shape), **held)


def flip(values, bits):
    size = lax.axis_size("dp")
    return lax.ppermute(values, "dp", [(at, at ^ bits) for at in range(size)])


def flip_tensor(values):
    return lax.ppermute(values, "tensor", [(0, 1), (1, 0)])


def flip_both(values, bits):
    size = 2 * lax.axis_size("dp")
    pairs = [(at, at ^ (2 * bits + 1)) for at in range(size)]
    return lax.ppermute(values, ("dp", "tensor"), pairs)


def dot_nt(left, right):
    return lax.dot_general(left, right, (((1,), (1,)), ((), ())), preferred_element_type=F32)


def dot_tn(left, right):
    return lax.dot_general(left, right, (((0,), (0,)), ((), ())), preferred_element_type=F32)


def mm(left, right):
    return jnp.dot(left, right, preferred_element_type=F32)


def lane_halves(rows):
    return lax.broadcasted_iota(jnp.int32, (rows, LANES), 1) < HEAD


def two_heads(block):
    low = lane_halves(block.shape[0])
    zero = jnp.zeros_like(block)
    return jnp.concatenate([jnp.where(low, block, zero), jnp.where(low, zero, block)], axis=0)


def scaled(queries):
    return queries * jnp.asarray(HEAD ** (-0.5), BF16)


def softmax_rows(scores):
    exponent = jnp.exp(scores - jnp.max(scores, axis=-1, keepdims=True))
    return exponent * (1.0 / jnp.sum(exponent, axis=-1, keepdims=True))


def attend_block(queries, keys, values):
    rows = queries.shape[0]
    probs = softmax_rows(dot_nt(two_heads(scaled(queries)), keys)).astype(BF16)
    mixed = mm(probs, values)
    return jnp.where(lane_halves(rows), mixed[:rows], mixed[rows:]).astype(BF16)


def norm_rows(values):
    average = jnp.mean(values, axis=-1, keepdims=True)
    centered = values - average
    variance = jnp.mean(centered * centered, axis=-1, keepdims=True)
    root = lax.rsqrt(variance + EPSILON)
    return centered * root, root


def norm_back(grad, unit, root, gain):
    grad_y = grad * gain
    inner = jnp.mean(grad_y, axis=-1, keepdims=True)
    along = jnp.mean(grad_y * unit, axis=-1, keepdims=True)
    return root * (grad_y - inner - unit * along)


def gelu_and_slope(values):
    square = values * values
    bent = jnp.tanh(GELU_A * values * (1.0 + GELU_B * square))
    half = 0.5 * (1.0 + bent)
    slope = half + 0.5 * values * (1.0 - bent * bent) * GELU_A * (1.0 + 3.0 * GELU_B * square)
    return values * half, slope


def gelu(values):
    return 0.5 * values * (1.0 + jnp.tanh(GELU_A * values * (1.0 + GELU_B * values * values)))


def join_kernel(count, *refs):
    rows = refs[0].shape[-2]
    for at in range(count):
        refs[count][..., at * rows : (at + 1) * rows, :] = refs[at][...]


def join(line, pieces):
    *lead, rows, columns = pieces[0].shape
    (result,) = line.run(
        functools.partial(join_kernel, len(pieces)),
        pieces,
        [shaped((*lead, rows * len(pieces), columns), pieces[0].dtype)],
        moved=4 * len(pieces) * pieces[0].size,
    )
    return result


def cut_qkv_kernel(place_ref, in_ref, out_ref, sem):
    rows = out_ref.shape[1]
    row = pl.multiple_of((place_ref[0] & 7) * rows, rows)
    copy = pltpu.make_async_copy(in_ref.at[:, pl.ds(row, rows), :], out_ref, sem)
    copy.start()
    copy.wait()


def cut_qkv(line, w_qkv, here):
    lead, rows, columns = w_qkv.shape
    (piece,) = line.run(
        cut_qkv_kernel,
        [w_qkv],
        [shaped((lead, rows // 8, columns), BF16)],
        in_specs=[ANYWHERE],
        scratch=[pltpu.SemaphoreType.DMA],
        place=here,
        moved=w_qkv.size // 2,
        room=ROOM_CUT,
    )
    return piece


def folded(rows, columns, width):
    tall = rows * columns // width
    rest, side = rows - tall, width - columns
    parts = [((0, tall, 0, columns), (0, tall, 0, columns))]
    for at in range(columns // side):
        parts.append(((at * rest, rest, columns, side), (tall, rest, at * side, side)))
    return tall, parts


def second_cut_kernel(place_ref, out_ref, in_ref, down_ref, bias_a, bias_b, *refs):
    vectors, (half, eighth, one, two, row_ref) = refs[:6], refs[6:]
    deep, width = out_ref.shape
    half[:deep, :] = out_ref[...]
    row_ref[0, :] = bias_b[...]
    left = jnp.concatenate(
        [jnp.concatenate([bias_a[0:1, :], bias_a[1:2, :]], axis=1)]
        + [row_ref[:, at : at + width] for at in range(0, row_ref.shape[1], width)],
        axis=0,
    )
    parts = []
    for _ in range(3):
        coarse = left.astype(BF16).astype(F32)
        parts.append(coarse)
        left = left - coarse
    parts.append(jnp.zeros((half.shape[0] - deep - 3 * left.shape[0], width), F32))
    half[deep:, :] = jnp.concatenate(parts, axis=0).astype(BF16)
    tall, parts = folded(*in_ref.shape, eighth.shape[1])
    for (row, high, column, wide), (top, _, side, _) in parts:
        eighth[row : row + high, column : column + wide] = in_ref[top : top + high, side : side + wide]
    eighth[tall:, :] = down_ref[...]
    for at in range(3):
        one[at, :] = vectors[at][...]
        two[at, :] = vectors[3 + at][...]


def second_cut(line, w_out, w_in, w_down, b_qv, b_in, vectors, here):
    width = w_out.shape[1]
    half, rows, deep = w_out.shape[0] // 2, w_in.shape[0] // 8, w_down.shape[0] // 8
    last = w_in.shape[1] // 4
    eighth = folded(rows, last, width)[0]
    shapes = [(half + 16, width), (eighth + deep, width), (3, width), (3, width), (1, b_in.shape[0])]
    return line.run(
        second_cut_kernel,
        [w_out, w_in, w_down, b_qv, b_in, *vectors],
        [shaped(shape, BF16 if at < 2 else F32) for at, shape in enumerate(shapes)],
        grid=(1,),
        in_specs=[
            pl.BlockSpec((half, width), lambda i, p: (p[0] & 1, 0)),
            pl.BlockSpec((rows, last), lambda i, p: (p[0] & 7, 3)),
            pl.BlockSpec((deep, width), lambda i, p: (p[0] & 7, 0)),
            whole(b_qv.shape),
            whole(b_in.shape),
            *[whole((width,)) for vector in vectors],
        ],
        out_specs=[whole(shape) for shape in shapes],
        place=here,
        moved=4 * (half + eighth + deep) * width,
        room=ROOM_CUT,
    )


def third_cut_kernel(place_ref, a, b, c, d, out_ref, in_ref, core, half, bias_a, bias_b):
    third, rows, inner = a.shape
    for at, ref in enumerate((a, b, c, d)):
        for section in range(third):
            row = (section * 4 + at) * rows
            core[row : row + rows, :] = ref[section]
    row = 4 * third * rows
    deep = out_ref.shape[0] - 16
    core[row : row + deep, :] = out_ref[:deep, :inner]
    core[row + deep :, :] = out_ref[:deep, inner:]
    half[...] = in_ref[...]
    parts = out_ref[deep:, :].astype(F32)
    width = parts.shape[1]
    count = 1 + bias_b.shape[1] // width
    total = parts[2 * count : 3 * count] + parts[count : 2 * count] + parts[:count]
    bias_a[0:1, :] = total[0:1, :inner]
    bias_a[1:2, :] = total[0:1, inner:]
    for at in range(count - 1):
        bias_b[:, at * width : (at + 1) * width] = total[1 + at : 2 + at, :]


def third_cut(line, qkv, out, w_in, here, after):
    third, rows, inner = qkv[0].shape
    height = 4 * third * rows + 2 * (out.shape[0] - 16)
    half = (w_in.shape[0] // 2, w_in.shape[1] // 4 * 3)
    shapes = [(height, inner), half, (2, inner), (1, w_in.shape[1])]
    return line.run(
        third_cut_kernel,
        [*qkv, out, w_in],
        [shaped(shape, BF16 if at < 2 else F32) for at, shape in enumerate(shapes)],
        grid=(1,),
        in_specs=[whole(item.shape) for item in [*qkv, out]]
        + [pl.BlockSpec(half, lambda i, p: (p[0] & 1, 0))],
        out_specs=[whole(shape) for shape in shapes],
        place=here,
        moved=4 * (height * inner + half[0] * half[1]),
        after=after,
    )


def first_assemble_kernel(place_ref, mine, near, qkv_ref, out_ref):
    third, width, inner = qkv_ref.shape
    rows, half = width // 8, out_ref.shape[0] // 2
    for core, ref in enumerate((mine, near)):
        for at in range(4):
            row = pl.multiple_of(((place_ref[0] ^ (2 * at + core)) & 7) * rows, rows)
            for section in range(third):
                start = (section * 4 + at) * rows
                qkv_ref[section, pl.ds(row, rows), :] = ref[start : start + rows, :]
        row = pl.multiple_of(((place_ref[0] ^ core) & 1) * half, half)
        start = 4 * third * rows
        out_ref[pl.ds(row, half), :inner] = ref[start : start + half, :]
        out_ref[pl.ds(row, half), inner:] = ref[start + half :, :]


def first_assemble(line, mine, near, width, inner, here):
    return line.run(
        first_assemble_kernel,
        [mine, near],
        [shaped((3, width, inner), BF16), shaped((inner, width), BF16)],
        place=here,
        moved=8 * mine.size,
    )


def fourth_cut_kernel(a, b, c, d, half_ref, eighths, half):
    rows = a.shape[0]
    for at, ref in enumerate((a, b, c, d)):
        eighths[at * rows : (at + 1) * rows, :] = ref[...]
    half[...] = half_ref[...]


def fourth_cut(line, eighths, half):
    rows, width = eighths[0].shape
    return line.run(
        fourth_cut_kernel,
        [*eighths, half],
        [shaped((4 * rows, width), BF16), shaped(half.shape, BF16)],
        moved=16 * rows * width,
    )


def second_assemble_kernel(place_ref, mine, near, half_mine, half_near, in_ref, down_ref):
    width = mine.shape[1]
    wide, last = half_mine.shape[1], in_ref.shape[1] - half_mine.shape[1]
    rows, deep, half = in_ref.shape[0] // 8, down_ref.shape[0] // 8, half_mine.shape[0]
    tall, parts = folded(rows, last, width)
    for core, (ref, half_ref) in enumerate(((mine, half_mine), (near, half_near))):
        for at in range(4):
            block = (place_ref[0] ^ (2 * at + core)) & 7
            start = at * (tall + deep)
            for (row, high, column, side), (top, _, left, _) in parts:
                to = pl.multiple_of(block * rows + top, 16)
                in_ref[pl.ds(to, high), wide + left : wide + left + side] = ref[
                    start + row : start + row + high, column : column + side
                ]
            down_ref[pl.ds(pl.multiple_of(block * deep, deep), deep), :] = ref[
                start + tall : start + tall + deep, :
            ]
        row = pl.multiple_of(((place_ref[0] ^ core) & 1) * half, half)
        in_ref[pl.ds(row, half), :wide] = half_ref[...]


def second_assemble(line, mine, near, half_mine, half_near, hidden, here):
    width = mine.shape[1]
    return line.run(
        second_assemble_kernel,
        [mine, near, half_mine, half_near],
        [shaped((width, hidden), BF16), shaped((hidden, width), BF16)],
        place=here,
        moved=8 * width * hidden,
    )


def project_kernel(tok_ref, few_ref, w_ref, bias_ref, k_ref, v_ref, q_ref, ctx_ref):
    tok = tok_ref[...]
    k_ref[...] = mm(tok, w_ref[1]).astype(BF16)
    v_ref[...] = (mm(tok, w_ref[2]) + bias_ref[1:2, :]).astype(BF16)
    q_ref[...] = (mm(few_ref[...], w_ref[0]) + bias_ref[0:1, :]).astype(BF16)
    for at in range(0, k_ref.shape[1], LANES):
        cut = slice(at, at + LANES)
        ctx_ref[:, cut] = attend_block(q_ref[:, cut], k_ref[:, cut], v_ref[:, cut])


def project(line, tokens, few, weights, bias, seqs):
    rows, width = tokens.shape
    inner = weights.shape[2]
    length, slots = rows // seqs, few.shape[0] // seqs
    long, short = (pl.BlockSpec((size, inner), lambda s: (s, 0)) for size in (length, slots))
    return line.run(
        project_kernel,
        [tokens, few, weights, bias],
        [shaped((rows, inner), BF16)] * 2 + [shaped((few.shape[0], inner), BF16)] * 2,
        grid=(seqs,),
        in_specs=[
            pl.BlockSpec((length, width), lambda s: (s, 0)),
            pl.BlockSpec((slots, width), lambda s: (s, 0)),
            whole(weights.shape),
            whole(bias.shape),
        ],
        out_specs=[long, long, short, short],
        flops=6 * rows * width * inner,
        room=16,
        moved=2 * (rows * width + 3 * width * inner + 2 * rows * inner),
    )


def first_norm_kernel(ctx_a, ctx_b, w_a, w_b, few_ref, vec_ref, sum_ref, low_ref):
    branch = mm(ctx_a[...], w_a[...]) + mm(ctx_b[...], w_b[...]) + vec_ref[0:1, :]
    total = few_ref[...].astype(F32) + branch
    sum_ref[...] = total
    low_ref[...] = (norm_rows(total)[0] * vec_ref[1:2, :] + vec_ref[2:3, :]).astype(BF16)


def first_norm(line, contexts, w_out, few, vectors):
    count, width = few.shape
    return line.run(
        first_norm_kernel,
        [*contexts, *w_out, few, vectors],
        [shaped((count, width), F32), shaped((count, width), BF16)],
        flops=2 * count * width * width,
        moved=2 * width * width + 14 * count * width,
    )


def ffn_part_kernel(low_ref, wi_ref, bi_ref, wd_ref, slope_ref, part_ref, total):
    step = pl.program_id(0)
    gate, slope = gelu_and_slope(mm(low_ref[...], wi_ref[...]) + bi_ref[...])
    slope_ref[...] = slope
    part = mm(gate.astype(BF16), wd_ref[...])

    @pl.when(step == 0)
    def _():
        total[...] = part

    @pl.when(step > 0)
    def _():
        total[...] += part

    @pl.when(step == pl.num_programs(0) - 1)
    def _():
        part_ref[...] = total[...]


def ffn_part(line, low, w_in, b_in, w_down):
    count, width = low.shape
    hidden = w_in.shape[1]
    steps = 4
    tile = hidden // steps
    flat = whole((count, width))
    return line.run(
        ffn_part_kernel,
        [low, w_in, b_in, w_down],
        [shaped((count, hidden), F32), shaped((count, width), F32)],
        grid=(steps,),
        in_specs=[
            flat,
            pl.BlockSpec((width, tile), lambda j: (0, j)),
            pl.BlockSpec((1, tile), lambda j: (0, j)),
            pl.BlockSpec((tile, width), lambda j: (j, 0)),
        ],
        out_specs=[pl.BlockSpec((count, tile), lambda j: (0, j)), flat],
        scratch=[pltpu.VMEM((count, width), F32)],
        flops=4 * count * width * hidden,
        moved=4 * width * hidden,
        transcendentals=count * hidden,
        room=12,
    )


def column_sum(values):
    return jnp.sum(values, axis=0, keepdims=True)


def ffn_last_kernel(
    low_ref, part_ref, sum_ref, grad_ref, one_ref, two_ref, wi_ref, bi_ref, wd_ref,
    g_ffn_ref, g_second_ref, slope_ref, sums_ref,
):
    gate, slope = gelu_and_slope(mm(low_ref[...], wi_ref[...]) + bi_ref[...])
    slope_ref[...] = slope
    ffn = part_ref[...] + mm(gate.astype(BF16), wd_ref[...]) + two_ref[0:1, :]
    normed = norm_rows(sum_ref[...])[0] * one_ref[1:2, :] + one_ref[2:3, :]
    unit, root = norm_rows(normed + ffn)
    grad = grad_ref[...]
    g_second = norm_back(grad, unit, root, two_ref[1:2, :])
    g_ffn = g_second.astype(BF16)
    g_ffn_ref[...] = g_ffn
    g_second_ref[...] = g_second
    sums = (column_sum(g_ffn.astype(F32)), column_sum(grad * unit), column_sum(grad))
    sums_ref[...] = jnp.concatenate([*sums, jnp.zeros((5, grad.shape[1]), F32)], axis=0)


def ffn_last(line, low, part, total, grad, one, two, w_in, b_in, w_down):
    count, width = low.shape
    hidden = w_in.shape[1]
    return line.run(
        ffn_last_kernel,
        [low, part, total, grad, one, two, w_in, b_in, w_down],
        [
            shaped((count, width), BF16),
            shaped((count, width), F32),
            shaped((count, hidden), F32),
            shaped((8, width), F32),
        ],
        flops=4 * count * width * hidden,
        moved=4 * width * hidden,
        room=12,
    )


def ffn_back_kernel(
    g_ffn_ref, g_second_ref, sum_ref, one_ref, sums_ref, slope_a, slope_b, wi_a, wi_b, wd_a, wd_b,
    g_branch_ref, g_first_ref, small_ref,
):
    g_ffn, g_normed = g_ffn_ref[...], g_second_ref[...]
    width = g_normed.shape[1]
    half = width // 2
    deep = slope_a.shape[1] // half
    for at, (slope, w_in, w_down) in enumerate(((slope_a, wi_a, wd_a), (slope_b, wi_b, wd_b))):
        g_pre = (slope[...] * dot_nt(g_ffn, w_down[...])).astype(BF16)
        bias = column_sum(g_pre.astype(F32))
        for row in range(deep):
            small_ref[at * deep + row : at * deep + row + 1, :] = bias[:, row * half : (row + 1) * half]
        g_normed = g_normed + dot_nt(g_pre, w_in[...])
    unit, root = norm_rows(sum_ref[...])
    g_first = norm_back(g_normed, unit, root, one_ref[1:2, :])
    g_branch = g_first.astype(BF16)
    g_first_ref[...] = g_first
    g_branch_ref[...] = g_branch
    vectors = (
        column_sum(g_branch.astype(F32)),
        column_sum(g_normed * unit),
        column_sum(g_normed),
        *[sums_ref[at : at + 1, :] for at in range(3)],
    )
    for at, vector in enumerate(vectors):
        row = 2 * deep + 2 * at
        small_ref[row : row + 1, :] = vector[:, :half]
        small_ref[row + 1 : row + 2, :] = vector[:, half:]
    count = 2 * deep + 12
    small_ref[count:, :] = jnp.zeros((small_ref.shape[0] - count, half), F32)


def ffn_back(line, g_ffn, g_second, total, one, sums, slopes, w_in, w_down):
    count, width = g_ffn.shape
    hidden = w_in[0].shape[1]
    rows = 2 * (hidden // (width // 2)) + 12
    return line.run(
        ffn_back_kernel,
        [g_ffn, g_second, total, one, sums, *slopes, *w_in, *w_down],
        [
            shaped((count, width), BF16),
            shaped((count, width), F32),
            shaped((-(-rows // 8) * 8, width // 2), F32),
        ],
        flops=8 * count * width * hidden,
        moved=8 * width * hidden,
        room=12,
    )


def ffn_grads_kernel(place_ref, wi_ref, wd_ref, bi_ref, *refs):
    normed_refs, grad_refs = refs[:2], refs[2:4]
    keep_down, send_down, keep_in, send_in = refs[4:8]
    down, up = refs[8:]
    width = normed_refs[0].shape[1]
    tile = wi_ref.shape[1] // 4
    hidden = pl.ds(pl.multiple_of((place_ref[0] >> 2) * tile, tile), tile)
    w_in, w_down, b_in = wi_ref[:, hidden], wd_ref[hidden, :], bi_ref[:, hidden]
    for at in range(2):
        normed, grad = normed_refs[at][...], grad_refs[at][...]
        gate, slope = gelu_and_slope(mm(normed, w_in) + b_in)
        pre = (slope * dot_nt(grad, w_down)).astype(BF16)
        down_part = dot_tn(gate.astype(BF16), grad)
        up_part = dot_tn(normed, pre)
        if at == 0:
            down[...] = down_part
            up[...] = up_part
        else:
            down[...] += down_part
            up[...] += up_part
    down_rows, up_rows = tile // 4, width // 4
    half = width // 2
    for slot in range(4):
        block = slot ^ (place_ref[0] & 3)
        low = down[pl.ds(pl.multiple_of(block * down_rows, down_rows), down_rows), :]
        block = (0, 2, 1, 3)[slot] ^ (place_ref[0] & 3)
        high = up[pl.ds(pl.multiple_of(block * up_rows, up_rows), up_rows), :]
        to_down, to_in = (keep_down, keep_in) if slot < 2 else (send_down, send_in)
        kind = to_down.dtype
        to_down[slot % 2, :down_rows, :] = low[:, :half].astype(kind)
        to_down[slot % 2, down_rows:, :] = low[:, half:].astype(kind)
        to_in[slot % 2, :, :] = high.astype(kind)


def ffn_grads(line, place, w_in, w_down, b_in, normed, grads):
    rows, width = normed[0].shape
    tile = w_in.shape[1] // 4
    shape = (2, 2 * (tile // 4), width // 2)
    wide = (2, width // 4, tile)
    return line.run(
        ffn_grads_kernel,
        [w_in, w_down, b_in, *normed, *grads],
        [shaped(shape, F32), shaped(shape, BF16), shaped(wide, F32), shaped(wide, BF16)],
        scratch=[pltpu.VMEM((tile, width), F32), pltpu.VMEM((width, tile), F32)],
        place=place,
        flops=16 * rows * width * tile,
        moved=12 * rows * width + 16 * width * tile,
        hint=HINT_GRADS,
        room=16,
    )


def attend_back_kernel(
    seqs, half, deep, place_ref, q_ref, k_ref, v_ref, g_branch_ref, w_out_ref, ctx_ref, tok_t_ref, few_ref,
    small_ref, dq_ref, dkv_ref, keep_ref, send_ref, total, little,
):
    few, inner = q_ref.shape
    rows = k_ref.shape[0]
    slots, length = few // seqs, rows // seqs
    low = lane_halves(slots)
    scale = HEAD ** (-0.5)
    g_branch = g_branch_ref[...]
    g_context = dot_nt(g_branch, w_out_ref[...]).astype(BF16)
    for seq in range(seqs):
        short, long = slice(seq * slots, (seq + 1) * slots), slice(seq * length, (seq + 1) * length)
        for at in range(0, inner, LANES):
            cut = slice(at, at + LANES)
            both, grads = two_heads(scaled(q_ref[short, cut])), two_heads(g_context[short, cut])
            keys, values = k_ref[long, cut], v_ref[long, cut]
            probs = softmax_rows(dot_nt(both, keys))
            grad_probs = dot_nt(grads, values)
            dkv_ref[long, inner + at : inner + at + LANES] = dot_tn(probs.astype(BF16), grads).astype(BF16)
            row_total = jnp.sum(grad_probs * probs, axis=-1, keepdims=True)
            grad_scores = (probs * (grad_probs - row_total)).astype(BF16)
            dq = mm(grad_scores, keys) * scale
            dq_ref[short, cut] = jnp.where(low, dq[:slots], dq[slots:]).astype(BF16)
            dkv_ref[long, cut] = dot_tn(grad_scores, both).astype(BF16)
    dq, dkv = dq_ref[...], dkv_ref[...]
    total[0] = dot_tn(few_ref[...], dq)
    both = mm(tok_t_ref[...], dkv)
    total[1] = both[:, :inner]
    total[2] = both[:, inner:]
    out_grad = dot_tn(ctx_ref[...], g_branch)
    total[3, :inner, :] = out_grad[:, :inner]
    total[3, inner:, :] = out_grad[:, inner:]
    little[...] = jnp.zeros_like(little)
    little[0, 0:1, :] = column_sum(dq.astype(F32))
    little[0, 1:2, :] = column_sum(dkv[:, inner:].astype(F32))
    for at in range(deep + 12):
        source = half * deep + at if at < deep else deep + at
        little[1 + at // 2, at % 2 : at % 2 + 1, :] = small_ref[source : source + 1, :]
    block_rows = total.shape[1] // 16
    pad = keep_ref.shape[1] - 4 * block_rows
    for slot in range(16):
        block = slot ^ place_ref[0]
        row = pl.multiple_of(block * block_rows, block_rows)
        to, kind = (keep_ref, F32) if slot < 8 else (send_ref, BF16)
        for section in range(4):
            cut = slice(section * block_rows, (section + 1) * block_rows)
            to[slot % 8, cut, :] = total[section, pl.ds(row, block_rows), :].astype(kind)
        pair = jnp.concatenate([little[block], jnp.zeros((pad - 8, inner), F32)], axis=0)
        to[slot % 8, 4 * block_rows :, :] = pair.astype(kind)


def attend_back(line, place, queries, keys, values, g_branch, w_out, context, tokens_t, few, small, seqs, half, deep):
    rows, inner = keys.shape
    width = tokens_t.shape[0]
    count = queries.shape[0]
    held = (8, 4 * (width // 16) + 16, inner)
    return line.run(
        functools.partial(attend_back_kernel, seqs, half, deep),
        [queries, keys, values, g_branch, w_out, context, tokens_t, few, small],
        [
            shaped((count, inner), BF16),
            shaped((rows, 2 * inner), BF16),
            shaped(held, F32),
            shaped(held, BF16),
        ],
        scratch=[pltpu.VMEM((4, width, inner), F32), pltpu.VMEM((16, 8, inner), F32)],
        place=place,
        hint=HINT_BACK,
        room=16,
        flops=4 * rows * width * inner + 24 * count * rows * inner,
        moved=20 * rows * inner,
    )


def sum_all_kernel(count, keep_ref, *refs):
    row = 0
    for ref in refs[:count]:
        part = slice(row, row + ref.shape[0])
        refs[count][part] = (keep_ref[part].astype(F32) + ref[...].astype(F32)).astype(BF16)
        row += ref.shape[0]


def sum_all(line, hint, keep, *arrived):
    (result,) = line.run(
        functools.partial(sum_all_kernel, len(arrived)), [keep, *arrived], [shaped(keep.shape, BF16)], hint=hint
    )
    return result


def sum_split_kernel(mine_ref, near_ref, upper, lower):
    rows = upper.shape[1]
    for slot in range(2):
        total = (mine_ref[slot].astype(F32) + near_ref[1 - slot].astype(F32)).astype(BF16)
        upper[slot] = total[:rows, :]
        lower[slot] = total[rows:, :]


def sum_split(line, hint, mine, near, rows):
    count, height, inner = mine.shape
    shapes = [shaped((count, rows, inner), BF16), shaped((count, height - rows, inner), BF16)]
    return line.run(sum_split_kernel, [mine, near], shapes, hint=hint)


def second_fold_kernel(down, down_near, up, up_near, down_out, up_keep, up_send):
    down_out[...] = (down[...] + down_near[...].astype(F32)).astype(BF16)
    total = up[...] + up_near[...].astype(F32)
    middle = total.shape[0] // 2
    up_keep[...] = total[:middle]
    up_send[...] = total[middle:].astype(BF16)


def second_fold(line, down, down_near, up, up_near, hint):
    half = (up.shape[0] // 2, *up.shape[1:])
    return line.run(
        second_fold_kernel,
        [down, down_near, up, up_near],
        [shaped(down.shape, BF16), shaped(half, F32), shaped(half, BF16)],
        hint=hint,
    )


def third_fold_kernel(down, down_near, up, up_near, down_out, up_out):
    for slot in range(2):
        down_out[slot] = (down[slot].astype(F32) + down_near[1 - slot].astype(F32)).astype(BF16)
    count = up.shape[0]
    up_out[:count] = up[...]
    up_out[count:] = up_near[...]


def third_fold(line, down, down_near, up, up_near, hint):
    shapes = [shaped(down.shape, BF16), shaped((2 * up.shape[0], *up.shape[1:]), BF16)]
    return line.run(third_fold_kernel, [down, down_near, up, up_near], shapes, hint=hint)


def append_kernel(count, *refs):
    groups, out = refs[:-count], refs[-count:]
    each = len(groups) // count
    for at in range(count):
        row = 0
        for ref in groups[at * each : (at + 1) * each]:
            out[at][row : row + ref.shape[0]] = ref[...]
            row += ref.shape[0]


def append(line, hint, *groups):
    shapes = [shaped((sum(item.shape[0] for item in group), *group[0].shape[1:]), BF16) for group in groups]
    return line.run(
        functools.partial(append_kernel, len(groups)),
        [item for group in groups for item in group],
        shapes,
        hint=hint,
    )


def cross_one_kernel(oth, oth_near, own, own_near, x_send, y_send, x_keep, y_keep_own, y_keep_oth):
    rows = x_send.shape[1]
    half = oth.shape[0] // 2
    x_send[...] = (oth[:, :rows, :] + oth_near[:, :rows, :].astype(F32)).astype(BF16)
    x_keep[...] = own[:, :rows, :] + own_near[:, :rows, :].astype(F32)
    for at, (keep, near, out) in enumerate(((own, own_near, y_keep_own), (oth, oth_near, y_keep_oth))):
        total = keep[:, rows:, :] + near[:, rows:, :].astype(F32)
        out[...] = total[:half]
        y_send[at] = total[half:].astype(BF16)


def cross_one(line, oth, oth_near, own, own_near, rows):
    count, height, inner = oth.shape
    half, last = count // 2, height - rows
    return line.run(
        cross_one_kernel,
        [oth, oth_near, own, own_near],
        [
            shaped((count, rows, inner), BF16),
            shaped((2, half, last, inner), BF16),
            shaped((count, rows, inner), F32),
            shaped((half, last, inner), F32),
            shaped((half, last, inner), F32),
        ],
        hint=2,
    )


def cross_two_kernel(x_keep, x_near, own, oth, y_near, y_send, x_send, first, last):
    half = own.shape[0]
    total = x_keep[...] + x_near[...].astype(F32)
    first[...] = total[:half]
    y_send[...] = total[half:].astype(BF16)
    total = own[...] + y_near[0].astype(F32)
    small = total.shape[1] - 16
    last[:, :small, :] = total[:, :small, :]
    last[:, small:, :] = total[:, small:, :].astype(BF16).astype(F32)
    x_send[...] = (oth[...] + y_near[1].astype(F32)).astype(BF16)


def cross_two(line, x_keep, x_near, own, oth, y_near, hint):
    half = (own.shape[0], x_keep.shape[1], x_keep.shape[2])
    return line.run(
        cross_two_kernel,
        [x_keep, x_near, own, oth, y_near],
        [shaped(half, BF16), shaped(own.shape, BF16), shaped(half, F32), shaped(own.shape, F32)],
        hint=hint,
    )


def cross_three_kernel(first, y_near, last, x_near, keep, *sends):
    rows, half = first.shape[1], first.shape[0] // 2
    for ref, near, cut in ((first, y_near, slice(0, rows)), (last, x_near, slice(rows, None))):
        total = ref[...] + near[...].astype(F32)
        keep[:, cut, :] = total[:half]
        for at, send in enumerate(sends):
            send[:, cut, :] = total[half + at : half + at + 1].astype(BF16)


def cross_three(line, first, y_near, last, x_near, hint):
    half, height, inner = first.shape[0] // 2, first.shape[1] + last.shape[1], first.shape[2]
    return line.run(
        cross_three_kernel,
        [first, y_near, last, x_near],
        [shaped((half, height, inner), F32)] + [shaped((1, height, inner), BF16)] * half,
        hint=hint,
    )


def unpack_attend_kernel(place_ref, *refs):
    blocks, (qkv_ref, out_ref), (wide, little, sems) = refs[:4], refs[4:6], refs[-3:]
    outs = refs[6:-3]
    inner = qkv_ref.shape[2]
    rows = qkv_ref.shape[1] // 16
    copies = []

    def place_rows(source, to):
        copy = pltpu.make_async_copy(source, to, sems.at[len(copies)])
        copy.start()
        copies.append(copy)

    for slot in range(16):
        core, at = slot // 8, slot % 8
        block = slot ^ place_ref[0]
        wide[slot, : 2 * rows, :] = blocks[2 * core][at].astype(F32)
        row = pl.multiple_of(block * rows, rows)
        for section in range(2):
            place_rows(wide.at[slot, pl.ds(section * rows, rows), :], qkv_ref.at[section, pl.ds(row, rows), :])
        block = ((at & 1) + (at & 2) * 2 + (at >> 2) * 2 + 8 * core) ^ place_ref[0]
        values = blocks[2 * core + 1][at].astype(F32)
        wide[slot, 2 * rows :, :] = values[: 2 * rows, :]
        little[block] = values[2 * rows : 2 * rows + 8, :]
        row = pl.multiple_of(block * rows, rows)
        place_rows(wide.at[slot, pl.ds(2 * rows, rows), :], qkv_ref.at[2, pl.ds(row, rows), :])
        row = pl.multiple_of((block & 7) * rows, rows)
        column = pl.multiple_of((block >> 3) * inner, inner)
        place_rows(wide.at[slot, pl.ds(3 * rows, rows), :], out_ref.at[pl.ds(row, rows), pl.ds(column, inner)])
    outs[0][...] = little[0, 0:2, :]
    row = 2
    for out in outs[1:]:
        for at in range(out.shape[0] // inner):
            out[pl.ds(at * inner, inner)] = little[row // 2, row % 2, :]
            row += 1
    for copy in copies:
        copy.wait()


def unpack_attend(line, place, blocks, width, hidden):
    inner = blocks[0].shape[2]
    rows = width // 16
    small = [(2, inner), (hidden,)] + [(width,)] * 6
    return line.run(
        unpack_attend_kernel,
        blocks,
        [shaped((3, width, inner), F32), shaped((inner, width), F32)] + [shaped(shape, F32) for shape in small],
        out_specs=[ANYWHERE] * 2 + [VMEM] * 8,
        scratch=[
            pltpu.VMEM((16, 4 * rows, inner), F32),
            pltpu.VMEM((16, 8, inner), F32),
            pltpu.SemaphoreType.DMA((64,)),
        ],
        place=place,
        room=20,
        hint=1,
    )


def unpack_ffn_kernel(first, place_ref, *refs):
    down_in, up_in = refs[:2]
    down_ref, in_ref, down, up, sems = refs[-5:]
    rows, half = down_ref.shape[0] // 16, down_ref.shape[1] // 2
    deep, wide = in_ref.shape[0] // 4, in_ref.shape[1] // 4
    copies = []

    def place_rows(source, to):
        copy = pltpu.make_async_copy(source, to, sems.at[len(copies)])
        copy.start()
        copies.append(copy)

    for slot in range(8):
        block = (slot if first else slot + 8) ^ place_ref[0]
        down[slot, :, :half] = down_in[slot, :rows, :].astype(F32)
        down[slot, :, half:] = down_in[slot, rows:, :].astype(F32)
        row = pl.multiple_of(block * rows, rows)
        place_rows(down.at[slot], down_ref.at[pl.ds(row, rows), :])
        block = ((slot & 1) + (slot & 2) * 2 + (slot >> 2) * 2 + (0 if first else 8)) ^ place_ref[0]
        up[slot] = up_in[slot].astype(F32)
        row = pl.multiple_of((block & 3) * deep, deep)
        column = pl.multiple_of((block >> 2) * wide, wide)
        place_rows(up.at[slot], in_ref.at[pl.ds(row, deep), pl.ds(column, wide)])
    for copy in copies:
        copy.wait()


def unpack_ffn(line, place, down, up, width, hidden, before=None):
    return line.run(
        functools.partial(unpack_ffn_kernel, before is None),
        [down, up, *(before or [])],
        [shaped((hidden, width), F32), shaped((width, hidden), F32)],
        in_specs=[VMEM] * 2 + [ANYWHERE] * (0 if before is None else 2),
        out_specs=[ANYWHERE] * 2,
        scratch=[
            pltpu.VMEM((8, hidden // 16, width), F32),
            pltpu.VMEM((8, width // 4, hidden // 4), F32),
            pltpu.SemaphoreType.DMA((16,)),
        ],
        aliases={} if before is None else {3: 0, 4: 1},
        place=place,
        moved=6 * width * hidden,
        room=20,
        hint=1,
    )


def attend_kernel(tok_ref, w_ref, bias_ref, k_ref, v_ref, out_ref):
    rows, inner = out_ref.shape
    low = lane_halves(rows)
    queries = scaled((mm(tok_ref[...], w_ref[0]) + bias_ref[0:1, :]).astype(BF16))
    for at in range(0, inner, LANES):
        cut = slice(at, at + LANES)
        block, keys, values = queries[:, cut], k_ref[:, cut], v_ref[:, cut]
        zero, one = jnp.zeros_like(block), jnp.ones_like(values)
        mixed = []
        for first in (True, False):
            head = jnp.where(low == first, block, zero)
            with_sums = jnp.where(lane_halves(values.shape[0]) == first, values, one)
            scores = dot_nt(head, keys)
            exponent = jnp.exp(scores - jnp.max(scores, axis=-1, keepdims=True)).astype(BF16)
            mixed.append(mm(exponent, with_sums))
        top = jnp.where(low, mixed[0], mixed[1])
        total = jnp.where(low, mixed[1], mixed[0])
        out_ref[:, cut] = (top / pltpu.roll(total, HEAD, 1)).astype(BF16)


def attend(line, tokens, weights, bias, keys, values, seqs, seq, hint=None):
    rows, width = tokens.shape
    inner = keys.shape[1]
    length = rows // seqs
    long = pl.BlockSpec((length, inner), lambda s: (seq, 0))
    (result,) = line.run(
        attend_kernel,
        [tokens, weights, bias, keys, values],
        [shaped((length, inner), BF16)],
        grid=(1,),
        in_specs=[
            pl.BlockSpec((length, width), lambda s: (seq, 0)),
            pl.BlockSpec((1, width, inner), lambda s: (0, 0, 0)),
            whole(bias.shape),
            long,
            long,
        ],
        out_specs=[pl.BlockSpec((length, inner), lambda s: (0, 0))],
        flops=2 * length * width * inner + 16 * length * length * inner,
        moved=2 * (length * width + width * inner + 3 * length * inner),
        transcendentals=length * length * inner // HEAD,
        room=16,
        hint=hint,
    )
    return result


def layer_kernel(
    tok_ref, ctx_a, ctx_b, wo_a, wo_b, wi_a, wi_b, bi_a, bi_b, wd_a, wd_b, one_ref, two_ref, out_ref,
):
    branch = mm(ctx_a[...], wo_a[...]) + mm(ctx_b[...], wo_b[...]) + one_ref[0:1, :]
    unit, _ = norm_rows(tok_ref[...].astype(F32) + branch)
    normed = unit * one_ref[1:2, :] + one_ref[2:3, :]
    low = normed.astype(BF16)
    total = normed + two_ref[0:1, :]
    for w_in, b_in, w_down in ((wi_a, bi_a, wd_a), (wi_b, bi_b, wd_b)):
        hidden = gelu(mm(low, w_in[...]) + b_in[...]).astype(BF16)
        total = total + mm(hidden, w_down[...])
    unit, _ = norm_rows(total)
    out_ref[...] = (unit * two_ref[1:2, :] + two_ref[2:3, :]).astype(BF16)


def layer_next_kernel(*refs):
    layer_kernel(*refs[:-2], refs[-1])


def layer(line, tokens, contexts, w_out, w_in, b_in, w_down, one, two, seq, mixed, hint):
    length, inner = contexts[0].shape
    width, hidden = tokens.shape[1], w_in[0].shape[1]
    tile = 256
    steps = length // tile
    ctx = pl.BlockSpec((tile, inner), lambda i: (i, 0))
    still = [*w_out, *w_in, *b_in, *w_down, one, two]
    row = pl.BlockSpec((tile, width), lambda i: (seq * steps + i, 0))
    args = [tokens, *contexts, *still]
    specs = [row, ctx, ctx] + [whole(item.shape, True) for item in still]
    (result,) = line.run(
        layer_kernel if mixed is None else layer_next_kernel,
        args if mixed is None else [*args, mixed],
        [shaped(tokens.shape, BF16)],
        grid=(steps,),
        in_specs=specs if mixed is None else [*specs, ANYWHERE],
        out_specs=[row],
        aliases={} if mixed is None else {len(args): 0},
        room=30,
        hint=hint,
        flops=2 * length * width * (width + 4 * hidden),
        moved=4 * width * (length + 2 * hidden),
        transcendentals=2 * length * hidden,
    )
    return result


def input_grad_kernel(
    dkv_a, dkv_b, dq_a, dq_b, w_a, w_b, g_first_ref, places_ref, out_ref
):
    length = out_ref.shape[0]
    slots = g_first_ref.shape[0]
    few = g_first_ref[...] + dot_nt(dq_a[...], w_a[0]) + dot_nt(dq_b[...], w_b[0])
    coarse = few.astype(BF16)
    fine = (few - coarse.astype(F32)).astype(BF16)
    picks = places_ref[0][:, 0:1] == lax.broadcasted_iota(jnp.int32, (slots, length), 1)
    picks = picks.astype(F32).astype(BF16)
    total = dot_tn(picks, coarse) + dot_tn(picks, fine)
    for dkv, w in ((dkv_a, w_a), (dkv_b, w_b)):
        inner = w.shape[2]
        total = total + dot_nt(dkv[:, :inner], w[1]) + dot_nt(dkv[:, inner:], w[2])
    out_ref[...] = total


def input_grad_next_kernel(*refs):
    input_grad_kernel(*refs[:-2], refs[-1])


def input_grad(line, backs, weights, g_first, places, seqs, seq, before):
    rows, inner = backs[0][1].shape[0], backs[0][0].shape[1]
    width = g_first.shape[1]
    length, slots = rows // seqs, g_first.shape[0] // seqs
    long = pl.BlockSpec((length, 2 * inner), lambda i: (seq, 0))
    short = pl.BlockSpec((slots, inner), lambda i: (seq, 0))
    args = [
        backs[0][1], backs[1][1], backs[0][0], backs[1][0],
        *weights, g_first, places,
    ]
    specs = (
        [long] * 2
        + [short] * 2
        + [whole(w.shape, True) for w in weights]
        + [
            pl.BlockSpec((slots, width), lambda i: (seq, 0)),
            pl.BlockSpec((1, slots, LANES), lambda i: (seq, 0, 0)),
        ]
    )
    (result,) = line.run(
        input_grad_kernel if before is None else input_grad_next_kernel,
        args if before is None else [*args, before],
        [shaped((rows, width), F32)],
        grid=(1,),
        in_specs=specs if before is None else [*specs, ANYWHERE],
        out_specs=[pl.BlockSpec((length, width), lambda i: (seq, 0))],
        aliases={} if before is None else {len(args): 0},
        flops=10 * length * width * inner,
        moved=20 * width * inner + 8 * length * width,
        room=24,
        hint=0.1,
    )
    return result


def pick_kernel(seqs, half_ref, starts_ref, tok_ref, grad_ref, few_ref, grad_few_ref, turned_ref, places_ref):
    slots, length = few_ref.shape[0], tok_ref.shape[0]
    spans = starts_ref.shape[1]
    seq = half_ref[0] * seqs + pl.program_id(0)
    starts = [starts_ref[seq, at] for at in range(spans)]
    row = lax.broadcasted_iota(jnp.int32, (slots, LANES), 0)
    places = row + starts[0]
    for at in range(1, spans):
        places = places + jnp.where(row >= SPAN * at, starts[at] - starts[at - 1] - SPAN, 0)
    fresh = row < SPAN * spans
    for at, start in enumerate(starts):
        covered = (places >= start) & (places < start + SPAN) & (row >= SPAN * (at + 1))
        fresh = fresh & jnp.logical_not(covered)
    places_ref[0] = places
    wide = jnp.concatenate([places] * (length // LANES), axis=1)
    picks = wide == lax.broadcasted_iota(jnp.int32, (slots, length), 1)
    picks = picks.astype(F32).astype(BF16)
    few_ref[...] = mm(picks, tok_ref[...]).astype(BF16)
    grad_few_ref[...] = mm(picks, grad_ref[...]) * fresh.astype(F32)[:, 0:1]
    turned_ref[...] = tok_ref[...].T


def pick(line, half, starts, slots, tokens, grads, seqs, after):
    rows, width = tokens.shape
    length = rows // seqs
    long = pl.BlockSpec((length, width), lambda s, p: (s, 0))
    short = pl.BlockSpec((slots, width), lambda s, p: (s, 0))
    return line.run(
        functools.partial(pick_kernel, seqs),
        [starts, tokens, grads],
        [
            shaped((seqs * slots, width), BF16),
            shaped((seqs * slots, width), F32),
            shaped((width, rows), BF16),
            shaped((seqs, slots, LANES), jnp.int32),
        ],
        grid=(seqs,),
        in_specs=[pl.BlockSpec(memory_space=pltpu.SMEM), long, long],
        out_specs=[
            short, short, pl.BlockSpec((width, length), lambda s, p: (0, s)),
            pl.BlockSpec((1, slots, LANES), lambda s, p: (s, 0, 0)),
        ],
        place=half,
        flops=4 * rows * slots * width,
        moved=6 * rows * width,
        room=ROOM_PICK,
        after=after,
    )


def body(
    tokens,
    grad_values,
    span_starts,
    w_qkv,
    b_qv,
    w_out,
    b_out,
    ln1_gain,
    ln1_bias,
    w_in,
    b_in,
    w_down,
    b_down,
    ln2_gain,
    ln2_bias,
):
    rows, width = tokens.shape
    inner = w_qkv.shape[2]
    hidden_half = w_in.shape[1]
    halves = lax.axis_size("tensor")
    seqs = span_starts.shape[0] // halves
    spans = span_starts.shape[1]
    length = rows // seqs
    half_at = lax.axis_index("tensor")
    me = lax.axis_index("dp")
    bits = lax.axis_size("dp").bit_length() - 1
    block_at = ((me & 1) << 3) | ((me & 2) << 1) | ((me & 4) >> 1) | ((me & 8) >> 3)
    place = block_at.reshape(1).astype(jnp.int32)
    rest = [1 << bit for bit in range(4, bits)]

    slots = -(-spans * SPAN // 16) * 16
    here = me.reshape(1)
    line = Line()

    w_qkv_own = jnp.transpose(w_qkv, (1, 0, 2))

    def chips_around(held):
        return [held, flip(held, 2), flip(held, 4), flip(held, 6)]

    arrived_qkv = flip_tensor(cut_qkv(line, w_qkv_own, here))
    half_out, eighth, vectors_one, vectors_two, b_in = second_cut(
        line, w_out, w_in, w_down, b_qv, b_in,
        [b_out, ln1_gain, ln1_bias, b_down, ln2_gain, ln2_bias], here,
    )
    around_qkv = chips_around(arrived_qkv)
    arrived_out, arrived_eighth = flip_tensor(half_out), flip_tensor(eighth)
    tokens_few, grad_few, tokens_t, places = pick(
        line, half_at.reshape(1), span_starts, slots, tokens, grad_values, seqs, [arrived_qkv]
    )
    own = project(line, tokens, tokens_few, w_qkv_own, b_qv, seqs)
    def attend_own(seq, hint=None):
        return attend(line, tokens, w_qkv_own, b_qv, own[0], own[1], seqs, seq, hint)

    core_first, half_in, b_qv_oth, b_in_oth = third_cut(
        line, around_qkv, arrived_out, w_in, here, [arrived_eighth]
    )
    b_qv_both, b_in_both = [b_qv, b_qv_oth], [b_in, b_in_oth]
    near_first = flip(core_first, 1)
    around_eighth = chips_around(arrived_eighth)
    arrived_in = flip_tensor(half_in)
    w_qkv_oth, w_out_oth = first_assemble(line, core_first, near_first, width, inner, here)
    w_qkv_both, w_out_both = [w_qkv_own, w_qkv_oth], [w_out, w_out_oth]
    oth = project(line, tokens, tokens_few, w_qkv_oth, b_qv_both[1], seqs)

    keys, values, queries_few, context_few = zip(own, oth)
    sum_few, normed_low = first_norm(line, context_few, w_out_both, tokens_few, vectors_one)

    def plane(values):
        return [values, flip_tensor(values), flip(values, 2), flip_both(values, 2)]

    slope_own, part = ffn_part(line, normed_low, w_in, b_in_both[0], w_down)
    core_second, held_in = fourth_cut(line, around_eighth, arrived_in)
    near_second, near_in = flip(core_second, 1), flip(held_in, 1)
    around_normed = plane(normed_low)
    w_in_oth, w_down_oth = second_assemble(
        line, core_second, near_second, held_in, near_in, hidden_half, here
    )
    w_in_both, w_down_both = [w_in, w_in_oth], [w_down, w_down_oth]
    g_ffn, g_second, slope_oth, sums = ffn_last(
        line, normed_low, part, sum_few, grad_few, vectors_one, vectors_two,
        w_in_both[1], b_in_both[1], w_down_both[1],
    )
    around_g = plane(g_ffn)
    g_branch, g_first, small_few = ffn_back(
        line, g_ffn, g_second, sum_few, vectors_one, sums, (slope_own, slope_oth), w_in_both, w_down_both
    )
    core_normed = join(line, around_normed)
    near_normed = flip(core_normed, 1)

    def back(at):
        return attend_back(
            line, place, queries_few[at], keys[at], values[at], g_branch, w_out_both[at],
            context_few[at], tokens_t, tokens_few, small_few, seqs, at, hidden_half // inner,
        )

    back_oth = back(1)
    near_oth = flip(back_oth[3], 1)
    core_g = join(line, around_g)
    near_g = flip(core_g, 1)
    back_own = back(0)
    near_own = flip(back_own[3], 1)
    keep_down, send_down, keep_in, send_in = ffn_grads(
        line, place, w_in, w_down, b_in_both[0], [core_normed, near_normed], [core_g, near_g]
    )
    z_down, z_in = flip(send_down, 4), flip(send_in, 8)
    x_send, y_send, x_keep, y_own, y_oth = cross_one(
        line, back_oth[2], near_oth, back_own[2], near_own, 112
    )
    x_near, y_near = flip_tensor(x_send), flip(y_send, 2)

    def attend_oth(seq, hint):
        return attend(
            line, tokens, w_qkv_oth, b_qv_both[1], keys[1], values[1], seqs, seq, hint
        )

    def over_rest_f32(total):
        return over_rest(total.astype(F32)) if rest else total

    def over_rest(total):
        for bit in rest:
            total = total + flip(total, bit)
        return total

    def layer_of(seq, mixed, hint):
        return layer(
            line, tokens, [ctx_own[seq], ctx_oth[seq]], w_out_both, w_in_both, b_in_both, w_down_both,
            vectors_one, vectors_two, seq, mixed, hint,
        )

    def input_grad_of(seq, before):
        return input_grad(line, [back_own, back_oth], w_qkv_both, g_first, places, seqs, seq, before)

    ctx_oth = [attend_oth(seq, 0.1) for seq in range(seqs)]
    ctx_own = [attend_own(seq, 0.1) for seq in range(1, seqs)]
    y_send, x_send, first, last = cross_two(line, x_keep, x_near, y_own, y_oth, y_near, H[0])
    y_near, x_near = flip(y_send, 2), flip_tensor(x_send)
    down, keep_in, send_in = second_fold(line, keep_down, z_down, keep_in, z_in, H[1])
    near_down, z_in = flip(down, 8), flip(send_in, 4)
    keep, *sends = cross_three(line, first, y_near, last, x_near, H[2])
    z_attn = [flip(send, 4) for send in sends]
    up = sum_all(line, H[3], over_rest(keep_in), over_rest(z_in))
    near_up = flip(up, 8)
    ctx_own.insert(0, attend_own(0, 0.1))
    d_tokens = None
    for seq in range(seqs):
        d_tokens = input_grad_of(seq, d_tokens)

    attn = sum_all(line, H[5], keep, *z_attn)
    near_attn = flip(attn, 8)
    down, up = third_fold(line, over_rest_f32(down), over_rest_f32(near_down), up, near_up, H[4])
    near_down, near_up = flip(down, 4), flip(up, 2)
    mixed = layer_of(0, None, 0.1)
    upper, lower = sum_split(line, H[7], over_rest_f32(attn), over_rest_f32(near_attn), width // 8)
    near_upper, near_lower = flip(upper, 4), flip(lower, 2)
    down, up = append(line, H[6], [down, near_down], [up, near_up])
    near_down, near_up = flip(down, 2), flip(up, 4)
    for seq in range(1, seqs):
        mixed = layer_of(seq, mixed, H[8])
    (upper,) = append(line, 1.5, [upper, near_upper])
    (lower,) = append(line, 1.5, [lower, near_lower])
    near_upper, near_lower = flip(upper, 2), flip(lower, 4)
    down, up = append(line, 1, [down, near_down], [up, near_up])
    near_down, near_up = flip(down, 1), flip(up, 1)
    ffn_sums = unpack_ffn(line, place, down, up, width, hidden_half)
    (upper,) = append(line, 1, [upper, near_upper])
    (lower,) = append(line, 1, [lower, near_lower])
    far_upper, far_lower = flip(upper, 1), flip(lower, 1)
    d_w_down, d_w_in = unpack_ffn(line, place, near_down, near_up, width, hidden_half, ffn_sums)
    d_w_qkv, d_w_out, *small = unpack_attend(line, place, [upper, lower, far_upper, far_lower], width, hidden_half)
    d_w_qkv = jnp.transpose(d_w_qkv, (1, 0, 2))
    d_b_qv, d_b_in, d_b_out, d_ln1_gain, d_ln1_bias, d_b_down, d_ln2_gain, d_ln2_bias = small

    return (
        mixed,
        d_tokens,
        d_w_qkv,
        d_b_qv,
        d_w_out,
        d_b_out,
        d_ln1_gain,
        d_ln1_bias,
        d_w_in,
        d_b_in,
        d_w_down,
        d_b_down,
        d_ln2_gain,
        d_ln2_bias,
    )


def solution(mesh):
    placed = (
        P(("dp", "tensor"), None),
        P(("dp", "tensor"), None),
        P("dp", None),
        P(None, None, "tensor"),
        P(None, "tensor"),
        P("tensor", None),
        P(),
        P(),
        P(),
        P(None, "tensor"),
        P("tensor"),
        P("tensor", None),
        P(),
        P(),
        P(),
    )
    return jax.shard_map(
        body,
        mesh=mesh,
        in_specs=placed,
        out_specs=(
            P(("dp", "tensor"), None),
            P(("dp", "tensor"), None),
            P(None, None, "tensor"),
            P(None, "tensor"),
            P("tensor", None),
            P(),
            P(),
            P(),
            P(None, "tensor"),
            P("tensor"),
            P("tensor", None),
            P(),
            P(),
            P(),
        ),
        check_vma=False,
    )
```

```python
import functools

import jax
import jax.numpy as jnp
from jax import lax
from jax.experimental import pallas as pl
from jax.experimental.pallas import tpu as pltpu
from jax.sharding import PartitionSpec as P

HEAD = 64
SPAN = 6
LANES = 128
EPSILON = 1e-05
F32 = jnp.float32
BF16 = jnp.bfloat16
GELU_A = (2.0 / 3.141592653589793) ** 0.5
GELU_B = 0.044715
ROOM_CUT, ROOM_PICK = 56, 24
HINT_GRADS, HINT_BACK = 15, 10
H = (0.2, 1, 0.5, 0.1, 0.3, 0.3, 1, 0.3, 0.3)
BYTES_US = 11_070_000
FLOPS_US = 3_459_000_000
ANYWHERE = pl.BlockSpec(memory_space=pl.ANY)
VMEM = pl.BlockSpec(memory_space=pltpu.VMEM)


class Line:
    def __init__(self):
        self.last = []

    def run(
        self, kernel, args, out_shape, grid=(), in_specs=None, out_specs=None, scratch=(), place=None,
        flops=0, moved=0, transcendentals=0, room=6, aliases=None, hint=None, after=(),
    ):
        ins, outs = len(args), len(out_shape)
        lead = 0 if place is None else 1
        after = list(after)
        if self.last and not any(arg is item for arg in args for item in self.last):
            after.append(min(self.last, key=lambda item: item.size))
        extra = len(after)
        small = min(item.size for item in out_shape) > 1 << 16

        def ordered(*refs):
            given, rest = refs[: lead + ins], refs[lead + ins + extra :]
            if small:
                rest[outs][...] = jnp.zeros((8, LANES), F32)
                rest = rest[:outs] + rest[outs + 1 :]
            kernel(*given, *rest)

        in_specs = list(in_specs or [VMEM] * ins) + [ANYWHERE] * extra
        out_specs = list(out_specs or [VMEM] * outs)
        out_shape = list(out_shape)
        if small:
            out_specs.append(pl.BlockSpec((8, LANES), lambda *at: (0, 0)) if grid else VMEM)
            out_shape.append(jax.ShapeDtypeStruct((8, LANES), F32))
        params = dict(
            out_shape=out_shape,
            compiler_params=pltpu.CompilerParams(vmem_limit_bytes=room << 20),
            cost_estimate=pl.CostEstimate(
                flops=int(flops if hint is None else hint * FLOPS_US),
                bytes_accessed=int(moved if hint is None else hint * BYTES_US),
                transcendentals=int(transcendentals if hint is None else 0),
            ),
            input_output_aliases=aliases or {},
        )
        if lead and grid:
            params["grid_spec"] = pltpu.PrefetchScalarGridSpec(
                num_scalar_prefetch=1, grid=grid, in_specs=in_specs, out_specs=out_specs, scratch_shapes=list(scratch)
            )
        else:
            if lead:
                in_specs = [pl.BlockSpec(memory_space=pltpu.SMEM)] + in_specs
            params.update(grid=grid, in_specs=in_specs, out_specs=out_specs, scratch_shapes=list(scratch))
        front = [] if place is None else [place]
        self.last = list(pl.pallas_call(ordered, **params)(*front, *args, *after))
        return self.last[:outs]


def shaped(shape, kind):
    return jax.ShapeDtypeStruct(tuple(shape), kind)


def whole(shape, once=False):
    held = dict(pipeline_mode=pl.Buffered(1)) if once else {}
    return pl.BlockSpec(shape, lambda *at: (0,) * len(shape), **held)


def flip(values, bits):
    size = lax.axis_size("dp")
    return lax.ppermute(values, "dp", [(at, at ^ bits) for at in range(size)])


def flip_tensor(values):
    return lax.ppermute(values, "tensor", [(0, 1), (1, 0)])


def flip_both(values, bits):
    size = 2 * lax.axis_size("dp")
    pairs = [(at, at ^ (2 * bits + 1)) for at in range(size)]
    return lax.ppermute(values, ("dp", "tensor"), pairs)


def dot_nt(left, right):
    return lax.dot_general(left, right, (((1,), (1,)), ((), ())), preferred_element_type=F32)


def dot_tn(left, right):
    return lax.dot_general(left, right, (((0,), (0,)), ((), ())), preferred_element_type=F32)


def mm(left, right):
    return jnp.dot(left, right, preferred_element_type=F32)


def lane_halves(rows):
    return lax.broadcasted_iota(jnp.int32, (rows, LANES), 1) < HEAD


def two_heads(block):
    low = lane_halves(block.shape[0])
    zero = jnp.zeros_like(block)
    return jnp.concatenate([jnp.where(low, block, zero), jnp.where(low, zero, block)], axis=0)


def scaled(queries):
    return queries * jnp.asarray(HEAD ** (-0.5), BF16)


def softmax_rows(scores):
    exponent = jnp.exp(scores - jnp.max(scores, axis=-1, keepdims=True))
    return exponent * (1.0 / jnp.sum(exponent, axis=-1, keepdims=True))


def attend_block(queries, keys, values):
    rows = queries.shape[0]
    probs = softmax_rows(dot_nt(two_heads(scaled(queries)), keys)).astype(BF16)
    mixed = mm(probs, values)
    return jnp.where(lane_halves(rows), mixed[:rows], mixed[rows:]).astype(BF16)


def norm_rows(values):
    average = jnp.mean(values, axis=-1, keepdims=True)
    centered = values - average
    variance = jnp.mean(centered * centered, axis=-1, keepdims=True)
    root = lax.rsqrt(variance + EPSILON)
    return centered * root, root


def norm_back(grad, unit, root, gain):
    grad_y = grad * gain
    inner = jnp.mean(grad_y, axis=-1, keepdims=True)
    along = jnp.mean(grad_y * unit, axis=-1, keepdims=True)
    return root * (grad_y - inner - unit * along)


def gelu_and_slope(values):
    square = values * values
    bent = jnp.tanh(GELU_A * values * (1.0 + GELU_B * square))
    half = 0.5 * (1.0 + bent)
    slope = half + 0.5 * values * (1.0 - bent * bent) * GELU_A * (1.0 + 3.0 * GELU_B * square)
    return values * half, slope


def gelu(values):
    return 0.5 * values * (1.0 + jnp.tanh(GELU_A * values * (1.0 + GELU_B * values * values)))


def join_kernel(count, *refs):
    rows = refs[0].shape[-2]
    for at in range(count):
        refs[count][..., at * rows : (at + 1) * rows, :] = refs[at][...]


def join(line, pieces):
    *lead, rows, columns = pieces[0].shape
    (result,) = line.run(
        functools.partial(join_kernel, len(pieces)),
        pieces,
        [shaped((*lead, rows * len(pieces), columns), pieces[0].dtype)],
        moved=4 * len(pieces) * pieces[0].size,
    )
    return result


def cut_qkv_kernel(place_ref, in_ref, out_ref, sem):
    rows = out_ref.shape[1]
    row = pl.multiple_of((place_ref[0] & 7) * rows, rows)
    copy = pltpu.make_async_copy(in_ref.at[:, pl.ds(row, rows), :], out_ref, sem)
    copy.start()
    copy.wait()


def cut_qkv(line, w_qkv, here):
    lead, rows, columns = w_qkv.shape
    (piece,) = line.run(
        cut_qkv_kernel,
        [w_qkv],
        [shaped((lead, rows // 8, columns), BF16)],
        in_specs=[ANYWHERE],
        scratch=[pltpu.SemaphoreType.DMA],
        place=here,
        moved=w_qkv.size // 2,
        room=ROOM_CUT,
    )
    return piece


def folded(rows, columns, width):
    tall = rows * columns // width
    rest, side = rows - tall, width - columns
    parts = [((0, tall, 0, columns), (0, tall, 0, columns))]
    for at in range(columns // side):
        parts.append(((at * rest, rest, columns, side), (tall, rest, at * side, side)))
    return tall, parts


def second_cut_kernel(place_ref, out_ref, in_ref, down_ref, bias_a, bias_b, *refs):
    vectors, (half, eighth, one, two, row_ref) = refs[:6], refs[6:]
    deep, width = out_ref.shape
    half[:deep, :] = out_ref[...]
    row_ref[0, :] = bias_b[...]
    left = jnp.concatenate(
        [jnp.concatenate([bias_a[0:1, :], bias_a[1:2, :]], axis=1)]
        + [row_ref[:, at : at + width] for at in range(0, row_ref.shape[1], width)],
        axis=0,
    )
    parts = []
    for _ in range(3):
        coarse = left.astype(BF16).astype(F32)
        parts.append(coarse)
        left = left - coarse
    parts.append(jnp.zeros((half.shape[0] - deep - 3 * left.shape[0], width), F32))
    half[deep:, :] = jnp.concatenate(parts, axis=0).astype(BF16)
    tall, parts = folded(*in_ref.shape, eighth.shape[1])
    for (row, high, column, wide), (top, _, side, _) in parts:
        eighth[row : row + high, column : column + wide] = in_ref[top : top + high, side : side + wide]
    eighth[tall:, :] = down_ref[...]
    for at in range(3):
        one[at, :] = vectors[at][...]
        two[at, :] = vectors[3 + at][...]


def second_cut(line, w_out, w_in, w_down, b_qv, b_in, vectors, here):
    width = w_out.shape[1]
    half, rows, deep = w_out.shape[0] // 2, w_in.shape[0] // 8, w_down.shape[0] // 8
    last = w_in.shape[1] // 4
    eighth = folded(rows, last, width)[0]
    shapes = [(half + 16, width), (eighth + deep, width), (3, width), (3, width), (1, b_in.shape[0])]
    return line.run(
        second_cut_kernel,
        [w_out, w_in, w_down, b_qv, b_in, *vectors],
        [shaped(shape, BF16 if at < 2 else F32) for at, shape in enumerate(shapes)],
        grid=(1,),
        in_specs=[
            pl.BlockSpec((half, width), lambda i, p: (p[0] & 1, 0)),
            pl.BlockSpec((rows, last), lambda i, p: (p[0] & 7, 3)),
            pl.BlockSpec((deep, width), lambda i, p: (p[0] & 7, 0)),
            whole(b_qv.shape),
            whole(b_in.shape),
            *[whole((width,)) for vector in vectors],
        ],
        out_specs=[whole(shape) for shape in shapes],
        place=here,
        moved=4 * (half + eighth + deep) * width,
        room=ROOM_CUT,
    )


def third_cut_kernel(place_ref, a, b, c, d, out_ref, in_ref, core, half, bias_a, bias_b):
    third, rows, inner = a.shape
    for at, ref in enumerate((a, b, c, d)):
        for section in range(third):
            row = (section * 4 + at) * rows
            core[row : row + rows, :] = ref[section]
    row = 4 * third * rows
    deep = out_ref.shape[0] - 16
    core[row : row + deep, :] = out_ref[:deep, :inner]
    core[row + deep :, :] = out_ref[:deep, inner:]
    half[...] = in_ref[...]
    parts = out_ref[deep:, :].astype(F32)
    width = parts.shape[1]
    count = 1 + bias_b.shape[1] // width
    total = parts[2 * count : 3 * count] + parts[count : 2 * count] + parts[:count]
    bias_a[0:1, :] = total[0:1, :inner]
    bias_a[1:2, :] = total[0:1, inner:]
    for at in range(count - 1):
        bias_b[:, at * width : (at + 1) * width] = total[1 + at : 2 + at, :]


def third_cut(line, qkv, out, w_in, here, after):
    third, rows, inner = qkv[0].shape
    height = 4 * third * rows + 2 * (out.shape[0] - 16)
    half = (w_in.shape[0] // 2, w_in.shape[1] // 4 * 3)
    shapes = [(height, inner), half, (2, inner), (1, w_in.shape[1])]
    return line.run(
        third_cut_kernel,
        [*qkv, out, w_in],
        [shaped(shape, BF16 if at < 2 else F32) for at, shape in enumerate(shapes)],
        grid=(1,),
        in_specs=[whole(item.shape) for item in [*qkv, out]]
        + [pl.BlockSpec(half, lambda i, p: (p[0] & 1, 0))],
        out_specs=[whole(shape) for shape in shapes],
        place=here,
        moved=4 * (height * inner + half[0] * half[1]),
        after=after,
    )


def first_assemble_kernel(place_ref, mine, near, qkv_ref, out_ref):
    third, width, inner = qkv_ref.shape
    rows, half = width // 8, out_ref.shape[0] // 2
    for core, ref in enumerate((mine, near)):
        for at in range(4):
            row = pl.multiple_of(((place_ref[0] ^ (2 * at + core)) & 7) * rows, rows)
            for section in range(third):
                start = (section * 4 + at) * rows
                qkv_ref[section, pl.ds(row, rows), :] = ref[start : start + rows, :]
        row = pl.multiple_of(((place_ref[0] ^ core) & 1) * half, half)
        start = 4 * third * rows
        out_ref[pl.ds(row, half), :inner] = ref[start : start + half, :]
        out_ref[pl.ds(row, half), inner:] = ref[start + half :, :]


def first_assemble(line, mine, near, width, inner, here):
    return line.run(
        first_assemble_kernel,
        [mine, near],
        [shaped((3, width, inner), BF16), shaped((inner, width), BF16)],
        place=here,
        moved=8 * mine.size,
    )


def fourth_cut_kernel(a, b, c, d, eighths):
    rows = a.shape[0]
    for at, ref in enumerate((a, b, c, d)):
        eighths[at * rows : (at + 1) * rows, :] = ref[...]


def fourth_cut(line, eighths, after):
    rows, width = eighths[0].shape
    (result,) = line.run(
        fourth_cut_kernel,
        eighths,
        [shaped((4 * rows, width), BF16)],
        moved=16 * rows * width,
        after=after,
    )
    return result


def second_assemble_kernel(place_ref, mine, near, half_mine, half_near, in_ref, down_ref):
    width = mine.shape[1]
    wide, last = half_mine.shape[1], in_ref.shape[1] - half_mine.shape[1]
    rows, deep, half = in_ref.shape[0] // 8, down_ref.shape[0] // 8, half_mine.shape[0]
    tall, parts = folded(rows, last, width)
    for core, (ref, half_ref) in enumerate(((mine, half_mine), (near, half_near))):
        for at in range(4):
            block = (place_ref[0] ^ (2 * at + core)) & 7
            start = at * (tall + deep)
            for (row, high, column, side), (top, _, left, _) in parts:
                to = pl.multiple_of(block * rows + top, 16)
                in_ref[pl.ds(to, high), wide + left : wide + left + side] = ref[
                    start + row : start + row + high, column : column + side
                ]
            down_ref[pl.ds(pl.multiple_of(block * deep, deep), deep), :] = ref[
                start + tall : start + tall + deep, :
            ]
        row = pl.multiple_of(((place_ref[0] ^ core) & 1) * half, half)
        in_ref[pl.ds(row, half), :wide] = half_ref[...]


def second_assemble(line, mine, near, half_mine, half_near, hidden, here):
    width = mine.shape[1]
    return line.run(
        second_assemble_kernel,
        [mine, near, half_mine, half_near],
        [shaped((width, hidden), BF16), shaped((hidden, width), BF16)],
        place=here,
        moved=8 * width * hidden,
    )


def project_kernel(tok_ref, few_ref, w_ref, bias_ref, k_ref, v_ref, q_ref, ctx_ref):
    tok = tok_ref[...]
    k_ref[...] = mm(tok, w_ref[1]).astype(BF16)
    v_ref[...] = (mm(tok, w_ref[2]) + bias_ref[1:2, :]).astype(BF16)
    q_ref[...] = (mm(few_ref[...], w_ref[0]) + bias_ref[0:1, :]).astype(BF16)
    for at in range(0, k_ref.shape[1], LANES):
        cut = slice(at, at + LANES)
        ctx_ref[:, cut] = attend_block(q_ref[:, cut], k_ref[:, cut], v_ref[:, cut])


def project(line, tokens, few, weights, bias, seqs):
    rows, width = tokens.shape
    inner = weights.shape[2]
    length, slots = rows // seqs, few.shape[0] // seqs
    long, short = (pl.BlockSpec((size, inner), lambda s: (s, 0)) for size in (length, slots))
    return line.run(
        project_kernel,
        [tokens, few, weights, bias],
        [shaped((rows, inner), BF16)] * 2 + [shaped((few.shape[0], inner), BF16)] * 2,
        grid=(seqs,),
        in_specs=[
            pl.BlockSpec((length, width), lambda s: (s, 0)),
            pl.BlockSpec((slots, width), lambda s: (s, 0)),
            whole(weights.shape),
            whole(bias.shape),
        ],
        out_specs=[long, long, short, short],
        flops=6 * rows * width * inner,
        room=16,
        moved=2 * (rows * width + 3 * width * inner + 2 * rows * inner),
    )


def first_norm_kernel(ctx_a, ctx_b, w_a, w_b, few_ref, vec_ref, sum_ref, low_ref):
    branch = mm(ctx_a[...], w_a[...]) + mm(ctx_b[...], w_b[...]) + vec_ref[0:1, :]
    total = few_ref[...].astype(F32) + branch
    sum_ref[...] = total
    low_ref[...] = (norm_rows(total)[0] * vec_ref[1:2, :] + vec_ref[2:3, :]).astype(BF16)


def first_norm(line, contexts, w_out, few, vectors):
    count, width = few.shape
    return line.run(
        first_norm_kernel,
        [*contexts, *w_out, few, vectors],
        [shaped((count, width), F32), shaped((count, width), BF16)],
        flops=2 * count * width * width,
        moved=2 * width * width + 14 * count * width,
    )


def ffn_part_kernel(low_ref, wi_ref, bi_ref, wd_ref, slope_ref, part_ref, total):
    step = pl.program_id(0)
    gate, slope = gelu_and_slope(mm(low_ref[...], wi_ref[...]) + bi_ref[...])
    slope_ref[...] = slope
    part = mm(gate.astype(BF16), wd_ref[...])

    @pl.when(step == 0)
    def _():
        total[...] = part

    @pl.when(step > 0)
    def _():
        total[...] += part

    @pl.when(step == pl.num_programs(0) - 1)
    def _():
        part_ref[...] = total[...]


def ffn_part(line, low, w_in, b_in, w_down):
    count, width = low.shape
    hidden = w_in.shape[1]
    steps = 4
    tile = hidden // steps
    flat = whole((count, width))
    return line.run(
        ffn_part_kernel,
        [low, w_in, b_in, w_down],
        [shaped((count, hidden), F32), shaped((count, width), F32)],
        grid=(steps,),
        in_specs=[
            flat,
            pl.BlockSpec((width, tile), lambda j: (0, j)),
            pl.BlockSpec((1, tile), lambda j: (0, j)),
            pl.BlockSpec((tile, width), lambda j: (j, 0)),
        ],
        out_specs=[pl.BlockSpec((count, tile), lambda j: (0, j)), flat],
        scratch=[pltpu.VMEM((count, width), F32)],
        flops=4 * count * width * hidden,
        moved=4 * width * hidden,
        transcendentals=count * hidden,
        room=12,
    )


def column_sum(values):
    return jnp.sum(values, axis=0, keepdims=True)


def ffn_last_kernel(
    low_ref, part_ref, sum_ref, grad_ref, one_ref, two_ref, wi_ref, bi_ref, wd_ref,
    g_ffn_ref, g_second_ref, slope_ref, sums_ref,
):
    gate, slope = gelu_and_slope(mm(low_ref[...], wi_ref[...]) + bi_ref[...])
    slope_ref[...] = slope
    ffn = part_ref[...] + mm(gate.astype(BF16), wd_ref[...]) + two_ref[0:1, :]
    normed = norm_rows(sum_ref[...])[0] * one_ref[1:2, :] + one_ref[2:3, :]
    unit, root = norm_rows(normed + ffn)
    grad = grad_ref[...]
    g_second = norm_back(grad, unit, root, two_ref[1:2, :])
    g_ffn = g_second.astype(BF16)
    g_ffn_ref[...] = g_ffn
    g_second_ref[...] = g_second
    sums = (column_sum(g_ffn.astype(F32)), column_sum(grad * unit), column_sum(grad))
    sums_ref[...] = jnp.concatenate([*sums, jnp.zeros((5, grad.shape[1]), F32)], axis=0)


def ffn_last(line, low, part, total, grad, one, two, w_in, b_in, w_down):
    count, width = low.shape
    hidden = w_in.shape[1]
    return line.run(
        ffn_last_kernel,
        [low, part, total, grad, one, two, w_in, b_in, w_down],
        [
            shaped((count, width), BF16),
            shaped((count, width), F32),
            shaped((count, hidden), F32),
            shaped((8, width), F32),
        ],
        flops=4 * count * width * hidden,
        moved=4 * width * hidden,
        room=12,
    )


def ffn_back_kernel(
    g_ffn_ref, g_second_ref, sum_ref, one_ref, sums_ref, slope_a, slope_b, wi_a, wi_b, wd_a, wd_b,
    g_branch_ref, g_first_ref, small_ref,
):
    g_ffn, g_normed = g_ffn_ref[...], g_second_ref[...]
    width = g_normed.shape[1]
    half = width // 2
    deep = slope_a.shape[1] // half
    for at, (slope, w_in, w_down) in enumerate(((slope_a, wi_a, wd_a), (slope_b, wi_b, wd_b))):
        g_pre = (slope[...] * dot_nt(g_ffn, w_down[...])).astype(BF16)
        bias = column_sum(g_pre.astype(F32))
        for row in range(deep):
            small_ref[at * deep + row : at * deep + row + 1, :] = bias[:, row * half : (row + 1) * half]
        g_normed = g_normed + dot_nt(g_pre, w_in[...])
    unit, root = norm_rows(sum_ref[...])
    g_first = norm_back(g_normed, unit, root, one_ref[1:2, :])
    g_branch = g_first.astype(BF16)
    g_first_ref[...] = g_first
    g_branch_ref[...] = g_branch
    vectors = (
        column_sum(g_branch.astype(F32)),
        column_sum(g_normed * unit),
        column_sum(g_normed),
        *[sums_ref[at : at + 1, :] for at in range(3)],
    )
    for at, vector in enumerate(vectors):
        row = 2 * deep + 2 * at
        small_ref[row : row + 1, :] = vector[:, :half]
        small_ref[row + 1 : row + 2, :] = vector[:, half:]
    count = 2 * deep + 12
    small_ref[count:, :] = jnp.zeros((small_ref.shape[0] - count, half), F32)


def ffn_back(line, g_ffn, g_second, total, one, sums, slopes, w_in, w_down):
    count, width = g_ffn.shape
    hidden = w_in[0].shape[1]
    rows = 2 * (hidden // (width // 2)) + 12
    return line.run(
        ffn_back_kernel,
        [g_ffn, g_second, total, one, sums, *slopes, *w_in, *w_down],
        [
            shaped((count, width), BF16),
            shaped((count, width), F32),
            shaped((-(-rows // 8) * 8, width // 2), F32),
        ],
        flops=8 * count * width * hidden,
        moved=8 * width * hidden,
        room=12,
    )


def ffn_grads_kernel(place_ref, wi_ref, wd_ref, bi_ref, *refs):
    normed_refs, grad_refs = refs[:2], refs[2:4]
    keep_down, send_down, keep_in, send_in = refs[4:8]
    down, up = refs[8:]
    width = normed_refs[0].shape[1]
    tile = wi_ref.shape[1] // 4
    hidden = pl.ds(pl.multiple_of((place_ref[0] >> 2) * tile, tile), tile)
    w_in, w_down, b_in = wi_ref[:, hidden], wd_ref[hidden, :], bi_ref[:, hidden]
    for at in range(2):
        normed, grad = normed_refs[at][...], grad_refs[at][...]
        gate, slope = gelu_and_slope(mm(normed, w_in) + b_in)
        pre = (slope * dot_nt(grad, w_down)).astype(BF16)
        down_part = dot_tn(gate.astype(BF16), grad)
        up_part = dot_tn(normed, pre)
        if at == 0:
            down[...] = down_part
            up[...] = up_part
        else:
            down[...] += down_part
            up[...] += up_part
    down_rows, up_rows = tile // 4, width // 4
    half = width // 2
    for slot in range(4):
        block = slot ^ (place_ref[0] & 3)
        low = down[pl.ds(pl.multiple_of(block * down_rows, down_rows), down_rows), :]
        block = (0, 2, 1, 3)[slot] ^ (place_ref[0] & 3)
        high = up[pl.ds(pl.multiple_of(block * up_rows, up_rows), up_rows), :]
        to_down, to_in = (keep_down, keep_in) if slot < 2 else (send_down, send_in)
        kind = to_down.dtype
        to_down[slot % 2, :down_rows, :] = low[:, :half].astype(kind)
        to_down[slot % 2, down_rows:, :] = low[:, half:].astype(kind)
        to_in[slot % 2, :, :] = high.astype(kind)


def ffn_grads(line, place, w_in, w_down, b_in, normed, grads):
    rows, width = normed[0].shape
    tile = w_in.shape[1] // 4
    shape = (2, 2 * (tile // 4), width // 2)
    wide = (2, width // 4, tile)
    return line.run(
        ffn_grads_kernel,
        [w_in, w_down, b_in, *normed, *grads],
        [shaped(shape, F32), shaped(shape, BF16), shaped(wide, F32), shaped(wide, BF16)],
        scratch=[pltpu.VMEM((tile, width), F32), pltpu.VMEM((width, tile), F32)],
        place=place,
        flops=16 * rows * width * tile,
        moved=12 * rows * width + 16 * width * tile,
        hint=HINT_GRADS,
        room=16,
    )


def attend_back_kernel(
    seqs, half, deep, place_ref, q_ref, k_ref, v_ref, g_branch_ref, w_out_ref, ctx_ref, tok_t_ref, few_ref,
    small_ref, dq_ref, dkv_ref, keep_ref, send_ref, total, little,
):
    few, inner = q_ref.shape
    rows = k_ref.shape[0]
    slots, length = few // seqs, rows // seqs
    low = lane_halves(slots)
    scale = HEAD ** (-0.5)
    g_branch = g_branch_ref[...]
    g_context = dot_nt(g_branch, w_out_ref[...]).astype(BF16)
    for seq in range(seqs):
        short, long = slice(seq * slots, (seq + 1) * slots), slice(seq * length, (seq + 1) * length)
        for at in range(0, inner, LANES):
            cut = slice(at, at + LANES)
            both, grads = two_heads(scaled(q_ref[short, cut])), two_heads(g_context[short, cut])
            keys, values = k_ref[long, cut], v_ref[long, cut]
            scores = dot_nt(keys, both)
            exponent = jnp.exp(scores - jnp.max(scores, axis=0, keepdims=True))
            probs = exponent * (1.0 / jnp.sum(exponent, axis=0, keepdims=True))
            grad_probs = dot_nt(values, grads)
            dkv_ref[long, inner + at : inner + at + LANES] = mm(probs.astype(BF16), grads).astype(BF16)
            slot_total = jnp.sum(grad_probs * probs, axis=0, keepdims=True)
            grad_scores = (probs * (grad_probs - slot_total)).astype(BF16)
            dq = dot_tn(grad_scores, keys) * scale
            dq_ref[short, cut] = jnp.where(low, dq[:slots], dq[slots:]).astype(BF16)
            dkv_ref[long, cut] = mm(grad_scores, both).astype(BF16)
    dq, dkv = dq_ref[...], dkv_ref[...]
    total[0] = dot_tn(few_ref[...], dq)
    both = mm(tok_t_ref[...], dkv)
    total[1] = both[:, :inner]
    total[2] = both[:, inner:]
    out_grad = dot_tn(ctx_ref[...], g_branch)
    total[3, :inner, :] = out_grad[:, :inner]
    total[3, inner:, :] = out_grad[:, inner:]
    little[...] = jnp.zeros_like(little)
    little[0, 0:1, :] = column_sum(dq.astype(F32))
    little[0, 1:2, :] = column_sum(dkv[:, inner:].astype(F32))
    for at in range(deep + 12):
        source = half * deep + at if at < deep else deep + at
        little[1 + at // 2, at % 2 : at % 2 + 1, :] = small_ref[source : source + 1, :]
    block_rows = total.shape[1] // 16
    pad = keep_ref.shape[1] - 4 * block_rows
    for slot in range(16):
        block = slot ^ place_ref[0]
        row = pl.multiple_of(block * block_rows, block_rows)
        to, kind = (keep_ref, F32) if slot < 8 else (send_ref, BF16)
        for section in range(4):
            cut = slice(section * block_rows, (section + 1) * block_rows)
            to[slot % 8, cut, :] = total[section, pl.ds(row, block_rows), :].astype(kind)
        pair = jnp.concatenate([little[block], jnp.zeros((pad - 8, inner), F32)], axis=0)
        to[slot % 8, 4 * block_rows :, :] = pair.astype(kind)


def attend_back(line, place, queries, keys, values, g_branch, w_out, context, tokens_t, few, small, seqs, half, deep):
    rows, inner = keys.shape
    width = tokens_t.shape[0]
    count = queries.shape[0]
    held = (8, 4 * (width // 16) + 16, inner)
    return line.run(
        functools.partial(attend_back_kernel, seqs, half, deep),
        [queries, keys, values, g_branch, w_out, context, tokens_t, few, small],
        [
            shaped((count, inner), BF16),
            shaped((rows, 2 * inner), BF16),
            shaped(held, F32),
            shaped(held, BF16),
        ],
        scratch=[pltpu.VMEM((4, width, inner), F32), pltpu.VMEM((16, 8, inner), F32)],
        place=place,
        hint=HINT_BACK,
        room=16,
        flops=4 * rows * width * inner + 24 * count * rows * inner,
        moved=20 * rows * inner,
    )


def sum_all_kernel(count, keep_ref, *refs):
    row = 0
    for ref in refs[:count]:
        part = slice(row, row + ref.shape[0])
        refs[count][part] = (keep_ref[part].astype(F32) + ref[...].astype(F32)).astype(BF16)
        row += ref.shape[0]


def sum_all(line, hint, keep, *arrived):
    (result,) = line.run(
        functools.partial(sum_all_kernel, len(arrived)), [keep, *arrived], [shaped(keep.shape, BF16)], hint=hint
    )
    return result


def sum_split_kernel(mine_ref, near_ref, upper, lower):
    rows = upper.shape[1]
    for slot in range(2):
        total = (mine_ref[slot].astype(F32) + near_ref[1 - slot].astype(F32)).astype(BF16)
        upper[slot] = total[:rows, :]
        lower[slot] = total[rows:, :]


def sum_split(line, hint, mine, near, rows):
    count, height, inner = mine.shape
    shapes = [shaped((count, rows, inner), BF16), shaped((count, height - rows, inner), BF16)]
    return line.run(sum_split_kernel, [mine, near], shapes, hint=hint)


def second_fold_kernel(down, down_near, up, up_near, down_out, up_keep, up_send):
    down_out[...] = (down[...] + down_near[...].astype(F32)).astype(BF16)
    total = up[...] + up_near[...].astype(F32)
    middle = total.shape[0] // 2
    up_keep[...] = total[:middle]
    up_send[...] = total[middle:].astype(BF16)


def second_fold(line, down, down_near, up, up_near, hint):
    half = (up.shape[0] // 2, *up.shape[1:])
    return line.run(
        second_fold_kernel,
        [down, down_near, up, up_near],
        [shaped(down.shape, BF16), shaped(half, F32), shaped(half, BF16)],
        hint=hint,
    )


def third_fold_kernel(down, down_near, up, up_near, down_out, up_out):
    for slot in range(2):
        down_out[slot] = (down[slot].astype(F32) + down_near[1 - slot].astype(F32)).astype(BF16)
    count = up.shape[0]
    up_out[:count] = up[...]
    up_out[count:] = up_near[...]


def third_fold(line, down, down_near, up, up_near, hint):
    shapes = [shaped(down.shape, BF16), shaped((2 * up.shape[0], *up.shape[1:]), BF16)]
    return line.run(third_fold_kernel, [down, down_near, up, up_near], shapes, hint=hint)


def append_kernel(count, *refs):
    groups, out = refs[:-count], refs[-count:]
    each = len(groups) // count
    for at in range(count):
        row = 0
        for ref in groups[at * each : (at + 1) * each]:
            out[at][row : row + ref.shape[0]] = ref[...]
            row += ref.shape[0]


def append(line, hint, *groups):
    shapes = [shaped((sum(item.shape[0] for item in group), *group[0].shape[1:]), BF16) for group in groups]
    return line.run(
        functools.partial(append_kernel, len(groups)),
        [item for group in groups for item in group],
        shapes,
        hint=hint,
    )


def cross_one_kernel(oth, oth_near, own, own_near, x_send, y_send, x_keep, y_keep_own, y_keep_oth):
    rows = x_send.shape[1]
    half = oth.shape[0] // 2
    x_send[...] = (oth[:, :rows, :] + oth_near[:, :rows, :].astype(F32)).astype(BF16)
    x_keep[...] = own[:, :rows, :] + own_near[:, :rows, :].astype(F32)
    for at, (keep, near, out) in enumerate(((own, own_near, y_keep_own), (oth, oth_near, y_keep_oth))):
        total = keep[:, rows:, :] + near[:, rows:, :].astype(F32)
        out[...] = total[:half]
        y_send[at] = total[half:].astype(BF16)


def cross_one(line, oth, oth_near, own, own_near, rows):
    count, height, inner = oth.shape
    half, last = count // 2, height - rows
    return line.run(
        cross_one_kernel,
        [oth, oth_near, own, own_near],
        [
            shaped((count, rows, inner), BF16),
            shaped((2, half, last, inner), BF16),
            shaped((count, rows, inner), F32),
            shaped((half, last, inner), F32),
            shaped((half, last, inner), F32),
        ],
        hint=2,
    )


def cross_two_kernel(x_keep, x_near, own, oth, y_near, y_send, x_send, first, last):
    half = own.shape[0]
    total = x_keep[...] + x_near[...].astype(F32)
    first[...] = total[:half]
    y_send[...] = total[half:].astype(BF16)
    total = own[...] + y_near[0].astype(F32)
    small = total.shape[1] - 16
    last[:, :small, :] = total[:, :small, :]
    last[:, small:, :] = total[:, small:, :].astype(BF16).astype(F32)
    x_send[...] = (oth[...] + y_near[1].astype(F32)).astype(BF16)


def cross_two(line, x_keep, x_near, own, oth, y_near, hint):
    half = (own.shape[0], x_keep.shape[1], x_keep.shape[2])
    return line.run(
        cross_two_kernel,
        [x_keep, x_near, own, oth, y_near],
        [shaped(half, BF16), shaped(own.shape, BF16), shaped(half, F32), shaped(own.shape, F32)],
        hint=hint,
    )


def cross_three_kernel(first, y_near, last, x_near, keep, *sends):
    rows, half = first.shape[1], first.shape[0] // 2
    for ref, near, cut in ((first, y_near, slice(0, rows)), (last, x_near, slice(rows, None))):
        total = ref[...] + near[...].astype(F32)
        keep[:, cut, :] = total[:half]
        for at, send in enumerate(sends):
            send[:, cut, :] = total[half + at : half + at + 1].astype(BF16)


def cross_three(line, first, y_near, last, x_near, hint):
    half, height, inner = first.shape[0] // 2, first.shape[1] + last.shape[1], first.shape[2]
    return line.run(
        cross_three_kernel,
        [first, y_near, last, x_near],
        [shaped((half, height, inner), F32)] + [shaped((1, height, inner), BF16)] * half,
        hint=hint,
    )


def unpack_attend_kernel(place_ref, *refs):
    blocks, (qkv_ref, out_ref), (wide, little, sems) = refs[:4], refs[4:6], refs[-3:]
    outs = refs[6:-3]
    inner = qkv_ref.shape[2]
    rows = qkv_ref.shape[1] // 16
    copies = []

    def place_rows(source, to):
        copy = pltpu.make_async_copy(source, to, sems.at[len(copies)])
        copy.start()
        copies.append(copy)

    for slot in range(16):
        core, at = slot // 8, slot % 8
        block = slot ^ place_ref[0]
        wide[slot, : 2 * rows, :] = blocks[2 * core][at].astype(F32)
        row = pl.multiple_of(block * rows, rows)
        for section in range(2):
            place_rows(wide.at[slot, pl.ds(section * rows, rows), :], qkv_ref.at[section, pl.ds(row, rows), :])
        block = ((at & 1) + (at & 2) * 2 + (at >> 2) * 2 + 8 * core) ^ place_ref[0]
        values = blocks[2 * core + 1][at].astype(F32)
        wide[slot, 2 * rows :, :] = values[: 2 * rows, :]
        little[block] = values[2 * rows : 2 * rows + 8, :]
        row = pl.multiple_of(block * rows, rows)
        place_rows(wide.at[slot, pl.ds(2 * rows, rows), :], qkv_ref.at[2, pl.ds(row, rows), :])
        row = pl.multiple_of((block & 7) * rows, rows)
        column = pl.multiple_of((block >> 3) * inner, inner)
        place_rows(wide.at[slot, pl.ds(3 * rows, rows), :], out_ref.at[pl.ds(row, rows), pl.ds(column, inner)])
    outs[0][...] = little[0, 0:2, :]
    row = 2
    for out in outs[1:]:
        for at in range(out.shape[0] // inner):
            out[pl.ds(at * inner, inner)] = little[row // 2, row % 2, :]
            row += 1
    for copy in copies:
        copy.wait()


def unpack_attend(line, place, blocks, width, hidden):
    inner = blocks[0].shape[2]
    rows = width // 16
    small = [(2, inner), (hidden,)] + [(width,)] * 6
    return line.run(
        unpack_attend_kernel,
        blocks,
        [shaped((3, width, inner), F32), shaped((inner, width), F32)] + [shaped(shape, F32) for shape in small],
        out_specs=[ANYWHERE] * 2 + [VMEM] * 8,
        scratch=[
            pltpu.VMEM((16, 4 * rows, inner), F32),
            pltpu.VMEM((16, 8, inner), F32),
            pltpu.SemaphoreType.DMA((64,)),
        ],
        place=place,
        room=20,
        hint=1,
    )


def unpack_ffn_kernel(first, place_ref, *refs):
    down_in, up_in = refs[:2]
    down_ref, in_ref, down, up, sems = refs[-5:]
    rows, half = down_ref.shape[0] // 16, down_ref.shape[1] // 2
    deep, wide = in_ref.shape[0] // 4, in_ref.shape[1] // 4
    copies = []

    def place_rows(source, to):
        copy = pltpu.make_async_copy(source, to, sems.at[len(copies)])
        copy.start()
        copies.append(copy)

    for slot in range(8):
        block = (slot if first else slot + 8) ^ place_ref[0]
        down[slot, :, :half] = down_in[slot, :rows, :].astype(F32)
        down[slot, :, half:] = down_in[slot, rows:, :].astype(F32)
        row = pl.multiple_of(block * rows, rows)
        place_rows(down.at[slot], down_ref.at[pl.ds(row, rows), :])
        block = ((slot & 1) + (slot & 2) * 2 + (slot >> 2) * 2 + (0 if first else 8)) ^ place_ref[0]
        up[slot] = up_in[slot].astype(F32)
        row = pl.multiple_of((block & 3) * deep, deep)
        column = pl.multiple_of((block >> 2) * wide, wide)
        place_rows(up.at[slot], in_ref.at[pl.ds(row, deep), pl.ds(column, wide)])
    for copy in copies:
        copy.wait()


def unpack_ffn(line, place, down, up, width, hidden, before=None):
    return line.run(
        functools.partial(unpack_ffn_kernel, before is None),
        [down, up, *(before or [])],
        [shaped((hidden, width), F32), shaped((width, hidden), F32)],
        in_specs=[VMEM] * 2 + [ANYWHERE] * (0 if before is None else 2),
        out_specs=[ANYWHERE] * 2,
        scratch=[
            pltpu.VMEM((8, hidden // 16, width), F32),
            pltpu.VMEM((8, width // 4, hidden // 4), F32),
            pltpu.SemaphoreType.DMA((16,)),
        ],
        aliases={} if before is None else {3: 0, 4: 1},
        place=place,
        moved=6 * width * hidden,
        room=20,
        hint=1,
    )


def attend_kernel(tok_ref, w_ref, bias_ref, k_ref, v_ref, out_ref):
    rows, inner = out_ref.shape
    low = lane_halves(rows)
    queries = scaled((mm(tok_ref[...], w_ref[0]) + bias_ref[0:1, :]).astype(BF16))
    for at in range(0, inner, LANES):
        cut = slice(at, at + LANES)
        block, keys, values = queries[:, cut], k_ref[:, cut], v_ref[:, cut]
        zero, one = jnp.zeros_like(block), jnp.ones_like(values)
        mixed = []
        for first in (True, False):
            head = jnp.where(low == first, block, zero)
            with_sums = jnp.where(lane_halves(values.shape[0]) == first, values, one)
            scores = dot_nt(head, keys)
            exponent = jnp.exp(scores - jnp.max(scores, axis=-1, keepdims=True)).astype(BF16)
            mixed.append(mm(exponent, with_sums))
        top = jnp.where(low, mixed[0], mixed[1])
        total = jnp.where(low, mixed[1], mixed[0])
        out_ref[:, cut] = (top / pltpu.roll(total, HEAD, 1)).astype(BF16)


def attend(line, tokens, weights, bias, keys, values, seqs, seq, hint=None):
    rows, width = tokens.shape
    inner = keys.shape[1]
    length = rows // seqs
    long = pl.BlockSpec((length, inner), lambda s: (seq, 0))
    (result,) = line.run(
        attend_kernel,
        [tokens, weights, bias, keys, values],
        [shaped((length, inner), BF16)],
        grid=(1,),
        in_specs=[
            pl.BlockSpec((length, width), lambda s: (seq, 0)),
            pl.BlockSpec((1, width, inner), lambda s: (0, 0, 0)),
            whole(bias.shape),
            long,
            long,
        ],
        out_specs=[pl.BlockSpec((length, inner), lambda s: (0, 0))],
        flops=2 * length * width * inner + 16 * length * length * inner,
        moved=2 * (length * width + width * inner + 3 * length * inner),
        transcendentals=length * length * inner // HEAD,
        room=16,
        hint=hint,
    )
    return result


def layer_kernel(
    tok_ref, ctx_a, ctx_b, wo_a, wo_b, wi_a, wi_b, bi_a, bi_b, wd_a, wd_b, one_ref, two_ref, out_ref,
):
    branch = mm(ctx_a[...], wo_a[...]) + mm(ctx_b[...], wo_b[...]) + one_ref[0:1, :]
    unit, _ = norm_rows(tok_ref[...].astype(F32) + branch)
    normed = unit * one_ref[1:2, :] + one_ref[2:3, :]
    low = normed.astype(BF16)
    total = normed + two_ref[0:1, :]
    for w_in, b_in, w_down in ((wi_a, bi_a, wd_a), (wi_b, bi_b, wd_b)):
        hidden = gelu(mm(low, w_in[...]) + b_in[...]).astype(BF16)
        total = total + mm(hidden, w_down[...])
    unit, _ = norm_rows(total)
    out_ref[...] = (unit * two_ref[1:2, :] + two_ref[2:3, :]).astype(BF16)


def layer_next_kernel(*refs):
    layer_kernel(*refs[:-2], refs[-1])


def layer(line, tokens, contexts, w_out, w_in, b_in, w_down, one, two, seq, mixed, hint):
    length, inner = contexts[0].shape
    width, hidden = tokens.shape[1], w_in[0].shape[1]
    tile = 256
    steps = length // tile
    ctx = pl.BlockSpec((tile, inner), lambda i: (i, 0))
    still = [*w_out, *w_in, *b_in, *w_down, one, two]
    row = pl.BlockSpec((tile, width), lambda i: (seq * steps + i, 0))
    args = [tokens, *contexts, *still]
    specs = [row, ctx, ctx] + [whole(item.shape, True) for item in still]
    (result,) = line.run(
        layer_kernel if mixed is None else layer_next_kernel,
        args if mixed is None else [*args, mixed],
        [shaped(tokens.shape, BF16)],
        grid=(steps,),
        in_specs=specs if mixed is None else [*specs, ANYWHERE],
        out_specs=[row],
        aliases={} if mixed is None else {len(args): 0},
        room=30,
        hint=hint,
        flops=2 * length * width * (width + 4 * hidden),
        moved=4 * width * (length + 2 * hidden),
        transcendentals=2 * length * hidden,
    )
    return result


def input_grad_kernel(
    dkv_a, dkv_b, dq_a, dq_b, w_a, w_b, g_first_ref, places_ref, out_ref
):
    length = out_ref.shape[0]
    slots = g_first_ref.shape[0]
    few = g_first_ref[...] + dot_nt(dq_a[...], w_a[0]) + dot_nt(dq_b[...], w_b[0])
    coarse = few.astype(BF16)
    fine = (few - coarse.astype(F32)).astype(BF16)
    picks = places_ref[0][:, 0:1] == lax.broadcasted_iota(jnp.int32, (slots, length), 1)
    picks = picks.astype(F32).astype(BF16)
    total = dot_tn(picks, coarse) + dot_tn(picks, fine)
    for dkv, w in ((dkv_a, w_a), (dkv_b, w_b)):
        inner = w.shape[2]
        total = total + dot_nt(dkv[:, :inner], w[1]) + dot_nt(dkv[:, inner:], w[2])
    out_ref[...] = total


def input_grad_next_kernel(*refs):
    input_grad_kernel(*refs[:-2], refs[-1])


def input_grad(line, backs, weights, g_first, places, seqs, seq, before):
    rows, inner = backs[0][1].shape[0], backs[0][0].shape[1]
    width = g_first.shape[1]
    length, slots = rows // seqs, g_first.shape[0] // seqs
    long = pl.BlockSpec((length, 2 * inner), lambda i: (seq, 0))
    short = pl.BlockSpec((slots, inner), lambda i: (seq, 0))
    args = [
        backs[0][1], backs[1][1], backs[0][0], backs[1][0],
        *weights, g_first, places,
    ]
    specs = (
        [long] * 2
        + [short] * 2
        + [whole(w.shape, True) for w in weights]
        + [
            pl.BlockSpec((slots, width), lambda i: (seq, 0)),
            pl.BlockSpec((1, slots, LANES), lambda i: (seq, 0, 0)),
        ]
    )
    (result,) = line.run(
        input_grad_kernel if before is None else input_grad_next_kernel,
        args if before is None else [*args, before],
        [shaped((rows, width), F32)],
        grid=(1,),
        in_specs=specs if before is None else [*specs, ANYWHERE],
        out_specs=[pl.BlockSpec((length, width), lambda i: (seq, 0))],
        aliases={} if before is None else {len(args): 0},
        flops=10 * length * width * inner,
        moved=20 * width * inner + 8 * length * width,
        room=24,
        hint=0.1,
    )
    return result


def pick_kernel(seqs, half_ref, starts_ref, tok_ref, grad_ref, few_ref, grad_few_ref, turned_ref, places_ref):
    slots, length = few_ref.shape[0], tok_ref.shape[0]
    spans = starts_ref.shape[1]
    seq = half_ref[0] * seqs + pl.program_id(0)
    starts = [starts_ref[seq, at] for at in range(spans)]
    row = lax.broadcasted_iota(jnp.int32, (slots, LANES), 0)
    places = row + starts[0]
    for at in range(1, spans):
        places = places + jnp.where(row >= SPAN * at, starts[at] - starts[at - 1] - SPAN, 0)
    fresh = row < SPAN * spans
    for at, start in enumerate(starts):
        covered = (places >= start) & (places < start + SPAN) & (row >= SPAN * (at + 1))
        fresh = fresh & jnp.logical_not(covered)
    places_ref[0] = places
    wide = jnp.concatenate([places] * (length // LANES), axis=1)
    picks = wide == lax.broadcasted_iota(jnp.int32, (slots, length), 1)
    picks = picks.astype(F32).astype(BF16)
    few_ref[...] = mm(picks, tok_ref[...]).astype(BF16)
    grad_few_ref[...] = mm(picks, grad_ref[...]) * fresh.astype(F32)[:, 0:1]
    turned_ref[...] = tok_ref[...].T


def pick(line, half, starts, slots, tokens, grads, seqs, after):
    rows, width = tokens.shape
    length = rows // seqs
    long = pl.BlockSpec((length, width), lambda s, p: (s, 0))
    short = pl.BlockSpec((slots, width), lambda s, p: (s, 0))
    return line.run(
        functools.partial(pick_kernel, seqs),
        [starts, tokens, grads],
        [
            shaped((seqs * slots, width), BF16),
            shaped((seqs * slots, width), F32),
            shaped((width, rows), BF16),
            shaped((seqs, slots, LANES), jnp.int32),
        ],
        grid=(seqs,),
        in_specs=[pl.BlockSpec(memory_space=pltpu.SMEM), long, long],
        out_specs=[
            short, short, pl.BlockSpec((width, length), lambda s, p: (0, s)),
            pl.BlockSpec((1, slots, LANES), lambda s, p: (s, 0, 0)),
        ],
        place=half,
        flops=4 * rows * slots * width,
        moved=6 * rows * width,
        room=ROOM_PICK,
        after=after,
    )


def body(
    tokens,
    grad_values,
    span_starts,
    w_qkv,
    b_qv,
    w_out,
    b_out,
    ln1_gain,
    ln1_bias,
    w_in,
    b_in,
    w_down,
    b_down,
    ln2_gain,
    ln2_bias,
):
    rows, width = tokens.shape
    inner = w_qkv.shape[2]
    hidden_half = w_in.shape[1]
    halves = lax.axis_size("tensor")
    seqs = span_starts.shape[0] // halves
    spans = span_starts.shape[1]
    length = rows // seqs
    half_at = lax.axis_index("tensor")
    me = lax.axis_index("dp")
    bits = lax.axis_size("dp").bit_length() - 1
    block_at = ((me & 1) << 3) | ((me & 2) << 1) | ((me & 4) >> 1) | ((me & 8) >> 3)
    place = block_at.reshape(1).astype(jnp.int32)
    rest = [1 << bit for bit in range(4, bits)]

    slots = -(-spans * SPAN // 16) * 16
    here = me.reshape(1)
    line = Line()

    w_qkv_own = jnp.transpose(w_qkv, (1, 0, 2))

    def chips_around(held):
        return [held, flip(held, 2), flip(held, 4), flip(held, 6)]

    arrived_qkv = flip_tensor(cut_qkv(line, w_qkv_own, here))
    half_out, eighth, vectors_one, vectors_two, b_in = second_cut(
        line, w_out, w_in, w_down, b_qv, b_in,
        [b_out, ln1_gain, ln1_bias, b_down, ln2_gain, ln2_bias], here,
    )
    around_qkv = chips_around(arrived_qkv)
    arrived_out, arrived_eighth = flip_tensor(half_out), flip_tensor(eighth)
    tokens_few, grad_few, tokens_t, places = pick(
        line, half_at.reshape(1), span_starts, slots, tokens, grad_values, seqs, [arrived_qkv]
    )
    own = project(line, tokens, tokens_few, w_qkv_own, b_qv, seqs)
    def attend_own(seq, hint=None):
        return attend(line, tokens, w_qkv_own, b_qv, own[0], own[1], seqs, seq, hint)

    core_first, half_in, b_qv_oth, b_in_oth = third_cut(
        line, around_qkv, arrived_out, w_in, here, [arrived_eighth]
    )
    b_qv_both, b_in_both = [b_qv, b_qv_oth], [b_in, b_in_oth]
    near_first = flip(core_first, 1)
    around_eighth = chips_around(arrived_eighth)
    arrived_in = flip_tensor(half_in)
    w_qkv_oth, w_out_oth = first_assemble(line, core_first, near_first, width, inner, here)
    w_qkv_both, w_out_both = [w_qkv_own, w_qkv_oth], [w_out, w_out_oth]
    oth = project(line, tokens, tokens_few, w_qkv_oth, b_qv_both[1], seqs)

    keys, values, queries_few, context_few = zip(own, oth)
    sum_few, normed_low = first_norm(line, context_few, w_out_both, tokens_few, vectors_one)

    def plane(values):
        return [values, flip_tensor(values), flip(values, 2), flip_both(values, 2)]

    slope_own, part = ffn_part(line, normed_low, w_in, b_in_both[0], w_down)
    core_second = fourth_cut(line, around_eighth, [arrived_in])
    near_second, near_in = flip(core_second, 1), flip(arrived_in, 1)
    around_normed = plane(normed_low)
    w_in_oth, w_down_oth = second_assemble(
        line, core_second, near_second, arrived_in, near_in, hidden_half, here
    )
    w_in_both, w_down_both = [w_in, w_in_oth], [w_down, w_down_oth]
    g_ffn, g_second, slope_oth, sums = ffn_last(
        line, normed_low, part, sum_few, grad_few, vectors_one, vectors_two,
        w_in_both[1], b_in_both[1], w_down_both[1],
    )
    around_g = plane(g_ffn)
    g_branch, g_first, small_few = ffn_back(
        line, g_ffn, g_second, sum_few, vectors_one, sums, (slope_own, slope_oth), w_in_both, w_down_both
    )
    core_normed = join(line, around_normed)
    near_normed = flip(core_normed, 1)

    def back(at):
        return attend_back(
            line, place, queries_few[at], keys[at], values[at], g_branch, w_out_both[at],
            context_few[at], tokens_t, tokens_few, small_few, seqs, at, hidden_half // inner,
        )

    back_oth = back(1)
    near_oth = flip(back_oth[3], 1)
    core_g = join(line, around_g)
    near_g = flip(core_g, 1)
    back_own = back(0)
    near_own = flip(back_own[3], 1)
    keep_down, send_down, keep_in, send_in = ffn_grads(
        line, place, w_in, w_down, b_in_both[0], [core_normed, near_normed], [core_g, near_g]
    )
    z_down, z_in = flip(send_down, 4), flip(send_in, 8)
    x_send, y_send, x_keep, y_own, y_oth = cross_one(
        line, back_oth[2], near_oth, back_own[2], near_own, 112
    )
    x_near, y_near = flip_tensor(x_send), flip(y_send, 2)

    def attend_oth(seq, hint):
        return attend(
            line, tokens, w_qkv_oth, b_qv_both[1], keys[1], values[1], seqs, seq, hint
        )

    def over_rest_f32(total):
        return over_rest(total.astype(F32)) if rest else total

    def over_rest(total):
        for bit in rest:
            total = total + flip(total, bit)
        return total

    def layer_of(seq, mixed, hint):
        return layer(
            line, tokens, [ctx_own[seq], ctx_oth[seq]], w_out_both, w_in_both, b_in_both, w_down_both,
            vectors_one, vectors_two, seq, mixed, hint,
        )

    def input_grad_of(seq, before):
        return input_grad(line, [back_own, back_oth], w_qkv_both, g_first, places, seqs, seq, before)

    ctx_oth = [attend_oth(seq, 0.1) for seq in range(seqs)]
    ctx_own = [attend_own(seq, 0.1) for seq in range(1, seqs)]
    y_send, x_send, first, last = cross_two(line, x_keep, x_near, y_own, y_oth, y_near, H[0])
    y_near, x_near = flip(y_send, 2), flip_tensor(x_send)
    down, keep_in, send_in = second_fold(line, keep_down, z_down, keep_in, z_in, H[1])
    near_down, z_in = flip(down, 8), flip(send_in, 4)
    keep, *sends = cross_three(line, first, y_near, last, x_near, H[2])
    z_attn = [flip(send, 4) for send in sends]
    up = sum_all(line, H[3], over_rest(keep_in), over_rest(z_in))
    near_up = flip(up, 8)
    ctx_own.insert(0, attend_own(0, 0.1))
    d_tokens = None
    for seq in range(seqs):
        d_tokens = input_grad_of(seq, d_tokens)

    attn = sum_all(line, H[5], keep, *z_attn)
    near_attn = flip(attn, 8)
    down, up = third_fold(line, over_rest_f32(down), over_rest_f32(near_down), up, near_up, H[4])
    near_down, near_up = flip(down, 4), flip(up, 2)
    mixed = layer_of(0, None, 0.1)
    upper, lower = sum_split(line, H[7], over_rest_f32(attn), over_rest_f32(near_attn), width // 8)
    near_upper, near_lower = flip(upper, 4), flip(lower, 2)
    down, up = append(line, H[6], [down, near_down], [up, near_up])
    near_down, near_up = flip(down, 2), flip(up, 4)
    for seq in range(1, seqs):
        mixed = layer_of(seq, mixed, H[8])
    (upper,) = append(line, 1.5, [upper, near_upper])
    (lower,) = append(line, 1.5, [lower, near_lower])
    near_upper, near_lower = flip(upper, 2), flip(lower, 4)
    down, up = append(line, 1, [down, near_down], [up, near_up])
    near_down, near_up = flip(down, 1), flip(up, 1)
    ffn_sums = unpack_ffn(line, place, down, up, width, hidden_half)
    (upper,) = append(line, 1, [upper, near_upper])
    (lower,) = append(line, 1, [lower, near_lower])
    far_upper, far_lower = flip(upper, 1), flip(lower, 1)
    d_w_down, d_w_in = unpack_ffn(line, place, near_down, near_up, width, hidden_half, ffn_sums)
    d_w_qkv, d_w_out, *small = unpack_attend(line, place, [upper, lower, far_upper, far_lower], width, hidden_half)
    d_w_qkv = jnp.transpose(d_w_qkv, (1, 0, 2))
    d_b_qv, d_b_in, d_b_out, d_ln1_gain, d_ln1_bias, d_b_down, d_ln2_gain, d_ln2_bias = small

    return (
        mixed,
        d_tokens,
        d_w_qkv,
        d_b_qv,
        d_w_out,
        d_b_out,
        d_ln1_gain,
        d_ln1_bias,
        d_w_in,
        d_b_in,
        d_w_down,
        d_b_down,
        d_ln2_gain,
        d_ln2_bias,
    )


def solution(mesh):
    placed = (
        P(("dp", "tensor"), None),
        P(("dp", "tensor"), None),
        P("dp", None),
        P(None, None, "tensor"),
        P(None, "tensor"),
        P("tensor", None),
        P(),
        P(),
        P(),
        P(None, "tensor"),
        P("tensor"),
        P("tensor", None),
        P(),
        P(),
        P(),
    )
    return jax.shard_map(
        body,
        mesh=mesh,
        in_specs=placed,
        out_specs=(
            P(("dp", "tensor"), None),
            P(("dp", "tensor"), None),
            P(None, None, "tensor"),
            P(None, "tensor"),
            P("tensor", None),
            P(),
            P(),
            P(),
            P(None, "tensor"),
            P("tensor"),
            P("tensor", None),
            P(),
            P(),
            P(),
        ),
        check_vma=False,
    )
```

```python
import functools

import jax
import jax.numpy as jnp
from jax import lax
from jax.experimental import pallas as pl
from jax.experimental.pallas import tpu as pltpu
from jax.sharding import PartitionSpec as P

HEAD = 64
SPAN = 6
LANES = 128
EPSILON = 1e-05
F32 = jnp.float32
BF16 = jnp.bfloat16
GELU_A = (2.0 / 3.141592653589793) ** 0.5
GELU_B = 0.044715
ROOM_CUT, ROOM_PICK = 56, 24
HINT_GRADS, HINT_BACK = 15, 10
H = (0.2, 1, 0.5, 0.1, 0.3, 0.3, 1, 0.3, 0.3)
BYTES_US = 11_070_000
FLOPS_US = 3_459_000_000
ANYWHERE = pl.BlockSpec(memory_space=pl.ANY)
VMEM = pl.BlockSpec(memory_space=pltpu.VMEM)


class Line:
    def __init__(self):
        self.last = []

    def run(
        self, kernel, args, out_shape, grid=(), in_specs=None, out_specs=None, scratch=(), place=None,
        flops=0, moved=0, transcendentals=0, room=6, aliases=None, hint=None, after=(),
    ):
        ins, outs = len(args), len(out_shape)
        lead = 0 if place is None else 1
        after = list(after)
        if self.last and not any(arg is item for arg in args for item in self.last):
            after.append(min(self.last, key=lambda item: item.size))
        extra = len(after)
        small = min(item.size for item in out_shape) > 1 << 16

        def ordered(*refs):
            given, rest = refs[: lead + ins], refs[lead + ins + extra :]
            if small:
                rest[outs][...] = jnp.zeros((8, LANES), F32)
                rest = rest[:outs] + rest[outs + 1 :]
            kernel(*given, *rest)

        in_specs = list(in_specs or [VMEM] * ins) + [ANYWHERE] * extra
        out_specs = list(out_specs or [VMEM] * outs)
        out_shape = list(out_shape)
        if small:
            out_specs.append(pl.BlockSpec((8, LANES), lambda *at: (0, 0)) if grid else VMEM)
            out_shape.append(jax.ShapeDtypeStruct((8, LANES), F32))
        params = dict(
            out_shape=out_shape,
            compiler_params=pltpu.CompilerParams(vmem_limit_bytes=room << 20),
            cost_estimate=pl.CostEstimate(
                flops=int(flops if hint is None else hint * FLOPS_US),
                bytes_accessed=int(moved if hint is None else hint * BYTES_US),
                transcendentals=int(transcendentals if hint is None else 0),
            ),
            input_output_aliases=aliases or {},
        )
        if lead and grid:
            params["grid_spec"] = pltpu.PrefetchScalarGridSpec(
                num_scalar_prefetch=1, grid=grid, in_specs=in_specs, out_specs=out_specs, scratch_shapes=list(scratch)
            )
        else:
            if lead:
                in_specs = [pl.BlockSpec(memory_space=pltpu.SMEM)] + in_specs
            params.update(grid=grid, in_specs=in_specs, out_specs=out_specs, scratch_shapes=list(scratch))
        front = [] if place is None else [place]
        self.last = list(pl.pallas_call(ordered, **params)(*front, *args, *after))
        return self.last[:outs]


def shaped(shape, kind):
    return jax.ShapeDtypeStruct(tuple(shape), kind)


def whole(shape, once=False):
    held = dict(pipeline_mode=pl.Buffered(1)) if once else {}
    return pl.BlockSpec(shape, lambda *at: (0,) * len(shape), **held)


def flip(values, bits):
    size = lax.axis_size("dp")
    return lax.ppermute(values, "dp", [(at, at ^ bits) for at in range(size)])


def flip_tensor(values):
    return lax.ppermute(values, "tensor", [(0, 1), (1, 0)])


def flip_both(values, bits):
    size = 2 * lax.axis_size("dp")
    pairs = [(at, at ^ (2 * bits + 1)) for at in range(size)]
    return lax.ppermute(values, ("dp", "tensor"), pairs)


def dot_nt(left, right):
    return lax.dot_general(left, right, (((1,), (1,)), ((), ())), preferred_element_type=F32)


def dot_tn(left, right):
    return lax.dot_general(left, right, (((0,), (0,)), ((), ())), preferred_element_type=F32)


def mm(left, right):
    return jnp.dot(left, right, preferred_element_type=F32)


def lane_halves(rows):
    return lax.broadcasted_iota(jnp.int32, (rows, LANES), 1) < HEAD


def two_heads(block):
    low = lane_halves(block.shape[0])
    zero = jnp.zeros_like(block)
    return jnp.concatenate([jnp.where(low, block, zero), jnp.where(low, zero, block)], axis=0)


def scaled(queries):
    return queries * jnp.asarray(HEAD ** (-0.5), BF16)


def softmax_rows(scores):
    exponent = jnp.exp(scores - jnp.max(scores, axis=-1, keepdims=True))
    return exponent * (1.0 / jnp.sum(exponent, axis=-1, keepdims=True))


def attend_block(queries, keys, values):
    rows = queries.shape[0]
    probs = softmax_rows(dot_nt(two_heads(scaled(queries)), keys)).astype(BF16)
    mixed = mm(probs, values)
    return jnp.where(lane_halves(rows), mixed[:rows], mixed[rows:]).astype(BF16)


def norm_rows(values):
    average = jnp.mean(values, axis=-1, keepdims=True)
    centered = values - average
    variance = jnp.mean(centered * centered, axis=-1, keepdims=True)
    root = lax.rsqrt(variance + EPSILON)
    return centered * root, root


def norm_back(grad, unit, root, gain):
    grad_y = grad * gain
    inner = jnp.mean(grad_y, axis=-1, keepdims=True)
    along = jnp.mean(grad_y * unit, axis=-1, keepdims=True)
    return root * (grad_y - inner - unit * along)


def gelu_and_slope(values):
    square = values * values
    bent = jnp.tanh(GELU_A * values * (1.0 + GELU_B * square))
    half = 0.5 * (1.0 + bent)
    slope = half + 0.5 * values * (1.0 - bent * bent) * GELU_A * (1.0 + 3.0 * GELU_B * square)
    return values * half, slope


def gelu(values):
    return 0.5 * values * (1.0 + jnp.tanh(GELU_A * values * (1.0 + GELU_B * values * values)))


def join_kernel(count, *refs):
    rows = refs[0].shape[-2]
    for at in range(count):
        refs[count][..., at * rows : (at + 1) * rows, :] = refs[at][...]


def join(line, pieces):
    *lead, rows, columns = pieces[0].shape
    (result,) = line.run(
        functools.partial(join_kernel, len(pieces)),
        pieces,
        [shaped((*lead, rows * len(pieces), columns), pieces[0].dtype)],
        moved=4 * len(pieces) * pieces[0].size,
    )
    return result


def cut_qkv_kernel(place_ref, in_ref, out_ref, sem):
    rows = out_ref.shape[1]
    row = pl.multiple_of((place_ref[0] & 7) * rows, rows)
    copy = pltpu.make_async_copy(in_ref.at[:, pl.ds(row, rows), :], out_ref, sem)
    copy.start()
    copy.wait()


def cut_qkv(line, w_qkv, here):
    lead, rows, columns = w_qkv.shape
    (piece,) = line.run(
        cut_qkv_kernel,
        [w_qkv],
        [shaped((lead, rows // 8, columns), BF16)],
        in_specs=[ANYWHERE],
        scratch=[pltpu.SemaphoreType.DMA],
        place=here,
        moved=w_qkv.size // 2,
        room=ROOM_CUT,
    )
    return piece


def folded(rows, columns, width):
    tall = rows * columns // width
    rest, side = rows - tall, width - columns
    parts = [((0, tall, 0, columns), (0, tall, 0, columns))]
    for at in range(columns // side):
        parts.append(((at * rest, rest, columns, side), (tall, rest, at * side, side)))
    return tall, parts


def second_cut_kernel(place_ref, out_ref, in_ref, down_ref, bias_a, bias_b, *refs):
    vectors, (half, eighth, one, two, row_ref) = refs[:6], refs[6:]
    deep, width = out_ref.shape
    half[:deep, :] = out_ref[...]
    row_ref[0, :] = bias_b[...]
    left = jnp.concatenate(
        [jnp.concatenate([bias_a[0:1, :], bias_a[1:2, :]], axis=1)]
        + [row_ref[:, at : at + width] for at in range(0, row_ref.shape[1], width)],
        axis=0,
    )
    parts = []
    for _ in range(3):
        coarse = left.astype(BF16).astype(F32)
        parts.append(coarse)
        left = left - coarse
    parts.append(jnp.zeros((half.shape[0] - deep - 3 * left.shape[0], width), F32))
    half[deep:, :] = jnp.concatenate(parts, axis=0).astype(BF16)
    tall, parts = folded(*in_ref.shape, eighth.shape[1])
    for (row, high, column, wide), (top, _, side, _) in parts:
        eighth[row : row + high, column : column + wide] = in_ref[top : top + high, side : side + wide]
    eighth[tall:, :] = down_ref[...]
    for at in range(3):
        one[at, :] = vectors[at][...]
        two[at, :] = vectors[3 + at][...]


def second_cut(line, w_out, w_in, w_down, b_qv, b_in, vectors, here):
    width = w_out.shape[1]
    half, rows, deep = w_out.shape[0] // 2, w_in.shape[0] // 8, w_down.shape[0] // 8
    last = w_in.shape[1] // 4
    eighth = folded(rows, last, width)[0]
    shapes = [(half + 16, width), (eighth + deep, width), (3, width), (3, width), (1, b_in.shape[0])]
    return line.run(
        second_cut_kernel,
        [w_out, w_in, w_down, b_qv, b_in, *vectors],
        [shaped(shape, BF16 if at < 2 else F32) for at, shape in enumerate(shapes)],
        grid=(1,),
        in_specs=[
            pl.BlockSpec((half, width), lambda i, p: (p[0] & 1, 0)),
            pl.BlockSpec((rows, last), lambda i, p: (p[0] & 7, 3)),
            pl.BlockSpec((deep, width), lambda i, p: (p[0] & 7, 0)),
            whole(b_qv.shape),
            whole(b_in.shape),
            *[whole((width,)) for vector in vectors],
        ],
        out_specs=[whole(shape) for shape in shapes],
        place=here,
        moved=4 * (half + eighth + deep) * width,
        room=ROOM_CUT,
    )


def third_cut_kernel(place_ref, a, b, c, d, out_ref, in_ref, core, half, bias_a, bias_b):
    third, rows, inner = a.shape
    for at, ref in enumerate((a, b, c, d)):
        for section in range(third):
            row = (section * 4 + at) * rows
            core[row : row + rows, :] = ref[section]
    row = 4 * third * rows
    deep = out_ref.shape[0] - 16
    core[row : row + deep, :] = out_ref[:deep, :inner]
    core[row + deep :, :] = out_ref[:deep, inner:]
    half[...] = in_ref[...]
    parts = out_ref[deep:, :].astype(F32)
    width = parts.shape[1]
    count = 1 + bias_b.shape[1] // width
    total = parts[2 * count : 3 * count] + parts[count : 2 * count] + parts[:count]
    bias_a[0:1, :] = total[0:1, :inner]
    bias_a[1:2, :] = total[0:1, inner:]
    for at in range(count - 1):
        bias_b[:, at * width : (at + 1) * width] = total[1 + at : 2 + at, :]


def third_cut(line, qkv, out, w_in, here, after):
    third, rows, inner = qkv[0].shape
    height = 4 * third * rows + 2 * (out.shape[0] - 16)
    half = (w_in.shape[0] // 2, w_in.shape[1] // 4 * 3)
    shapes = [(height, inner), half, (2, inner), (1, w_in.shape[1])]
    return line.run(
        third_cut_kernel,
        [*qkv, out, w_in],
        [shaped(shape, BF16 if at < 2 else F32) for at, shape in enumerate(shapes)],
        grid=(1,),
        in_specs=[whole(item.shape) for item in [*qkv, out]]
        + [pl.BlockSpec(half, lambda i, p: (p[0] & 1, 0))],
        out_specs=[whole(shape) for shape in shapes],
        place=here,
        moved=4 * (height * inner + half[0] * half[1]),
        after=after,
    )


def first_assemble_kernel(place_ref, mine, near, qkv_ref, out_ref):
    third, width, inner = qkv_ref.shape
    rows, half = width // 8, out_ref.shape[0] // 2
    for core, ref in enumerate((mine, near)):
        for at in range(4):
            row = pl.multiple_of(((place_ref[0] ^ (2 * at + core)) & 7) * rows, rows)
            for section in range(third):
                start = (section * 4 + at) * rows
                qkv_ref[section, pl.ds(row, rows), :] = ref[start : start + rows, :]
        row = pl.multiple_of(((place_ref[0] ^ core) & 1) * half, half)
        start = 4 * third * rows
        out_ref[pl.ds(row, half), :inner] = ref[start : start + half, :]
        out_ref[pl.ds(row, half), inner:] = ref[start + half :, :]


def first_assemble(line, mine, near, width, inner, here):
    return line.run(
        first_assemble_kernel,
        [mine, near],
        [shaped((3, width, inner), BF16), shaped((inner, width), BF16)],
        place=here,
        moved=8 * mine.size,
    )


def fourth_cut_kernel(a, b, c, d, eighths):
    rows = a.shape[0]
    for at, ref in enumerate((a, b, c, d)):
        eighths[at * rows : (at + 1) * rows, :] = ref[...]


def fourth_cut(line, eighths, after):
    rows, width = eighths[0].shape
    (result,) = line.run(
        fourth_cut_kernel,
        eighths,
        [shaped((4 * rows, width), BF16)],
        moved=16 * rows * width,
        after=after,
    )
    return result


def second_assemble_kernel(core, place_ref, ref, half_ref, *refs):
    in_ref, down_ref = refs[-2:]
    width = ref.shape[1]
    wide, last = half_ref.shape[1], in_ref.shape[1] - half_ref.shape[1]
    rows, deep, half = in_ref.shape[0] // 8, down_ref.shape[0] // 8, half_ref.shape[0]
    tall, parts = folded(rows, last, width)
    for at in range(4):
        block = (place_ref[0] ^ (2 * at + core)) & 7
        start = at * (tall + deep)
        for (row, high, column, side), (top, _, left, _) in parts:
            to = pl.multiple_of(block * rows + top, 16)
            in_ref[pl.ds(to, high), wide + left : wide + left + side] = ref[
                start + row : start + row + high, column : column + side
            ]
        down_ref[pl.ds(pl.multiple_of(block * deep, deep), deep), :] = ref[
            start + tall : start + tall + deep, :
        ]
    row = pl.multiple_of(((place_ref[0] ^ core) & 1) * half, half)
    in_ref[pl.ds(row, half), :wide] = half_ref[...]


def second_assemble(line, core, pieces, half, hidden, here, before=()):
    width = pieces.shape[1]
    return line.run(
        functools.partial(second_assemble_kernel, core),
        [pieces, half, *before],
        [shaped((width, hidden), BF16), shaped((hidden, width), BF16)],
        aliases={3: 0, 4: 1} if before else {},
        place=here,
        hint=0.3,
    )


def project_kernel(tok_ref, few_ref, w_ref, bias_ref, k_ref, v_ref, q_ref, ctx_ref):
    tok = tok_ref[...]
    k_ref[...] = mm(tok, w_ref[1]).astype(BF16)
    v_ref[...] = (mm(tok, w_ref[2]) + bias_ref[1:2, :]).astype(BF16)
    q_ref[...] = (mm(few_ref[...], w_ref[0]) + bias_ref[0:1, :]).astype(BF16)
    for at in range(0, k_ref.shape[1], LANES):
        cut = slice(at, at + LANES)
        ctx_ref[:, cut] = attend_block(q_ref[:, cut], k_ref[:, cut], v_ref[:, cut])


def project(line, tokens, few, weights, bias, seqs):
    rows, width = tokens.shape
    inner = weights.shape[2]
    length, slots = rows // seqs, few.shape[0] // seqs
    long, short = (pl.BlockSpec((size, inner), lambda s: (s, 0)) for size in (length, slots))
    return line.run(
        project_kernel,
        [tokens, few, weights, bias],
        [shaped((rows, inner), BF16)] * 2 + [shaped((few.shape[0], inner), BF16)] * 2,
        grid=(seqs,),
        in_specs=[
            pl.BlockSpec((length, width), lambda s: (s, 0)),
            pl.BlockSpec((slots, width), lambda s: (s, 0)),
            whole(weights.shape),
            whole(bias.shape),
        ],
        out_specs=[long, long, short, short],
        flops=6 * rows * width * inner,
        room=16,
        moved=2 * (rows * width + 3 * width * inner + 2 * rows * inner),
    )


def first_norm_kernel(ctx_a, ctx_b, w_a, w_b, few_ref, vec_ref, sum_ref, low_ref):
    branch = mm(ctx_a[...], w_a[...]) + mm(ctx_b[...], w_b[...]) + vec_ref[0:1, :]
    total = few_ref[...].astype(F32) + branch
    sum_ref[...] = total
    low_ref[...] = (norm_rows(total)[0] * vec_ref[1:2, :] + vec_ref[2:3, :]).astype(BF16)


def first_norm(line, contexts, w_out, few, vectors):
    count, width = few.shape
    return line.run(
        first_norm_kernel,
        [*contexts, *w_out, few, vectors],
        [shaped((count, width), F32), shaped((count, width), BF16)],
        flops=2 * count * width * width,
        moved=2 * width * width + 14 * count * width,
    )


def ffn_part_kernel(low_ref, wi_ref, bi_ref, wd_ref, slope_ref, part_ref, total):
    step = pl.program_id(0)
    gate, slope = gelu_and_slope(mm(low_ref[...], wi_ref[...]) + bi_ref[...])
    slope_ref[...] = slope
    part = mm(gate.astype(BF16), wd_ref[...])

    @pl.when(step == 0)
    def _():
        total[...] = part

    @pl.when(step > 0)
    def _():
        total[...] += part

    @pl.when(step == pl.num_programs(0) - 1)
    def _():
        part_ref[...] = total[...]


def ffn_part(line, low, w_in, b_in, w_down):
    count, width = low.shape
    hidden = w_in.shape[1]
    steps = 4
    tile = hidden // steps
    flat = whole((count, width))
    return line.run(
        ffn_part_kernel,
        [low, w_in, b_in, w_down],
        [shaped((count, hidden), F32), shaped((count, width), F32)],
        grid=(steps,),
        in_specs=[
            flat,
            pl.BlockSpec((width, tile), lambda j: (0, j)),
            pl.BlockSpec((1, tile), lambda j: (0, j)),
            pl.BlockSpec((tile, width), lambda j: (j, 0)),
        ],
        out_specs=[pl.BlockSpec((count, tile), lambda j: (0, j)), flat],
        scratch=[pltpu.VMEM((count, width), F32)],
        flops=4 * count * width * hidden,
        moved=4 * width * hidden,
        transcendentals=count * hidden,
        room=12,
    )


def column_sum(values):
    return jnp.sum(values, axis=0, keepdims=True)


def ffn_last_kernel(
    low_ref, part_ref, sum_ref, grad_ref, one_ref, two_ref, wi_ref, bi_ref, wd_ref,
    g_ffn_ref, g_second_ref, slope_ref, sums_ref,
):
    gate, slope = gelu_and_slope(mm(low_ref[...], wi_ref[...]) + bi_ref[...])
    slope_ref[...] = slope
    ffn = part_ref[...] + mm(gate.astype(BF16), wd_ref[...]) + two_ref[0:1, :]
    normed = norm_rows(sum_ref[...])[0] * one_ref[1:2, :] + one_ref[2:3, :]
    unit, root = norm_rows(normed + ffn)
    grad = grad_ref[...]
    g_second = norm_back(grad, unit, root, two_ref[1:2, :])
    g_ffn = g_second.astype(BF16)
    g_ffn_ref[...] = g_ffn
    g_second_ref[...] = g_second
    sums = (column_sum(g_ffn.astype(F32)), column_sum(grad * unit), column_sum(grad))
    sums_ref[...] = jnp.concatenate([*sums, jnp.zeros((5, grad.shape[1]), F32)], axis=0)


def ffn_last(line, low, part, total, grad, one, two, w_in, b_in, w_down):
    count, width = low.shape
    hidden = w_in.shape[1]
    return line.run(
        ffn_last_kernel,
        [low, part, total, grad, one, two, w_in, b_in, w_down],
        [
            shaped((count, width), BF16),
            shaped((count, width), F32),
            shaped((count, hidden), F32),
            shaped((8, width), F32),
        ],
        flops=4 * count * width * hidden,
        moved=4 * width * hidden,
        room=12,
    )


def ffn_back_kernel(
    g_ffn_ref, g_second_ref, sum_ref, one_ref, sums_ref, slope_a, slope_b, wi_a, wi_b, wd_a, wd_b,
    g_branch_ref, g_first_ref, small_ref,
):
    g_ffn, g_normed = g_ffn_ref[...], g_second_ref[...]
    width = g_normed.shape[1]
    half = width // 2
    deep = slope_a.shape[1] // half
    for at, (slope, w_in, w_down) in enumerate(((slope_a, wi_a, wd_a), (slope_b, wi_b, wd_b))):
        g_pre = (slope[...] * dot_nt(g_ffn, w_down[...])).astype(BF16)
        bias = column_sum(g_pre.astype(F32))
        for row in range(deep):
            small_ref[at * deep + row : at * deep + row + 1, :] = bias[:, row * half : (row + 1) * half]
        g_normed = g_normed + dot_nt(g_pre, w_in[...])
    unit, root = norm_rows(sum_ref[...])
    g_first = norm_back(g_normed, unit, root, one_ref[1:2, :])
    g_branch = g_first.astype(BF16)
    g_first_ref[...] = g_first
    g_branch_ref[...] = g_branch
    vectors = (
        column_sum(g_branch.astype(F32)),
        column_sum(g_normed * unit),
        column_sum(g_normed),
        *[sums_ref[at : at + 1, :] for at in range(3)],
    )
    for at, vector in enumerate(vectors):
        row = 2 * deep + 2 * at
        small_ref[row : row + 1, :] = vector[:, :half]
        small_ref[row + 1 : row + 2, :] = vector[:, half:]
    count = 2 * deep + 12
    small_ref[count:, :] = jnp.zeros((small_ref.shape[0] - count, half), F32)


def ffn_back(line, g_ffn, g_second, total, one, sums, slopes, w_in, w_down):
    count, width = g_ffn.shape
    hidden = w_in[0].shape[1]
    rows = 2 * (hidden // (width // 2)) + 12
    return line.run(
        ffn_back_kernel,
        [g_ffn, g_second, total, one, sums, *slopes, *w_in, *w_down],
        [
            shaped((count, width), BF16),
            shaped((count, width), F32),
            shaped((-(-rows // 8) * 8, width // 2), F32),
        ],
        flops=8 * count * width * hidden,
        moved=8 * width * hidden,
        room=12,
    )


def ffn_grads_kernel(place_ref, wi_ref, wd_ref, bi_ref, *refs):
    normed_refs, grad_refs = refs[:2], refs[2:4]
    keep_down, send_down, keep_in, send_in = refs[4:8]
    down, up = refs[8:]
    width = normed_refs[0].shape[1]
    tile = wi_ref.shape[1] // 4
    hidden = pl.ds(pl.multiple_of((place_ref[0] >> 2) * tile, tile), tile)
    w_in, w_down, b_in = wi_ref[:, hidden], wd_ref[hidden, :], bi_ref[:, hidden]
    for at in range(2):
        normed, grad = normed_refs[at][...], grad_refs[at][...]
        gate, slope = gelu_and_slope(mm(normed, w_in) + b_in)
        pre = (slope * dot_nt(grad, w_down)).astype(BF16)
        down_part = dot_tn(gate.astype(BF16), grad)
        up_part = dot_tn(normed, pre)
        if at == 0:
            down[...] = down_part
            up[...] = up_part
        else:
            down[...] += down_part
            up[...] += up_part
    down_rows, up_rows = tile // 4, width // 4
    half = width // 2
    for slot in range(4):
        block = slot ^ (place_ref[0] & 3)
        low = down[pl.ds(pl.multiple_of(block * down_rows, down_rows), down_rows), :]
        block = (0, 2, 1, 3)[slot] ^ (place_ref[0] & 3)
        high = up[pl.ds(pl.multiple_of(block * up_rows, up_rows), up_rows), :]
        to_down, to_in = (keep_down, keep_in) if slot < 2 else (send_down, send_in)
        kind = to_down.dtype
        to_down[slot % 2, :down_rows, :] = low[:, :half].astype(kind)
        to_down[slot % 2, down_rows:, :] = low[:, half:].astype(kind)
        to_in[slot % 2, :, :] = high.astype(kind)


def ffn_grads(line, place, w_in, w_down, b_in, normed, grads):
    rows, width = normed[0].shape
    tile = w_in.shape[1] // 4
    shape = (2, 2 * (tile // 4), width // 2)
    wide = (2, width // 4, tile)
    return line.run(
        ffn_grads_kernel,
        [w_in, w_down, b_in, *normed, *grads],
        [shaped(shape, F32), shaped(shape, BF16), shaped(wide, F32), shaped(wide, BF16)],
        scratch=[pltpu.VMEM((tile, width), F32), pltpu.VMEM((width, tile), F32)],
        place=place,
        flops=16 * rows * width * tile,
        moved=12 * rows * width + 16 * width * tile,
        hint=HINT_GRADS,
        room=16,
    )


def attend_back_kernel(
    seqs, half, deep, place_ref, q_ref, k_ref, v_ref, g_branch_ref, w_out_ref, ctx_ref, tok_t_ref, few_ref,
    small_ref, dq_ref, dkv_ref, keep_ref, send_ref, total, little,
):
    few, inner = q_ref.shape
    rows = k_ref.shape[0]
    slots, length = few // seqs, rows // seqs
    low = lane_halves(slots)
    scale = HEAD ** (-0.5)
    g_branch = g_branch_ref[...]
    g_context = dot_nt(g_branch, w_out_ref[...]).astype(BF16)
    for seq in range(seqs):
        short, long = slice(seq * slots, (seq + 1) * slots), slice(seq * length, (seq + 1) * length)
        for at in range(0, inner, LANES):
            cut = slice(at, at + LANES)
            both, grads = two_heads(scaled(q_ref[short, cut])), two_heads(g_context[short, cut])
            keys, values = k_ref[long, cut], v_ref[long, cut]
            scores = dot_nt(keys, both)
            exponent = jnp.exp(scores - jnp.max(scores, axis=0, keepdims=True))
            probs = exponent * (1.0 / jnp.sum(exponent, axis=0, keepdims=True))
            grad_probs = dot_nt(values, grads)
            dkv_ref[long, inner + at : inner + at + LANES] = mm(probs.astype(BF16), grads).astype(BF16)
            slot_total = jnp.sum(grad_probs * probs, axis=0, keepdims=True)
            grad_scores = (probs * (grad_probs - slot_total)).astype(BF16)
            dq = dot_tn(grad_scores, keys) * scale
            dq_ref[short, cut] = jnp.where(low, dq[:slots], dq[slots:]).astype(BF16)
            dkv_ref[long, cut] = mm(grad_scores, both).astype(BF16)
    dq, dkv = dq_ref[...], dkv_ref[...]
    total[0] = dot_tn(few_ref[...], dq)
    both = mm(tok_t_ref[...], dkv)
    total[1] = both[:, :inner]
    total[2] = both[:, inner:]
    out_grad = dot_tn(ctx_ref[...], g_branch)
    total[3, :inner, :] = out_grad[:, :inner]
    total[3, inner:, :] = out_grad[:, inner:]
    little[...] = jnp.zeros_like(little)
    little[0, 0:1, :] = column_sum(dq.astype(F32))
    little[0, 1:2, :] = column_sum(dkv[:, inner:].astype(F32))
    for at in range(deep + 12):
        source = half * deep + at if at < deep else deep + at
        little[1 + at // 2, at % 2 : at % 2 + 1, :] = small_ref[source : source + 1, :]
    block_rows = total.shape[1] // 16
    pad = keep_ref.shape[1] - 4 * block_rows
    for slot in range(16):
        block = slot ^ place_ref[0]
        row = pl.multiple_of(block * block_rows, block_rows)
        to, kind = (keep_ref, F32) if slot < 8 else (send_ref, BF16)
        for section in range(4):
            cut = slice(section * block_rows, (section + 1) * block_rows)
            to[slot % 8, cut, :] = total[section, pl.ds(row, block_rows), :].astype(kind)
        pair = jnp.concatenate([little[block], jnp.zeros((pad - 8, inner), F32)], axis=0)
        to[slot % 8, 4 * block_rows :, :] = pair.astype(kind)


def attend_back(line, place, queries, keys, values, g_branch, w_out, context, tokens_t, few, small, seqs, half, deep):
    rows, inner = keys.shape
    width = tokens_t.shape[0]
    count = queries.shape[0]
    held = (8, 4 * (width // 16) + 16, inner)
    return line.run(
        functools.partial(attend_back_kernel, seqs, half, deep),
        [queries, keys, values, g_branch, w_out, context, tokens_t, few, small],
        [
            shaped((count, inner), BF16),
            shaped((rows, 2 * inner), BF16),
            shaped(held, F32),
            shaped(held, BF16),
        ],
        scratch=[pltpu.VMEM((4, width, inner), F32), pltpu.VMEM((16, 8, inner), F32)],
        place=place,
        hint=HINT_BACK,
        room=16,
        flops=4 * rows * width * inner + 24 * count * rows * inner,
        moved=20 * rows * inner,
    )


def sum_all_kernel(count, keep_ref, *refs):
    row = 0
    for ref in refs[:count]:
        part = slice(row, row + ref.shape[0])
        refs[count][part] = (keep_ref[part].astype(F32) + ref[...].astype(F32)).astype(BF16)
        row += ref.shape[0]


def sum_all(line, hint, keep, *arrived):
    (result,) = line.run(
        functools.partial(sum_all_kernel, len(arrived)), [keep, *arrived], [shaped(keep.shape, BF16)], hint=hint
    )
    return result


def sum_split_kernel(mine_ref, near_ref, upper, lower):
    rows = upper.shape[1]
    for slot in range(2):
        total = (mine_ref[slot].astype(F32) + near_ref[1 - slot].astype(F32)).astype(BF16)
        upper[slot] = total[:rows, :]
        lower[slot] = total[rows:, :]


def sum_split(line, hint, mine, near, rows):
    count, height, inner = mine.shape
    shapes = [shaped((count, rows, inner), BF16), shaped((count, height - rows, inner), BF16)]
    return line.run(sum_split_kernel, [mine, near], shapes, hint=hint)


def second_fold_kernel(down, down_near, up, up_near, down_out, up_keep, up_send):
    down_out[...] = (down[...] + down_near[...].astype(F32)).astype(BF16)
    total = up[...] + up_near[...].astype(F32)
    middle = total.shape[0] // 2
    up_keep[...] = total[:middle]
    up_send[...] = total[middle:].astype(BF16)


def second_fold(line, down, down_near, up, up_near, hint):
    half = (up.shape[0] // 2, *up.shape[1:])
    return line.run(
        second_fold_kernel,
        [down, down_near, up, up_near],
        [shaped(down.shape, BF16), shaped(half, F32), shaped(half, BF16)],
        hint=hint,
    )


def third_fold_kernel(down, down_near, up, up_near, down_out, up_out):
    for slot in range(2):
        down_out[slot] = (down[slot].astype(F32) + down_near[1 - slot].astype(F32)).astype(BF16)
    count = up.shape[0]
    up_out[:count] = up[...]
    up_out[count:] = up_near[...]


def third_fold(line, down, down_near, up, up_near, hint):
    shapes = [shaped(down.shape, BF16), shaped((2 * up.shape[0], *up.shape[1:]), BF16)]
    return line.run(third_fold_kernel, [down, down_near, up, up_near], shapes, hint=hint)


def append_kernel(count, *refs):
    groups, out = refs[:-count], refs[-count:]
    each = len(groups) // count
    for at in range(count):
        row = 0
        for ref in groups[at * each : (at + 1) * each]:
            out[at][row : row + ref.shape[0]] = ref[...]
            row += ref.shape[0]


def append(line, hint, *groups):
    shapes = [shaped((sum(item.shape[0] for item in group), *group[0].shape[1:]), BF16) for group in groups]
    return line.run(
        functools.partial(append_kernel, len(groups)),
        [item for group in groups for item in group],
        shapes,
        hint=hint,
    )


def cross_one_kernel(oth, oth_near, own, own_near, x_send, y_send, x_keep, y_keep_own, y_keep_oth):
    rows = x_send.shape[1]
    half = oth.shape[0] // 2
    x_send[...] = (oth[:, :rows, :] + oth_near[:, :rows, :].astype(F32)).astype(BF16)
    x_keep[...] = own[:, :rows, :] + own_near[:, :rows, :].astype(F32)
    for at, (keep, near, out) in enumerate(((own, own_near, y_keep_own), (oth, oth_near, y_keep_oth))):
        total = keep[:, rows:, :] + near[:, rows:, :].astype(F32)
        out[...] = total[:half]
        y_send[at] = total[half:].astype(BF16)


def cross_one(line, oth, oth_near, own, own_near, rows):
    count, height, inner = oth.shape
    half, last = count // 2, height - rows
    return line.run(
        cross_one_kernel,
        [oth, oth_near, own, own_near],
        [
            shaped((count, rows, inner), BF16),
            shaped((2, half, last, inner), BF16),
            shaped((count, rows, inner), F32),
            shaped((half, last, inner), F32),
            shaped((half, last, inner), F32),
        ],
        hint=2,
    )


def cross_two_kernel(x_keep, x_near, own, oth, y_near, y_send, x_send, first, last):
    half = own.shape[0]
    total = x_keep[...] + x_near[...].astype(F32)
    first[...] = total[:half]
    y_send[...] = total[half:].astype(BF16)
    total = own[...] + y_near[0].astype(F32)
    small = total.shape[1] - 16
    last[:, :small, :] = total[:, :small, :]
    last[:, small:, :] = total[:, small:, :].astype(BF16).astype(F32)
    x_send[...] = (oth[...] + y_near[1].astype(F32)).astype(BF16)


def cross_two(line, x_keep, x_near, own, oth, y_near, hint):
    half = (own.shape[0], x_keep.shape[1], x_keep.shape[2])
    return line.run(
        cross_two_kernel,
        [x_keep, x_near, own, oth, y_near],
        [shaped(half, BF16), shaped(own.shape, BF16), shaped(half, F32), shaped(own.shape, F32)],
        hint=hint,
    )


def cross_three_kernel(first, y_near, last, x_near, keep, *sends):
    rows, half = first.shape[1], first.shape[0] // 2
    for ref, near, cut in ((first, y_near, slice(0, rows)), (last, x_near, slice(rows, None))):
        total = ref[...] + near[...].astype(F32)
        keep[:, cut, :] = total[:half]
        for at, send in enumerate(sends):
            send[:, cut, :] = total[half + at : half + at + 1].astype(BF16)


def cross_three(line, first, y_near, last, x_near, hint):
    half, height, inner = first.shape[0] // 2, first.shape[1] + last.shape[1], first.shape[2]
    return line.run(
        cross_three_kernel,
        [first, y_near, last, x_near],
        [shaped((half, height, inner), F32)] + [shaped((1, height, inner), BF16)] * half,
        hint=hint,
    )


def unpack_attend_kernel(place_ref, *refs):
    blocks, (qkv_ref, out_ref), (wide, little, sems) = refs[:4], refs[4:6], refs[-3:]
    outs = refs[6:-3]
    inner = qkv_ref.shape[2]
    rows = qkv_ref.shape[1] // 16
    copies = []

    def place_rows(source, to):
        copy = pltpu.make_async_copy(source, to, sems.at[len(copies)])
        copy.start()
        copies.append(copy)

    for slot in range(16):
        core, at = slot // 8, slot % 8
        block = slot ^ place_ref[0]
        wide[slot, : 2 * rows, :] = blocks[2 * core][at].astype(F32)
        row = pl.multiple_of(block * rows, rows)
        for section in range(2):
            place_rows(wide.at[slot, pl.ds(section * rows, rows), :], qkv_ref.at[section, pl.ds(row, rows), :])
        block = ((at & 1) + (at & 2) * 2 + (at >> 2) * 2 + 8 * core) ^ place_ref[0]
        values = blocks[2 * core + 1][at].astype(F32)
        wide[slot, 2 * rows :, :] = values[: 2 * rows, :]
        little[block] = values[2 * rows : 2 * rows + 8, :]
        row = pl.multiple_of(block * rows, rows)
        place_rows(wide.at[slot, pl.ds(2 * rows, rows), :], qkv_ref.at[2, pl.ds(row, rows), :])
        row = pl.multiple_of((block & 7) * rows, rows)
        column = pl.multiple_of((block >> 3) * inner, inner)
        place_rows(wide.at[slot, pl.ds(3 * rows, rows), :], out_ref.at[pl.ds(row, rows), pl.ds(column, inner)])
    outs[0][...] = little[0, 0:2, :]
    row = 2
    for out in outs[1:]:
        for at in range(out.shape[0] // inner):
            out[pl.ds(at * inner, inner)] = little[row // 2, row % 2, :]
            row += 1
    for copy in copies:
        copy.wait()


def unpack_attend(line, place, blocks, width, hidden):
    inner = blocks[0].shape[2]
    rows = width // 16
    small = [(2, inner), (hidden,)] + [(width,)] * 6
    return line.run(
        unpack_attend_kernel,
        blocks,
        [shaped((3, width, inner), F32), shaped((inner, width), F32)] + [shaped(shape, F32) for shape in small],
        out_specs=[ANYWHERE] * 2 + [VMEM] * 8,
        scratch=[
            pltpu.VMEM((16, 4 * rows, inner), F32),
            pltpu.VMEM((16, 8, inner), F32),
            pltpu.SemaphoreType.DMA((64,)),
        ],
        place=place,
        room=20,
        hint=1,
    )


def unpack_ffn_kernel(first, place_ref, *refs):
    down_in, up_in = refs[:2]
    down_ref, in_ref, down, up, sems = refs[-5:]
    rows, half = down_ref.shape[0] // 16, down_ref.shape[1] // 2
    deep, wide = in_ref.shape[0] // 4, in_ref.shape[1] // 4
    copies = []

    def place_rows(source, to):
        copy = pltpu.make_async_copy(source, to, sems.at[len(copies)])
        copy.start()
        copies.append(copy)

    for slot in range(8):
        block = (slot if first else slot + 8) ^ place_ref[0]
        down[slot, :, :half] = down_in[slot, :rows, :].astype(F32)
        down[slot, :, half:] = down_in[slot, rows:, :].astype(F32)
        row = pl.multiple_of(block * rows, rows)
        place_rows(down.at[slot], down_ref.at[pl.ds(row, rows), :])
        block = ((slot & 1) + (slot & 2) * 2 + (slot >> 2) * 2 + (0 if first else 8)) ^ place_ref[0]
        up[slot] = up_in[slot].astype(F32)
        row = pl.multiple_of((block & 3) * deep, deep)
        column = pl.multiple_of((block >> 2) * wide, wide)
        place_rows(up.at[slot], in_ref.at[pl.ds(row, deep), pl.ds(column, wide)])
    for copy in copies:
        copy.wait()


def unpack_ffn(line, place, down, up, width, hidden, before=None):
    return line.run(
        functools.partial(unpack_ffn_kernel, before is None),
        [down, up, *(before or [])],
        [shaped((hidden, width), F32), shaped((width, hidden), F32)],
        in_specs=[VMEM] * 2 + [ANYWHERE] * (0 if before is None else 2),
        out_specs=[ANYWHERE] * 2,
        scratch=[
            pltpu.VMEM((8, hidden // 16, width), F32),
            pltpu.VMEM((8, width // 4, hidden // 4), F32),
            pltpu.SemaphoreType.DMA((16,)),
        ],
        aliases={} if before is None else {3: 0, 4: 1},
        place=place,
        moved=6 * width * hidden,
        room=20,
        hint=1,
    )


def attend_kernel(tok_ref, w_ref, bias_ref, k_ref, v_ref, out_ref):
    rows, inner = out_ref.shape
    low = lane_halves(rows)
    queries = scaled((mm(tok_ref[...], w_ref[0]) + bias_ref[0:1, :]).astype(BF16))
    for at in range(0, inner, LANES):
        cut = slice(at, at + LANES)
        block, keys, values = queries[:, cut], k_ref[:, cut], v_ref[:, cut]
        zero, one = jnp.zeros_like(block), jnp.ones_like(values)
        mixed = []
        for first in (True, False):
            head = jnp.where(low == first, block, zero)
            with_sums = jnp.where(lane_halves(values.shape[0]) == first, values, one)
            scores = dot_nt(head, keys)
            exponent = jnp.exp(scores - jnp.max(scores, axis=-1, keepdims=True)).astype(BF16)
            mixed.append(mm(exponent, with_sums))
        top = jnp.where(low, mixed[0], mixed[1])
        total = jnp.where(low, mixed[1], mixed[0])
        out_ref[:, cut] = (top / pltpu.roll(total, HEAD, 1)).astype(BF16)


def attend(line, tokens, weights, bias, keys, values, seqs, seq, hint=None):
    rows, width = tokens.shape
    inner = keys.shape[1]
    length = rows // seqs
    long = pl.BlockSpec((length, inner), lambda s: (seq, 0))
    (result,) = line.run(
        attend_kernel,
        [tokens, weights, bias, keys, values],
        [shaped((length, inner), BF16)],
        grid=(1,),
        in_specs=[
            pl.BlockSpec((length, width), lambda s: (seq, 0)),
            pl.BlockSpec((1, width, inner), lambda s: (0, 0, 0)),
            whole(bias.shape),
            long,
            long,
        ],
        out_specs=[pl.BlockSpec((length, inner), lambda s: (0, 0))],
        flops=2 * length * width * inner + 16 * length * length * inner,
        moved=2 * (length * width + width * inner + 3 * length * inner),
        transcendentals=length * length * inner // HEAD,
        room=16,
        hint=hint,
    )
    return result


def layer_kernel(
    tok_ref, ctx_a, ctx_b, wo_a, wo_b, wi_a, wi_b, bi_a, bi_b, wd_a, wd_b, one_ref, two_ref, out_ref,
):
    branch = mm(ctx_a[...], wo_a[...]) + mm(ctx_b[...], wo_b[...]) + one_ref[0:1, :]
    unit, _ = norm_rows(tok_ref[...].astype(F32) + branch)
    normed = unit * one_ref[1:2, :] + one_ref[2:3, :]
    low = normed.astype(BF16)
    total = normed + two_ref[0:1, :]
    for w_in, b_in, w_down in ((wi_a, bi_a, wd_a), (wi_b, bi_b, wd_b)):
        hidden = gelu(mm(low, w_in[...]) + b_in[...]).astype(BF16)
        total = total + mm(hidden, w_down[...])
    unit, _ = norm_rows(total)
    out_ref[...] = (unit * two_ref[1:2, :] + two_ref[2:3, :]).astype(BF16)


def layer_next_kernel(*refs):
    layer_kernel(*refs[:-2], refs[-1])


def layer(line, tokens, contexts, w_out, w_in, b_in, w_down, one, two, seq, mixed, hint):
    length, inner = contexts[0].shape
    width, hidden = tokens.shape[1], w_in[0].shape[1]
    tile = 256
    steps = length // tile
    ctx = pl.BlockSpec((tile, inner), lambda i: (i, 0))
    still = [*w_out, *w_in, *b_in, *w_down, one, two]
    row = pl.BlockSpec((tile, width), lambda i: (seq * steps + i, 0))
    args = [tokens, *contexts, *still]
    specs = [row, ctx, ctx] + [whole(item.shape, True) for item in still]
    (result,) = line.run(
        layer_kernel if mixed is None else layer_next_kernel,
        args if mixed is None else [*args, mixed],
        [shaped(tokens.shape, BF16)],
        grid=(steps,),
        in_specs=specs if mixed is None else [*specs, ANYWHERE],
        out_specs=[row],
        aliases={} if mixed is None else {len(args): 0},
        room=30,
        hint=hint,
        flops=2 * length * width * (width + 4 * hidden),
        moved=4 * width * (length + 2 * hidden),
        transcendentals=2 * length * hidden,
    )
    return result


def input_grad_kernel(
    dkv_a, dkv_b, dq_a, dq_b, w_a, w_b, g_first_ref, places_ref, out_ref
):
    length = out_ref.shape[0]
    slots = g_first_ref.shape[0]
    few = g_first_ref[...] + dot_nt(dq_a[...], w_a[0]) + dot_nt(dq_b[...], w_b[0])
    coarse = few.astype(BF16)
    fine = (few - coarse.astype(F32)).astype(BF16)
    picks = places_ref[0][:, 0:1] == lax.broadcasted_iota(jnp.int32, (slots, length), 1)
    picks = picks.astype(F32).astype(BF16)
    total = dot_tn(picks, coarse) + dot_tn(picks, fine)
    for dkv, w in ((dkv_a, w_a), (dkv_b, w_b)):
        inner = w.shape[2]
        total = total + dot_nt(dkv[:, :inner], w[1]) + dot_nt(dkv[:, inner:], w[2])
    out_ref[...] = total


def input_grad_next_kernel(*refs):
    input_grad_kernel(*refs[:-2], refs[-1])


def input_grad(line, backs, weights, g_first, places, seqs, seq, before):
    rows, inner = backs[0][1].shape[0], backs[0][0].shape[1]
    width = g_first.shape[1]
    length, slots = rows // seqs, g_first.shape[0] // seqs
    long = pl.BlockSpec((length, 2 * inner), lambda i: (seq, 0))
    short = pl.BlockSpec((slots, inner), lambda i: (seq, 0))
    args = [
        backs[0][1], backs[1][1], backs[0][0], backs[1][0],
        *weights, g_first, places,
    ]
    specs = (
        [long] * 2
        + [short] * 2
        + [whole(w.shape, True) for w in weights]
        + [
            pl.BlockSpec((slots, width), lambda i: (seq, 0)),
            pl.BlockSpec((1, slots, LANES), lambda i: (seq, 0, 0)),
        ]
    )
    (result,) = line.run(
        input_grad_kernel if before is None else input_grad_next_kernel,
        args if before is None else [*args, before],
        [shaped((rows, width), F32)],
        grid=(1,),
        in_specs=specs if before is None else [*specs, ANYWHERE],
        out_specs=[pl.BlockSpec((length, width), lambda i: (seq, 0))],
        aliases={} if before is None else {len(args): 0},
        flops=10 * length * width * inner,
        moved=20 * width * inner + 8 * length * width,
        room=24,
        hint=0.1,
    )
    return result


def pick_kernel(seqs, half_ref, starts_ref, tok_ref, grad_ref, few_ref, grad_few_ref, turned_ref, places_ref):
    slots, length = few_ref.shape[0], tok_ref.shape[0]
    spans = starts_ref.shape[1]
    seq = half_ref[0] * seqs + pl.program_id(0)
    starts = [starts_ref[seq, at] for at in range(spans)]
    row = lax.broadcasted_iota(jnp.int32, (slots, LANES), 0)
    places = row + starts[0]
    for at in range(1, spans):
        places = places + jnp.where(row >= SPAN * at, starts[at] - starts[at - 1] - SPAN, 0)
    fresh = row < SPAN * spans
    for at, start in enumerate(starts):
        covered = (places >= start) & (places < start + SPAN) & (row >= SPAN * (at + 1))
        fresh = fresh & jnp.logical_not(covered)
    places_ref[0] = places
    wide = jnp.concatenate([places] * (length // LANES), axis=1)
    picks = wide == lax.broadcasted_iota(jnp.int32, (slots, length), 1)
    picks = picks.astype(F32).astype(BF16)
    few_ref[...] = mm(picks, tok_ref[...]).astype(BF16)
    grad_few_ref[...] = mm(picks, grad_ref[...]) * fresh.astype(F32)[:, 0:1]
    turned_ref[...] = tok_ref[...].T


def pick(line, half, starts, slots, tokens, grads, seqs, after):
    rows, width = tokens.shape
    length = rows // seqs
    long = pl.BlockSpec((length, width), lambda s, p: (s, 0))
    short = pl.BlockSpec((slots, width), lambda s, p: (s, 0))
    return line.run(
        functools.partial(pick_kernel, seqs),
        [starts, tokens, grads],
        [
            shaped((seqs * slots, width), BF16),
            shaped((seqs * slots, width), F32),
            shaped((width, rows), BF16),
            shaped((seqs, slots, LANES), jnp.int32),
        ],
        grid=(seqs,),
        in_specs=[pl.BlockSpec(memory_space=pltpu.SMEM), long, long],
        out_specs=[
            short, short, pl.BlockSpec((width, length), lambda s, p: (0, s)),
            pl.BlockSpec((1, slots, LANES), lambda s, p: (s, 0, 0)),
        ],
        place=half,
        flops=4 * rows * slots * width,
        moved=6 * rows * width,
        room=ROOM_PICK,
        after=after,
    )


def body(
    tokens,
    grad_values,
    span_starts,
    w_qkv,
    b_qv,
    w_out,
    b_out,
    ln1_gain,
    ln1_bias,
    w_in,
    b_in,
    w_down,
    b_down,
    ln2_gain,
    ln2_bias,
):
    rows, width = tokens.shape
    inner = w_qkv.shape[2]
    hidden_half = w_in.shape[1]
    halves = lax.axis_size("tensor")
    seqs = span_starts.shape[0] // halves
    spans = span_starts.shape[1]
    length = rows // seqs
    half_at = lax.axis_index("tensor")
    me = lax.axis_index("dp")
    bits = lax.axis_size("dp").bit_length() - 1
    block_at = ((me & 1) << 3) | ((me & 2) << 1) | ((me & 4) >> 1) | ((me & 8) >> 3)
    place = block_at.reshape(1).astype(jnp.int32)
    rest = [1 << bit for bit in range(4, bits)]

    slots = -(-spans * SPAN // 16) * 16
    here = me.reshape(1)
    line = Line()

    w_qkv_own = jnp.transpose(w_qkv, (1, 0, 2))

    def chips_around(held):
        return [held, flip(held, 2), flip(held, 4), flip(held, 6)]

    arrived_qkv = flip_tensor(cut_qkv(line, w_qkv_own, here))
    half_out, eighth, vectors_one, vectors_two, b_in = second_cut(
        line, w_out, w_in, w_down, b_qv, b_in,
        [b_out, ln1_gain, ln1_bias, b_down, ln2_gain, ln2_bias], here,
    )
    around_qkv = chips_around(arrived_qkv)
    arrived_out, arrived_eighth = flip_tensor(half_out), flip_tensor(eighth)
    tokens_few, grad_few, tokens_t, places = pick(
        line, half_at.reshape(1), span_starts, slots, tokens, grad_values, seqs, [arrived_qkv]
    )
    own = project(line, tokens, tokens_few, w_qkv_own, b_qv, seqs)
    def attend_own(seq, hint=None):
        return attend(line, tokens, w_qkv_own, b_qv, own[0], own[1], seqs, seq, hint)

    core_first, half_in, b_qv_oth, b_in_oth = third_cut(
        line, around_qkv, arrived_out, w_in, here, [arrived_eighth]
    )
    b_qv_both, b_in_both = [b_qv, b_qv_oth], [b_in, b_in_oth]
    near_first = flip(core_first, 1)
    around_eighth = chips_around(arrived_eighth)
    arrived_in = flip_tensor(half_in)
    w_qkv_oth, w_out_oth = first_assemble(line, core_first, near_first, width, inner, here)
    w_qkv_both, w_out_both = [w_qkv_own, w_qkv_oth], [w_out, w_out_oth]
    oth = project(line, tokens, tokens_few, w_qkv_oth, b_qv_both[1], seqs)

    keys, values, queries_few, context_few = zip(own, oth)
    sum_few, normed_low = first_norm(line, context_few, w_out_both, tokens_few, vectors_one)

    def plane(values):
        return [values, flip_tensor(values), flip(values, 2), flip_both(values, 2)]

    slope_own, part = ffn_part(line, normed_low, w_in, b_in_both[0], w_down)
    core_second = fourth_cut(line, around_eighth, [arrived_in])
    near_second, near_in = flip(core_second, 1), flip(arrived_in, 1)
    around_normed = plane(normed_low)
    half_done = second_assemble(line, 0, core_second, arrived_in, hidden_half, here)
    w_in_oth, w_down_oth = second_assemble(line, 1, near_second, near_in, hidden_half, here, half_done)
    w_in_both, w_down_both = [w_in, w_in_oth], [w_down, w_down_oth]
    g_ffn, g_second, slope_oth, sums = ffn_last(
        line, normed_low, part, sum_few, grad_few, vectors_one, vectors_two,
        w_in_both[1], b_in_both[1], w_down_both[1],
    )
    around_g = plane(g_ffn)
    g_branch, g_first, small_few = ffn_back(
        line, g_ffn, g_second, sum_few, vectors_one, sums, (slope_own, slope_oth), w_in_both, w_down_both
    )
    core_normed = join(line, around_normed)
    near_normed = flip(core_normed, 1)

    def back(at):
        return attend_back(
            line, place, queries_few[at], keys[at], values[at], g_branch, w_out_both[at],
            context_few[at], tokens_t, tokens_few, small_few, seqs, at, hidden_half // inner,
        )

    back_oth = back(1)
    near_oth = flip(back_oth[3], 1)
    core_g = join(line, around_g)
    near_g = flip(core_g, 1)
    back_own = back(0)
    near_own = flip(back_own[3], 1)
    keep_down, send_down, keep_in, send_in = ffn_grads(
        line, place, w_in, w_down, b_in_both[0], [core_normed, near_normed], [core_g, near_g]
    )
    z_down, z_in = flip(send_down, 4), flip(send_in, 8)
    x_send, y_send, x_keep, y_own, y_oth = cross_one(
        line, back_oth[2], near_oth, back_own[2], near_own, 112
    )
    x_near, y_near = flip_tensor(x_send), flip(y_send, 2)

    def attend_oth(seq, hint):
        return attend(
            line, tokens, w_qkv_oth, b_qv_both[1], keys[1], values[1], seqs, seq, hint
        )

    def over_rest_f32(total):
        return over_rest(total.astype(F32)) if rest else total

    def over_rest(total):
        for bit in rest:
            total = total + flip(total, bit)
        return total

    def layer_of(seq, mixed, hint):
        return layer(
            line, tokens, [ctx_own[seq], ctx_oth[seq]], w_out_both, w_in_both, b_in_both, w_down_both,
            vectors_one, vectors_two, seq, mixed, hint,
        )

    def input_grad_of(seq, before):
        return input_grad(line, [back_own, back_oth], w_qkv_both, g_first, places, seqs, seq, before)

    ctx_oth = [attend_oth(seq, 0.1) for seq in range(seqs)]
    ctx_own = [attend_own(seq, 0.1) for seq in range(1, seqs)]
    y_send, x_send, first, last = cross_two(line, x_keep, x_near, y_own, y_oth, y_near, H[0])
    y_near, x_near = flip(y_send, 2), flip_tensor(x_send)
    down, keep_in, send_in = second_fold(line, keep_down, z_down, keep_in, z_in, H[1])
    near_down, z_in = flip(down, 8), flip(send_in, 4)
    keep, *sends = cross_three(line, first, y_near, last, x_near, H[2])
    z_attn = [flip(send, 4) for send in sends]
    up = sum_all(line, H[3], over_rest(keep_in), over_rest(z_in))
    near_up = flip(up, 8)
    ctx_own.insert(0, attend_own(0, 0.1))
    d_tokens = None
    for seq in range(seqs):
        d_tokens = input_grad_of(seq, d_tokens)

    attn = sum_all(line, H[5], keep, *z_attn)
    near_attn = flip(attn, 8)
    down, up = third_fold(line, over_rest_f32(down), over_rest_f32(near_down), up, near_up, H[4])
    near_down, near_up = flip(down, 4), flip(up, 2)
    mixed = layer_of(0, None, 0.1)
    upper, lower = sum_split(line, H[7], over_rest_f32(attn), over_rest_f32(near_attn), width // 8)
    near_upper, near_lower = flip(upper, 4), flip(lower, 2)
    down, up = append(line, H[6], [down, near_down], [up, near_up])
    near_down, near_up = flip(down, 2), flip(up, 4)
    for seq in range(1, seqs):
        mixed = layer_of(seq, mixed, H[8])
    (upper,) = append(line, 1.5, [upper, near_upper])
    (lower,) = append(line, 1.5, [lower, near_lower])
    near_upper, near_lower = flip(upper, 2), flip(lower, 4)
    down, up = append(line, 1, [down, near_down], [up, near_up])
    near_down, near_up = flip(down, 1), flip(up, 1)
    ffn_sums = unpack_ffn(line, place, down, up, width, hidden_half)
    (upper,) = append(line, 1, [upper, near_upper])
    (lower,) = append(line, 1, [lower, near_lower])
    far_upper, far_lower = flip(upper, 1), flip(lower, 1)
    d_w_down, d_w_in = unpack_ffn(line, place, near_down, near_up, width, hidden_half, ffn_sums)
    d_w_qkv, d_w_out, *small = unpack_attend(line, place, [upper, lower, far_upper, far_lower], width, hidden_half)
    d_w_qkv = jnp.transpose(d_w_qkv, (1, 0, 2))
    d_b_qv, d_b_in, d_b_out, d_ln1_gain, d_ln1_bias, d_b_down, d_ln2_gain, d_ln2_bias = small

    return (
        mixed,
        d_tokens,
        d_w_qkv,
        d_b_qv,
        d_w_out,
        d_b_out,
        d_ln1_gain,
        d_ln1_bias,
        d_w_in,
        d_b_in,
        d_w_down,
        d_b_down,
        d_ln2_gain,
        d_ln2_bias,
    )


def solution(mesh):
    placed = (
        P(("dp", "tensor"), None),
        P(("dp", "tensor"), None),
        P("dp", None),
        P(None, None, "tensor"),
        P(None, "tensor"),
        P("tensor", None),
        P(),
        P(),
        P(),
        P(None, "tensor"),
        P("tensor"),
        P("tensor", None),
        P(),
        P(),
        P(),
    )
    return jax.shard_map(
        body,
        mesh=mesh,
        in_specs=placed,
        out_specs=(
            P(("dp", "tensor"), None),
            P(("dp", "tensor"), None),
            P(None, None, "tensor"),
            P(None, "tensor"),
            P("tensor", None),
            P(),
            P(),
            P(),
            P(None, "tensor"),
            P("tensor"),
            P("tensor", None),
            P(),
            P(),
            P(),
        ),
        check_vma=False,
    )
```
